32 devices in a mesh: lead: 4 (over x, core), lat: 2 (over y), lon: 4 (over z).
Axes of the slice: x: 2, y: 2, z: 4, core: 2. Of those that a mesh axis runs over, the one named last changes fastest.
Arguments:
- head_grads: bfloat16 [8, 8, 8, 128, 128], P('lead', None, 'lat', 'lon'), may hold values from -6 to 6
- head_weights: bfloat16 [8, 9, 256, 128], P('lead'), may hold values from -0.0625 to 0.0625
- encoder_input: bfloat16 [8, 8, 128, 128], P('lead', 'lat', 'lon'), may hold values from -6 to 6
- pre_first: bfloat16 [8, 8, 128, 256], P('lead', 'lat', 'lon'), may hold values from -8 to 8
- pre_second: bfloat16 [8, 8, 128, 256], P('lead', 'lat', 'lon'), may hold values from -8 to 8
- w_first: bfloat16 [9, 128, 256], replicated, may hold values from -0.1875 to 0.1875
- w_second: bfloat16 [9, 256, 256], replicated, may hold values from -0.125 to 0.125
Outputs:
- input_grad: bfloat16 [8, 8, 128, 128], P('lead', 'lat', 'lon')
- weight_grad_first: float32 [294912], P(('lat', 'lon'))
- weight_grad_second: float32 [589824], P(('lat', 'lon'))
The draws below stay inside these ranges and needn't reach their ends.
All inputs are finite; a program needn't handle non-finite values.
Results may differ from the reference program's by a relative error of at most 0.022.
Values may be sent and summed in bfloat16 or wider, within the bound.
No kernel may reach another device: no remote copies, remote signals or barrier semaphores. Data moves between devices by JAX's collectives and lax.ppermute only.
A program may use at most 64 MiB of HBM per device.

```python
import jax
import jax.numpy as jnp
from jax import lax

D = 256
HC = 128
C_IN = 128
HEAD_DEV = 2
HEADS = 8
BATCH = 8
ROWS = 8
COLS = 128
N_LEAD = 4


def level_of(key, dims, cuts, smallest, high):
    def one(dim, blocks):
        draws = jax.random.uniform(jax.random.fold_in(jax.random.fold_in(key, 6), dim), (blocks,), jnp.float32, smallest / len(cuts), high / len(cuts))
        return jnp.repeat(jnp.exp(draws), dims[dim] // blocks).reshape((-1,) + (1,) * (len(dims) - dim - 1))

    loudness = one(*cuts[0])
    for cut in cuts[1:]:
        loudness = loudness * one(*cut)
    return loudness


def bell_draw(rng, shape, spread, reach, cuts=(), dtype=jnp.bfloat16):
    factor_of = level_of(rng, shape, cuts, -0.22, 0.18) if cuts else 1.0
    values = jax.random.normal(rng, shape, jnp.float32) * spread * factor_of
    return jnp.minimum(jnp.maximum(values, -reach), reach).astype(dtype)


def setup_inputs(seed: int = 0) -> dict:
    splits = jax.random.split(jax.random.key(seed), 8)
    head_grads = bell_draw(splits[0], (HEADS, BATCH, ROWS, COLS, HC), 1.0, 6.0, ((0, 4), (2, 2), (3, 4)))
    head_weights = bell_draw(splits[1], (HEADS, 9, D, HC), (9 * HC * HEADS) ** -0.5, 0.0625, ((0, 4),))
    encoder_input = bell_draw(splits[2], (BATCH, ROWS, COLS, C_IN), 1.0, 6.0, ((0, 4), (1, 2), (2, 4)))
    pre_first = bell_draw(splits[3], (BATCH, ROWS, COLS, D), 1.5, 8.0, ((0, 4), (1, 2), (2, 4)))
    pre_second = bell_draw(splits[4], (BATCH, ROWS, COLS, D), 1.5, 8.0, ((0, 4), (1, 2), (2, 4)))
    w_first = bell_draw(splits[5], (9, C_IN, D), (9 * C_IN) ** -0.5, 0.1875)
    w_second = bell_draw(splits[6], (9, D, D), (9 * D) ** -0.5, 0.125)
    return {"head_grads": head_grads, "head_weights": head_weights, "encoder_input": encoder_input, "pre_first": pre_first, "pre_second": pre_second, "w_first": w_first, "w_second": w_second}


OFFSETS = [(-1, -1), (-1, 0), (-1, 1), (0, -1), (0, 0), (0, 1), (1, -1), (1, 0), (1, 1)]

def gelu_value(values):
    return 0.5 * values * (1.0 + lax.erf(values * 0.7071067811865476))

def gelu_slope(values):
    return 0.5 * (1.0 + lax.erf(values * 0.7071067811865476)) + values * jnp.exp(-0.5 * values * values) * 0.3989422804014327

def shifted(source, step_row, step_col):
    rolled = jnp.roll(source, -step_col, axis=source.ndim - 2)
    widths = [(0, 0)] * (source.ndim - 3) + [(1, 1), (0, 0), (0, 0)]
    padded = jnp.pad(rolled, widths)
    return lax.slice_in_dim(padded, 1 + step_row, 1 + step_row + ROWS, axis=source.ndim - 3)

def reference(head_grads, head_weights, encoder_input, pre_first, pre_second, w_first, w_second):
    grouped_grads = head_grads.reshape(N_LEAD, HEAD_DEV, BATCH, ROWS, COLS, HC)
    grouped_weights = head_weights.reshape(N_LEAD, HEAD_DEV, 9, D, HC)

    def add_group(carry, pair):
        grads_group, weights_group = pair
        summed = jnp.zeros((BATCH, ROWS, COLS, D), jnp.float32)
        for offset, (step_row, step_col) in enumerate(OFFSETS):
            moved = shifted(grads_group, -step_row, -step_col).astype(jnp.float32)
            summed = summed + jnp.einsum('hbrcj,hdj->brcd', moved, weights_group[:, offset].astype(jnp.float32))
        rounded = lax.optimization_barrier(summed.astype(jnp.bfloat16))
        return (carry + rounded.astype(jnp.float32), None)
    latent_grad, _ = lax.scan(add_group, jnp.zeros((BATCH, ROWS, COLS, D), jnp.float32), (grouped_grads, grouped_weights))
    pre_two = pre_second.astype(jnp.float32)
    pre_one = pre_first.astype(jnp.float32)
    da_second = (latent_grad * gelu_slope(pre_two)).astype(jnp.bfloat16)
    act_first = gelu_value(pre_one).astype(jnp.bfloat16)
    grad_second = []
    linear_first = jnp.zeros((BATCH, ROWS, COLS, D), jnp.float32)
    for offset, (step_row, step_col) in enumerate(OFFSETS):
        grad_second.append(jnp.einsum('brci,brcd->id', shifted(act_first, step_row, step_col).astype(jnp.float32), da_second.astype(jnp.float32)))
        linear_first = linear_first + jnp.einsum('brcd,id->brci', shifted(da_second, -step_row, -step_col).astype(jnp.float32), w_second[offset].astype(jnp.float32))
    da_first = (linear_first * gelu_slope(pre_one)).astype(jnp.bfloat16)
    grad_first = []
    input_sum = jnp.zeros((BATCH, ROWS, COLS, C_IN), jnp.float32)
    for offset, (step_row, step_col) in enumerate(OFFSETS):
        grad_first.append(jnp.einsum('brcj,brcd->jd', shifted(encoder_input, step_row, step_col).astype(jnp.float32), da_first.astype(jnp.float32)))
        input_sum = input_sum + jnp.einsum('brcd,jd->brcj', shifted(da_first, -step_row, -step_col).astype(jnp.float32), w_first[offset].astype(jnp.float32))
    input_grad = input_sum.astype(jnp.bfloat16)
    norm_factor = 1.0 / jnp.sqrt(jnp.float32(BATCH * ROWS * COLS))
    weight_grad_first = (jnp.stack(grad_first) * norm_factor).reshape(-1)
    weight_grad_second = (jnp.stack(grad_second) * norm_factor).reshape(-1)
    return (input_grad, weight_grad_first, weight_grad_second)
```

```python
import functools
import math

import jax
import jax.numpy as jnp
from jax import lax
from jax.experimental import pallas as pl
from jax.experimental.pallas import tpu as pltpu
from jax.sharding import PartitionSpec as P

BF = jnp.bfloat16
F32 = jnp.float32
STEPS = (-1, 0, 1)
EDGE = 4
LANES = 128
VMEM_BYTES = 24 * 1024 * 1024


def erf_part(values):
    return 0.5 * (1.0 + lax.erf(values * 0.7071067811865476))


def gelu_slope(values):
    return erf_part(values) + values * jnp.exp(-0.5 * values * values) * 0.3989422804014327


def gelu_value(values):
    return values * erf_part(values)


def dot_last(left, right):
    return lax.dot_general(left, right, (((1,), (1,)), ((), ())), preferred_element_type=F32)


def dot_plain(left, right):
    return lax.dot_general(left, right, (((1,), (0,)), ((), ())), preferred_element_type=F32)


def run(name, kernel, out_shape, arrays, scratch=(), scalars=None, flops=0):
    specs = [pl.BlockSpec(memory_space=pltpu.VMEM)] * len(arrays)
    if scalars is not None:
        specs = [pl.BlockSpec(memory_space=pltpu.SMEM)] + specs
        arrays = [scalars] + list(arrays)
    touched = sum(a.size * a.dtype.itemsize for a in arrays)
    touched += sum(math.prod(s.shape) * s.dtype.itemsize for s in out_shape)
    return pl.pallas_call(
        kernel,
        name=name,
        out_shape=out_shape,
        in_specs=specs,
        out_specs=[pl.BlockSpec(memory_space=pltpu.VMEM)] * len(out_shape),
        scratch_shapes=list(scratch),
        compiler_params=pltpu.CompilerParams(vmem_limit_bytes=VMEM_BYTES),
        cost_estimate=pl.CostEstimate(flops=flops, bytes_accessed=touched, transcendentals=0),
    )(*arrays)


def pack_kernel(grads_ref, second_ref, first_ref, right_ref, left_ref, edges, edges_wide, packed):
    heads, batch, height, breadth, _ = grads_ref.shape
    samples = second_ref.shape[0]
    rows = 6 * height
    for side, out_ref in ((0, right_ref), (1, left_ref)):
        start = breadth - 8 if side == 0 else 0
        for h in range(heads):
            for b in range(batch):
                block = grads_ref[h, b, :, start : start + 8, :].astype(F32)
                edges[(h * batch + b) * height * 8 : (h * batch + b + 1) * height * 8, :] = block.reshape(height * 8, LANES)
        for j, ref in enumerate((second_ref, first_ref)):
            for s in range(samples):
                block = ref[s, :, start : start + 8, :].astype(F32)
                at = (j * samples + s) * height * 8
                for half in range(2):
                    lanes = slice(half * LANES, (half + 1) * LANES)
                    edges_wide[half, at : at + height * 8, :] = block[:, :, lanes].reshape(height * 8, LANES)
        for b in range(batch):
            for col in range(3):
                inner = 5 + col if side == 0 else col
                for h in range(heads):
                    at = b * rows + (col * 2 + h) * height
                    packed[at : at + height, :] = edges[pl.ds((h * batch + b) * height * 8 + inner, height, stride=8), :]
        for s in range(samples):
            for q in range(3):
                j, col, width = (0, q, 2) if q < 2 else (1, 0, 1)
                inner = 8 - width + col if side == 0 else col
                for half in range(2):
                    at = (batch + s) * rows + (q * 2 + half) * height
                    packed[at : at + height, :] = edges_wide[
                        half, pl.ds((j * samples + s) * height * 8 + inner, height, stride=8), :
                    ]
        out_ref[...] = packed[...].astype(BF).reshape(out_ref.shape)


def pack(head_grads, pre_second, pre_first):
    heads, batch, height, _, _ = head_grads.shape
    samples = pre_second.shape[0]
    shape = jax.ShapeDtypeStruct((batch + samples, 6 * height, LANES), BF)
    return run(
        "pack_columns",
        pack_kernel,
        [shape, shape],
        [head_grads, pre_second, pre_first],
        [
            pltpu.VMEM((heads * batch * height * 8, LANES), F32),
            pltpu.VMEM((2, 2 * samples * height * 8, LANES), F32),
            pltpu.VMEM(((batch + samples) * 6 * height, LANES), F32),
        ],
    )


def heads_kernel(at_ref, grads_ref, low_ref, high_ref, weights_ref, out_ref, wide, shifted, total):
    heads, batch, height, breadth, _ = grads_ref.shape
    slots, _, kept, depth = out_ref.shape
    pitch = kept + 16
    own = 8 + EDGE
    for slot in range(slots):
        group = at_ref[1] if slot < slots // 2 else 1 - at_ref[1]
        b = (2 * group + at_ref[0]) * (slots // 2) + slot % (slots // 2)
        low = low_ref[b].astype(F32)
        high = high_ref[b].astype(F32)
        for r in range(height):
            at = (slot * height + r) * pitch + own
            for h in range(heads):
                wide[h, at : at + breadth, :] = grads_ref[h, b, r].astype(F32)
        for col in range(3):
            for h in range(heads):
                here = (col * 2 + h) * height
                at = slot * height * pitch + own + col
                wide[h, pl.ds(at - 3, height, stride=pitch), :] = low[here : here + height]
                wide[h, pl.ds(at + breadth, height, stride=pitch), :] = high[here : here + height]
        for v in STEPS:
            for h in range(heads):
                starts = [(slot * height + r) * pitch + 8 - v for r in range(height)]
                moved = jnp.concatenate([wide[h, at : at + kept, :] for at in starts], axis=0).astype(BF)
                lane = ((v + 1) * heads + h) * LANES
                shifted[slot * height * kept : (slot + 1) * height * kept, lane : lane + LANES] = moved
    total[:, height:, :, :] = jnp.zeros((slots, 2, kept, depth), F32)
    for u in STEPS:
        weights = jnp.concatenate(
            [weights_ref[h, 3 * (u + 1) + (v + 1)] for v in STEPS for h in range(heads)], axis=1
        )
        part = dot_last(shifted[...], weights).reshape(slots, height, kept, depth)
        if u == -1:
            total[:, :height] = part
        else:
            total[:, 1 + u : 1 + u + height] += part
    out_ref[...] = total[...].astype(BF)


def head_conv(scalars, head_grads, low, high, head_weights, samples):
    heads, batch, height, breadth, _ = head_grads.shape
    depth = head_weights.shape[2]
    kept = breadth + 2 * EDGE
    slots = 2 * samples
    return run(
        "head_conv",
        heads_kernel,
        [jax.ShapeDtypeStruct((slots, height + 2, kept, depth), BF)],
        [head_grads, low, high, head_weights],
        [
            pltpu.VMEM((heads, slots * height * (kept + 16), LANES), F32),
            pltpu.VMEM((slots * height * kept, 3 * heads * LANES), BF),
            pltpu.VMEM((slots, height + 2, kept, depth), F32),
        ],
        scalars,
        flops=2 * slots * height * kept * 9 * heads * LANES * depth,
    )[0]


def saved_kernel(second_ref, first_ref, input_ref, low_ref, high_ref, second_out, first_out, slope_second, slope_first, act_out, input_out, wide):
    samples, height, breadth, depth = second_ref.shape
    kept = breadth + 2 * EDGE
    batch = low_ref.shape[0] - samples
    for ref, width, out_ref, slope_ref in (
        (second_ref, 2, second_out, slope_second),
        (first_ref, 1, first_out, slope_first),
    ):
        wide[...] = jnp.zeros(wide.shape, F32)
        for s in range(samples):
            for r in range(height):
                at = (s * height + r) * kept + EDGE
                for half in range(2):
                    lanes = slice(half * LANES, (half + 1) * LANES)
                    wide[half, at : at + breadth, :] = ref[s, r, :, lanes].astype(F32)
            low = low_ref[batch + s].astype(F32)
            high = high_ref[batch + s].astype(F32)
            for col in range(width):
                for half in range(2):
                    here = ((col if width == 2 else 2) * 2 + half) * height
                    at = s * height * kept + EDGE + col
                    wide[half, pl.ds(at - width, height, stride=kept), :] = low[here : here + height]
                    wide[half, pl.ds(at + breadth, height, stride=kept), :] = high[here : here + height]
        value = jnp.concatenate([wide[0], wide[1]], axis=1)
        out_ref[...] = value.astype(BF).reshape(out_ref.shape)
        slope_ref[...] = gelu_slope(value).reshape(slope_ref.shape)
    active = gelu_value(first_ref[...].astype(F32).reshape(samples * height * breadth, depth)).astype(BF).astype(F32)
    act_out[...] = active.T.astype(BF)
    cells = input_ref[...].astype(F32).reshape(samples * height * breadth, input_ref.shape[3])
    input_out[...] = cells.T.astype(BF)


def saved(pre_second, pre_first, encoder_input, low, high):
    samples, height, breadth, depth = pre_second.shape
    kept = breadth + 2 * EDGE
    cells = samples * height * breadth
    return run(
        "saved_parts",
        saved_kernel,
        [
            jax.ShapeDtypeStruct((samples, height, kept, depth), BF),
            jax.ShapeDtypeStruct((samples, height, kept, depth), BF),
            jax.ShapeDtypeStruct((samples, height, kept, depth), F32),
            jax.ShapeDtypeStruct((samples, height, kept, depth), F32),
            jax.ShapeDtypeStruct((depth, cells), BF),
            jax.ShapeDtypeStruct((encoder_input.shape[3], cells), BF),
        ],
        [pre_second, pre_first, encoder_input, low, high],
        [pltpu.VMEM((2, samples * height * kept, LANES), F32)],
    )


def spread_kernel(at_ref, mine_ref, got_ref, second_ref, first_ref, own_ref, cross_ref, *strips):
    samples = own_ref.shape[0]
    height = second_ref.shape[1]
    total = mine_ref[...].astype(F32) + got_ref[...].astype(F32)
    total = total.astype(BF)
    own_ref[...] = total[:samples]
    cross_ref[...] = total[samples:]
    for way in range(len(strips) // 2):
        line_ref, corner_ref = strips[2 * way], strips[2 * way + 1]
        down = at_ref[way]
        line_ref[:, 0:3] = own_ref[:, pl.ds((height - 1) * down, 3)]
        corner_ref[...] = cross_ref[:, pl.ds((height - 1) * down, 3)]
        line_ref[:, 3:5] = second_ref[:, pl.ds((height - 2) * down, 2)]
        line_ref[:, 5:6] = first_ref[:, pl.ds((height - 1) * down, 1)]


def spread(scalars, mine, got, second, first, ways):
    slots, rows, kept, depth = mine.shape
    samples = slots // 2
    whole = jax.ShapeDtypeStruct((samples, rows, kept, depth), BF)
    strips = [
        jax.ShapeDtypeStruct((samples, 6, kept, depth), BF),
        jax.ShapeDtypeStruct((samples, 3, kept, depth), BF),
    ] * ways
    return run("core_sum", spread_kernel, [whole, whole] + strips, [mine, got, second, first], (), scalars)


def encoder_kernel(norm_factor, ways, at_ref, own_ref, cross_ref, *refs):
    strips, refs = refs[: 2 * ways], refs[2 * ways :]
    slope_second_ref, slope_first_ref, act_ref, input_ref, w_second_ref = refs[:5]
    moved_out, first_mine, first_other, second_mine, second_other = refs[5:10]
    latent, slope_second, slope_first, wide, cat, cat_own, wide_first = refs[10:]
    samples, rows, kept, depth = own_ref.shape
    height = rows - 2
    breadth = kept - 2 * EDGE
    lat, bands, core = at_ref[0], at_ref[1], at_ref[2]
    own = 8 + EDGE
    blank = jnp.zeros((samples, kept, depth), F32)
    latent[:, 0] = blank
    latent[:, height + 3] = blank
    latent[:, 1 : height + 3] = own_ref[...].astype(F32) + cross_ref[...].astype(F32)
    slope_second[:, 2 : 2 + height] = slope_second_ref[...]
    slope_first[:, 1 : 1 + height] = slope_first_ref[...]
    for way in range(ways):
        line_ref, corner_ref = strips[2 * way], strips[2 * way + 1]
        below = at_ref[3 + way]
        at = (height + 1) * below
        latent[:, pl.ds(at, 3)] += line_ref[:, 0:3].astype(F32) + corner_ref[...].astype(F32)
        slope_second[:, pl.ds((height + 2) * below, 2)] = gelu_slope(line_ref[:, 3:5].astype(F32))
        slope_first[:, pl.ds((height + 1) * below, 1)] = gelu_slope(line_ref[:, 5:6].astype(F32))
    for i in range(height + 4):
        row = lat * height + i - 2
        valid = jnp.logical_and(row >= 0, row < bands * height)
        value = latent[:, i] * slope_second[:, i]
        if i < 2 or i >= height + 2:
            value = jnp.where(valid, value, 0.0)
        wide[:, i, 8 : 8 + kept, :] = value.astype(BF).astype(F32)
    for v in STEPS:
        lanes = slice((v + 1) * depth, (v + 2) * depth)
        cat[:, :, :, lanes] = wide[:, :, 8 - v : 8 - v + kept + 8, :].astype(BF)
        cat_own[:, :, :, lanes] = wide[:, 1 : height + 3, own - v : own - v + breadth, :].astype(BF)
    linear = None
    for u in STEPS:
        weights = jnp.concatenate([w_second_ref[3 * (u + 1) + (v + 1)] for v in STEPS], axis=1)
        left = cat[:, 1 - u : 1 - u + rows].reshape(samples * rows * (kept + 8), 3 * depth)
        part = dot_last(left, weights)
        linear = part if linear is None else linear + part
    linear = linear.reshape(samples, rows, kept + 8, depth)
    for i in range(rows):
        row = lat * height + i - 1
        valid = jnp.logical_and(row >= 0, row < bands * height)
        value = linear[:, i, :kept] * slope_first[:, i]
        if i < 1 or i >= height + 1:
            value = jnp.where(valid, value, 0.0)
        wide_first[:, i, 8 : 8 + kept, :] = value.astype(BF).astype(F32)
    for v in STEPS:
        lanes = slice((v + 1) * depth, (v + 2) * depth)
        moved_out[:, :, :, lanes] = wide_first[:, :, own - v : own - v + breadth, :].astype(BF)
    for left_ref, source, mine_ref, other_ref in (
        (input_ref, moved_out, first_mine, first_other),
        (act_ref, cat_own, second_mine, second_other),
    ):
        for u in STEPS:
            right = source[:, 1 - u : 1 - u + height].reshape(samples * height * breadth, 3 * depth)
            part = dot_plain(left_ref[...], right) * norm_factor
            for v in STEPS:
                k = 3 * (u + 1) + (v + 1)
                lower = part[:, (v + 1) * depth : (v + 1) * depth + LANES]
                upper = part[:, (v + 1) * depth + LANES : (v + 2) * depth]
                mine_ref[k] = jnp.where(core == 0, lower, upper).astype(BF)
                other_ref[k] = jnp.where(core == 0, upper, lower).astype(BF)


def encoder(scalars, ways, norm_factor, own, cross, strips, slope_second, slope_first, act, cells_in, w_second):
    samples, rows, kept, depth = own.shape
    height, breadth = rows - 2, kept - 2 * EDGE
    channels = cells_in.shape[0]
    return run(
        "encoder_grads",
        functools.partial(encoder_kernel, norm_factor, ways),
        [
            jax.ShapeDtypeStruct((samples, rows, breadth, 3 * depth), BF),
            jax.ShapeDtypeStruct((9, channels, LANES), BF),
            jax.ShapeDtypeStruct((9, channels, LANES), BF),
            jax.ShapeDtypeStruct((9, depth, LANES), BF),
            jax.ShapeDtypeStruct((9, depth, LANES), BF),
        ],
        [own, cross, *strips, slope_second, slope_first, act, cells_in, w_second],
        [
            pltpu.VMEM((samples, height + 4, kept, depth), F32),
            pltpu.VMEM((samples, height + 4, kept, depth), F32),
            pltpu.VMEM((samples, height + 2, kept, depth), F32),
            pltpu.VMEM((samples, height + 4, kept + 24, depth), F32),
            pltpu.VMEM((samples, height + 4, kept + 8, 3 * depth), BF),
            pltpu.VMEM((samples, height + 2, breadth, 3 * depth), BF),
            pltpu.VMEM((samples, height + 2, kept + 16, depth), F32),
        ],
        scalars,
        flops=2 * 9 * depth * (samples * rows * (kept + 8) * depth + samples * height * breadth * (depth + channels)),
    )


def input_kernel(moved_ref, w_first_ref, out_ref):
    samples, rows, breadth, triple = moved_ref.shape
    height = rows - 2
    total = None
    for u in STEPS:
        weights = jnp.concatenate([w_first_ref[3 * (u + 1) + (v + 1)] for v in STEPS], axis=1)
        part = dot_last(moved_ref[:, 1 - u : 1 - u + height].reshape(samples * height * breadth, triple), weights)
        total = part if total is None else total + part
    out_ref[...] = total.astype(BF).reshape(out_ref.shape)


def input_conv(moved, w_first):
    samples, rows, breadth, triple = moved.shape
    shape = (samples, rows - 2, breadth, w_first.shape[1])
    return run(
        "input_conv",
        input_kernel,
        [jax.ShapeDtypeStruct(shape, BF)],
        [moved, w_first],
        flops=2 * 3 * math.prod(shape) * triple,
    )[0]


def join_kernel(rows_first, at_ref, mine_ref, cross_ref, core_ref, both_ref, first_ref, second_ref):
    here = mine_ref[...].astype(F32) + cross_ref[...].astype(F32)
    there = core_ref[...].astype(F32) + both_ref[...].astype(F32)
    core = at_ref[2]
    lower = jnp.where(core == 0, here, there)
    upper = jnp.where(core == 0, there, here)
    rows_second = here.shape[0] - rows_first
    for half, value in ((0, lower), (1, upper)):
        first_ref[pl.ds(half, rows_first, stride=2), :] = value[:rows_first]
        second_ref[pl.ds(half, rows_second, stride=2), :] = value[rows_first:]


def swap(array, axis, flip):
    count = lax.axis_size(axis)
    return lax.ppermute(array, axis, [(i, i ^ flip) for i in range(count)])


def around(array, axis, step, periodic=True):
    count = lax.axis_size(axis)
    pairs = [(i, (i + step) % count) for i in range(count) if periodic or 0 <= i + step < count]
    return lax.ppermute(array, axis, pairs)


def corner(array, step):
    lead, lat = lax.axis_size("lead"), lax.axis_size("lat")
    pairs = []
    for a in range(lead):
        for b in range(lat):
            target = (b ^ 1) if step is None else b + step
            if 0 <= target < lat:
                pairs.append((a * lat + b, (a ^ 2) * lat + target))
    return lax.ppermute(array, ("lead", "lat"), pairs)


def per_device(head_grads, head_weights, encoder_input, pre_first, pre_second, w_first, w_second):
    samples, height, breadth, _ = encoder_input.shape
    bands, columns = lax.axis_size("lat"), lax.axis_size("lon")
    lead, lat, lon = lax.axis_index("lead"), lax.axis_index("lat"), lax.axis_index("lon")
    core, chip = lead % 2, lead // 2
    cells_total = samples * lax.axis_size("lead") * height * bands * breadth * columns
    norm_factor = 1.0 / math.sqrt(cells_total)

    to_right, to_left = pack(head_grads, pre_second, pre_first)
    low = around(to_right, "lon", 1)
    high = around(to_left, "lon", -1)

    theirs = head_conv(jnp.stack([1 - core, chip]).astype(jnp.int32), head_grads, low, high, head_weights, samples)
    got = swap(theirs, "lead", 1)
    mine = head_conv(jnp.stack([core, chip]).astype(jnp.int32), head_grads, low, high, head_weights, samples)
    second, first, slope_second, slope_first, act, cells_in = saved(pre_second, pre_first, encoder_input, low, high)

    if bands == 2:
        steps = [None]
        goes_down = jnp.stack([1 - lat])
        from_below = jnp.stack([1 - lat])
    else:
        steps = [1, -1]
        goes_down = jnp.array([1, 0])
        from_below = jnp.array([0, 1])
    spreads = spread(goes_down.astype(jnp.int32), mine, got, second, first, len(steps))
    own = spreads[0]
    cross = swap(spreads[1], "lead", 2)
    strips = []
    for way, step in enumerate(steps):
        line, angle = spreads[2 + 2 * way], spreads[3 + 2 * way]
        strips.append(swap(line, "lat", 1) if step is None else around(line, "lat", step, False))
        strips.append(corner(angle, step))

    place = jnp.concatenate([jnp.stack([lat, jnp.int32(bands), core]), from_below]).astype(jnp.int32)
    moved, first_mine, first_other, second_mine, second_other = encoder(
        place, len(steps), norm_factor, own, cross, strips, slope_second, slope_first, act, cells_in, w_second
    )
    input_grad = input_conv(moved, w_first)

    first_got = swap(first_other, "lead", 1)
    second_got = swap(second_other, "lead", 1)
    shares = bands * columns

    def in_shares(array):
        return array.reshape(bands, columns, -1, LANES)

    def add(*terms):
        total = terms[0].astype(F32)
        for term in terms[1:]:
            total = total + term.astype(F32)
        return total

    rows_first = first_mine.size // LANES // shares
    total = jnp.concatenate(
        [in_shares(add(first_mine, first_got)), in_shares(add(second_mine, second_got))], axis=2
    ).astype(BF)
    left = bands
    while left > 1:
        left //= 2
        bit = (lat // left) % 2
        halves = total.reshape((2, left) + total.shape[1:])
        away = lax.dynamic_index_in_dim(halves, 1 - bit, 0, keepdims=False)
        keep = lax.dynamic_index_in_dim(halves, bit, 0, keepdims=False)
        total = add(keep, swap(away, "lat", left)).astype(BF)
    total = total[0]
    parts = [lax.dynamic_index_in_dim(total, lon, 0, keepdims=False)]
    for step in range(1, columns):
        away = lax.dynamic_index_in_dim(total, (lon + step) % columns, 0, keepdims=False)
        parts.append(around(away, "lon", step))
    share = add(*parts).astype(BF)
    peers = [swap(share, "lead", flip) for flip in (2, 1, 3)]
    rows_second = share.shape[0] - rows_first
    result_first, result_second = run(
        "join_halves",
        functools.partial(join_kernel, rows_first),
        [
            jax.ShapeDtypeStruct((2 * rows_first, LANES), F32),
            jax.ShapeDtypeStruct((2 * rows_second, LANES), F32),
        ],
        [share, *peers],
        (),
        place,
    )
    return input_grad, result_first.reshape(-1), result_second.reshape(-1)


def solution(mesh):
    in_specs = (
        P("lead", None, "lat", "lon", None),
        P("lead", None, None, None),
        P("lead", "lat", "lon", None),
        P("lead", "lat", "lon", None),
        P("lead", "lat", "lon", None),
        P(),
        P(),
    )
    out_specs = (P("lead", "lat", "lon", None), P(("lat", "lon")), P(("lat", "lon")))
    return jax.shard_map(
        per_device, mesh=mesh, in_specs=in_specs, out_specs=out_specs, check_vma=False
    )
```

```python
import functools
import math

import jax
import jax.numpy as jnp
from jax import lax
from jax.experimental import pallas as pl
from jax.experimental.pallas import tpu as pltpu
from jax.sharding import PartitionSpec as P

BF = jnp.bfloat16
F32 = jnp.float32
STEPS = (-1, 0, 1)
EDGE = 4
LANES = 128
VMEM_BYTES = 24 * 1024 * 1024


def erf_part(values):
    return 0.5 * (1.0 + lax.erf(values * 0.7071067811865476))


def gelu_slope(values):
    return erf_part(values) + values * jnp.exp(-0.5 * values * values) * 0.3989422804014327


def gelu_value(values):
    return values * erf_part(values)


def dot_last(left, right):
    return lax.dot_general(left, right, (((1,), (1,)), ((), ())), preferred_element_type=F32)


def dot_plain(left, right):
    return lax.dot_general(left, right, (((1,), (0,)), ((), ())), preferred_element_type=F32)


def core_and_chip():
    lead = lax.axis_index("lead")
    return lax.rem(lead, 2), lax.div(lead, 2)


def run(name, kernel, out_shape, arrays, scratch=(), flops=0, far=False):
    specs = [pl.BlockSpec(memory_space=pltpu.HBM if far else pltpu.VMEM)] * len(arrays)
    if far:
        arrays = [pltpu.with_memory_space_constraint(a, pltpu.HBM) for a in arrays]
    touched = sum(a.size * a.dtype.itemsize for a in arrays)
    touched += sum(math.prod(s.shape) * s.dtype.itemsize for s in out_shape)
    return pl.pallas_call(
        kernel,
        name=name,
        out_shape=out_shape,
        in_specs=specs,
        out_specs=[pl.BlockSpec(memory_space=pltpu.VMEM)] * len(out_shape),
        scratch_shapes=list(scratch),
        compiler_params=pltpu.CompilerParams(vmem_limit_bytes=VMEM_BYTES),
        cost_estimate=pl.CostEstimate(flops=flops, bytes_accessed=touched, transcendentals=0),
    )(*arrays)


def pack_kernel(grads_far, second_far, first_far, right_ref, left_ref, grads_near, second_near, first_near, edges, edges_wide, packed, sems):
    heads, batch, height, breadth, _ = grads_far.shape
    samples = second_far.shape[0]
    rows = 6 * height
    copies = []
    for side in range(2):
        columns = pl.ds(breadth - 16 if side == 0 else 0, 16)
        for j, (far, near) in enumerate(((grads_far, grads_near), (second_far, second_near), (first_far, first_near))):
            source = far.at[:, :, :, columns, :] if j == 0 else far.at[:, :, columns, :]
            copies.append(pltpu.make_async_copy(source, near.at[side], sems.at[side, j]))
            copies[-1].start()
    for copy in copies:
        copy.wait()
    for side, out_ref in ((0, right_ref), (1, left_ref)):
        start = 8 if side == 0 else 0
        grads_ref, second_ref, first_ref = grads_near.at[side], second_near.at[side], first_near.at[side]
        for h in range(heads):
            for b in range(batch):
                block = grads_ref[h, b, :, start : start + 8, :].astype(F32)
                edges[(h * batch + b) * height * 8 : (h * batch + b + 1) * height * 8, :] = block.reshape(height * 8, LANES)
        for j, ref in enumerate((second_ref, first_ref)):
            for s in range(samples):
                block = ref[s, :, start : start + 8, :].astype(F32)
                at = (j * samples + s) * height * 8
                for half in range(2):
                    lanes = slice(half * LANES, (half + 1) * LANES)
                    edges_wide[half, at : at + height * 8, :] = block[:, :, lanes].reshape(height * 8, LANES)
        for b in range(batch):
            for col in range(3):
                inner = 5 + col if side == 0 else col
                for h in range(heads):
                    at = b * rows + (col * 2 + h) * height
                    packed[at : at + height, :] = edges[pl.ds((h * batch + b) * height * 8 + inner, height, stride=8), :]
        for s in range(samples):
            for q in range(3):
                j, col, width = (0, q, 2) if q < 2 else (1, 0, 1)
                inner = 8 - width + col if side == 0 else col
                for half in range(2):
                    at = (batch + s) * rows + (q * 2 + half) * height
                    packed[at : at + height, :] = edges_wide[
                        half, pl.ds((j * samples + s) * height * 8 + inner, height, stride=8), :
                    ]
        out_ref[...] = packed[...].astype(BF).reshape(out_ref.shape)


def pack(head_grads, pre_second, pre_first):
    heads, batch, height, _, _ = head_grads.shape
    samples = pre_second.shape[0]
    shape = jax.ShapeDtypeStruct((batch + samples, 6 * height, LANES), BF)
    return run(
        "pack_columns",
        pack_kernel,
        [shape, shape],
        [head_grads, pre_second, pre_first],
        [
            pltpu.VMEM((2, heads, batch, height, 16, LANES), BF),
            pltpu.VMEM((2, samples, height, 16, 2 * LANES), BF),
            pltpu.VMEM((2, samples, height, 16, 2 * LANES), BF),
            pltpu.VMEM((heads * batch * height * 8, LANES), F32),
            pltpu.VMEM((2, 2 * samples * height * 8, LANES), F32),
            pltpu.VMEM(((batch + samples) * 6 * height, LANES), F32),
            pltpu.SemaphoreType.DMA((2, 3)),
        ],
        far=True,
    )


def stage_kernel(*refs):
    count = len(refs) // 2
    sems = refs[-1]
    copies = [pltpu.make_async_copy(refs[i], refs[count + i], sems.at[i]) for i in range(count)]
    for copy in copies:
        copy.start()
    for copy in copies:
        copy.wait()


def stage(*arrays):
    shapes = [pltpu.VMEM(a.shape, a.dtype) for a in arrays]
    return run("stage", stage_kernel, shapes, list(arrays), [pltpu.SemaphoreType.DMA((len(arrays),))], far=True, flops=1 << 30)


def heads_kernel(other_core, grads_ref, low_ref, high_ref, weights_ref, out_ref, wide, shifted, total):
    heads, batch, height, breadth, _ = grads_ref.shape
    slots, _, kept, depth = out_ref.shape
    pitch = kept + 16
    own = 8 + EDGE
    core, chip = core_and_chip()
    core = 1 - core if other_core else core
    for slot in range(slots):
        group = chip if slot < slots // 2 else 1 - chip
        b = (2 * group + core) * (slots // 2) + slot % (slots // 2)
        low = low_ref[b].astype(F32)
        high = high_ref[b].astype(F32)
        for r in range(height):
            at = (slot * height + r) * pitch + own
            for h in range(heads):
                wide[h, at : at + breadth, :] = grads_ref[h, b, r].astype(F32)
        for col in range(3):
            for h in range(heads):
                here = (col * 2 + h) * height
                at = slot * height * pitch + own + col
                wide[h, pl.ds(at - 3, height, stride=pitch), :] = low[here : here + height]
                wide[h, pl.ds(at + breadth, height, stride=pitch), :] = high[here : here + height]
        for v in STEPS:
            for h in range(heads):
                starts = [(slot * height + r) * pitch + 8 - v for r in range(height)]
                moved = jnp.concatenate([wide[h, at : at + kept, :] for at in starts], axis=0).astype(BF)
                lane = ((v + 1) * heads + h) * LANES
                shifted[slot * height * kept : (slot + 1) * height * kept, lane : lane + LANES] = moved
    total[:, height:, :, :] = jnp.zeros((slots, 2, kept, depth), F32)
    for u in STEPS:
        weights = jnp.concatenate(
            [weights_ref[h, 3 * (u + 1) + (v + 1)] for v in STEPS for h in range(heads)], axis=1
        )
        part = dot_last(shifted[...], weights).reshape(slots, height, kept, depth)
        if u == -1:
            total[:, :height] = part
        else:
            total[:, 1 + u : 1 + u + height] += part
    out_ref[...] = total[...].astype(BF)


def head_conv(other_core, head_grads, low, high, head_weights, samples):
    heads, batch, height, breadth, _ = head_grads.shape
    depth = head_weights.shape[2]
    kept = breadth + 2 * EDGE
    slots = 2 * samples
    return run(
        "head_conv",
        functools.partial(heads_kernel, other_core),
        [jax.ShapeDtypeStruct((slots, height + 2, kept, depth), BF)],
        [head_grads, low, high, head_weights],
        [
            pltpu.VMEM((heads, slots * height * (kept + 16), LANES), F32),
            pltpu.VMEM((slots * height * kept, 3 * heads * LANES), BF),
            pltpu.VMEM((slots, height + 2, kept, depth), F32),
        ],
        flops=2 * slots * height * kept * 9 * heads * LANES * depth,
    )[0]


def saved_kernel(second_ref, first_ref, input_ref, low_ref, high_ref, second_out, first_out, slope_second, slope_first, act_out, input_out, wide):
    samples, height, breadth, depth = second_ref.shape
    kept = breadth + 2 * EDGE
    batch = low_ref.shape[0] - samples
    for ref, width, out_ref, slope_ref in (
        (second_ref, 2, second_out, slope_second),
        (first_ref, 1, first_out, slope_first),
    ):
        wide[...] = jnp.zeros(wide.shape, F32)
        for s in range(samples):
            for r in range(height):
                at = (s * height + r) * kept + EDGE
                for half in range(2):
                    lanes = slice(half * LANES, (half + 1) * LANES)
                    wide[half, at : at + breadth, :] = ref[s, r, :, lanes].astype(F32)
            low = low_ref[batch + s].astype(F32)
            high = high_ref[batch + s].astype(F32)
            for col in range(width):
                for half in range(2):
                    here = ((col if width == 2 else 2) * 2 + half) * height
                    at = s * height * kept + EDGE + col
                    wide[half, pl.ds(at - width, height, stride=kept), :] = low[here : here + height]
                    wide[half, pl.ds(at + breadth, height, stride=kept), :] = high[here : here + height]
        value = jnp.concatenate([wide[0], wide[1]], axis=1)
        out_ref[...] = value.astype(BF).reshape(out_ref.shape)
        slope_ref[...] = gelu_slope(value).reshape(slope_ref.shape)
    active = gelu_value(first_ref[...].astype(F32).reshape(samples * height * breadth, depth)).astype(BF).astype(F32)
    act_out[...] = active.T.astype(BF)
    cells = input_ref[...].astype(F32).reshape(samples * height * breadth, input_ref.shape[3])
    input_out[...] = cells.T.astype(BF)


def saved(pre_second, pre_first, encoder_input, low, high):
    samples, height, breadth, depth = pre_second.shape
    kept = breadth + 2 * EDGE
    cells = samples * height * breadth
    return run(
        "saved_parts",
        saved_kernel,
        [
            jax.ShapeDtypeStruct((samples, height, kept, depth), BF),
            jax.ShapeDtypeStruct((samples, height, kept, depth), BF),
            jax.ShapeDtypeStruct((samples, height, kept, depth), F32),
            jax.ShapeDtypeStruct((samples, height, kept, depth), F32),
            jax.ShapeDtypeStruct((depth, cells), BF),
            jax.ShapeDtypeStruct((encoder_input.shape[3], cells), BF),
        ],
        [pre_second, pre_first, encoder_input, low, high],
        [pltpu.VMEM((2, samples * height * kept, LANES), F32)],
    )


def spread_kernel(mine_ref, got_ref, second_ref, first_ref, own_ref, cross_ref, *strips):
    samples = own_ref.shape[0]
    height = second_ref.shape[1]
    total = mine_ref[...].astype(F32) + got_ref[...].astype(F32)
    total = total.astype(BF)
    own_ref[...] = total[:samples]
    cross_ref[...] = total[samples:]
    for way in range(len(strips) // 2):
        line_ref, corner_ref = strips[2 * way], strips[2 * way + 1]
        down = 1 - lax.axis_index("lat") if len(strips) == 2 else 1 - way
        line_ref[:, 0:3] = own_ref[:, pl.ds((height - 1) * down, 3)]
        corner_ref[...] = cross_ref[:, pl.ds((height - 1) * down, 3)]
        line_ref[:, 3:5] = second_ref[:, pl.ds((height - 2) * down, 2)]
        line_ref[:, 5:6] = first_ref[:, pl.ds((height - 1) * down, 1)]


def spread(mine, got, second, first, ways):
    slots, rows, kept, depth = mine.shape
    samples = slots // 2
    whole = jax.ShapeDtypeStruct((samples, rows, kept, depth), BF)
    strips = [
        jax.ShapeDtypeStruct((samples, 6, kept, depth), BF),
        jax.ShapeDtypeStruct((samples, 3, kept, depth), BF),
    ] * ways
    return run("core_sum", spread_kernel, [whole, whole] + strips, [mine, got, second, first])


def latent_kernel(ways, bands, own_ref, cross_ref, *refs):
    strips, refs = refs[: 2 * ways], refs[2 * ways :]
    slope_second_ref, slope_first_ref, grad_ref, away_ref, slope_out, latent, slope_second = refs
    samples, rows, kept, depth = own_ref.shape
    height = rows - 2
    lat = lax.axis_index("lat")
    _, chip = core_and_chip()
    blank = jnp.zeros((samples, kept, depth), F32)
    latent[:, 0] = blank
    latent[:, height + 3] = blank
    latent[:, 1 : height + 3] = own_ref[...].astype(F32) + cross_ref[...].astype(F32)
    slope_second[:, 2 : 2 + height] = slope_second_ref[...]
    slope_out[:, 1 : 1 + height] = slope_first_ref[...]
    for way in range(ways):
        line_ref, corner_ref = strips[2 * way], strips[2 * way + 1]
        below = 1 - lat if ways == 1 else way
        at = (height + 1) * below
        latent[:, pl.ds(at, 3)] += line_ref[:, 0:3].astype(F32) + corner_ref[...].astype(F32)
        slope_second[:, pl.ds((height + 2) * below, 2)] = gelu_slope(line_ref[:, 3:5].astype(F32))
        slope_out[:, pl.ds((height + 1) * below, 1)] = gelu_slope(line_ref[:, 5:6].astype(F32))
    for i in range(height + 4):
        row = lat * height + i - 2
        valid = jnp.logical_and(row >= 0, row < bands * height)
        value = latent[:, i] * slope_second[:, i]
        if i < 2 or i >= height + 2:
            value = jnp.where(valid, value, 0.0)
        grad_ref[:, i] = value.astype(BF)
        if 0 < i < height + 3:
            away_ref[:, i - 1] = jnp.where(chip == 0, value[:, :, LANES:], value[:, :, :LANES]).astype(BF)


def latent_grads(ways, bands, own, cross, strips, slope_second, slope_first):
    samples, rows, kept, depth = own.shape
    return run(
        "latent_grads",
        functools.partial(latent_kernel, ways, bands),
        [
            jax.ShapeDtypeStruct((samples, rows + 2, kept, depth), BF),
            jax.ShapeDtypeStruct((samples, rows, kept, LANES), BF),
            jax.ShapeDtypeStruct((samples, rows, kept, depth), F32),
        ],
        [own, cross, *strips, slope_second, slope_first],
        [
            pltpu.VMEM((samples, rows + 2, kept, depth), F32),
            pltpu.VMEM((samples, rows + 2, kept, depth), F32),
        ],
    )


def encoder_kernel(norm_factor, bands, grad_ref, slope_ref, input_ref, weights_ref, moved_out, mine_ref, other_ref, wide, cat, wide_first):
    samples, tall, kept, depth = grad_ref.shape
    rows = tall - 2
    height = rows - 2
    breadth = kept - 2 * EDGE
    lat = lax.axis_index("lat")
    core, _ = core_and_chip()
    own = 8 + EDGE
    wide[:, :, 8 : 8 + kept, :] = grad_ref[...].astype(F32)
    for v in STEPS:
        lanes = slice((v + 1) * depth, (v + 2) * depth)
        cat[:, :, :, lanes] = wide[:, :, 8 - v : 8 - v + kept + 8, :].astype(BF)
    linear = None
    for u in STEPS:
        weights = jnp.concatenate([weights_ref[3 * (u + 1) + (v + 1)] for v in STEPS], axis=1)
        left = cat[:, 1 - u : 1 - u + rows].reshape(samples * rows * (kept + 8), 3 * depth)
        part = dot_last(left, weights)
        linear = part if linear is None else linear + part
    linear = linear.reshape(samples, rows, kept + 8, depth)
    for i in range(rows):
        row = lat * height + i - 1
        valid = jnp.logical_and(row >= 0, row < bands * height)
        value = linear[:, i, :kept] * slope_ref[:, i]
        if i < 1 or i >= height + 1:
            value = jnp.where(valid, value, 0.0)
        wide_first[:, i, 8 : 8 + kept, :] = value.astype(BF).astype(F32)
    for v in STEPS:
        lanes = slice((v + 1) * depth, (v + 2) * depth)
        moved_out[:, :, :, lanes] = wide_first[:, :, own - v : own - v + breadth, :].astype(BF)
    for u in STEPS:
        right = moved_out[:, 1 - u : 1 - u + height].reshape(samples * height * breadth, 3 * depth)
        part = dot_plain(input_ref[...], right) * norm_factor
        for v in STEPS:
            k = 3 * (u + 1) + (v + 1)
            lower = part[:, (v + 1) * depth : (v + 1) * depth + LANES]
            upper = part[:, (v + 1) * depth + LANES : (v + 2) * depth]
            mine_ref[k] = jnp.where(core == 0, lower, upper).astype(BF)
            other_ref[k] = jnp.where(core == 0, upper, lower).astype(BF)


def encoder(norm_factor, bands, grad, slope, cells_in, w_second):
    samples, tall, kept, depth = grad.shape
    rows, height, breadth = tall - 2, tall - 4, kept - 2 * EDGE
    channels = cells_in.shape[0]
    half = jax.ShapeDtypeStruct((9, channels, LANES), BF)
    return run(
        "encoder_grads",
        functools.partial(encoder_kernel, norm_factor, bands),
        [jax.ShapeDtypeStruct((samples, rows, breadth, 3 * depth), BF), half, half],
        [grad, slope, cells_in, w_second],
        [
            pltpu.VMEM((samples, tall, kept + 24, depth), F32),
            pltpu.VMEM((samples, tall, kept + 8, 3 * depth), BF),
            pltpu.VMEM((samples, rows, kept + 16, depth), F32),
        ],
        flops=2 * 9 * depth * (samples * rows * (kept + 8) * depth + samples * height * breadth * channels),
    )


def second_kernel(norm_factor, shares, grad_ref, got_ref, act_ref, act_got_ref, *refs):
    full_ref, wide, cat = refs[-3:]
    samples, tall, kept, depth = grad_ref.shape
    rows, height, breadth = tall - 2, tall - 4, kept - 2 * EDGE
    core, chip = core_and_chip()
    own = 8 + EDGE
    lower = grad_ref[:, 1 : 1 + rows, :, :LANES].astype(F32)
    upper = grad_ref[:, 1 : 1 + rows, :, LANES:].astype(F32)
    wide[:samples, :, 8 : 8 + kept, :] = jnp.where(chip == 0, lower, upper)
    wide[samples:, :, 8 : 8 + kept, :] = got_ref[...].astype(F32)
    for v in STEPS:
        lanes = slice((v + 1) * LANES, (v + 2) * LANES)
        cat[:, :, :, lanes] = wide[:, :, own - v : own - v + breadth, :].astype(BF)
    cells = samples * height * breadth
    for u in STEPS:
        right = cat[:, 1 - u : 1 - u + height].reshape(2 * cells, 3 * LANES)
        part = dot_plain(act_ref[...], right[:cells]) + dot_plain(act_got_ref[...], right[cells:])
        part = part * norm_factor
        for v in STEPS:
            k = 3 * (u + 1) + (v + 1)
            full_ref[k * depth : (k + 1) * depth, :] = part[:, (v + 1) * LANES : (v + 2) * LANES].astype(BF)
    if len(refs) == 5:
        size = 9 * depth // shares // 2
        for i in range(shares):
            for out_ref, half in ((refs[0], core), (refs[1], 1 - core)):
                out_ref[i] = full_ref[pl.ds(pl.multiple_of((2 * i + half) * size, 16), size), :]


def second_grads(norm_factor, shares, grad, got, act, act_got):
    samples, tall, kept, depth = grad.shape
    rows, height, breadth = tall - 2, tall - 4, kept - 2 * EDGE
    size = 9 * depth // shares // 2
    inside = size % 16 == 0
    half = jax.ShapeDtypeStruct((shares, size, LANES), BF)
    scratch = [
        pltpu.VMEM((2 * samples, rows, kept + 16, LANES), F32),
        pltpu.VMEM((2 * samples, rows, breadth, 3 * LANES), BF),
    ]
    results = run(
        "second_weight_grads",
        functools.partial(second_kernel, norm_factor, shares),
        [half, half] if inside else [jax.ShapeDtypeStruct((9 * depth, LANES), BF)],
        [grad, got, act, act_got],
        [pltpu.VMEM((9 * depth, LANES), BF)] + scratch if inside else scratch,
        flops=2 * 9 * depth * LANES * 2 * samples * height * breadth,
    )
    if inside:
        return results
    halves = results[0].reshape(shares, 2, size, LANES)
    core, _ = core_and_chip()
    return [lax.dynamic_index_in_dim(halves, part, 1, keepdims=False) for part in (core, 1 - core)]


def act_kernel(source_ref, out_ref):
    samples, height, breadth, depth = source_ref.shape
    active = gelu_value(source_ref[...].astype(F32).reshape(samples * height * breadth, depth)).astype(BF).astype(F32)
    out_ref[...] = active.T.astype(BF)


def activated(source):
    samples, height, breadth, depth = source.shape
    return run("activated", act_kernel, [jax.ShapeDtypeStruct((depth, samples * height * breadth), BF)], [source])[0]


def other_band_kernel(*refs):
    terms, out_ref = refs[:-1], refs[-1]
    band = 1 - lax.rem(lax.axis_index("lat"), 2)
    for layer in range(2):
        parts = [t[band].astype(F32) for t in terms[layer * len(terms) // 2 : (layer + 1) * len(terms) // 2]]
        out_ref[layer] = sum(parts[1:], parts[0]).astype(BF)


def own_band_kernel(*refs):
    columns = refs[0].shape[1]
    terms, came, outs = refs[: -columns - 1], refs[-columns - 1], refs[-columns:]
    band, lon = lax.rem(lax.axis_index("lat"), 2), lax.axis_index("lon")
    for step in range(columns):
        block = lax.rem(lon + step, columns)
        for layer in range(2):
            parts = [t[band, block].astype(F32) for t in terms[layer * len(terms) // 2 : (layer + 1) * len(terms) // 2]]
            outs[step][layer] = sum(parts, came[layer, block].astype(F32)).astype(BF)


def sum_kernel(*refs):
    total = refs[0][...].astype(F32)
    for ref in refs[1:-1]:
        total = total + ref[...].astype(F32)
    refs[-1][...] = total.astype(BF)


def input_kernel(moved_ref, w_first_ref, out_ref):
    samples, rows, breadth, triple = moved_ref.shape
    height = rows - 2
    total = None
    for u in STEPS:
        weights = jnp.concatenate([w_first_ref[3 * (u + 1) + (v + 1)] for v in STEPS], axis=1)
        part = dot_last(moved_ref[:, 1 - u : 1 - u + height].reshape(samples * height * breadth, triple), weights)
        total = part if total is None else total + part
    out_ref[...] = total.astype(BF).reshape(out_ref.shape)


def input_conv(moved, w_first):
    samples, rows, breadth, triple = moved.shape
    shape = (samples, rows - 2, breadth, w_first.shape[1])
    return run(
        "input_conv",
        input_kernel,
        [jax.ShapeDtypeStruct(shape, BF)],
        [moved, w_first],
        flops=2 * 3 * math.prod(shape) * triple,
    )[0]


def join_kernel(mine_ref, cross_ref, core_ref, both_ref, first_ref, second_ref):
    core, chip = core_and_chip()
    rows = mine_ref.shape[1]
    here = mine_ref[0].astype(F32) + cross_ref[0].astype(F32)
    there = core_ref[0].astype(F32) + both_ref[0].astype(F32)
    first_ref[pl.ds(0, rows, stride=2), :] = jnp.where(core == 0, here, there)
    first_ref[pl.ds(1, rows, stride=2), :] = jnp.where(core == 0, there, here)
    mine, cross, other, both = (ref[1].astype(F32) for ref in (mine_ref, cross_ref, core_ref, both_ref))
    for part in range(2):
        near, far = jnp.where(core == part, mine, other), jnp.where(core == part, cross, both)
        second_ref[pl.ds(2 * rows * part, rows, stride=2), :] = jnp.where(chip == 0, near, far)
        second_ref[pl.ds(2 * rows * part + 1, rows, stride=2), :] = jnp.where(chip == 0, far, near)


def swap(array, axis, flip):
    count = lax.axis_size(axis)
    return lax.ppermute(array, axis, [(i, i ^ flip) for i in range(count)])


def around(array, axis, step, periodic=True):
    count = lax.axis_size(axis)
    pairs = [(i, (i + step) % count) for i in range(count) if periodic or 0 <= i + step < count]
    return lax.ppermute(array, axis, pairs)


def corner(array, step):
    lead, lat = lax.axis_size("lead"), lax.axis_size("lat")
    pairs = []
    for a in range(lead):
        for b in range(lat):
            target = (b ^ 1) if step is None else b + step
            if 0 <= target < lat:
                pairs.append((a * lat + b, (a ^ 2) * lat + target))
    return lax.ppermute(array, ("lead", "lat"), pairs)


def per_device(head_grads, head_weights, encoder_input, pre_first, pre_second, w_first, w_second):
    samples, height, breadth, _ = encoder_input.shape
    bands, columns = lax.axis_size("lat"), lax.axis_size("lon")
    cells_total = samples * lax.axis_size("lead") * height * bands * breadth * columns
    norm_factor = 1.0 / math.sqrt(cells_total)

    to_right, to_left = pack(head_grads, pre_second, pre_first)
    to_right, to_left, to_cross = lax.optimization_barrier((to_right, to_left, pre_first))
    low = around(to_right, "lon", 1)
    high = around(to_left, "lon", -1)
    act_got = activated(swap(to_cross, "lead", 2))
    head_grads, head_weights, w_second, pre_second, pre_first, encoder_input = stage(
        head_grads, head_weights, w_second, pre_second, pre_first, encoder_input
    )
    low, high, act_got = lax.optimization_barrier((low, high, act_got))

    theirs = head_conv(True, head_grads, low, high, head_weights, samples)
    got = swap(theirs, "lead", 1)
    mine = head_conv(False, head_grads, low, high, head_weights, samples)
    second, first, slope_second, slope_first, act, cells_in = saved(pre_second, pre_first, encoder_input, low, high)

    steps = [None] if bands == 2 else [1, -1]
    spreads = spread(mine, got, second, first, len(steps))
    own = spreads[0]
    cross = swap(spreads[1], "lead", 2)
    strips = []
    for way, step in enumerate(steps):
        line, angle = spreads[2 + 2 * way], spreads[3 + 2 * way]
        strips.append(swap(line, "lat", 1) if step is None else around(line, "lat", step, False))
        strips.append(corner(angle, step))

    grad, away, slope = latent_grads(len(steps), bands, own, cross, strips, slope_second, slope_first)
    grad_got = swap(away, "lead", 2)
    moved, first_mine, first_other = encoder(norm_factor, bands, grad, slope, cells_in, w_second)
    input_grad = input_conv(moved, w_first)
    first_got = swap(first_other, "lead", 1)
    second_mine, second_other = second_grads(norm_factor, bands * columns, grad, grad_got, act, act_got)
    second_got = swap(second_other, "lead", 1)

    terms = [[first_mine, first_got], [second_mine, second_got]]
    left = bands
    if left > 2:
        lat = lax.axis_index("lat")
        summed = jnp.stack([a.reshape(-1, LANES).astype(F32) + b.reshape(-1, LANES).astype(F32) for a, b in terms])
        summed = summed.astype(BF)
        while left > 2:
            left //= 2
            bit = (lat // left) % 2
            parts = summed.reshape(2, 2, -1, LANES)
            send = lax.dynamic_index_in_dim(parts, 1 - bit, 1, keepdims=False)
            keep = lax.dynamic_index_in_dim(parts, bit, 1, keepdims=False)
            summed = (keep.astype(F32) + swap(send, "lat", left).astype(F32)).astype(BF)
        terms = [[summed[0]], [summed[1]]]
    blocks = [t.reshape(2, columns, -1, LANES) for ts in terms for t in ts]
    shape = blocks[0].shape
    rows = shape[2]
    sent = run("other_band", other_band_kernel, [jax.ShapeDtypeStruct(shape, BF)], blocks)[0]
    came = swap(sent, "lat", 1)
    share_shape = jax.ShapeDtypeStruct((2, rows, LANES), BF)
    shares = run("own_band", own_band_kernel, [share_shape] * columns, blocks + [came])
    parts = [around(shares[step], "lon", step) for step in range(1, columns)]
    share = run("share", sum_kernel, [share_shape], [shares[0], *parts])[0]
    peers = [swap(share, "lead", flip) for flip in (2, 1, 3)]
    result_first, result_second = run(
        "join_halves",
        join_kernel,
        [jax.ShapeDtypeStruct((2 * rows, LANES), F32), jax.ShapeDtypeStruct((4 * rows, LANES), F32)],
        [share, *peers],
    )
    return input_grad, result_first.reshape(-1), result_second.reshape(-1)


def solution(mesh):
    in_specs = (
        P("lead", None, "lat", "lon", None),
        P("lead", None, None, None),
        P("lead", "lat", "lon", None),
        P("lead", "lat", "lon", None),
        P("lead", "lat", "lon", None),
        P(),
        P(),
    )
    out_specs = (P("lead", "lat", "lon", None), P(("lat", "lon")), P(("lat", "lon")))
    return jax.shard_map(
        per_device, mesh=mesh, in_specs=in_specs, out_specs=out_specs, check_vma=False
    )
```

```python
import functools
import math

import jax
import jax.numpy as jnp
from jax import lax
from jax.experimental import pallas as pl
from jax.experimental.pallas import tpu as pltpu
from jax.sharding import PartitionSpec as P

BF = jnp.bfloat16
F32 = jnp.float32
STEPS = (-1, 0, 1)
EDGE = 4
LANES = 128
VMEM_BYTES = 24 * 1024 * 1024


def erf_part(values):
    return 0.5 * (1.0 + lax.erf(values * 0.7071067811865476))


def gelu_slope(values):
    return erf_part(values) + values * jnp.exp(-0.5 * values * values) * 0.3989422804014327


def gelu_value(values):
    return values * erf_part(values)


def dot_last(left, right):
    return lax.dot_general(left, right, (((1,), (1,)), ((), ())), preferred_element_type=F32)


def dot_plain(left, right):
    return lax.dot_general(left, right, (((1,), (0,)), ((), ())), preferred_element_type=F32)


def core_and_chip():
    lead = lax.axis_index("lead")
    return lax.rem(lead, 2), lax.div(lead, 2)


def run(name, kernel, out_shape, arrays, scratch=(), flops=0, far=False):
    specs = [pl.BlockSpec(memory_space=pltpu.HBM if far else pltpu.VMEM)] * len(arrays)
    if far:
        arrays = [pltpu.with_memory_space_constraint(a, pltpu.HBM) for a in arrays]
    touched = sum(a.size * a.dtype.itemsize for a in arrays)
    touched += sum(math.prod(s.shape) * s.dtype.itemsize for s in out_shape)
    return pl.pallas_call(
        kernel,
        name=name,
        out_shape=out_shape,
        in_specs=specs,
        out_specs=[pl.BlockSpec(memory_space=pltpu.VMEM)] * len(out_shape),
        scratch_shapes=list(scratch),
        compiler_params=pltpu.CompilerParams(vmem_limit_bytes=VMEM_BYTES),
        cost_estimate=pl.CostEstimate(flops=1, bytes_accessed=1, transcendentals=0),
    )(*arrays)


def pack_kernel(with_tile, grads_far, second_far, first_far, input_far, right_ref, left_ref, *refs):
    grads_near, second_near, first_near, edges, edges_wide, packed, sems, tile_sems = refs[-8:]
    heads, batch, height, breadth, _ = grads_far.shape
    samples = second_far.shape[0]
    rows = 6 * height
    copies = []
    for side in range(2):
        columns = pl.ds(breadth - 16 if side == 0 else 0, 16)
        for j, (far, near) in enumerate(((grads_far, grads_near), (second_far, second_near), (first_far, first_near))):
            source = far.at[:, :, :, columns, :] if j == 0 else far.at[:, :, columns, :]
            copies.append(pltpu.make_async_copy(source, near.at[side], sems.at[side, j]))
            copies[-1].start()
    tile_copies = []
    if with_tile:
        for j, far in enumerate((second_far, second_far, first_far, first_far, input_far)):
            source = far.at[:, :, :, pl.ds(LANES * (j % 2), LANES)] if j < 4 else far
            target = refs[0].at[j] if j < 2 else refs[1].at[j - 2]
            tile_copies.append(pltpu.make_async_copy(source, target, tile_sems.at[j]))
            tile_copies[-1].start()
    for copy in copies:
        copy.wait()
    for side, out_ref in ((0, right_ref), (1, left_ref)):
        start = 8 if side == 0 else 0
        grads_ref, second_ref, first_ref = grads_near.at[side], second_near.at[side], first_near.at[side]
        for h in range(heads):
            for b in range(batch):
                block = grads_ref[h, b, :, start : start + 8, :].astype(F32)
                edges[(h * batch + b) * height * 8 : (h * batch + b + 1) * height * 8, :] = block.reshape(height * 8, LANES)
        for j, ref in enumerate((second_ref, first_ref)):
            for s in range(samples):
                block = ref[s, :, start : start + 8, :].astype(F32)
                at = (j * samples + s) * height * 8
                for half in range(2):
                    lanes = slice(half * LANES, (half + 1) * LANES)
                    edges_wide[half, at : at + height * 8, :] = block[:, :, lanes].reshape(height * 8, LANES)
        for b in range(batch):
            for col in range(3):
                inner = 5 + col if side == 0 else col
                for h in range(heads):
                    at = b * rows + (col * 2 + h) * height
                    packed[at : at + height, :] = edges[pl.ds((h * batch + b) * height * 8 + inner, height, stride=8), :]
        for s in range(samples):
            for q in range(3):
                j, col, width = (0, q, 2) if q < 2 else (1, 0, 1)
                inner = 8 - width + col if side == 0 else col
                for half in range(2):
                    at = (batch + s) * rows + (q * 2 + half) * height
                    packed[at : at + height, :] = edges_wide[
                        half, pl.ds((j * samples + s) * height * 8 + inner, height, stride=8), :
                    ]
        out_ref[...] = packed[...].astype(BF).reshape(out_ref.shape)
    for copy in tile_copies:
        copy.wait()


def pack(head_grads, pre_second, pre_first, encoder_input, with_tile):
    heads, batch, height, _, _ = head_grads.shape
    samples = pre_second.shape[0]
    shape = jax.ShapeDtypeStruct((batch + samples, 6 * height, LANES), BF)
    tiles = [jax.ShapeDtypeStruct((count,) + encoder_input.shape, BF) for count in (2, 3)]
    return run(
        "pack_columns",
        functools.partial(pack_kernel, with_tile),
        [shape, shape] + tiles * with_tile,
        [head_grads, pre_second, pre_first, encoder_input],
        [
            pltpu.VMEM((2, heads, batch, height, 16, LANES), BF),
            pltpu.VMEM((2, samples, height, 16, 2 * LANES), BF),
            pltpu.VMEM((2, samples, height, 16, 2 * LANES), BF),
            pltpu.VMEM((heads * batch * height * 8, LANES), F32),
            pltpu.VMEM((2, 2 * samples * height * 8, LANES), F32),
            pltpu.VMEM(((batch + samples) * 6 * height, LANES), F32),
            pltpu.SemaphoreType.DMA((2, 3)),
            pltpu.SemaphoreType.DMA((5,)),
        ],
        far=True,
    )


def stage_kernel(*refs):
    count = len(refs) // 2
    sems = refs[-1]
    copies = [pltpu.make_async_copy(refs[i], refs[count + i], sems.at[i]) for i in range(count)]
    for copy in copies:
        copy.start()
    for copy in copies:
        copy.wait()


def stage(*arrays):
    shapes = [pltpu.VMEM(a.shape, a.dtype) for a in arrays]
    return run("stage", stage_kernel, shapes, list(arrays), [pltpu.SemaphoreType.DMA((len(arrays),))], far=True, flops=1 << 30)


def heads_kernel(other_core, other_chip, samples, grads_ref, low_ref, high_ref, weights_ref, out_ref, wide, shifted, total):
    heads, batch, height, breadth, _ = grads_ref.shape
    slots, _, kept, depth = out_ref.shape
    pitch = kept + 16
    own = 8 + EDGE
    core, chip = core_and_chip()
    core = 1 - core if other_core else core
    for slot in range(slots):
        group = 1 - chip if other_chip != (slot >= samples) else chip
        b = (2 * group + core) * samples + slot % samples
        low = low_ref[b].astype(F32)
        high = high_ref[b].astype(F32)
        for r in range(height):
            at = (slot * height + r) * pitch + own
            for h in range(heads):
                wide[h, at : at + breadth, :] = grads_ref[h, b, r].astype(F32)
        for col in range(3):
            for h in range(heads):
                here = (col * 2 + h) * height
                at = slot * height * pitch + own + col
                wide[h, pl.ds(at - 3, height, stride=pitch), :] = low[here : here + height]
                wide[h, pl.ds(at + breadth, height, stride=pitch), :] = high[here : here + height]
        for v in STEPS:
            for h in range(heads):
                starts = [(slot * height + r) * pitch + 8 - v for r in range(height)]
                moved = jnp.concatenate([wide[h, at : at + kept, :] for at in starts], axis=0).astype(BF)
                lane = ((v + 1) * heads + h) * LANES
                shifted[slot * height * kept : (slot + 1) * height * kept, lane : lane + LANES] = moved
    total[:, height:, :, :] = jnp.zeros((slots, 2, kept, depth), F32)
    for u in STEPS:
        weights = jnp.concatenate(
            [weights_ref[h, 3 * (u + 1) + (v + 1)] for v in STEPS for h in range(heads)], axis=1
        )
        part = dot_last(shifted[...], weights).reshape(slots, height, kept, depth)
        if u == -1:
            total[:, :height] = part
        else:
            total[:, 1 + u : 1 + u + height] += part
    if out_ref.shape[1] == height + 2:
        out_ref[...] = total[...].astype(BF)
    else:
        out_ref[...] = total[:, pl.ds(1 - lax.axis_index("lat"), height + 1)].astype(BF)


def head_conv(other_core, other_chip, head_grads, low, high, head_weights, slots, rows):
    samples = head_grads.shape[1] // lax.axis_size("lead")
    heads, batch, height, breadth, _ = head_grads.shape
    depth = head_weights.shape[2]
    kept = breadth + 2 * EDGE
    return run(
        "head_conv",
        functools.partial(heads_kernel, other_core, other_chip, samples),
        [jax.ShapeDtypeStruct((slots, rows, kept, depth), BF)],
        [head_grads, low, high, head_weights],
        [
            pltpu.VMEM((heads, slots * height * (kept + 16), LANES), F32),
            pltpu.VMEM((slots * height * kept, 3 * heads * LANES), BF),
            pltpu.VMEM((slots, height + 2, kept, depth), F32),
        ],
        flops=2 * slots * height * kept * 9 * heads * LANES * depth,
    )[0]


def saved_kernel(second_ref, first_ref, input_ref, low_ref, high_ref, second_out, first_out, slope_second, slope_first, act_out, input_out, wide):
    samples, height, breadth, depth = second_ref.shape
    kept = breadth + 2 * EDGE
    batch = low_ref.shape[0] - samples
    for ref, width, out_ref, slope_ref in (
        (second_ref, 2, second_out, slope_second),
        (first_ref, 1, first_out, slope_first),
    ):
        wide[...] = jnp.zeros(wide.shape, F32)
        for s in range(samples):
            for r in range(height):
                at = (s * height + r) * kept + EDGE
                for half in range(2):
                    lanes = slice(half * LANES, (half + 1) * LANES)
                    wide[half, at : at + breadth, :] = ref[s, r, :, lanes].astype(F32)
            low = low_ref[batch + s].astype(F32)
            high = high_ref[batch + s].astype(F32)
            for col in range(width):
                for half in range(2):
                    here = ((col if width == 2 else 2) * 2 + half) * height
                    at = s * height * kept + EDGE + col
                    wide[half, pl.ds(at - width, height, stride=kept), :] = low[here : here + height]
                    wide[half, pl.ds(at + breadth, height, stride=kept), :] = high[here : here + height]
        value = jnp.concatenate([wide[0], wide[1]], axis=1)
        out_ref[...] = value.astype(BF).reshape(out_ref.shape)
        slope_ref[...] = gelu_slope(value).reshape(slope_ref.shape)
    active = gelu_value(first_ref[...].astype(F32).reshape(samples * height * breadth, depth)).astype(BF).astype(F32)
    act_out[...] = active.T.astype(BF)
    cells = input_ref[...].astype(F32).reshape(samples * height * breadth, input_ref.shape[3])
    input_out[...] = cells.T.astype(BF)


def saved(pre_second, pre_first, encoder_input, low, high):
    samples, height, breadth, depth = pre_second.shape
    kept = breadth + 2 * EDGE
    cells = samples * height * breadth
    return run(
        "saved_parts",
        saved_kernel,
        [
            jax.ShapeDtypeStruct((samples, height, kept, depth), BF),
            jax.ShapeDtypeStruct((samples, height, kept, depth), BF),
            jax.ShapeDtypeStruct((samples, height, kept, depth), F32),
            jax.ShapeDtypeStruct((samples, height, kept, depth), F32),
            jax.ShapeDtypeStruct((depth, cells), BF),
            jax.ShapeDtypeStruct((encoder_input.shape[3], cells), BF),
        ],
        [pre_second, pre_first, encoder_input, low, high],
        [pltpu.VMEM((2, samples * height * kept, LANES), F32)],
    )


def goes_down(way, ways):
    return 1 - lax.axis_index("lat") if ways == 1 else 1 - way


def cross_kernel(mine_ref, got_ref, cross_ref, *strips):
    height = mine_ref.shape[1] - 2
    cross_ref[...] = (mine_ref[...].astype(F32) + got_ref[...].astype(F32)).astype(BF)
    for way, corner_ref in enumerate(strips):
        corner_ref[...] = cross_ref[:, pl.ds((height - 1) * goes_down(way, len(strips)), 3)]


def own_kernel(mine_ref, got_ref, second_ref, first_ref, own_ref, *strips):
    height = second_ref.shape[1]
    own_ref[...] = (mine_ref[...].astype(F32) + got_ref[...].astype(F32)).astype(BF)
    for way, line_ref in enumerate(strips):
        down = goes_down(way, len(strips))
        line_ref[:, 0:3] = own_ref[:, pl.ds((height - 1) * down, 3)]
        line_ref[:, 3:5] = second_ref[:, pl.ds((height - 2) * down, 2)]
        line_ref[:, 5:6] = first_ref[:, pl.ds((height - 1) * down, 1)]


def spread_cross(mine, got, ways):
    samples, _, kept, depth = mine.shape
    strip = jax.ShapeDtypeStruct((samples, 3, kept, depth), BF)
    return run("core_sum_cross", cross_kernel, [jax.ShapeDtypeStruct(mine.shape, BF)] + [strip] * ways, [mine, got])


def spread_own(mine, got, second, first, ways):
    samples, _, kept, depth = mine.shape
    strip = jax.ShapeDtypeStruct((samples, 6, kept, depth), BF)
    return run("core_sum_own", own_kernel, [jax.ShapeDtypeStruct(mine.shape, BF)] + [strip] * ways, [mine, got, second, first])


def latent_kernel(ways, bands, own_ref, cross_ref, *refs):
    strips, refs = refs[: 2 * ways], refs[2 * ways :]
    slope_second_ref, slope_first_ref, grad_ref, away_ref, slope_out, latent, slope_second = refs
    samples, rows, kept, depth = own_ref.shape
    height = rows - 2
    lat = lax.axis_index("lat")
    _, chip = core_and_chip()
    blank = jnp.zeros((samples, kept, depth), F32)
    latent[:, 0] = blank
    latent[:, height + 3] = blank
    latent[:, 1 : height + 3] = own_ref[...].astype(F32) + cross_ref[...].astype(F32)
    slope_second[:, 2 : 2 + height] = slope_second_ref[...]
    slope_out[:, 1 : 1 + height] = slope_first_ref[...]
    for way in range(ways):
        line_ref, corner_ref = strips[2 * way], strips[2 * way + 1]
        below = 1 - lat if ways == 1 else way
        at = (height + 1) * below
        latent[:, pl.ds(at, 3)] += line_ref[:, 0:3].astype(F32) + corner_ref[...].astype(F32)
        slope_second[:, pl.ds((height + 2) * below, 2)] = gelu_slope(line_ref[:, 3:5].astype(F32))
        slope_out[:, pl.ds((height + 1) * below, 1)] = gelu_slope(line_ref[:, 5:6].astype(F32))
    for i in range(height + 4):
        row = lat * height + i - 2
        valid = jnp.logical_and(row >= 0, row < bands * height)
        value = latent[:, i] * slope_second[:, i]
        if i < 2 or i >= height + 2:
            value = jnp.where(valid, value, 0.0)
        grad_ref[:, i] = value.astype(BF)
        if 0 < i < height + 3:
            away_ref[:, i - 1] = jnp.where(chip == 0, value[:, :, LANES:], value[:, :, :LANES]).astype(BF)


def latent_grads(ways, bands, own, cross, strips, slope_second, slope_first):
    samples, rows, kept, depth = own.shape
    return run(
        "latent_grads",
        functools.partial(latent_kernel, ways, bands),
        [
            jax.ShapeDtypeStruct((samples, rows + 2, kept, depth), BF),
            jax.ShapeDtypeStruct((samples, rows, kept, LANES), BF),
            jax.ShapeDtypeStruct((samples, rows, kept, depth), F32),
        ],
        [own, cross, *strips, slope_second, slope_first],
        [
            pltpu.VMEM((samples, rows + 2, kept, depth), F32),
            pltpu.VMEM((samples, rows + 2, kept, depth), F32),
        ],
    )


def encoder_kernel(norm_factor, bands, grad_ref, slope_ref, input_ref, weights_ref, moved_out, mine_ref, other_ref, wide, cat, wide_first):
    samples, tall, kept, depth = grad_ref.shape
    rows = tall - 2
    height = rows - 2
    breadth = kept - 2 * EDGE
    lat = lax.axis_index("lat")
    core, _ = core_and_chip()
    own = 8 + EDGE
    wide[:, :, 8 : 8 + kept, :] = grad_ref[...].astype(F32)
    for v in STEPS:
        lanes = slice((v + 1) * depth, (v + 2) * depth)
        cat[:, :, :, lanes] = wide[:, :, 8 - v : 8 - v + kept + 8, :].astype(BF)
    linear = None
    for u in STEPS:
        weights = jnp.concatenate([weights_ref[3 * (u + 1) + (v + 1)] for v in STEPS], axis=1)
        left = cat[:, 1 - u : 1 - u + rows].reshape(samples * rows * (kept + 8), 3 * depth)
        part = dot_last(left, weights)
        linear = part if linear is None else linear + part
    linear = linear.reshape(samples, rows, kept + 8, depth)
    for i in range(rows):
        row = lat * height + i - 1
        valid = jnp.logical_and(row >= 0, row < bands * height)
        value = linear[:, i, :kept] * slope_ref[:, i]
        if i < 1 or i >= height + 1:
            value = jnp.where(valid, value, 0.0)
        wide_first[:, i, 8 : 8 + kept, :] = value.astype(BF).astype(F32)
    for v in STEPS:
        lanes = slice((v + 1) * depth, (v + 2) * depth)
        moved_out[:, :, :, lanes] = wide_first[:, :, own - v : own - v + breadth, :].astype(BF)
    for u in STEPS:
        right = moved_out[:, 1 - u : 1 - u + height].reshape(samples * height * breadth, 3 * depth)
        part = dot_plain(input_ref[...], right) * norm_factor
        for v in STEPS:
            k = 3 * (u + 1) + (v + 1)
            lower = part[:, (v + 1) * depth : (v + 1) * depth + LANES]
            upper = part[:, (v + 1) * depth + LANES : (v + 2) * depth]
            mine_ref[k] = jnp.where(core == 0, lower, upper).astype(BF)
            other_ref[k] = jnp.where(core == 0, upper, lower).astype(BF)


def encoder(norm_factor, bands, grad, slope, cells_in, w_second):
    samples, tall, kept, depth = grad.shape
    rows, height, breadth = tall - 2, tall - 4, kept - 2 * EDGE
    channels = cells_in.shape[0]
    half = jax.ShapeDtypeStruct((9, channels, LANES), BF)
    return run(
        "encoder_grads",
        functools.partial(encoder_kernel, norm_factor, bands),
        [jax.ShapeDtypeStruct((samples, rows, breadth, 3 * depth), BF), half, half],
        [grad, slope, cells_in, w_second],
        [
            pltpu.VMEM((samples, tall, kept + 24, depth), F32),
            pltpu.VMEM((samples, tall, kept + 8, 3 * depth), BF),
            pltpu.VMEM((samples, rows, kept + 16, depth), F32),
        ],
        flops=2 * 9 * depth * (samples * rows * (kept + 8) * depth + samples * height * breadth * channels),
    )


def second_kernel(norm_factor, shares, grad_ref, got_ref, act_ref, act_got_ref, *refs):
    full_ref, wide, cat = refs[-3:]
    samples, tall, kept, depth = grad_ref.shape
    rows, height, breadth = tall - 2, tall - 4, kept - 2 * EDGE
    core, chip = core_and_chip()
    own = 8 + EDGE
    lower = grad_ref[:, 1 : 1 + rows, :, :LANES].astype(F32)
    upper = grad_ref[:, 1 : 1 + rows, :, LANES:].astype(F32)
    wide[:samples, :, 8 : 8 + kept, :] = jnp.where(chip == 0, lower, upper)
    wide[samples:, :, 8 : 8 + kept, :] = got_ref[...].astype(F32)
    for v in STEPS:
        lanes = slice((v + 1) * LANES, (v + 2) * LANES)
        cat[:, :, :, lanes] = wide[:, :, own - v : own - v + breadth, :].astype(BF)
    cells = samples * height * breadth
    for u in STEPS:
        right = cat[:, 1 - u : 1 - u + height].reshape(2 * cells, 3 * LANES)
        part = dot_plain(act_ref[...], right[:cells]) + dot_plain(act_got_ref[...], right[cells:])
        part = part * norm_factor
        for v in STEPS:
            k = 3 * (u + 1) + (v + 1)
            full_ref[k * depth : (k + 1) * depth, :] = part[:, (v + 1) * LANES : (v + 2) * LANES].astype(BF)
    if len(refs) == 5:
        size = 9 * depth // shares // 2
        for i in range(shares):
            for out_ref, half in ((refs[0], core), (refs[1], 1 - core)):
                out_ref[i] = full_ref[pl.ds(pl.multiple_of((2 * i + half) * size, 16), size), :]


def second_grads(norm_factor, shares, grad, got, act, act_got):
    samples, tall, kept, depth = grad.shape
    rows, height, breadth = tall - 2, tall - 4, kept - 2 * EDGE
    size = 9 * depth // shares // 2
    inside = size % 16 == 0
    half = jax.ShapeDtypeStruct((shares, size, LANES), BF)
    scratch = [
        pltpu.VMEM((2 * samples, rows, kept + 16, LANES), F32),
        pltpu.VMEM((2 * samples, rows, breadth, 3 * LANES), BF),
    ]
    results = run(
        "second_weight_grads",
        functools.partial(second_kernel, norm_factor, shares),
        [half, half] if inside else [jax.ShapeDtypeStruct((9 * depth, LANES), BF)],
        [grad, got, act, act_got],
        [pltpu.VMEM((9 * depth, LANES), BF)] + scratch if inside else scratch,
        flops=2 * 9 * depth * LANES * 2 * samples * height * breadth,
    )
    if inside:
        return results
    halves = results[0].reshape(shares, 2, size, LANES)
    core, _ = core_and_chip()
    return [lax.dynamic_index_in_dim(halves, part, 1, keepdims=False) for part in (core, 1 - core)]


def act_kernel(source_ref, out_ref):
    samples, height, breadth, depth = source_ref.shape
    active = gelu_value(source_ref[...].astype(F32).reshape(samples * height * breadth, depth)).astype(BF).astype(F32)
    out_ref[...] = active.T.astype(BF)


def activated(source):
    samples, height, breadth, depth = source.shape
    return run("activated", act_kernel, [jax.ShapeDtypeStruct((depth, samples * height * breadth), BF)], [source])[0]


def other_band_kernel(*refs):
    band = 1 - lax.rem(lax.axis_index("lat"), 2)
    parts = [t[band].astype(F32) for t in refs[:-1]]
    refs[-1][...] = sum(parts[1:], parts[0]).astype(BF)


def partner(index, step, count):
    return index ^ step if count & (count - 1) == 0 else (index + step) % count


def own_band_kernel(*refs):
    columns = refs[0].shape[1]
    terms, came, outs = refs[: -columns - 2], refs[-columns - 2 : -columns], refs[-columns:]
    band, lon = lax.rem(lax.axis_index("lat"), 2), lax.axis_index("lon")
    for step in range(columns):
        block = partner(lon, step, columns)
        for layer in range(2):
            parts = [t[band, block].astype(F32) for t in terms[layer * len(terms) // 2 : (layer + 1) * len(terms) // 2]]
            outs[step][layer] = sum(parts, came[layer][block].astype(F32)).astype(BF)


def sum_kernel(*refs):
    total = refs[0][...].astype(F32)
    for ref in refs[1:-1]:
        total = total + ref[...].astype(F32)
    refs[-1][...] = total.astype(BF)


def input_kernel(moved_ref, w_first_ref, out_ref):
    samples, rows, breadth, triple = moved_ref.shape
    height = rows - 2
    total = None
    for u in STEPS:
        weights = jnp.concatenate([w_first_ref[3 * (u + 1) + (v + 1)] for v in STEPS], axis=1)
        part = dot_last(moved_ref[:, 1 - u : 1 - u + height].reshape(samples * height * breadth, triple), weights)
        total = part if total is None else total + part
    out_ref[...] = total.astype(BF).reshape(out_ref.shape)


def input_conv(moved, w_first):
    samples, rows, breadth, triple = moved.shape
    shape = (samples, rows - 2, breadth, w_first.shape[1])
    return run(
        "input_conv",
        input_kernel,
        [jax.ShapeDtypeStruct(shape, BF)],
        [moved, w_first],
        flops=2 * 3 * math.prod(shape) * triple,
    )[0]


def chips_kernel(mine_ref, cross_ref, out_ref):
    _, chip = core_and_chip()
    out_ref[0] = (mine_ref[0].astype(F32) + cross_ref[0].astype(F32)).astype(BF)
    out_ref[1] = jnp.where(chip == 0, mine_ref[1], cross_ref[1])
    out_ref[2] = jnp.where(chip == 0, cross_ref[1], mine_ref[1])


def cores_kernel(mine_ref, other_ref, first_ref, second_ref):
    core, _ = core_and_chip()
    rows = mine_ref.shape[1]
    mine, other = (ref[...].astype(F32) for ref in (mine_ref, other_ref))
    for part in range(2):
        value = jnp.where(core == part, mine, other)
        first_ref[pl.ds(part, rows, stride=2), :] = value[0]
        second_ref[pl.ds(2 * rows * part, rows, stride=2), :] = value[1]
        second_ref[pl.ds(2 * rows * part + 1, rows, stride=2), :] = value[2]


def swap(array, axis, flip):
    count = lax.axis_size(axis)
    return lax.ppermute(array, axis, [(i, i ^ flip) for i in range(count)])


def around(array, axis, step, periodic=True):
    count = lax.axis_size(axis)
    pairs = [(i, (i + step) % count) for i in range(count) if periodic or 0 <= i + step < count]
    return lax.ppermute(array, axis, pairs)


def corner(array, step):
    lead, lat = lax.axis_size("lead"), lax.axis_size("lat")
    pairs = []
    for a in range(lead):
        for b in range(lat):
            target = (b ^ 1) if step is None else b + step
            if 0 <= target < lat:
                pairs.append((a * lat + b, (a ^ 2) * lat + target))
    return lax.ppermute(array, ("lead", "lat"), pairs)


def other_band(terms, columns):
    shape = (columns, terms[0].size // LANES // columns // 2, LANES)
    return run("other_band", other_band_kernel, [jax.ShapeDtypeStruct(shape, BF)], [t.reshape(2, *shape) for t in terms])[0]


def pairwise(terms, bands):
    lat = lax.axis_index("lat")
    total = sum(t.reshape(-1, LANES).astype(F32) for t in terms).astype(BF)
    left = bands
    while left > 2:
        left //= 2
        bit = (lat // left) % 2
        halves = total.reshape(2, -1, LANES)
        send = lax.dynamic_index_in_dim(halves, 1 - bit, 0, keepdims=False)
        keep = lax.dynamic_index_in_dim(halves, bit, 0, keepdims=False)
        total = (keep.astype(F32) + swap(send, "lat", left).astype(F32)).astype(BF)
    return total


def near_kernel(second_ref, first_ref, low_ref, high_ref, slope_second, slope_first, halo_ref, wide, cells):
    samples, height, breadth, depth = second_ref.shape
    kept = breadth + 2 * EDGE
    batch = low_ref.shape[0] - samples
    for ref, width, first_cell, slope_ref in ((second_ref, 2, 0, slope_second), (first_ref, 1, 4 * height, slope_first)):
        wide[...] = jnp.zeros(wide.shape, F32)
        for s in range(samples):
            for r in range(height):
                at = (s * height + r) * kept + EDGE
                for half in range(2):
                    wide[half, at : at + breadth, :] = ref[s, r, :, half * LANES : (half + 1) * LANES].astype(F32)
            for side, packed_ref in ((0, low_ref), (1, high_ref)):
                packed = packed_ref[batch + s].astype(F32)
                for col in range(width):
                    for half in range(2):
                        here = ((col if width == 2 else 2) * 2 + half) * height
                        value = packed[here : here + height]
                        at = s * height * kept + EDGE + col + (breadth if side else -width)
                        wide[half, pl.ds(at, height, stride=kept), :] = value
                        at = first_cell + (side * width + col) * height
                        cells[s, at : at + height, half * LANES : (half + 1) * LANES] = value
        value = jnp.concatenate([wide[0], wide[1]], axis=1)
        slope_ref[...] = gelu_slope(value).reshape(slope_ref.shape)
    halo_ref[...] = cells[...].astype(BF)


def near_parts(pre_second, pre_first, low, high):
    samples, height, breadth, depth = pre_second.shape
    kept = breadth + 2 * EDGE
    slope = jax.ShapeDtypeStruct((samples, height, kept, depth), F32)
    return run(
        "near_parts",
        near_kernel,
        [slope, slope, jax.ShapeDtypeStruct((samples, 6 * height, depth), BF)],
        [pre_second, pre_first, low, high],
        [pltpu.VMEM((2, samples * height * kept, LANES), F32), pltpu.VMEM((samples, 6 * height, depth), F32)],
    )


def far_kernel(first_ref, input_ref, tile_second, tile_ref, slope_second, slope_first, act_out, input_out, wide, act, cells):
    samples, height, breadth, depth = first_ref.shape
    kept = breadth + 2 * EDGE
    lat = lax.axis_index("lat")
    for source_ref, slope_ref in ((tile_second, slope_second), (tile_ref, slope_first)):
        wide[...] = jnp.zeros(wide.shape, F32)
        for s in range(samples):
            for half in range(2):
                for r in range(height):
                    at = (s * height + r) * kept + EDGE
                    wide[half, at : at + breadth, :] = source_ref[half, s, r].astype(F32)
        value = jnp.concatenate([wide[0], wide[1]], axis=1)
        slope_ref[...] = gelu_slope(value).reshape(slope_ref.shape)
    own, other = pl.ds(height * lat, height), pl.ds(height * (1 - lat), height)
    act[:, own] = gelu_value(first_ref[...].astype(F32))
    act[:, other] = jnp.concatenate([gelu_value(tile_ref[half].astype(F32)) for half in range(2)], axis=-1)
    cells[:, own] = input_ref[...].astype(F32)
    cells[:, other] = tile_ref[2].astype(F32)
    act_out[...] = act[...].reshape(act_out.shape[1], depth).T.astype(BF)
    input_out[...] = cells[...].reshape(input_out.shape[1], input_out.shape[0]).T.astype(BF)


def far_parts(pre_first, encoder_input, tile_second, tile):
    samples, height, breadth, depth = pre_first.shape
    channels = encoder_input.shape[3]
    kept = breadth + 2 * EDGE
    cells = 2 * samples * height * breadth
    slope = jax.ShapeDtypeStruct((samples, height, kept, depth), F32)
    return run(
        "far_parts",
        far_kernel,
        [slope, slope, jax.ShapeDtypeStruct((depth, cells), BF), jax.ShapeDtypeStruct((channels, cells), BF)],
        [pre_first, encoder_input, tile_second, tile],
        [
            pltpu.VMEM((2, samples * height * kept, LANES), F32),
            pltpu.VMEM((samples, 2 * height, breadth, depth), F32),
            pltpu.VMEM((samples, 2 * height, breadth, channels), F32),
        ],
    )


def put_slopes(slope, near_ref, far_ref, halo_ref, width, first_cell):
    samples, height, kept, _ = near_ref.shape
    lat = lax.axis_index("lat")
    other = pl.ds(height * (1 - lat), height)
    slope[:, pl.ds(height * lat, height)] = near_ref[...]
    slope[:, other] = far_ref[...]
    for s in range(samples):
        beside = gelu_slope(halo_ref[s].astype(F32))
        for side in range(2):
            for col in range(width):
                here = first_cell + (side * width + col) * height
                at = kept - EDGE + col if side else EDGE - width + col
                slope[s, other, at, :] = beside[here : here + height]


def globe_kernel(own_ref, cross_ref, line_ref, corner_ref, near_ref, far_ref, halo_ref, cat_ref, moved_ref, latent, slope, wide):
    samples, rows, kept, depth = own_ref.shape
    height = rows - 1
    tall = 2 * height
    breadth = kept - 2 * EDGE
    lat = lax.axis_index("lat")
    own = 8 + EDGE
    latent[...] = jnp.zeros(latent.shape, F32)
    latent[:, pl.ds((height - 1) * lat, rows)] = own_ref[...].astype(F32) + cross_ref[...].astype(F32)
    latent[:, pl.ds((height - 1) * (1 - lat), rows)] += line_ref[...].astype(F32) + corner_ref[...].astype(F32)
    put_slopes(slope, near_ref, far_ref, halo_ref, 2, 0)
    wide[:, :, 8 : 8 + kept, :] = (latent[...] * slope[...]).astype(BF).astype(F32)
    for v in STEPS:
        lanes = slice((v + 1) * depth, (v + 2) * depth)
        cat_ref[:, 1 : 1 + tall, :, lanes] = wide[:, :, 8 - v : 8 - v + kept + 8, :].astype(BF)
        moved_ref[v + 1, :, 1 : 1 + tall] = wide[:, :, own - v : own - v + breadth, :].astype(BF)
    for row in (0, tall + 1):
        cat_ref[:, row] = jnp.zeros(cat_ref.shape[:1] + cat_ref.shape[2:], BF)
        moved_ref[:, :, row] = jnp.zeros(moved_ref.shape[:2] + moved_ref.shape[3:], BF)


def globe(own, cross, line, angle, near, far, halo):
    samples, rows, kept, depth = own.shape
    tall, breadth = 2 * (rows - 1), kept - 2 * EDGE
    return run(
        "latent_grads",
        globe_kernel,
        [
            jax.ShapeDtypeStruct((samples, tall + 2, kept + 8, 3 * depth), BF),
            jax.ShapeDtypeStruct((3, samples, tall + 2, breadth, depth), BF),
        ],
        [own, cross, line, angle, near, far, halo],
        [
            pltpu.VMEM((samples, tall, kept, depth), F32),
            pltpu.VMEM((samples, tall, kept, depth), F32),
            pltpu.VMEM((samples, tall, kept + 24, depth), F32),
        ],
    )


def band_rows(norm_factor, left_ref, moved_ref, mine_ref, other_ref):
    channels, cells = left_ref.shape
    _, samples, padded, breadth, depth = moved_ref.shape
    tall = padded - 2
    lat = lax.axis_index("lat")
    core, _ = core_and_chip()
    half = channels // 2

    def put(left, u, v, start, size):
        right = moved_ref[v + 1, :, pl.ds(1 - u, tall)].reshape(cells, depth)
        part = dot_plain(left, right) * norm_factor
        lower, upper = part[:, :LANES], part[:, LANES:]
        here = pl.ds(pl.multiple_of(start, half), size)
        mine_ref[here, :] = jnp.where(core == 0, lower, upper).astype(BF)
        other_ref[here, :] = jnp.where(core == 0, upper, lower).astype(BF)

    for j in range(4):
        (u0, v0), (u1, v1) = (divmod(k, 3) for k in (j, 5 + j))
        put(left_ref[...], u0 - 1 + lat * (u1 - u0), v0 - 1 + lat * (v1 - v0), lat * half + j * channels, channels)
    put(left_ref[pl.ds(pl.multiple_of(lat * half, half), half), :], 0, 0, (1 - lat) * 4 * channels, half)


def second_band_kernel(norm_factor, moved_ref, act_ref, mine_ref, other_ref):
    band_rows(norm_factor, act_ref, moved_ref, mine_ref, other_ref)


def first_band_kernel(norm_factor, cat_ref, near_ref, far_ref, halo_ref, input_ref, weights_ref, moved_ref, mine_ref, other_ref, slope, wide):
    samples, padded, broad, triple = cat_ref.shape
    tall, kept, depth = padded - 2, broad - 8, triple // 3
    height = tall // 2
    breadth = kept - 2 * EDGE
    lat = lax.axis_index("lat")
    own = 8 + EDGE
    put_slopes(slope, near_ref, far_ref, halo_ref, 1, 4 * height)
    linear = None
    for u in STEPS:
        weights = jnp.concatenate([weights_ref[3 * (u + 1) + (v + 1)] for v in STEPS], axis=1)
        part = dot_last(cat_ref[:, 1 - u : 1 - u + tall].reshape(samples * tall * broad, triple), weights)
        linear = part if linear is None else linear + part
    linear = linear.reshape(samples, tall, broad, depth)[:, :, :kept]
    wide[:, :, 8 : 8 + kept, :] = (linear * slope[...]).astype(BF).astype(F32)
    for v in STEPS:
        moved_ref[v + 1, :, 1 : 1 + tall] = wide[:, :, own - v : own - v + breadth, :].astype(BF)
    for row in (0, tall + 1):
        moved_ref[:, :, row] = jnp.zeros(moved_ref.shape[:2] + moved_ref.shape[3:], BF)
    band_rows(norm_factor, input_ref, moved_ref, mine_ref, other_ref)


def second_band(norm_factor, moved, act):
    half = jax.ShapeDtypeStruct((9 * act.shape[0] // 2, LANES), BF)
    return run("second_weight_grads", functools.partial(second_band_kernel, norm_factor), [half, half], [moved, act])


def first_band(norm_factor, cat, near, far, halo, cells_in, w_second):
    samples, padded, broad, triple = cat.shape
    tall, kept, depth = padded - 2, broad - 8, triple // 3
    breadth = kept - 2 * EDGE
    half = jax.ShapeDtypeStruct((9 * cells_in.shape[0] // 2, LANES), BF)
    return run(
        "encoder_grads",
        functools.partial(first_band_kernel, norm_factor),
        [jax.ShapeDtypeStruct((3, samples, padded, breadth, depth), BF), half, half],
        [cat, near, far, halo, cells_in, w_second],
        [pltpu.VMEM((samples, tall, kept, depth), F32), pltpu.VMEM((samples, tall, kept + 16, depth), F32)],
    )


def input_band_kernel(moved_ref, w_first_ref, out_ref):
    samples, height, breadth, channels = out_ref.shape
    depth = moved_ref.shape[4]
    lat = lax.axis_index("lat")
    total = None
    for u in STEPS:
        weights = jnp.concatenate([w_first_ref[3 * (u + 1) + (v + 1)] for v in STEPS], axis=1)
        left = [moved_ref[v + 1, :, pl.ds(height * lat + 1 - u, height)].reshape(-1, depth) for v in STEPS]
        part = dot_last(jnp.concatenate(left, axis=1), weights)
        total = part if total is None else total + part
    out_ref[...] = total.astype(BF).reshape(out_ref.shape)


def blocks_kernel(first_mine, first_got, second_mine, second_got, *outs):
    lon = lax.axis_index("lon")
    rows = first_mine.shape[1]
    for step, out_ref in enumerate(outs):
        block = partner(lon, step, len(outs))
        out_ref[:rows] = (first_mine[block].astype(F32) + first_got[block].astype(F32)).astype(BF)
        out_ref[rows:] = (second_mine[block].astype(F32) + second_got[block].astype(F32)).astype(BF)


def halves_kernel(mine_ref, other_ref, first_ref, second_ref):
    core, _ = core_and_chip()
    mine, other = mine_ref[...].astype(F32), other_ref[...].astype(F32)
    rows = mine.shape[0] // 3
    for part in range(2):
        value = jnp.where(core == part, mine, other)
        first_ref[pl.ds(part, rows, stride=2), :] = value[:rows]
        second_ref[pl.ds(part, 2 * rows, stride=2), :] = value[rows:]


def to_partner(array, step):
    count = lax.axis_size("lon")
    return lax.ppermute(array, "lon", [(partner(i, step, count), i) for i in range(count)])


def two_bands(head_grads, head_weights, encoder_input, pre_first, pre_second, w_first, w_second, norm_factor):
    samples, height, breadth, _ = encoder_input.shape
    columns = lax.axis_size("lon")
    to_right, to_left, tile_second, tile = pack(head_grads, pre_second, pre_first, encoder_input, True)
    low = around(to_right, "lon", 1)
    high = around(to_left, "lon", -1)
    tile_second = swap(tile_second, "lat", 1)
    head_grads, head_weights, w_second, pre_second, pre_first, encoder_input = stage(
        head_grads, head_weights, w_second, pre_second, pre_first, encoder_input
    )
    tile = swap(tile, "lat", 1)
    low, high, tile_second, tile = lax.optimization_barrier((low, high, tile_second, tile))
    heads_of = functools.partial(
        head_conv,
        head_grads=head_grads,
        low=low,
        high=high,
        head_weights=head_weights,
        slots=2 * samples,
        rows=height + 1,
    )
    got = swap(heads_of(True, False), "lead", 1)
    near_second, near_first, halo = near_parts(pre_second, pre_first, low, high)
    mine = heads_of(False, False)
    got, halo = lax.optimization_barrier((got, halo))
    halo = swap(halo, "lat", 1)
    part_shape = jax.ShapeDtypeStruct((samples,) + mine.shape[1:], BF)
    own, cross = run("core_sum", core_sum_kernel, [part_shape, part_shape], [mine, got])
    cross_got, line_got, corner_got = swap(cross, "lead", 2), swap(own, "lat", 1), corner(cross, None)
    far_second, far_first, act, cells_in = far_parts(pre_first, encoder_input, tile_second, tile)

    cat, moved = globe(own, cross_got, line_got, corner_got, near_second, far_second, halo)
    second_mine, second_other = second_band(norm_factor, moved, act)
    second_got = swap(second_other, "lead", 1)
    moved_first, first_mine, first_other = first_band(norm_factor, cat, near_first, far_first, halo, cells_in, w_second)
    first_got = swap(first_other, "lead", 1)
    input_grad = run(
        "input_conv", input_band_kernel, [jax.ShapeDtypeStruct(encoder_input.shape, BF)], [moved_first, w_first]
    )[0]

    blocks = [t.reshape(columns, -1, LANES) for t in (first_mine, first_got, second_mine, second_got)]
    rows = blocks[0].shape[1]
    share_shape = jax.ShapeDtypeStruct((3 * rows, LANES), BF)
    shares = run("blocks", blocks_kernel, [share_shape] * columns, blocks)
    parts = [to_partner(shares[step], step) for step in range(1, columns)]
    share = run("share", sum_kernel, [share_shape], [shares[0], *parts])[0]
    both = run("chips", sum_kernel, [share_shape], [share, swap(share, "lead", 2)])[0]
    result_first, result_second = run(
        "cores",
        halves_kernel,
        [jax.ShapeDtypeStruct((2 * rows, LANES), F32), jax.ShapeDtypeStruct((4 * rows, LANES), F32)],
        [both, swap(both, "lead", 1)],
    )
    return input_grad, result_first.reshape(-1), result_second.reshape(-1)


def core_sum_kernel(mine_ref, got_ref, own_ref, cross_ref):
    samples = own_ref.shape[0]
    for ref, part in ((own_ref, slice(0, samples)), (cross_ref, slice(samples, 2 * samples))):
        ref[...] = (mine_ref[part].astype(F32) + got_ref[part].astype(F32)).astype(BF)


def general(head_grads, head_weights, encoder_input, pre_first, pre_second, w_first, w_second, norm_factor):
    samples, height, breadth, _ = encoder_input.shape
    bands, columns = lax.axis_size("lat"), lax.axis_size("lon")
    to_right, to_left = pack(head_grads, pre_second, pre_first, encoder_input, False)
    to_right, to_left, to_cross = lax.optimization_barrier((to_right, to_left, pre_first))
    low = around(to_right, "lon", 1)
    high = around(to_left, "lon", -1)
    act_got = activated(swap(to_cross, "lead", 2))
    head_grads, head_weights, w_second, pre_second, pre_first, encoder_input = stage(
        head_grads, head_weights, w_second, pre_second, pre_first, encoder_input
    )
    low, high, act_got = lax.optimization_barrier((low, high, act_got))

    steps = [1, -1]
    heads_of = functools.partial(head_conv, head_grads=head_grads, high=high, head_weights=head_weights, slots=samples, rows=height + 2)
    got_cross = swap(heads_of(True, True, low=low), "lead", 1)
    got_own = swap(heads_of(True, False, low=low), "lead", 1)
    cross, *angles = spread_cross(heads_of(False, True, low=low), got_cross, len(steps))
    low_later, cross, *angles = lax.optimization_barrier((low, cross, *angles))
    cross = swap(cross, "lead", 2)
    angles = [corner(angle, step) for angle, step in zip(angles, steps)]
    second, first, slope_second, slope_first, act, cells_in = saved(pre_second, pre_first, encoder_input, low, high)
    own, *lines = spread_own(heads_of(False, False, low=low_later), got_own, second, first, len(steps))
    lines = [swap(line, "lat", 1) if step is None else around(line, "lat", step, False) for line, step in zip(lines, steps)]
    strips = [strip for pair in zip(lines, angles) for strip in pair]

    grad, away, slope = latent_grads(len(steps), bands, own, cross, strips, slope_second, slope_first)
    grad_got = swap(away, "lead", 2)
    moved, first_mine, first_other = encoder(norm_factor, bands, grad, slope, cells_in, w_second)
    input_grad = input_conv(moved, w_first)
    first_got = swap(first_other, "lead", 1)
    second_mine, second_other = second_grads(norm_factor, bands * columns, grad, grad_got, act, act_got)
    second_got = swap(second_other, "lead", 1)

    first_terms = [pairwise([first_mine, first_got], bands)]
    second_terms = [pairwise([second_mine, second_got], bands)]
    first_came = swap(other_band(first_terms, columns), "lat", 1)
    second_came = swap(other_band(second_terms, columns), "lat", 1)
    blocks = [t.reshape(2, columns, -1, LANES) for t in first_terms + second_terms]
    rows = blocks[0].shape[2]
    share_shape = jax.ShapeDtypeStruct((2, rows, LANES), BF)
    shares = run("own_band", own_band_kernel, [share_shape] * columns, blocks + [first_came, second_came])
    parts = [to_partner(shares[step], step) for step in range(1, columns)]
    share = run("share", sum_kernel, [share_shape], [shares[0], *parts])[0]
    both = run("chips", chips_kernel, [jax.ShapeDtypeStruct((3, rows, LANES), BF)], [share, swap(share, "lead", 2)])[0]
    result_first, result_second = run(
        "cores",
        cores_kernel,
        [jax.ShapeDtypeStruct((2 * rows, LANES), F32), jax.ShapeDtypeStruct((4 * rows, LANES), F32)],
        [both, swap(both, "lead", 1)],
    )
    return input_grad, result_first.reshape(-1), result_second.reshape(-1)


def per_device(head_grads, head_weights, encoder_input, pre_first, pre_second, w_first, w_second):
    samples, height, breadth, channels = encoder_input.shape
    bands, columns = lax.axis_size("lat"), lax.axis_size("lon")
    cells_total = samples * lax.axis_size("lead") * height * bands * breadth * columns
    norm_factor = 1.0 / math.sqrt(cells_total)
    plan = two_bands if bands == 2 and 9 * channels // (bands * columns) % 16 == 0 else general
    return plan(head_grads, head_weights, encoder_input, pre_first, pre_second, w_first, w_second, norm_factor)


def solution(mesh):
    in_specs = (
        P("lead", None, "lat", "lon", None),
        P("lead", None, None, None),
        P("lead", "lat", "lon", None),
        P("lead", "lat", "lon", None),
        P("lead", "lat", "lon", None),
        P(),
        P(),
    )
    out_specs = (P("lead", "lat", "lon", None), P(("lat", "lon")), P(("lat", "lon")))
    return jax.shard_map(
        per_device, mesh=mesh, in_specs=in_specs, out_specs=out_specs, check_vma=False
    )
```

```python
import functools
import math

import jax
import jax.numpy as jnp
from jax import lax
from jax.experimental import pallas as pl
from jax.experimental.pallas import tpu as pltpu
from jax.sharding import PartitionSpec as P

BF = jnp.bfloat16
F32 = jnp.float32
STEPS = (-1, 0, 1)
EDGE = 4
LANES = 128
VMEM_BYTES = 24 * 1024 * 1024


def erf_part(values):
    return 0.5 * (1.0 + lax.erf(values * 0.7071067811865476))


def gelu_slope(values):
    return erf_part(values) + values * jnp.exp(-0.5 * values * values) * 0.3989422804014327


def gelu_value(values):
    return values * erf_part(values)


def dot_last(left, right):
    return lax.dot_general(left, right, (((1,), (1,)), ((), ())), preferred_element_type=F32)


def dot_plain(left, right):
    return lax.dot_general(left, right, (((1,), (0,)), ((), ())), preferred_element_type=F32)


def core_and_chip():
    lead = lax.axis_index("lead")
    return lax.rem(lead, 2), lax.div(lead, 2)


def run(name, kernel, out_shape, arrays, scratch=(), flops=0, far=False):
    specs = [pl.BlockSpec(memory_space=pltpu.HBM if far else pltpu.VMEM)] * len(arrays)
    if far:
        arrays = [pltpu.with_memory_space_constraint(a, pltpu.HBM) for a in arrays]
    touched = sum(a.size * a.dtype.itemsize for a in arrays)
    touched += sum(math.prod(s.shape) * s.dtype.itemsize for s in out_shape)
    return pl.pallas_call(
        kernel,
        name=name,
        out_shape=out_shape,
        in_specs=specs,
        out_specs=[pl.BlockSpec(memory_space=pltpu.VMEM)] * len(out_shape),
        scratch_shapes=list(scratch),
        compiler_params=pltpu.CompilerParams(vmem_limit_bytes=VMEM_BYTES),
        cost_estimate=pl.CostEstimate(flops=1, bytes_accessed=1, transcendentals=0),
    )(*arrays)


def pack_kernel(grads_far, second_far, first_far, right_ref, left_ref, grads_near, second_near, first_near, edges, edges_wide, packed, sems):
    heads, batch, height, breadth, _ = grads_far.shape
    samples = second_far.shape[0]
    rows = 6 * height
    copies = []
    for side in range(2):
        columns = pl.ds(breadth - 16 if side == 0 else 0, 16)
        for j, (far, near) in enumerate(((grads_far, grads_near), (second_far, second_near), (first_far, first_near))):
            source = far.at[:, :, :, columns, :] if j == 0 else far.at[:, :, columns, :]
            copies.append(pltpu.make_async_copy(source, near.at[side], sems.at[side, j]))
            copies[-1].start()
    for copy in copies:
        copy.wait()
    for side, out_ref in ((0, right_ref), (1, left_ref)):
        start = 8 if side == 0 else 0
        grads_ref, second_ref, first_ref = grads_near.at[side], second_near.at[side], first_near.at[side]
        for h in range(heads):
            for b in range(batch):
                block = grads_ref[h, b, :, start : start + 8, :].astype(F32)
                edges[(h * batch + b) * height * 8 : (h * batch + b + 1) * height * 8, :] = block.reshape(height * 8, LANES)
        for j, ref in enumerate((second_ref, first_ref)):
            for s in range(samples):
                block = ref[s, :, start : start + 8, :].astype(F32)
                at = (j * samples + s) * height * 8
                for half in range(2):
                    lanes = slice(half * LANES, (half + 1) * LANES)
                    edges_wide[half, at : at + height * 8, :] = block[:, :, lanes].reshape(height * 8, LANES)
        for b in range(batch):
            for col in range(3):
                inner = 5 + col if side == 0 else col
                for h in range(heads):
                    at = b * rows + (col * 2 + h) * height
                    packed[at : at + height, :] = edges[pl.ds((h * batch + b) * height * 8 + inner, height, stride=8), :]
        for s in range(samples):
            for q in range(3):
                j, col, width = (0, q, 2) if q < 2 else (1, 0, 1)
                inner = 8 - width + col if side == 0 else col
                for half in range(2):
                    at = (batch + s) * rows + (q * 2 + half) * height
                    packed[at : at + height, :] = edges_wide[
                        half, pl.ds((j * samples + s) * height * 8 + inner, height, stride=8), :
                    ]
        out_ref[...] = packed[...].astype(BF).reshape(out_ref.shape)


def pack(head_grads, pre_second, pre_first):
    heads, batch, height, _, _ = head_grads.shape
    samples = pre_second.shape[0]
    shape = jax.ShapeDtypeStruct((batch + samples, 6 * height, LANES), BF)
    return run(
        "pack_columns",
        pack_kernel,
        [shape, shape],
        [head_grads, pre_second, pre_first],
        [
            pltpu.VMEM((2, heads, batch, height, 16, LANES), BF),
            pltpu.VMEM((2, samples, height, 16, 2 * LANES), BF),
            pltpu.VMEM((2, samples, height, 16, 2 * LANES), BF),
            pltpu.VMEM((heads * batch * height * 8, LANES), F32),
            pltpu.VMEM((2, 2 * samples * height * 8, LANES), F32),
            pltpu.VMEM(((batch + samples) * 6 * height, LANES), F32),
            pltpu.SemaphoreType.DMA((2, 3)),
        ],
        far=True,
    )


def stage_kernel(*refs):
    count = len(refs) // 2
    sems = refs[-1]
    copies = [pltpu.make_async_copy(refs[i], refs[count + i], sems.at[i]) for i in range(count)]
    for copy in copies:
        copy.start()
    for copy in copies:
        copy.wait()


def stage(*arrays):
    shapes = [pltpu.VMEM(a.shape, a.dtype) for a in arrays]
    return run("stage", stage_kernel, shapes, list(arrays), [pltpu.SemaphoreType.DMA((len(arrays),))], far=True, flops=1 << 30)


def heads_kernel(other_core, other_chip, samples, grads_ref, low_ref, high_ref, weights_ref, out_ref, wide, shifted, total):
    heads, batch, height, breadth, _ = grads_ref.shape
    slots, _, kept, depth = out_ref.shape
    pitch = kept + 16
    own = 8 + EDGE
    core, chip = core_and_chip()
    core = 1 - core if other_core else core
    for slot in range(slots):
        group = 1 - chip if other_chip != (slot >= samples) else chip
        b = (2 * group + core) * samples + slot % samples
        low = low_ref[b].astype(F32)
        high = high_ref[b].astype(F32)
        for r in range(height):
            at = (slot * height + r) * pitch + own
            for h in range(heads):
                wide[h, at : at + breadth, :] = grads_ref[h, b, r].astype(F32)
        for col in range(3):
            for h in range(heads):
                here = (col * 2 + h) * height
                at = slot * height * pitch + own + col
                wide[h, pl.ds(at - 3, height, stride=pitch), :] = low[here : here + height]
                wide[h, pl.ds(at + breadth, height, stride=pitch), :] = high[here : here + height]
        for v in STEPS:
            for h in range(heads):
                starts = [(slot * height + r) * pitch + 8 - v for r in range(height)]
                moved = jnp.concatenate([wide[h, at : at + kept, :] for at in starts], axis=0).astype(BF)
                lane = ((v + 1) * heads + h) * LANES
                shifted[slot * height * kept : (slot + 1) * height * kept, lane : lane + LANES] = moved
    total[:, height:, :, :] = jnp.zeros((slots, 2, kept, depth), F32)
    for u in STEPS:
        weights = jnp.concatenate(
            [weights_ref[h, 3 * (u + 1) + (v + 1)] for v in STEPS for h in range(heads)], axis=1
        )
        part = dot_last(shifted[...], weights).reshape(slots, height, kept, depth)
        if u == -1:
            total[:, :height] = part
        else:
            total[:, 1 + u : 1 + u + height] += part
    if out_ref.shape[1] == height + 2:
        out_ref[...] = total[...].astype(BF)
    else:
        out_ref[...] = total[:, pl.ds(1 - lax.axis_index("lat"), height + 1)].astype(BF)


def head_conv(other_core, other_chip, head_grads, low, high, head_weights, slots, rows):
    samples = head_grads.shape[1] // lax.axis_size("lead")
    heads, batch, height, breadth, _ = head_grads.shape
    depth = head_weights.shape[2]
    kept = breadth + 2 * EDGE
    return run(
        "head_conv",
        functools.partial(heads_kernel, other_core, other_chip, samples),
        [jax.ShapeDtypeStruct((slots, rows, kept, depth), BF)],
        [head_grads, low, high, head_weights],
        [
            pltpu.VMEM((heads, slots * height * (kept + 16), LANES), F32),
            pltpu.VMEM((slots * height * kept, 3 * heads * LANES), BF),
            pltpu.VMEM((slots, height + 2, kept, depth), F32),
        ],
        flops=2 * slots * height * kept * 9 * heads * LANES * depth,
    )[0]


def saved_kernel(second_ref, first_ref, input_ref, low_ref, high_ref, second_out, first_out, slope_second, slope_first, act_out, input_out, wide):
    samples, height, breadth, depth = second_ref.shape
    kept = breadth + 2 * EDGE
    batch = low_ref.shape[0] - samples
    for ref, width, out_ref, slope_ref in (
        (second_ref, 2, second_out, slope_second),
        (first_ref, 1, first_out, slope_first),
    ):
        wide[...] = jnp.zeros(wide.shape, F32)
        for s in range(samples):
            for r in range(height):
                at = (s * height + r) * kept + EDGE
                for half in range(2):
                    lanes = slice(half * LANES, (half + 1) * LANES)
                    wide[half, at : at + breadth, :] = ref[s, r, :, lanes].astype(F32)
            low = low_ref[batch + s].astype(F32)
            high = high_ref[batch + s].astype(F32)
            for col in range(width):
                for half in range(2):
                    here = ((col if width == 2 else 2) * 2 + half) * height
                    at = s * height * kept + EDGE + col
                    wide[half, pl.ds(at - width, height, stride=kept), :] = low[here : here + height]
                    wide[half, pl.ds(at + breadth, height, stride=kept), :] = high[here : here + height]
        value = jnp.concatenate([wide[0], wide[1]], axis=1)
        out_ref[...] = value.astype(BF).reshape(out_ref.shape)
        slope_ref[...] = gelu_slope(value).reshape(slope_ref.shape)
    active = gelu_value(first_ref[...].astype(F32).reshape(samples * height * breadth, depth)).astype(BF).astype(F32)
    act_out[...] = active.T.astype(BF)
    cells = input_ref[...].astype(F32).reshape(samples * height * breadth, input_ref.shape[3])
    input_out[...] = cells.T.astype(BF)


def saved(pre_second, pre_first, encoder_input, low, high):
    samples, height, breadth, depth = pre_second.shape
    kept = breadth + 2 * EDGE
    cells = samples * height * breadth
    return run(
        "saved_parts",
        saved_kernel,
        [
            jax.ShapeDtypeStruct((samples, height, kept, depth), BF),
            jax.ShapeDtypeStruct((samples, height, kept, depth), BF),
            jax.ShapeDtypeStruct((samples, height, kept, depth), F32),
            jax.ShapeDtypeStruct((samples, height, kept, depth), F32),
            jax.ShapeDtypeStruct((depth, cells), BF),
            jax.ShapeDtypeStruct((encoder_input.shape[3], cells), BF),
        ],
        [pre_second, pre_first, encoder_input, low, high],
        [pltpu.VMEM((2, samples * height * kept, LANES), F32)],
    )


def goes_down(way, ways):
    return 1 - lax.axis_index("lat") if ways == 1 else 1 - way


def cross_kernel(mine_ref, got_ref, cross_ref, *strips):
    height = mine_ref.shape[1] - 2
    cross_ref[...] = (mine_ref[...].astype(F32) + got_ref[...].astype(F32)).astype(BF)
    for way, corner_ref in enumerate(strips):
        corner_ref[...] = cross_ref[:, pl.ds((height - 1) * goes_down(way, len(strips)), 3)]


def own_kernel(mine_ref, got_ref, second_ref, first_ref, own_ref, *strips):
    height = second_ref.shape[1]
    own_ref[...] = (mine_ref[...].astype(F32) + got_ref[...].astype(F32)).astype(BF)
    for way, line_ref in enumerate(strips):
        down = goes_down(way, len(strips))
        line_ref[:, 0:3] = own_ref[:, pl.ds((height - 1) * down, 3)]
        line_ref[:, 3:5] = second_ref[:, pl.ds((height - 2) * down, 2)]
        line_ref[:, 5:6] = first_ref[:, pl.ds((height - 1) * down, 1)]


def spread_cross(mine, got, ways):
    samples, _, kept, depth = mine.shape
    strip = jax.ShapeDtypeStruct((samples, 3, kept, depth), BF)
    return run("core_sum_cross", cross_kernel, [jax.ShapeDtypeStruct(mine.shape, BF)] + [strip] * ways, [mine, got])


def spread_own(mine, got, second, first, ways):
    samples, _, kept, depth = mine.shape
    strip = jax.ShapeDtypeStruct((samples, 6, kept, depth), BF)
    return run("core_sum_own", own_kernel, [jax.ShapeDtypeStruct(mine.shape, BF)] + [strip] * ways, [mine, got, second, first])


def latent_kernel(ways, bands, own_ref, cross_ref, *refs):
    strips, refs = refs[: 2 * ways], refs[2 * ways :]
    slope_second_ref, slope_first_ref, grad_ref, away_ref, slope_out, latent, slope_second = refs
    samples, rows, kept, depth = own_ref.shape
    height = rows - 2
    lat = lax.axis_index("lat")
    _, chip = core_and_chip()
    blank = jnp.zeros((samples, kept, depth), F32)
    latent[:, 0] = blank
    latent[:, height + 3] = blank
    latent[:, 1 : height + 3] = own_ref[...].astype(F32) + cross_ref[...].astype(F32)
    slope_second[:, 2 : 2 + height] = slope_second_ref[...]
    slope_out[:, 1 : 1 + height] = slope_first_ref[...]
    for way in range(ways):
        line_ref, corner_ref = strips[2 * way], strips[2 * way + 1]
        below = 1 - lat if ways == 1 else way
        at = (height + 1) * below
        latent[:, pl.ds(at, 3)] += line_ref[:, 0:3].astype(F32) + corner_ref[...].astype(F32)
        slope_second[:, pl.ds((height + 2) * below, 2)] = gelu_slope(line_ref[:, 3:5].astype(F32))
        slope_out[:, pl.ds((height + 1) * below, 1)] = gelu_slope(line_ref[:, 5:6].astype(F32))
    for i in range(height + 4):
        row = lat * height + i - 2
        valid = jnp.logical_and(row >= 0, row < bands * height)
        value = latent[:, i] * slope_second[:, i]
        if i < 2 or i >= height + 2:
            value = jnp.where(valid, value, 0.0)
        grad_ref[:, i] = value.astype(BF)
        if 0 < i < height + 3:
            away_ref[:, i - 1] = jnp.where(chip == 0, value[:, :, LANES:], value[:, :, :LANES]).astype(BF)


def latent_grads(ways, bands, own, cross, strips, slope_second, slope_first):
    samples, rows, kept, depth = own.shape
    return run(
        "latent_grads",
        functools.partial(latent_kernel, ways, bands),
        [
            jax.ShapeDtypeStruct((samples, rows + 2, kept, depth), BF),
            jax.ShapeDtypeStruct((samples, rows, kept, LANES), BF),
            jax.ShapeDtypeStruct((samples, rows, kept, depth), F32),
        ],
        [own, cross, *strips, slope_second, slope_first],
        [
            pltpu.VMEM((samples, rows + 2, kept, depth), F32),
            pltpu.VMEM((samples, rows + 2, kept, depth), F32),
        ],
    )


def encoder_kernel(norm_factor, bands, grad_ref, slope_ref, input_ref, weights_ref, moved_out, mine_ref, other_ref, wide, cat, wide_first):
    samples, tall, kept, depth = grad_ref.shape
    rows = tall - 2
    height = rows - 2
    breadth = kept - 2 * EDGE
    lat = lax.axis_index("lat")
    core, _ = core_and_chip()
    own = 8 + EDGE
    wide[:, :, 8 : 8 + kept, :] = grad_ref[...].astype(F32)
    for v in STEPS:
        lanes = slice((v + 1) * depth, (v + 2) * depth)
        cat[:, :, :, lanes] = wide[:, :, 8 - v : 8 - v + kept + 8, :].astype(BF)
    linear = None
    for u in STEPS:
        weights = jnp.concatenate([weights_ref[3 * (u + 1) + (v + 1)] for v in STEPS], axis=1)
        left = cat[:, 1 - u : 1 - u + rows].reshape(samples * rows * (kept + 8), 3 * depth)
        part = dot_last(left, weights)
        linear = part if linear is None else linear + part
    linear = linear.reshape(samples, rows, kept + 8, depth)
    for i in range(rows):
        row = lat * height + i - 1
        valid = jnp.logical_and(row >= 0, row < bands * height)
        value = linear[:, i, :kept] * slope_ref[:, i]
        if i < 1 or i >= height + 1:
            value = jnp.where(valid, value, 0.0)
        wide_first[:, i, 8 : 8 + kept, :] = value.astype(BF).astype(F32)
    for v in STEPS:
        lanes = slice((v + 1) * depth, (v + 2) * depth)
        moved_out[:, :, :, lanes] = wide_first[:, :, own - v : own - v + breadth, :].astype(BF)
    for u in STEPS:
        right = moved_out[:, 1 - u : 1 - u + height].reshape(samples * height * breadth, 3 * depth)
        part = dot_plain(input_ref[...], right) * norm_factor
        for v in STEPS:
            k = 3 * (u + 1) + (v + 1)
            lower = part[:, (v + 1) * depth : (v + 1) * depth + LANES]
            upper = part[:, (v + 1) * depth + LANES : (v + 2) * depth]
            mine_ref[k] = jnp.where(core == 0, lower, upper).astype(BF)
            other_ref[k] = jnp.where(core == 0, upper, lower).astype(BF)


def encoder(norm_factor, bands, grad, slope, cells_in, w_second):
    samples, tall, kept, depth = grad.shape
    rows, height, breadth = tall - 2, tall - 4, kept - 2 * EDGE
    channels = cells_in.shape[0]
    half = jax.ShapeDtypeStruct((9, channels, LANES), BF)
    return run(
        "encoder_grads",
        functools.partial(encoder_kernel, norm_factor, bands),
        [jax.ShapeDtypeStruct((samples, rows, breadth, 3 * depth), BF), half, half],
        [grad, slope, cells_in, w_second],
        [
            pltpu.VMEM((samples, tall, kept + 24, depth), F32),
            pltpu.VMEM((samples, tall, kept + 8, 3 * depth), BF),
            pltpu.VMEM((samples, rows, kept + 16, depth), F32),
        ],
        flops=2 * 9 * depth * (samples * rows * (kept + 8) * depth + samples * height * breadth * channels),
    )


def second_kernel(norm_factor, shares, grad_ref, got_ref, act_ref, act_got_ref, *refs):
    full_ref, wide, cat = refs[-3:]
    samples, tall, kept, depth = grad_ref.shape
    rows, height, breadth = tall - 2, tall - 4, kept - 2 * EDGE
    core, chip = core_and_chip()
    own = 8 + EDGE
    lower = grad_ref[:, 1 : 1 + rows, :, :LANES].astype(F32)
    upper = grad_ref[:, 1 : 1 + rows, :, LANES:].astype(F32)
    wide[:samples, :, 8 : 8 + kept, :] = jnp.where(chip == 0, lower, upper)
    wide[samples:, :, 8 : 8 + kept, :] = got_ref[...].astype(F32)
    for v in STEPS:
        lanes = slice((v + 1) * LANES, (v + 2) * LANES)
        cat[:, :, :, lanes] = wide[:, :, own - v : own - v + breadth, :].astype(BF)
    cells = samples * height * breadth
    for u in STEPS:
        right = cat[:, 1 - u : 1 - u + height].reshape(2 * cells, 3 * LANES)
        part = dot_plain(act_ref[...], right[:cells]) + dot_plain(act_got_ref[...], right[cells:])
        part = part * norm_factor
        for v in STEPS:
            k = 3 * (u + 1) + (v + 1)
            full_ref[k * depth : (k + 1) * depth, :] = part[:, (v + 1) * LANES : (v + 2) * LANES].astype(BF)
    if len(refs) == 5:
        size = 9 * depth // shares // 2
        for i in range(shares):
            for out_ref, half in ((refs[0], core), (refs[1], 1 - core)):
                out_ref[i] = full_ref[pl.ds(pl.multiple_of((2 * i + half) * size, 16), size), :]


def second_grads(norm_factor, shares, grad, got, act, act_got):
    samples, tall, kept, depth = grad.shape
    rows, height, breadth = tall - 2, tall - 4, kept - 2 * EDGE
    size = 9 * depth // shares // 2
    inside = size % 16 == 0
    half = jax.ShapeDtypeStruct((shares, size, LANES), BF)
    scratch = [
        pltpu.VMEM((2 * samples, rows, kept + 16, LANES), F32),
        pltpu.VMEM((2 * samples, rows, breadth, 3 * LANES), BF),
    ]
    results = run(
        "second_weight_grads",
        functools.partial(second_kernel, norm_factor, shares),
        [half, half] if inside else [jax.ShapeDtypeStruct((9 * depth, LANES), BF)],
        [grad, got, act, act_got],
        [pltpu.VMEM((9 * depth, LANES), BF)] + scratch if inside else scratch,
        flops=2 * 9 * depth * LANES * 2 * samples * height * breadth,
    )
    if inside:
        return results
    halves = results[0].reshape(shares, 2, size, LANES)
    core, _ = core_and_chip()
    return [lax.dynamic_index_in_dim(halves, part, 1, keepdims=False) for part in (core, 1 - core)]


def act_kernel(source_ref, out_ref):
    samples, height, breadth, depth = source_ref.shape
    active = gelu_value(source_ref[...].astype(F32).reshape(samples * height * breadth, depth)).astype(BF).astype(F32)
    out_ref[...] = active.T.astype(BF)


def activated(source):
    samples, height, breadth, depth = source.shape
    return run("activated", act_kernel, [jax.ShapeDtypeStruct((depth, samples * height * breadth), BF)], [source])[0]


def other_band_kernel(*refs):
    band = 1 - lax.rem(lax.axis_index("lat"), 2)
    parts = [t[band].astype(F32) for t in refs[:-1]]
    refs[-1][...] = sum(parts[1:], parts[0]).astype(BF)


def partner(index, step, count):
    return index ^ step if count & (count - 1) == 0 else (index + step) % count


def own_band_kernel(*refs):
    columns = refs[0].shape[1]
    terms, came, outs = refs[: -columns - 2], refs[-columns - 2 : -columns], refs[-columns:]
    band, lon = lax.rem(lax.axis_index("lat"), 2), lax.axis_index("lon")
    for step in range(columns):
        block = partner(lon, step, columns)
        for layer in range(2):
            parts = [t[band, block].astype(F32) for t in terms[layer * len(terms) // 2 : (layer + 1) * len(terms) // 2]]
            outs[step][layer] = sum(parts, came[layer][block].astype(F32)).astype(BF)


def sum_kernel(*refs):
    total = refs[0][...].astype(F32)
    for ref in refs[1:-1]:
        total = total + ref[...].astype(F32)
    refs[-1][...] = total.astype(BF)


def input_kernel(moved_ref, w_first_ref, out_ref):
    samples, rows, breadth, triple = moved_ref.shape
    height = rows - 2
    total = None
    for u in STEPS:
        weights = jnp.concatenate([w_first_ref[3 * (u + 1) + (v + 1)] for v in STEPS], axis=1)
        part = dot_last(moved_ref[:, 1 - u : 1 - u + height].reshape(samples * height * breadth, triple), weights)
        total = part if total is None else total + part
    out_ref[...] = total.astype(BF).reshape(out_ref.shape)


def input_conv(moved, w_first):
    samples, rows, breadth, triple = moved.shape
    shape = (samples, rows - 2, breadth, w_first.shape[1])
    return run(
        "input_conv",
        input_kernel,
        [jax.ShapeDtypeStruct(shape, BF)],
        [moved, w_first],
        flops=2 * 3 * math.prod(shape) * triple,
    )[0]


def chips_kernel(mine_ref, cross_ref, out_ref):
    _, chip = core_and_chip()
    out_ref[0] = (mine_ref[0].astype(F32) + cross_ref[0].astype(F32)).astype(BF)
    out_ref[1] = jnp.where(chip == 0, mine_ref[1], cross_ref[1])
    out_ref[2] = jnp.where(chip == 0, cross_ref[1], mine_ref[1])


def cores_kernel(mine_ref, other_ref, first_ref, second_ref):
    core, _ = core_and_chip()
    rows = mine_ref.shape[1]
    mine, other = (ref[...].astype(F32) for ref in (mine_ref, other_ref))
    for part in range(2):
        value = jnp.where(core == part, mine, other)
        first_ref[pl.ds(part, rows, stride=2), :] = value[0]
        second_ref[pl.ds(2 * rows * part, rows, stride=2), :] = value[1]
        second_ref[pl.ds(2 * rows * part + 1, rows, stride=2), :] = value[2]


def swap(array, axis, flip):
    count = lax.axis_size(axis)
    return lax.ppermute(array, axis, [(i, i ^ flip) for i in range(count)])


def around(array, axis, step, periodic=True):
    count = lax.axis_size(axis)
    pairs = [(i, (i + step) % count) for i in range(count) if periodic or 0 <= i + step < count]
    return lax.ppermute(array, axis, pairs)


def corner(array, step):
    lead, lat = lax.axis_size("lead"), lax.axis_size("lat")
    pairs = []
    for a in range(lead):
        for b in range(lat):
            target = (b ^ 1) if step is None else b + step
            if 0 <= target < lat:
                pairs.append((a * lat + b, (a ^ 2) * lat + target))
    return lax.ppermute(array, ("lead", "lat"), pairs)


def other_band(terms, columns):
    shape = (columns, terms[0].size // LANES // columns // 2, LANES)
    return run("other_band", other_band_kernel, [jax.ShapeDtypeStruct(shape, BF)], [t.reshape(2, *shape) for t in terms])[0]


def pairwise(terms, bands):
    lat = lax.axis_index("lat")
    total = sum(t.reshape(-1, LANES).astype(F32) for t in terms).astype(BF)
    left = bands
    while left > 2:
        left //= 2
        bit = (lat // left) % 2
        halves = total.reshape(2, -1, LANES)
        send = lax.dynamic_index_in_dim(halves, 1 - bit, 0, keepdims=False)
        keep = lax.dynamic_index_in_dim(halves, bit, 0, keepdims=False)
        total = (keep.astype(F32) + swap(send, "lat", left).astype(F32)).astype(BF)
    return total


def near_kernel(second_ref, first_ref, input_ref, low_ref, high_ref, slope_second, slope_first, halo_ref, wide, cells):
    samples, height, breadth, depth = second_ref.shape
    kept = breadth + 2 * EDGE
    batch = low_ref.shape[0] - samples
    for ref, width, first_cell, slope_ref in ((second_ref, 2, 0, slope_second), (first_ref, 1, 4 * height, slope_first)):
        wide[...] = jnp.zeros(wide.shape, F32)
        for s in range(samples):
            for r in range(height):
                at = (s * height + r) * kept + EDGE
                for half in range(2):
                    wide[half, at : at + breadth, :] = ref[s, r, :, half * LANES : (half + 1) * LANES].astype(F32)
            for side, packed_ref in ((0, low_ref), (1, high_ref)):
                packed = packed_ref[batch + s].astype(F32)
                for col in range(width):
                    for half in range(2):
                        here = ((col if width == 2 else 2) * 2 + half) * height
                        value = packed[here : here + height]
                        at = s * height * kept + EDGE + col + (breadth if side else -width)
                        wide[half, pl.ds(at, height, stride=kept), :] = value
                        at = first_cell + (side * width + col) * height
                        cells[s, at : at + height, half * LANES : (half + 1) * LANES] = value
        value = jnp.concatenate([wide[0], wide[1]], axis=1)
        slope_ref[...] = gelu_slope(value).reshape(slope_ref.shape)
    halo_ref[:, : cells.shape[1]] = cells[...].astype(BF)
    half = height // 2
    for part in range(2):
        values = input_ref[:, part * half : (part + 1) * half].reshape(samples, half * breadth, LANES)
        halo_ref[:, cells.shape[1] :, part * LANES : (part + 1) * LANES] = values


def near_parts(pre_second, pre_first, encoder_input, low, high):
    samples, height, breadth, depth = pre_second.shape
    kept = breadth + 2 * EDGE
    slope = jax.ShapeDtypeStruct((samples, height, kept, depth), F32)
    return run(
        "near_parts",
        near_kernel,
        [slope, slope, jax.ShapeDtypeStruct((samples, 6 * height + height * breadth // 2, depth), BF)],
        [pre_second, pre_first, encoder_input, low, high],
        [pltpu.VMEM((2, samples * height * kept, LANES), F32), pltpu.VMEM((samples, 6 * height, depth), F32)],
    )


def far_kernel(first_ref, tile_second, tile_first, slope_second, slope_first, act_out, wide, act):
    samples, height, breadth, depth = first_ref.shape
    kept = breadth + 2 * EDGE
    lat = lax.axis_index("lat")
    for source_ref, slope_ref in ((tile_second, slope_second), (tile_first, slope_first)):
        wide[...] = jnp.zeros(wide.shape, F32)
        for s in range(samples):
            for half in range(2):
                for r in range(height):
                    at = (s * height + r) * kept + EDGE
                    wide[half, at : at + breadth, :] = source_ref[s, r, :, half * LANES : (half + 1) * LANES].astype(F32)
        value = jnp.concatenate([wide[0], wide[1]], axis=1)
        slope_ref[...] = gelu_slope(value).reshape(slope_ref.shape)
    own, other = pl.ds(height * lat, height), pl.ds(height * (1 - lat), height)
    act[:, own] = gelu_value(first_ref[...].astype(F32))
    act[:, other] = gelu_value(tile_first[...].astype(F32))
    act_out[...] = act[...].reshape(act_out.shape[1], depth).T.astype(BF)


def far_parts(pre_first, tile_second, tile_first):
    samples, height, breadth, depth = pre_first.shape
    kept = breadth + 2 * EDGE
    slope = jax.ShapeDtypeStruct((samples, height, kept, depth), F32)
    return run(
        "far_parts",
        far_kernel,
        [slope, slope, jax.ShapeDtypeStruct((depth, 2 * samples * height * breadth), BF)],
        [pre_first, tile_second, tile_first],
        [
            pltpu.VMEM((2, samples * height * kept, LANES), F32),
            pltpu.VMEM((samples, 2 * height, breadth, depth), F32),
        ],
    )


def put_slopes(slope, near_ref, far_ref, halo_ref, width, first_cell):
    samples, height, kept, _ = near_ref.shape
    lat = lax.axis_index("lat")
    other = pl.ds(height * (1 - lat), height)
    slope[:, pl.ds(height * lat, height)] = near_ref[...]
    slope[:, other] = far_ref[...]
    for s in range(samples):
        beside = gelu_slope(halo_ref[s].astype(F32))
        for side in range(2):
            for col in range(width):
                here = first_cell + (side * width + col) * height
                at = kept - EDGE + col if side else EDGE - width + col
                slope[s, other, at, :] = beside[here : here + height]


def globe_kernel(near_ref, far_ref, halo_ref, *refs):
    cat_ref, moved_ref, latent, slope, wide = refs[-5:]
    samples = near_ref.shape[0]
    totals, lines = refs[:samples], refs[samples : 2 * samples]
    rows, kept, depth = totals[0].shape
    height = rows - 1
    tall = 2 * height
    breadth = kept - 2 * EDGE
    lat = lax.axis_index("lat")
    own = 8 + EDGE
    latent[...] = jnp.zeros(latent.shape, F32)
    for s in range(samples):
        latent[s, pl.ds((height - 1) * lat, rows)] = totals[s][...].astype(F32)
        latent[s, pl.ds((height - 1) * (1 - lat), rows)] += lines[s][...].astype(F32)
    put_slopes(slope, near_ref, far_ref, halo_ref, 2, 0)
    wide[:, :, 8 : 8 + kept, :] = (latent[...] * slope[...]).astype(BF).astype(F32)
    for v in STEPS:
        lanes = slice((v + 1) * depth, (v + 2) * depth)
        cat_ref[:, 1 : 1 + tall, :, lanes] = wide[:, :, 8 - v : 8 - v + kept, :].astype(BF)
        moved_ref[v + 1, :, 1 : 1 + tall] = wide[:, :, own - v : own - v + breadth, :].astype(BF)
    for row in (0, tall + 1):
        cat_ref[:, row] = jnp.zeros(cat_ref.shape[:1] + cat_ref.shape[2:], BF)
        moved_ref[:, :, row] = jnp.zeros(moved_ref.shape[:2] + moved_ref.shape[3:], BF)


def globe(totals, lines, near, far, halo):
    samples, (rows, kept, depth) = len(totals), totals[0].shape
    tall, breadth = 2 * (rows - 1), kept - 2 * EDGE
    return run(
        "latent_grads",
        globe_kernel,
        [
            jax.ShapeDtypeStruct((samples, tall + 2, kept, 3 * depth), BF),
            jax.ShapeDtypeStruct((3, samples, tall + 2, breadth, depth), BF),
        ],
        [near, far, halo, *totals, *lines],
        [
            pltpu.VMEM((samples, tall, kept, depth), F32),
            pltpu.VMEM((samples, tall, kept, depth), F32),
            pltpu.VMEM((samples, tall, kept + 24, depth), F32),
        ],
    )


def band_rows(norm_factor, left_all, moved_ref, mine_ref, other_ref):
    channels, cells = left_all.shape
    _, samples, padded, breadth, depth = moved_ref.shape
    tall = padded - 2
    lat = lax.axis_index("lat")
    core, _ = core_and_chip()
    half = channels // 2

    def put(left, u, v, start, size):
        right = moved_ref[v + 1, :, pl.ds(1 - u, tall)].reshape(cells, depth)
        part = dot_plain(left, right) * norm_factor
        lower, upper = part[:, :LANES], part[:, LANES:]
        here = pl.ds(pl.multiple_of(start, half), size)
        mine_ref[here, :] = jnp.where(core == 0, lower, upper).astype(BF)
        other_ref[here, :] = jnp.where(core == 0, upper, lower).astype(BF)

    for j in range(4):
        (u0, v0), (u1, v1) = (divmod(k, 3) for k in (j, 5 + j))
        put(left_all, u0 - 1 + lat * (u1 - u0), v0 - 1 + lat * (v1 - v0), lat * half + j * channels, channels)
    put(jnp.where(lat == 0, left_all[:half], left_all[half:]), 0, 0, (1 - lat) * 4 * channels, half)


def second_band_kernel(norm_factor, moved_ref, act_ref, mine_ref, other_ref):
    band_rows(norm_factor, act_ref[...], moved_ref, mine_ref, other_ref)


def first_band_kernel(norm_factor, cat_ref, near_ref, far_ref, halo_ref, input_ref, weights_ref, moved_ref, mine_ref, other_ref, slope, wide, cells):
    samples, padded, broad, triple = cat_ref.shape
    tall, kept, depth = padded - 2, broad, triple // 3
    height = tall // 2
    breadth = kept - 2 * EDGE
    lat = lax.axis_index("lat")
    own = 8 + EDGE
    put_slopes(slope, near_ref, far_ref, halo_ref, 1, 4 * height)
    linear = None
    for u in STEPS:
        weights = jnp.concatenate([weights_ref[3 * (u + 1) + (v + 1)] for v in STEPS], axis=1)
        part = dot_last(cat_ref[:, 1 - u : 1 - u + tall].reshape(samples * tall * broad, triple), weights)
        linear = part if linear is None else linear + part
    linear = linear.reshape(samples, tall, broad, depth)
    wide[:, :, 8 : 8 + kept, :] = (linear * slope[...]).astype(BF).astype(F32)
    for v in STEPS:
        moved_ref[v + 1, :, 1 : 1 + tall] = wide[:, :, own - v : own - v + breadth, :].astype(BF)
    for row in (0, tall + 1):
        moved_ref[:, :, row] = jnp.zeros(moved_ref.shape[:2] + moved_ref.shape[3:], BF)
    cells[:, pl.ds(height * lat, height)] = input_ref[...].astype(F32)
    half = height // 2
    for part in range(2):
        values = halo_ref[:, 6 * height :, part * LANES : (part + 1) * LANES].astype(F32)
        cells[:, pl.ds(height * (1 - lat) + part * half, half)] = values.reshape(samples, half, breadth, LANES)
    band_rows(norm_factor, cells[...].reshape(samples * tall * breadth, LANES).T.astype(BF), moved_ref, mine_ref, other_ref)


def second_band(norm_factor, moved, act):
    half = jax.ShapeDtypeStruct((9 * act.shape[0] // 2, LANES), BF)
    return run("second_weight_grads", functools.partial(second_band_kernel, norm_factor), [half, half], [moved, act])


def first_band(norm_factor, cat, near, far, halo, encoder_input, w_second):
    samples, padded, broad, triple = cat.shape
    tall, kept, depth = padded - 2, broad, triple // 3
    breadth = kept - 2 * EDGE
    half = jax.ShapeDtypeStruct((9 * encoder_input.shape[3] // 2, LANES), BF)
    return run(
        "encoder_grads",
        functools.partial(first_band_kernel, norm_factor),
        [jax.ShapeDtypeStruct((3, samples, padded, breadth, depth), BF), half, half],
        [cat, near, far, halo, encoder_input, w_second],
        [
            pltpu.VMEM((samples, tall, kept, depth), F32),
            pltpu.VMEM((samples, tall, kept + 16, depth), F32),
            pltpu.VMEM((samples, tall, breadth, LANES), F32),
        ],
    )


def input_band_kernel(moved_ref, w_first_ref, out_ref):
    samples, height, breadth, channels = out_ref.shape
    depth = moved_ref.shape[4]
    lat = lax.axis_index("lat")
    total = None
    for u in STEPS:
        weights = jnp.concatenate([w_first_ref[3 * (u + 1) + (v + 1)] for v in STEPS], axis=1)
        left = [moved_ref[v + 1, :, pl.ds(height * lat + 1 - u, height)].reshape(-1, depth) for v in STEPS]
        part = dot_last(jnp.concatenate(left, axis=1), weights)
        total = part if total is None else total + part
    out_ref[...] = total.astype(BF).reshape(out_ref.shape)


def blocks_kernel(first_mine, first_got, second_mine, second_got, *outs):
    lon = lax.axis_index("lon")
    rows = first_mine.shape[1]
    for step, out_ref in enumerate(outs):
        block = partner(lon, step, len(outs))
        out_ref[:rows] = (first_mine[block].astype(F32) + first_got[block].astype(F32)).astype(BF)
        out_ref[rows:] = (second_mine[block].astype(F32) + second_got[block].astype(F32)).astype(BF)


def halves_kernel(mine_ref, other_ref, first_ref, second_ref):
    core, _ = core_and_chip()
    mine, other = mine_ref[...].astype(F32), other_ref[...].astype(F32)
    rows = mine.shape[0] // 3
    for part in range(2):
        value = jnp.where(core == part, mine, other)
        first_ref[pl.ds(part, rows, stride=2), :] = value[:rows]
        second_ref[pl.ds(part, 2 * rows, stride=2), :] = value[rows:]


def to_partner(array, step):
    count = lax.axis_size("lon")
    return lax.ppermute(array, "lon", [(partner(i, step, count), i) for i in range(count)])


def two_bands(head_grads, head_weights, encoder_input, pre_first, pre_second, w_first, w_second, norm_factor):
    samples, height, breadth, _ = encoder_input.shape
    columns = lax.axis_size("lon")
    tiles = [swap(array, "lat", 1) for array in (pre_second, pre_first)]
    to_right, to_left = pack(head_grads, pre_second, pre_first)
    low = around(to_right, "lon", 1)
    high = around(to_left, "lon", -1)
    head_grads, head_weights, w_second, pre_second, pre_first, encoder_input = stage(
        head_grads, head_weights, w_second, pre_second, pre_first, encoder_input
    )
    low, high, *tiles = lax.optimization_barrier((low, high, *tiles))
    heads_of = functools.partial(
        head_conv,
        head_grads=head_grads,
        low=low,
        high=high,
        head_weights=head_weights,
        slots=2 * samples,
        rows=height + 1,
    )
    got = swap(heads_of(True, False), "lead", 1)
    near_second, near_first, halo = near_parts(pre_second, pre_first, encoder_input, low, high)
    mine = heads_of(False, False)
    halo = swap(halo, "lat", 1)
    part_shape = jax.ShapeDtypeStruct(mine.shape[1:], BF)
    parts = run("core_sum", core_sum_kernel, [part_shape] * (2 * samples), [mine, got])
    cross = [swap(part, "lead", 2) for part in parts[samples:]]
    cross[0], halo = lax.optimization_barrier((cross[0], halo))
    totals = [run("chip_sum", sum_kernel, [part_shape], [parts[s], cross[s]])[0] for s in range(samples)]
    lines = [swap(total, "lat", 1) for total in totals]
    far_second, far_first, act = far_parts(pre_first, *tiles)

    cat, moved = globe(totals, lines, near_second, far_second, halo)
    second_mine, second_other = second_band(norm_factor, moved, act)
    second_got = swap(second_other, "lead", 1)
    moved_first, first_mine, first_other = first_band(norm_factor, cat, near_first, far_first, halo, encoder_input, w_second)
    first_got = swap(first_other, "lead", 1)
    input_grad = run(
        "input_conv", input_band_kernel, [jax.ShapeDtypeStruct(encoder_input.shape, BF)], [moved_first, w_first]
    )[0]

    blocks = [t.reshape(columns, -1, LANES) for t in (first_mine, first_got, second_mine, second_got)]
    rows = blocks[0].shape[1]
    share_shape = jax.ShapeDtypeStruct((3 * rows, LANES), BF)
    shares = run("blocks", blocks_kernel, [share_shape] * columns, blocks)
    parts = [to_partner(shares[step], step) for step in [*range(2, columns), 1]]
    share = run("share", sum_kernel, [share_shape], [shares[0], *parts])[0]
    both = run("chips", sum_kernel, [share_shape], [share, swap(share, "lead", 2)])[0]
    result_first, result_second = run(
        "cores",
        halves_kernel,
        [jax.ShapeDtypeStruct((2 * rows, LANES), F32), jax.ShapeDtypeStruct((4 * rows, LANES), F32)],
        [both, swap(both, "lead", 1)],
    )
    return input_grad, result_first.reshape(-1), result_second.reshape(-1)


def core_sum_kernel(mine_ref, got_ref, *outs):
    for slot, out_ref in enumerate(outs):
        out_ref[...] = (mine_ref[slot].astype(F32) + got_ref[slot].astype(F32)).astype(BF)


def general(head_grads, head_weights, encoder_input, pre_first, pre_second, w_first, w_second, norm_factor):
    samples, height, breadth, _ = encoder_input.shape
    bands, columns = lax.axis_size("lat"), lax.axis_size("lon")
    to_right, to_left = pack(head_grads, pre_second, pre_first)
    to_right, to_left, to_cross = lax.optimization_barrier((to_right, to_left, pre_first))
    low = around(to_right, "lon", 1)
    high = around(to_left, "lon", -1)
    act_got = activated(swap(to_cross, "lead", 2))
    head_grads, head_weights, w_second, pre_second, pre_first, encoder_input = stage(
        head_grads, head_weights, w_second, pre_second, pre_first, encoder_input
    )
    low, high, act_got = lax.optimization_barrier((low, high, act_got))

    steps = [1, -1]
    heads_of = functools.partial(head_conv, head_grads=head_grads, high=high, head_weights=head_weights, slots=samples, rows=height + 2)
    got_cross = swap(heads_of(True, True, low=low), "lead", 1)
    got_own = swap(heads_of(True, False, low=low), "lead", 1)
    cross, *angles = spread_cross(heads_of(False, True, low=low), got_cross, len(steps))
    low_later, cross, *angles = lax.optimization_barrier((low, cross, *angles))
    cross = swap(cross, "lead", 2)
    angles = [corner(angle, step) for angle, step in zip(angles, steps)]
    second, first, slope_second, slope_first, act, cells_in = saved(pre_second, pre_first, encoder_input, low, high)
    own, *lines = spread_own(heads_of(False, False, low=low_later), got_own, second, first, len(steps))
    lines = [swap(line, "lat", 1) if step is None else around(line, "lat", step, False) for line, step in zip(lines, steps)]
    strips = [strip for pair in zip(lines, angles) for strip in pair]

    grad, away, slope = latent_grads(len(steps), bands, own, cross, strips, slope_second, slope_first)
    grad_got = swap(away, "lead", 2)
    moved, first_mine, first_other = encoder(norm_factor, bands, grad, slope, cells_in, w_second)
    input_grad = input_conv(moved, w_first)
    first_got = swap(first_other, "lead", 1)
    second_mine, second_other = second_grads(norm_factor, bands * columns, grad, grad_got, act, act_got)
    second_got = swap(second_other, "lead", 1)

    first_terms = [pairwise([first_mine, first_got], bands)]
    second_terms = [pairwise([second_mine, second_got], bands)]
    first_came = swap(other_band(first_terms, columns), "lat", 1)
    second_came = swap(other_band(second_terms, columns), "lat", 1)
    blocks = [t.reshape(2, columns, -1, LANES) for t in first_terms + second_terms]
    rows = blocks[0].shape[2]
    share_shape = jax.ShapeDtypeStruct((2, rows, LANES), BF)
    shares = run("own_band", own_band_kernel, [share_shape] * columns, blocks + [first_came, second_came])
    parts = [to_partner(shares[step], step) for step in [*range(2, columns), 1]]
    share = run("share", sum_kernel, [share_shape], [shares[0], *parts])[0]
    both = run("chips", chips_kernel, [jax.ShapeDtypeStruct((3, rows, LANES), BF)], [share, swap(share, "lead", 2)])[0]
    result_first, result_second = run(
        "cores",
        cores_kernel,
        [jax.ShapeDtypeStruct((2 * rows, LANES), F32), jax.ShapeDtypeStruct((4 * rows, LANES), F32)],
        [both, swap(both, "lead", 1)],
    )
    return input_grad, result_first.reshape(-1), result_second.reshape(-1)


def per_device(head_grads, head_weights, encoder_input, pre_first, pre_second, w_first, w_second):
    samples, height, breadth, channels = encoder_input.shape
    bands, columns = lax.axis_size("lat"), lax.axis_size("lon")
    cells_total = samples * lax.axis_size("lead") * height * bands * breadth * columns
    norm_factor = 1.0 / math.sqrt(cells_total)
    plan = two_bands if bands == 2 and 9 * channels // (bands * columns) % 16 == 0 else general
    return plan(head_grads, head_weights, encoder_input, pre_first, pre_second, w_first, w_second, norm_factor)


def solution(mesh):
    in_specs = (
        P("lead", None, "lat", "lon", None),
        P("lead", None, None, None),
        P("lead", "lat", "lon", None),
        P("lead", "lat", "lon", None),
        P("lead", "lat", "lon", None),
        P(),
        P(),
    )
    out_specs = (P("lead", "lat", "lon", None), P(("lat", "lon")), P(("lat", "lon")))
    return jax.shard_map(
        per_device, mesh=mesh, in_specs=in_specs, out_specs=out_specs, check_vma=False
    )
```

```python
import functools
import math

import jax
import jax.numpy as jnp
from jax import lax
from jax.experimental import pallas as pl
from jax.experimental.pallas import tpu as pltpu
from jax.sharding import PartitionSpec as P

BF = jnp.bfloat16
F32 = jnp.float32
STEPS = (-1, 0, 1)
EDGE = 4
LANES = 128
VMEM_BYTES = 24 * 1024 * 1024


def erf_part(values):
    return 0.5 * (1.0 + lax.erf(values * 0.7071067811865476))


def gelu_slope(values):
    return erf_part(values) + values * jnp.exp(-0.5 * values * values) * 0.3989422804014327


def gelu_value(values):
    return values * erf_part(values)


def dot_last(left, right):
    return lax.dot_general(left, right, (((1,), (1,)), ((), ())), preferred_element_type=F32)


def dot_plain(left, right):
    return lax.dot_general(left, right, (((1,), (0,)), ((), ())), preferred_element_type=F32)


def core_and_chip():
    lead = lax.axis_index("lead")
    return lax.rem(lead, 2), lax.div(lead, 2)


def run(name, kernel, out_shape, arrays, scratch=(), flops=0, far=False):
    specs = [pl.BlockSpec(memory_space=pltpu.HBM if far else pltpu.VMEM)] * len(arrays)
    if far:
        arrays = [pltpu.with_memory_space_constraint(a, pltpu.HBM) for a in arrays]
    touched = sum(a.size * a.dtype.itemsize for a in arrays)
    touched += sum(math.prod(s.shape) * s.dtype.itemsize for s in out_shape)
    return pl.pallas_call(
        kernel,
        name=name,
        out_shape=out_shape,
        in_specs=specs,
        out_specs=[pl.BlockSpec(memory_space=pltpu.VMEM)] * len(out_shape),
        scratch_shapes=list(scratch),
        compiler_params=pltpu.CompilerParams(vmem_limit_bytes=VMEM_BYTES),
        cost_estimate=pl.CostEstimate(flops=1, bytes_accessed=1, transcendentals=0),
    )(*arrays)


def pack_kernel(grads_far, second_far, first_far, right_ref, left_ref, grads_near, second_near, first_near, edges, edges_wide, packed, sems):
    heads, batch, height, breadth, _ = grads_far.shape
    samples = second_far.shape[0]
    rows = 6 * height
    copies = []
    for side in range(2):
        columns = pl.ds(breadth - 16 if side == 0 else 0, 16)
        for j, (far, near) in enumerate(((grads_far, grads_near), (second_far, second_near), (first_far, first_near))):
            source = far.at[:, :, :, columns, :] if j == 0 else far.at[:, :, columns, :]
            copies.append(pltpu.make_async_copy(source, near.at[side], sems.at[side, j]))
            copies[-1].start()
    for copy in copies:
        copy.wait()
    for side, out_ref in ((0, right_ref), (1, left_ref)):
        start = 8 if side == 0 else 0
        grads_ref, second_ref, first_ref = grads_near.at[side], second_near.at[side], first_near.at[side]
        for h in range(heads):
            for b in range(batch):
                block = grads_ref[h, b, :, start : start + 8, :].astype(F32)
                edges[(h * batch + b) * height * 8 : (h * batch + b + 1) * height * 8, :] = block.reshape(height * 8, LANES)
        for j, ref in enumerate((second_ref, first_ref)):
            for s in range(samples):
                block = ref[s, :, start : start + 8, :].astype(F32)
                at = (j * samples + s) * height * 8
                for half in range(2):
                    lanes = slice(half * LANES, (half + 1) * LANES)
                    edges_wide[half, at : at + height * 8, :] = block[:, :, lanes].reshape(height * 8, LANES)
        for b in range(batch):
            for col in range(3):
                inner = 5 + col if side == 0 else col
                for h in range(heads):
                    at = b * rows + (col * 2 + h) * height
                    packed[at : at + height, :] = edges[pl.ds((h * batch + b) * height * 8 + inner, height, stride=8), :]
        for s in range(samples):
            for q in range(3):
                j, col, width = (0, q, 2) if q < 2 else (1, 0, 1)
                inner = 8 - width + col if side == 0 else col
                for half in range(2):
                    at = (batch + s) * rows + (q * 2 + half) * height
                    packed[at : at + height, :] = edges_wide[
                        half, pl.ds((j * samples + s) * height * 8 + inner, height, stride=8), :
                    ]
        out_ref[...] = packed[...].astype(BF).reshape(out_ref.shape)


def pack(head_grads, pre_second, pre_first):
    heads, batch, height, _, _ = head_grads.shape
    samples = pre_second.shape[0]
    shape = jax.ShapeDtypeStruct((batch + samples, 6 * height, LANES), BF)
    return run(
        "pack_columns",
        pack_kernel,
        [shape, shape],
        [head_grads, pre_second, pre_first],
        [
            pltpu.VMEM((2, heads, batch, height, 16, LANES), BF),
            pltpu.VMEM((2, samples, height, 16, 2 * LANES), BF),
            pltpu.VMEM((2, samples, height, 16, 2 * LANES), BF),
            pltpu.VMEM((heads * batch * height * 8, LANES), F32),
            pltpu.VMEM((2, 2 * samples * height * 8, LANES), F32),
            pltpu.VMEM(((batch + samples) * 6 * height, LANES), F32),
            pltpu.SemaphoreType.DMA((2, 3)),
        ],
        far=True,
    )


def stage_kernel(*refs):
    count = len(refs) // 2
    sems = refs[-1]
    copies = [pltpu.make_async_copy(refs[i], refs[count + i], sems.at[i]) for i in range(count)]
    for copy in copies:
        copy.start()
    for copy in copies:
        copy.wait()


def stage(*arrays):
    shapes = [pltpu.VMEM(a.shape, a.dtype) for a in arrays]
    return run("stage", stage_kernel, shapes, list(arrays), [pltpu.SemaphoreType.DMA((len(arrays),))], far=True, flops=1 << 30)


def heads_kernel(other_core, other_chip, sample, samples, grads_ref, low_ref, high_ref, weights_ref, out_ref, wide, shifted, total):
    heads, batch, height, breadth, _ = grads_ref.shape
    slots, _, kept, depth = out_ref.shape
    pitch = kept + 16
    own = 8 + EDGE
    core, chip = core_and_chip()
    core = 1 - core if other_core else core
    for slot in range(slots):
        if sample is None:
            group, s = 1 - chip if other_chip else chip, slot
        else:
            group, s = 1 - chip if slot % 2 else chip, sample + slot // 2
        b = (2 * group + core) * samples + s
        low = low_ref[b].astype(F32)
        high = high_ref[b].astype(F32)
        for r in range(height):
            at = (slot * height + r) * pitch + own
            for h in range(heads):
                wide[h, at : at + breadth, :] = grads_ref[h, b, r].astype(F32)
        for col in range(3):
            for h in range(heads):
                here = (col * 2 + h) * height
                at = slot * height * pitch + own + col
                wide[h, pl.ds(at - 3, height, stride=pitch), :] = low[here : here + height]
                wide[h, pl.ds(at + breadth, height, stride=pitch), :] = high[here : here + height]
        for v in STEPS:
            for h in range(heads):
                starts = [(slot * height + r) * pitch + 8 - v for r in range(height)]
                moved = jnp.concatenate([wide[h, at : at + kept, :] for at in starts], axis=0).astype(BF)
                lane = ((v + 1) * heads + h) * LANES
                shifted[slot * height * kept : (slot + 1) * height * kept, lane : lane + LANES] = moved
    total[:, height:, :, :] = jnp.zeros((slots, 2, kept, depth), F32)
    for u in STEPS:
        weights = jnp.concatenate(
            [weights_ref[h, 3 * (u + 1) + (v + 1)] for v in STEPS for h in range(heads)], axis=1
        )
        part = dot_last(shifted[...], weights).reshape(slots, height, kept, depth)
        if u == -1:
            total[:, :height] = part
        else:
            total[:, 1 + u : 1 + u + height] += part
    if out_ref.shape[1] == height + 2:
        out_ref[...] = total[...].astype(BF)
    else:
        out_ref[...] = total[:, pl.ds(1 - lax.axis_index("lat"), height + 1)].astype(BF)


def head_conv(other_core, other_chip, sample, head_grads, low, high, head_weights, slots, rows):
    samples = head_grads.shape[1] // lax.axis_size("lead")
    heads, batch, height, breadth, _ = head_grads.shape
    depth = head_weights.shape[2]
    kept = breadth + 2 * EDGE
    return run(
        "head_conv",
        functools.partial(heads_kernel, other_core, other_chip, sample, samples),
        [jax.ShapeDtypeStruct((slots, rows, kept, depth), BF)],
        [head_grads, low, high, head_weights],
        [
            pltpu.VMEM((heads, slots * height * (kept + 16), LANES), F32),
            pltpu.VMEM((slots * height * kept, 3 * heads * LANES), BF),
            pltpu.VMEM((slots, height + 2, kept, depth), F32),
        ],
        flops=2 * slots * height * kept * 9 * heads * LANES * depth,
    )[0]


def saved_kernel(second_ref, first_ref, input_ref, low_ref, high_ref, second_out, first_out, slope_second, slope_first, act_out, input_out, wide):
    samples, height, breadth, depth = second_ref.shape
    kept = breadth + 2 * EDGE
    batch = low_ref.shape[0] - samples
    for ref, width, out_ref, slope_ref in (
        (second_ref, 2, second_out, slope_second),
        (first_ref, 1, first_out, slope_first),
    ):
        wide[...] = jnp.zeros(wide.shape, F32)
        for s in range(samples):
            for r in range(height):
                at = (s * height + r) * kept + EDGE
                for half in range(2):
                    lanes = slice(half * LANES, (half + 1) * LANES)
                    wide[half, at : at + breadth, :] = ref[s, r, :, lanes].astype(F32)
            low = low_ref[batch + s].astype(F32)
            high = high_ref[batch + s].astype(F32)
            for col in range(width):
                for half in range(2):
                    here = ((col if width == 2 else 2) * 2 + half) * height
                    at = s * height * kept + EDGE + col
                    wide[half, pl.ds(at - width, height, stride=kept), :] = low[here : here + height]
                    wide[half, pl.ds(at + breadth, height, stride=kept), :] = high[here : here + height]
        value = jnp.concatenate([wide[0], wide[1]], axis=1)
        out_ref[...] = value.astype(BF).reshape(out_ref.shape)
        slope_ref[...] = gelu_slope(value).reshape(slope_ref.shape)
    active = gelu_value(first_ref[...].astype(F32).reshape(samples * height * breadth, depth)).astype(BF).astype(F32)
    act_out[...] = active.T.astype(BF)
    cells = input_ref[...].astype(F32).reshape(samples * height * breadth, input_ref.shape[3])
    input_out[...] = cells.T.astype(BF)


def saved(pre_second, pre_first, encoder_input, low, high):
    samples, height, breadth, depth = pre_second.shape
    kept = breadth + 2 * EDGE
    cells = samples * height * breadth
    return run(
        "saved_parts",
        saved_kernel,
        [
            jax.ShapeDtypeStruct((samples, height, kept, depth), BF),
            jax.ShapeDtypeStruct((samples, height, kept, depth), BF),
            jax.ShapeDtypeStruct((samples, height, kept, depth), F32),
            jax.ShapeDtypeStruct((samples, height, kept, depth), F32),
            jax.ShapeDtypeStruct((depth, cells), BF),
            jax.ShapeDtypeStruct((encoder_input.shape[3], cells), BF),
        ],
        [pre_second, pre_first, encoder_input, low, high],
        [pltpu.VMEM((2, samples * height * kept, LANES), F32)],
    )


def goes_down(way, ways):
    return 1 - lax.axis_index("lat") if ways == 1 else 1 - way


def cross_kernel(mine_ref, got_ref, cross_ref, *strips):
    height = mine_ref.shape[1] - 2
    cross_ref[...] = (mine_ref[...].astype(F32) + got_ref[...].astype(F32)).astype(BF)
    for way, corner_ref in enumerate(strips):
        corner_ref[...] = cross_ref[:, pl.ds((height - 1) * goes_down(way, len(strips)), 3)]


def own_kernel(mine_ref, got_ref, second_ref, first_ref, own_ref, *strips):
    height = second_ref.shape[1]
    own_ref[...] = (mine_ref[...].astype(F32) + got_ref[...].astype(F32)).astype(BF)
    for way, line_ref in enumerate(strips):
        down = goes_down(way, len(strips))
        line_ref[:, 0:3] = own_ref[:, pl.ds((height - 1) * down, 3)]
        line_ref[:, 3:5] = second_ref[:, pl.ds((height - 2) * down, 2)]
        line_ref[:, 5:6] = first_ref[:, pl.ds((height - 1) * down, 1)]


def spread_cross(mine, got, ways):
    samples, _, kept, depth = mine.shape
    strip = jax.ShapeDtypeStruct((samples, 3, kept, depth), BF)
    return run("core_sum_cross", cross_kernel, [jax.ShapeDtypeStruct(mine.shape, BF)] + [strip] * ways, [mine, got])


def spread_own(mine, got, second, first, ways):
    samples, _, kept, depth = mine.shape
    strip = jax.ShapeDtypeStruct((samples, 6, kept, depth), BF)
    return run("core_sum_own", own_kernel, [jax.ShapeDtypeStruct(mine.shape, BF)] + [strip] * ways, [mine, got, second, first])


def latent_kernel(ways, bands, own_ref, cross_ref, *refs):
    strips, refs = refs[: 2 * ways], refs[2 * ways :]
    slope_second_ref, slope_first_ref, grad_ref, away_ref, slope_out, latent, slope_second = refs
    samples, rows, kept, depth = own_ref.shape
    height = rows - 2
    lat = lax.axis_index("lat")
    _, chip = core_and_chip()
    blank = jnp.zeros((samples, kept, depth), F32)
    latent[:, 0] = blank
    latent[:, height + 3] = blank
    latent[:, 1 : height + 3] = own_ref[...].astype(F32) + cross_ref[...].astype(F32)
    slope_second[:, 2 : 2 + height] = slope_second_ref[...]
    slope_out[:, 1 : 1 + height] = slope_first_ref[...]
    for way in range(ways):
        line_ref, corner_ref = strips[2 * way], strips[2 * way + 1]
        below = 1 - lat if ways == 1 else way
        at = (height + 1) * below
        latent[:, pl.ds(at, 3)] += line_ref[:, 0:3].astype(F32) + corner_ref[...].astype(F32)
        slope_second[:, pl.ds((height + 2) * below, 2)] = gelu_slope(line_ref[:, 3:5].astype(F32))
        slope_out[:, pl.ds((height + 1) * below, 1)] = gelu_slope(line_ref[:, 5:6].astype(F32))
    for i in range(height + 4):
        row = lat * height + i - 2
        valid = jnp.logical_and(row >= 0, row < bands * height)
        value = latent[:, i] * slope_second[:, i]
        if i < 2 or i >= height + 2:
            value = jnp.where(valid, value, 0.0)
        grad_ref[:, i] = value.astype(BF)
        if 0 < i < height + 3:
            away_ref[:, i - 1] = jnp.where(chip == 0, value[:, :, LANES:], value[:, :, :LANES]).astype(BF)


def latent_grads(ways, bands, own, cross, strips, slope_second, slope_first):
    samples, rows, kept, depth = own.shape
    return run(
        "latent_grads",
        functools.partial(latent_kernel, ways, bands),
        [
            jax.ShapeDtypeStruct((samples, rows + 2, kept, depth), BF),
            jax.ShapeDtypeStruct((samples, rows, kept, LANES), BF),
            jax.ShapeDtypeStruct((samples, rows, kept, depth), F32),
        ],
        [own, cross, *strips, slope_second, slope_first],
        [
            pltpu.VMEM((samples, rows + 2, kept, depth), F32),
            pltpu.VMEM((samples, rows + 2, kept, depth), F32),
        ],
    )


def encoder_kernel(norm_factor, bands, grad_ref, slope_ref, input_ref, weights_ref, moved_out, mine_ref, other_ref, wide, cat, wide_first):
    samples, tall, kept, depth = grad_ref.shape
    rows = tall - 2
    height = rows - 2
    breadth = kept - 2 * EDGE
    lat = lax.axis_index("lat")
    core, _ = core_and_chip()
    own = 8 + EDGE
    wide[:, :, 8 : 8 + kept, :] = grad_ref[...].astype(F32)
    for v in STEPS:
        lanes = slice((v + 1) * depth, (v + 2) * depth)
        cat[:, :, :, lanes] = wide[:, :, 8 - v : 8 - v + kept + 8, :].astype(BF)
    linear = None
    for u in STEPS:
        weights = jnp.concatenate([weights_ref[3 * (u + 1) + (v + 1)] for v in STEPS], axis=1)
        left = cat[:, 1 - u : 1 - u + rows].reshape(samples * rows * (kept + 8), 3 * depth)
        part = dot_last(left, weights)
        linear = part if linear is None else linear + part
    linear = linear.reshape(samples, rows, kept + 8, depth)
    for i in range(rows):
        row = lat * height + i - 1
        valid = jnp.logical_and(row >= 0, row < bands * height)
        value = linear[:, i, :kept] * slope_ref[:, i]
        if i < 1 or i >= height + 1:
            value = jnp.where(valid, value, 0.0)
        wide_first[:, i, 8 : 8 + kept, :] = value.astype(BF).astype(F32)
    for v in STEPS:
        lanes = slice((v + 1) * depth, (v + 2) * depth)
        moved_out[:, :, :, lanes] = wide_first[:, :, own - v : own - v + breadth, :].astype(BF)
    for u in STEPS:
        right = moved_out[:, 1 - u : 1 - u + height].reshape(samples * height * breadth, 3 * depth)
        part = dot_plain(input_ref[...], right) * norm_factor
        for v in STEPS:
            k = 3 * (u + 1) + (v + 1)
            lower = part[:, (v + 1) * depth : (v + 1) * depth + LANES]
            upper = part[:, (v + 1) * depth + LANES : (v + 2) * depth]
            mine_ref[k] = jnp.where(core == 0, lower, upper).astype(BF)
            other_ref[k] = jnp.where(core == 0, upper, lower).astype(BF)


def encoder(norm_factor, bands, grad, slope, cells_in, w_second):
    samples, tall, kept, depth = grad.shape
    rows, height, breadth = tall - 2, tall - 4, kept - 2 * EDGE
    channels = cells_in.shape[0]
    half = jax.ShapeDtypeStruct((9, channels, LANES), BF)
    return run(
        "encoder_grads",
        functools.partial(encoder_kernel, norm_factor, bands),
        [jax.ShapeDtypeStruct((samples, rows, breadth, 3 * depth), BF), half, half],
        [grad, slope, cells_in, w_second],
        [
            pltpu.VMEM((samples, tall, kept + 24, depth), F32),
            pltpu.VMEM((samples, tall, kept + 8, 3 * depth), BF),
            pltpu.VMEM((samples, rows, kept + 16, depth), F32),
        ],
        flops=2 * 9 * depth * (samples * rows * (kept + 8) * depth + samples * height * breadth * channels),
    )


def second_kernel(norm_factor, shares, grad_ref, got_ref, act_ref, act_got_ref, *refs):
    full_ref, wide, cat = refs[-3:]
    samples, tall, kept, depth = grad_ref.shape
    rows, height, breadth = tall - 2, tall - 4, kept - 2 * EDGE
    core, chip = core_and_chip()
    own = 8 + EDGE
    lower = grad_ref[:, 1 : 1 + rows, :, :LANES].astype(F32)
    upper = grad_ref[:, 1 : 1 + rows, :, LANES:].astype(F32)
    wide[:samples, :, 8 : 8 + kept, :] = jnp.where(chip == 0, lower, upper)
    wide[samples:, :, 8 : 8 + kept, :] = got_ref[...].astype(F32)
    for v in STEPS:
        lanes = slice((v + 1) * LANES, (v + 2) * LANES)
        cat[:, :, :, lanes] = wide[:, :, own - v : own - v + breadth, :].astype(BF)
    cells = samples * height * breadth
    for u in STEPS:
        right = cat[:, 1 - u : 1 - u + height].reshape(2 * cells, 3 * LANES)
        part = dot_plain(act_ref[...], right[:cells]) + dot_plain(act_got_ref[...], right[cells:])
        part = part * norm_factor
        for v in STEPS:
            k = 3 * (u + 1) + (v + 1)
            full_ref[k * depth : (k + 1) * depth, :] = part[:, (v + 1) * LANES : (v + 2) * LANES].astype(BF)
    if len(refs) == 5:
        size = 9 * depth // shares // 2
        for i in range(shares):
            for out_ref, half in ((refs[0], core), (refs[1], 1 - core)):
                out_ref[i] = full_ref[pl.ds(pl.multiple_of((2 * i + half) * size, 16), size), :]


def second_grads(norm_factor, shares, grad, got, act, act_got):
    samples, tall, kept, depth = grad.shape
    rows, height, breadth = tall - 2, tall - 4, kept - 2 * EDGE
    size = 9 * depth // shares // 2
    inside = size % 16 == 0
    half = jax.ShapeDtypeStruct((shares, size, LANES), BF)
    scratch = [
        pltpu.VMEM((2 * samples, rows, kept + 16, LANES), F32),
        pltpu.VMEM((2 * samples, rows, breadth, 3 * LANES), BF),
    ]
    results = run(
        "second_weight_grads",
        functools.partial(second_kernel, norm_factor, shares),
        [half, half] if inside else [jax.ShapeDtypeStruct((9 * depth, LANES), BF)],
        [grad, got, act, act_got],
        [pltpu.VMEM((9 * depth, LANES), BF)] + scratch if inside else scratch,
        flops=2 * 9 * depth * LANES * 2 * samples * height * breadth,
    )
    if inside:
        return results
    halves = results[0].reshape(shares, 2, size, LANES)
    core, _ = core_and_chip()
    return [lax.dynamic_index_in_dim(halves, part, 1, keepdims=False) for part in (core, 1 - core)]


def act_kernel(source_ref, out_ref):
    samples, height, breadth, depth = source_ref.shape
    active = gelu_value(source_ref[...].astype(F32).reshape(samples * height * breadth, depth)).astype(BF).astype(F32)
    out_ref[...] = active.T.astype(BF)


def activated(source):
    samples, height, breadth, depth = source.shape
    return run("activated", act_kernel, [jax.ShapeDtypeStruct((depth, samples * height * breadth), BF)], [source])[0]


def other_band_kernel(*refs):
    band = 1 - lax.rem(lax.axis_index("lat"), 2)
    parts = [t[band].astype(F32) for t in refs[:-1]]
    refs[-1][...] = sum(parts[1:], parts[0]).astype(BF)


def partner(index, step, count):
    return index ^ step if count & (count - 1) == 0 else (index + step) % count


def own_band_kernel(*refs):
    columns = refs[0].shape[1]
    terms, came, outs = refs[: -columns - 2], refs[-columns - 2 : -columns], refs[-columns:]
    band, lon = lax.rem(lax.axis_index("lat"), 2), lax.axis_index("lon")
    for step in range(columns):
        block = partner(lon, step, columns)
        for layer in range(2):
            parts = [t[band, block].astype(F32) for t in terms[layer * len(terms) // 2 : (layer + 1) * len(terms) // 2]]
            outs[step][layer] = sum(parts, came[layer][block].astype(F32)).astype(BF)


def sum_kernel(*refs):
    total = refs[0][...].astype(F32)
    for ref in refs[1:-1]:
        total = total + ref[...].astype(F32)
    refs[-1][...] = total.astype(BF)


def input_kernel(moved_ref, w_first_ref, out_ref):
    samples, rows, breadth, triple = moved_ref.shape
    height = rows - 2
    total = None
    for u in STEPS:
        weights = jnp.concatenate([w_first_ref[3 * (u + 1) + (v + 1)] for v in STEPS], axis=1)
        part = dot_last(moved_ref[:, 1 - u : 1 - u + height].reshape(samples * height * breadth, triple), weights)
        total = part if total is None else total + part
    out_ref[...] = total.astype(BF).reshape(out_ref.shape)


def input_conv(moved, w_first):
    samples, rows, breadth, triple = moved.shape
    shape = (samples, rows - 2, breadth, w_first.shape[1])
    return run(
        "input_conv",
        input_kernel,
        [jax.ShapeDtypeStruct(shape, BF)],
        [moved, w_first],
        flops=2 * 3 * math.prod(shape) * triple,
    )[0]


def chips_kernel(mine_ref, cross_ref, out_ref):
    _, chip = core_and_chip()
    out_ref[0] = (mine_ref[0].astype(F32) + cross_ref[0].astype(F32)).astype(BF)
    out_ref[1] = jnp.where(chip == 0, mine_ref[1], cross_ref[1])
    out_ref[2] = jnp.where(chip == 0, cross_ref[1], mine_ref[1])


def cores_kernel(mine_ref, other_ref, first_ref, second_ref):
    core, _ = core_and_chip()
    rows = mine_ref.shape[1]
    mine, other = (ref[...].astype(F32) for ref in (mine_ref, other_ref))
    for part in range(2):
        value = jnp.where(core == part, mine, other)
        first_ref[pl.ds(part, rows, stride=2), :] = value[0]
        second_ref[pl.ds(2 * rows * part, rows, stride=2), :] = value[1]
        second_ref[pl.ds(2 * rows * part + 1, rows, stride=2), :] = value[2]


def swap(array, axis, flip):
    count = lax.axis_size(axis)
    return lax.ppermute(array, axis, [(i, i ^ flip) for i in range(count)])


def around(array, axis, step, periodic=True):
    count = lax.axis_size(axis)
    pairs = [(i, (i + step) % count) for i in range(count) if periodic or 0 <= i + step < count]
    return lax.ppermute(array, axis, pairs)


def corner(array, step):
    lead, lat = lax.axis_size("lead"), lax.axis_size("lat")
    pairs = []
    for a in range(lead):
        for b in range(lat):
            target = (b ^ 1) if step is None else b + step
            if 0 <= target < lat:
                pairs.append((a * lat + b, (a ^ 2) * lat + target))
    return lax.ppermute(array, ("lead", "lat"), pairs)


def other_band(terms, columns):
    shape = (columns, terms[0].size // LANES // columns // 2, LANES)
    return run("other_band", other_band_kernel, [jax.ShapeDtypeStruct(shape, BF)], [t.reshape(2, *shape) for t in terms])[0]


def pairwise(terms, bands):
    lat = lax.axis_index("lat")
    total = sum(t.reshape(-1, LANES).astype(F32) for t in terms).astype(BF)
    left = bands
    while left > 2:
        left //= 2
        bit = (lat // left) % 2
        halves = total.reshape(2, -1, LANES)
        send = lax.dynamic_index_in_dim(halves, 1 - bit, 0, keepdims=False)
        keep = lax.dynamic_index_in_dim(halves, bit, 0, keepdims=False)
        total = (keep.astype(F32) + swap(send, "lat", left).astype(F32)).astype(BF)
    return total


def near_kernel(second_ref, first_ref, input_ref, low_ref, high_ref, slope_second, slope_first, halo_ref, wide, cells):
    samples, height, breadth, depth = second_ref.shape
    kept = breadth + 2 * EDGE
    batch = low_ref.shape[0] - samples
    for ref, width, first_cell, slope_ref in ((second_ref, 2, 0, slope_second), (first_ref, 1, 4 * height, slope_first)):
        wide[...] = jnp.zeros(wide.shape, F32)
        for s in range(samples):
            for r in range(height):
                at = (s * height + r) * kept + EDGE
                for half in range(2):
                    wide[half, at : at + breadth, :] = ref[s, r, :, half * LANES : (half + 1) * LANES].astype(F32)
            for side, packed_ref in ((0, low_ref), (1, high_ref)):
                packed = packed_ref[batch + s].astype(F32)
                for col in range(width):
                    for half in range(2):
                        here = ((col if width == 2 else 2) * 2 + half) * height
                        value = packed[here : here + height]
                        at = s * height * kept + EDGE + col + (breadth if side else -width)
                        wide[half, pl.ds(at, height, stride=kept), :] = value
                        at = first_cell + (side * width + col) * height
                        cells[s, at : at + height, half * LANES : (half + 1) * LANES] = value
        value = jnp.concatenate([wide[0], wide[1]], axis=1)
        slope_ref[...] = gelu_slope(value).reshape(slope_ref.shape)
    halo_ref[:, : cells.shape[1]] = cells[...].astype(BF)
    half = height // 2
    for part in range(2):
        values = input_ref[:, part * half : (part + 1) * half].reshape(samples, half * breadth, LANES)
        halo_ref[:, cells.shape[1] :, part * LANES : (part + 1) * LANES] = values


def near_parts(pre_second, pre_first, encoder_input, low, high):
    samples, height, breadth, depth = pre_second.shape
    kept = breadth + 2 * EDGE
    slope = jax.ShapeDtypeStruct((samples, height, kept, depth), F32)
    return run(
        "near_parts",
        near_kernel,
        [slope, slope, jax.ShapeDtypeStruct((samples, 6 * height + height * breadth // 2, depth), BF)],
        [pre_second, pre_first, encoder_input, low, high],
        [pltpu.VMEM((2, samples * height * kept, LANES), F32), pltpu.VMEM((samples, 6 * height, depth), F32)],
    )


def far_kernel(first_ref, tile_second, tile_first, slope_second, slope_first, act_out, wide, act):
    samples, height, breadth, depth = first_ref.shape
    kept = breadth + 2 * EDGE
    lat = lax.axis_index("lat")
    for source_ref, slope_ref in ((tile_second, slope_second), (tile_first, slope_first)):
        wide[...] = jnp.zeros(wide.shape, F32)
        for s in range(samples):
            for half in range(2):
                for r in range(height):
                    at = (s * height + r) * kept + EDGE
                    wide[half, at : at + breadth, :] = source_ref[s, r, :, half * LANES : (half + 1) * LANES].astype(F32)
        value = jnp.concatenate([wide[0], wide[1]], axis=1)
        slope_ref[...] = gelu_slope(value).reshape(slope_ref.shape)
    own, other = pl.ds(height * lat, height), pl.ds(height * (1 - lat), height)
    act[:, own] = gelu_value(first_ref[...].astype(F32))
    act[:, other] = gelu_value(tile_first[...].astype(F32))
    act_out[...] = act[...].reshape(act_out.shape[1], depth).T.astype(BF)


def far_parts(pre_first, tile_second, tile_first):
    samples, height, breadth, depth = pre_first.shape
    kept = breadth + 2 * EDGE
    slope = jax.ShapeDtypeStruct((samples, height, kept, depth), F32)
    return run(
        "far_parts",
        far_kernel,
        [slope, slope, jax.ShapeDtypeStruct((depth, 2 * samples * height * breadth), BF)],
        [pre_first, tile_second, tile_first],
        [
            pltpu.VMEM((2, samples * height * kept, LANES), F32),
            pltpu.VMEM((samples, 2 * height, breadth, depth), F32),
        ],
    )


def put_slopes(sample, slope, near_ref, far_ref, halo_ref, width, first_cell):
    _, height, kept, _ = near_ref.shape
    lat = lax.axis_index("lat")
    other = pl.ds(height * (1 - lat), height)
    slope[pl.ds(height * lat, height)] = near_ref[sample]
    slope[other] = far_ref[sample]
    beside = gelu_slope(halo_ref[sample, : 6 * height].astype(F32))
    for side in range(2):
        for col in range(width):
            here = first_cell + (side * width + col) * height
            at = kept - EDGE + col if side else EDGE - width + col
            slope[other, at, :] = beside[here : here + height]


def globe_kernel(sample, near_ref, far_ref, halo_ref, total_ref, line_ref, cat_ref, moved_ref, latent, slope, wide):
    rows, kept, depth = total_ref.shape
    height = rows - 1
    tall = 2 * height
    breadth = kept - 2 * EDGE
    lat = lax.axis_index("lat")
    own = 8 + EDGE
    latent[...] = jnp.zeros(latent.shape, F32)
    latent[pl.ds((height - 1) * lat, rows)] = total_ref[...].astype(F32)
    latent[pl.ds((height - 1) * (1 - lat), rows)] += line_ref[...].astype(F32)
    put_slopes(sample, slope, near_ref, far_ref, halo_ref, 2, 0)
    wide[:, 8 : 8 + kept, :] = (latent[...] * slope[...]).astype(BF).astype(F32)
    for v in STEPS:
        lanes = slice((v + 1) * depth, (v + 2) * depth)
        cat_ref[1 : 1 + tall, :, lanes] = wide[:, 8 - v : 8 - v + kept, :].astype(BF)
        moved_ref[v + 1, 1 : 1 + tall] = wide[:, own - v : own - v + breadth, :].astype(BF)
    for row in (0, tall + 1):
        cat_ref[row] = jnp.zeros(cat_ref.shape[1:], BF)
        moved_ref[:, row] = jnp.zeros(moved_ref.shape[:1] + moved_ref.shape[2:], BF)


def globe(sample, total, line, near, far, halo):
    rows, kept, depth = total.shape
    tall, breadth = 2 * (rows - 1), kept - 2 * EDGE
    return run(
        "latent_grads",
        functools.partial(globe_kernel, sample),
        [
            jax.ShapeDtypeStruct((tall + 2, kept, 3 * depth), BF),
            jax.ShapeDtypeStruct((3, tall + 2, breadth, depth), BF),
        ],
        [near, far, halo, total, line],
        [
            pltpu.VMEM((tall, kept, depth), F32),
            pltpu.VMEM((tall, kept, depth), F32),
            pltpu.VMEM((tall, kept + 24, depth), F32),
        ],
    )


def band_rows(norm_factor, lefts, moved, mine_ref, other_ref):
    channels, cells = lefts[0].shape
    _, padded, breadth, depth = moved[0].shape
    tall = padded - 2
    lat = lax.axis_index("lat")
    core, _ = core_and_chip()
    half = channels // 2

    def put(parts, u, v, start, size):
        total = None
        for left, ref in zip(parts, moved):
            part = dot_plain(left, ref[v + 1, pl.ds(1 - u, tall)].reshape(cells, depth))
            total = part if total is None else total + part
        total = total * norm_factor
        lower, upper = total[:, :LANES], total[:, LANES:]
        here = pl.ds(pl.multiple_of(start, half), size)
        mine_ref[here, :] = jnp.where(core == 0, lower, upper).astype(BF)
        other_ref[here, :] = jnp.where(core == 0, upper, lower).astype(BF)

    for j in range(4):
        (u0, v0), (u1, v1) = (divmod(k, 3) for k in (j, 5 + j))
        put(lefts, u0 - 1 + lat * (u1 - u0), v0 - 1 + lat * (v1 - v0), lat * half + j * channels, channels)
    put([jnp.where(lat == 0, left[:half], left[half:]) for left in lefts], 0, 0, (1 - lat) * 4 * channels, half)


def second_band_kernel(norm_factor, act_ref, *refs):
    moved, (mine_ref, other_ref) = refs[:-2], refs[-2:]
    cells = act_ref.shape[1] // len(moved)
    lefts = [act_ref[:, s * cells : (s + 1) * cells] for s in range(len(moved))]
    band_rows(norm_factor, lefts, moved, mine_ref, other_ref)


def second_band(norm_factor, act, moved):
    half = jax.ShapeDtypeStruct((9 * act.shape[0] // 2, LANES), BF)
    return run("second_weight_grads", functools.partial(second_band_kernel, norm_factor), [half, half], [act, *moved])


def first_kernel(sample, cat_ref, near_ref, far_ref, halo_ref, weights_ref, moved_ref, slope, wide):
    padded, kept, triple = cat_ref.shape
    tall, depth = padded - 2, triple // 3
    breadth = kept - 2 * EDGE
    own = 8 + EDGE
    put_slopes(sample, slope, near_ref, far_ref, halo_ref, 1, 2 * tall)
    linear = None
    for u in STEPS:
        weights = jnp.concatenate([weights_ref[3 * (u + 1) + (v + 1)] for v in STEPS], axis=1)
        part = dot_last(cat_ref[1 - u : 1 - u + tall].reshape(tall * kept, triple), weights)
        linear = part if linear is None else linear + part
    wide[:, 8 : 8 + kept, :] = (linear.reshape(tall, kept, depth) * slope[...]).astype(BF).astype(F32)
    for v in STEPS:
        moved_ref[v + 1, 1 : 1 + tall] = wide[:, own - v : own - v + breadth, :].astype(BF)
    for row in (0, tall + 1):
        moved_ref[:, row] = jnp.zeros(moved_ref.shape[:1] + moved_ref.shape[2:], BF)


def first_grad(sample, cat, near, far, halo, w_second):
    padded, kept, triple = cat.shape
    tall, depth = padded - 2, triple // 3
    return run(
        "second_conv",
        functools.partial(first_kernel, sample),
        [jax.ShapeDtypeStruct((3, padded, kept - 2 * EDGE, depth), BF)],
        [cat, near, far, halo, w_second],
        [pltpu.VMEM((tall, kept, depth), F32), pltpu.VMEM((tall, kept + 16, depth), F32)],
    )[0]


def first_band_kernel(norm_factor, halo_ref, input_ref, *refs):
    moved, (mine_ref, other_ref, cells) = refs[:-3], refs[-3:]
    samples, height, breadth, channels = input_ref.shape
    lat = lax.axis_index("lat")
    cells[:, pl.ds(height * lat, height)] = input_ref[...].astype(F32)
    half = height // 2
    for part in range(2):
        values = halo_ref[:, 6 * height :, part * LANES : (part + 1) * LANES].astype(F32)
        cells[:, pl.ds(height * (1 - lat) + part * half, half)] = values.reshape(samples, half, breadth, LANES)
    lefts = [cells[s].reshape(2 * height * breadth, channels).T.astype(BF) for s in range(samples)]
    band_rows(norm_factor, lefts, moved, mine_ref, other_ref)


def first_band(norm_factor, halo, encoder_input, moved):
    samples, height, breadth, channels = encoder_input.shape
    half = jax.ShapeDtypeStruct((9 * channels // 2, LANES), BF)
    return run(
        "first_weight_grads",
        functools.partial(first_band_kernel, norm_factor),
        [half, half],
        [halo, encoder_input, *moved],
        [pltpu.VMEM((samples, 2 * height, breadth, channels), F32)],
    )


def input_band_kernel(w_first_ref, *refs):
    moved, out_ref = refs[:-1], refs[-1]
    _, height, breadth, channels = out_ref.shape
    depth = moved[0].shape[3]
    lat = lax.axis_index("lat")
    total = None
    for u in STEPS:
        weights = jnp.concatenate([w_first_ref[3 * (u + 1) + (v + 1)] for v in STEPS], axis=1)
        here = pl.ds(height * lat + 1 - u, height)
        left = [jnp.concatenate([ref[v + 1, here].reshape(-1, depth) for v in STEPS], axis=1) for ref in moved]
        part = dot_last(jnp.concatenate(left, axis=0), weights)
        total = part if total is None else total + part
    out_ref[...] = total.astype(BF).reshape(out_ref.shape)


def blocks_kernel(first_mine, first_got, second_mine, second_got, *outs):
    lon = lax.axis_index("lon")
    rows = first_mine.shape[1]
    for step, out_ref in enumerate(outs):
        block = partner(lon, step, len(outs))
        out_ref[:rows] = (first_mine[block].astype(F32) + first_got[block].astype(F32)).astype(BF)
        out_ref[rows:] = (second_mine[block].astype(F32) + second_got[block].astype(F32)).astype(BF)


def halves_kernel(mine_ref, other_ref, first_ref, second_ref):
    core, _ = core_and_chip()
    mine, other = mine_ref[...].astype(F32), other_ref[...].astype(F32)
    rows = mine.shape[0] // 3
    for part in range(2):
        value = jnp.where(core == part, mine, other)
        first_ref[pl.ds(part, rows, stride=2), :] = value[:rows]
        second_ref[pl.ds(part, 2 * rows, stride=2), :] = value[rows:]


def to_partner(array, step):
    count = lax.axis_size("lon")
    return lax.ppermute(array, "lon", [(partner(i, step, count), i) for i in range(count)])


def two_bands(head_grads, head_weights, encoder_input, pre_first, pre_second, w_first, w_second, norm_factor):
    samples, height, breadth, _ = encoder_input.shape
    columns = lax.axis_size("lon")
    tiles = [swap(array, "lat", 1) for array in (pre_second, pre_first)]
    to_right, to_left = pack(head_grads, pre_second, pre_first)
    low = around(to_right, "lon", 1)
    high = around(to_left, "lon", -1)
    head_grads, head_weights, w_second, pre_second, pre_first, encoder_input = stage(
        head_grads, head_weights, w_second, pre_second, pre_first, encoder_input
    )
    low, high, *tiles = lax.optimization_barrier((low, high, *tiles))
    heads_of = functools.partial(
        head_conv,
        head_grads=head_grads,
        low=low,
        high=high,
        head_weights=head_weights,
        slots=2 * samples,
        rows=height + 1,
    )
    everyone = range(samples)
    got = swap(heads_of(True, False, 0), "lead", 1)
    part_shape = jax.ShapeDtypeStruct(got.shape[1:], BF)
    parts = run("core_sum", core_sum_kernel, [part_shape] * (2 * samples), [heads_of(False, False, 0), got])
    own, cross = parts[0::2], [swap(part, "lead", 2) for part in parts[1::2]]
    near_second, near_first, halo = near_parts(pre_second, pre_first, encoder_input, low, high)
    halo = swap(halo, "lat", 1)
    cross[-1], halo = lax.optimization_barrier((cross[-1], halo))
    totals = [run("chip_sum", sum_kernel, [part_shape], [own[s], cross[s]])[0] for s in everyone]
    lines = [swap(total, "lat", 1) for total in totals]
    far_second, far_first, act = far_parts(pre_first, *tiles)

    moved_second, moved_first = [], []
    for s in everyone:
        cat, moved = globe(s, totals[s], lines[s], near_second, far_second, halo)
        moved_second.append(moved)
        if s < samples - 1:
            moved_first.append(first_grad(s, cat, near_first, far_first, halo, w_second))
            near_second, moved_first[s] = lax.optimization_barrier((near_second, moved_first[s]))
    second_mine, second_other = second_band(norm_factor, act, moved_second)
    second_got = swap(second_other, "lead", 1)
    moved_first.append(first_grad(samples - 1, cat, near_first, far_first, halo, w_second))
    first_mine, first_other = first_band(norm_factor, halo, encoder_input, moved_first)
    first_got = swap(first_other, "lead", 1)
    input_grad = run(
        "input_conv", input_band_kernel, [jax.ShapeDtypeStruct(encoder_input.shape, BF)], [w_first, *moved_first]
    )[0]

    blocks = [t.reshape(columns, -1, LANES) for t in (first_mine, first_got, second_mine, second_got)]
    rows = blocks[0].shape[1]
    share_shape = jax.ShapeDtypeStruct((3 * rows, LANES), BF)
    shares = run("blocks", blocks_kernel, [share_shape] * columns, blocks)
    parts = [to_partner(shares[step], step) for step in [*range(2, columns), 1]]
    share = run("share", sum_kernel, [share_shape], [shares[0], *parts])[0]
    both = run("chips", sum_kernel, [share_shape], [share, swap(share, "lead", 2)])[0]
    result_first, result_second = run(
        "cores",
        halves_kernel,
        [jax.ShapeDtypeStruct((2 * rows, LANES), F32), jax.ShapeDtypeStruct((4 * rows, LANES), F32)],
        [both, swap(both, "lead", 1)],
    )
    return input_grad, result_first.reshape(-1), result_second.reshape(-1)


def core_sum_kernel(mine_ref, got_ref, *outs):
    for slot, out_ref in enumerate(outs):
        out_ref[...] = (mine_ref[slot].astype(F32) + got_ref[slot].astype(F32)).astype(BF)


def general(head_grads, head_weights, encoder_input, pre_first, pre_second, w_first, w_second, norm_factor):
    samples, height, breadth, _ = encoder_input.shape
    bands, columns = lax.axis_size("lat"), lax.axis_size("lon")
    to_right, to_left = pack(head_grads, pre_second, pre_first)
    to_right, to_left, to_cross = lax.optimization_barrier((to_right, to_left, pre_first))
    low = around(to_right, "lon", 1)
    high = around(to_left, "lon", -1)
    act_got = activated(swap(to_cross, "lead", 2))
    head_grads, head_weights, w_second, pre_second, pre_first, encoder_input = stage(
        head_grads, head_weights, w_second, pre_second, pre_first, encoder_input
    )
    low, high, act_got = lax.optimization_barrier((low, high, act_got))

    steps = [1, -1]
    heads_of = functools.partial(head_conv, head_grads=head_grads, high=high, head_weights=head_weights, slots=samples, rows=height + 2)
    got_cross = swap(heads_of(True, True, None, low=low), "lead", 1)
    got_own = swap(heads_of(True, False, None, low=low), "lead", 1)
    cross, *angles = spread_cross(heads_of(False, True, None, low=low), got_cross, len(steps))
    low_later, cross, *angles = lax.optimization_barrier((low, cross, *angles))
    cross = swap(cross, "lead", 2)
    angles = [corner(angle, step) for angle, step in zip(angles, steps)]
    second, first, slope_second, slope_first, act, cells_in = saved(pre_second, pre_first, encoder_input, low, high)
    own, *lines = spread_own(heads_of(False, False, None, low=low_later), got_own, second, first, len(steps))
    lines = [swap(line, "lat", 1) if step is None else around(line, "lat", step, False) for line, step in zip(lines, steps)]
    strips = [strip for pair in zip(lines, angles) for strip in pair]

    grad, away, slope = latent_grads(len(steps), bands, own, cross, strips, slope_second, slope_first)
    grad_got = swap(away, "lead", 2)
    moved, first_mine, first_other = encoder(norm_factor, bands, grad, slope, cells_in, w_second)
    input_grad = input_conv(moved, w_first)
    first_got = swap(first_other, "lead", 1)
    second_mine, second_other = second_grads(norm_factor, bands * columns, grad, grad_got, act, act_got)
    second_got = swap(second_other, "lead", 1)

    first_terms = [pairwise([first_mine, first_got], bands)]
    second_terms = [pairwise([second_mine, second_got], bands)]
    first_came = swap(other_band(first_terms, columns), "lat", 1)
    second_came = swap(other_band(second_terms, columns), "lat", 1)
    blocks = [t.reshape(2, columns, -1, LANES) for t in first_terms + second_terms]
    rows = blocks[0].shape[2]
    share_shape = jax.ShapeDtypeStruct((2, rows, LANES), BF)
    shares = run("own_band", own_band_kernel, [share_shape] * columns, blocks + [first_came, second_came])
    parts = [to_partner(shares[step], step) for step in [*range(2, columns), 1]]
    share = run("share", sum_kernel, [share_shape], [shares[0], *parts])[0]
    both = run("chips", chips_kernel, [jax.ShapeDtypeStruct((3, rows, LANES), BF)], [share, swap(share, "lead", 2)])[0]
    result_first, result_second = run(
        "cores",
        cores_kernel,
        [jax.ShapeDtypeStruct((2 * rows, LANES), F32), jax.ShapeDtypeStruct((4 * rows, LANES), F32)],
        [both, swap(both, "lead", 1)],
    )
    return input_grad, result_first.reshape(-1), result_second.reshape(-1)


def per_device(head_grads, head_weights, encoder_input, pre_first, pre_second, w_first, w_second):
    samples, height, breadth, channels = encoder_input.shape
    bands, columns = lax.axis_size("lat"), lax.axis_size("lon")
    cells_total = samples * lax.axis_size("lead") * height * bands * breadth * columns
    norm_factor = 1.0 / math.sqrt(cells_total)
    plan = two_bands if bands == 2 and 9 * channels // (bands * columns) % 16 == 0 else general
    return plan(head_grads, head_weights, encoder_input, pre_first, pre_second, w_first, w_second, norm_factor)


def solution(mesh):
    in_specs = (
        P("lead", None, "lat", "lon", None),
        P("lead", None, None, None),
        P("lead", "lat", "lon", None),
        P("lead", "lat", "lon", None),
        P("lead", "lat", "lon", None),
        P(),
        P(),
    )
    out_specs = (P("lead", "lat", "lon", None), P(("lat", "lon")), P(("lat", "lon")))
    return jax.shard_map(
        per_device, mesh=mesh, in_specs=in_specs, out_specs=out_specs, check_vma=False
    )
```

```python
import functools
import math

import jax
import jax.numpy as jnp
from jax import lax
from jax.experimental import pallas as pl
from jax.experimental.pallas import tpu as pltpu
from jax.sharding import PartitionSpec as P

BF = jnp.bfloat16
F32 = jnp.float32
STEPS = (-1, 0, 1)
EDGE = 4
LANES = 128
VMEM_BYTES = 24 * 1024 * 1024


def erf_part(values):
    return 0.5 * (1.0 + lax.erf(values * 0.7071067811865476))


def gelu_slope(values):
    return erf_part(values) + values * jnp.exp(-0.5 * values * values) * 0.3989422804014327


def gelu_value(values):
    return values * erf_part(values)


def dot_last(left, right):
    return lax.dot_general(left, right, (((1,), (1,)), ((), ())), preferred_element_type=F32)


def dot_plain(left, right):
    return lax.dot_general(left, right, (((1,), (0,)), ((), ())), preferred_element_type=F32)


def core_and_chip():
    lead = lax.axis_index("lead")
    return lax.rem(lead, 2), lax.div(lead, 2)


def run(name, kernel, out_shape, arrays, scratch=(), flops=0, far=False):
    specs = [pl.BlockSpec(memory_space=pltpu.HBM if far else pltpu.VMEM)] * len(arrays)
    if far:
        arrays = [pltpu.with_memory_space_constraint(a, pltpu.HBM) for a in arrays]
    touched = sum(a.size * a.dtype.itemsize for a in arrays)
    touched += sum(math.prod(s.shape) * s.dtype.itemsize for s in out_shape)
    return pl.pallas_call(
        kernel,
        name=name,
        out_shape=out_shape,
        in_specs=specs,
        out_specs=[pl.BlockSpec(memory_space=pltpu.VMEM)] * len(out_shape),
        scratch_shapes=list(scratch),
        compiler_params=pltpu.CompilerParams(vmem_limit_bytes=VMEM_BYTES),
        cost_estimate=pl.CostEstimate(flops=1, bytes_accessed=1, transcendentals=0),
    )(*arrays)


def pack_kernel(grads_far, second_far, first_far, right_ref, left_ref, grads_near, second_near, first_near, edges, edges_wide, packed, sems):
    heads, batch, height, breadth, _ = grads_far.shape
    samples = second_far.shape[0]
    rows = 6 * height
    copies = []
    for side in range(2):
        columns = pl.ds(breadth - 16 if side == 0 else 0, 16)
        for j, (far, near) in enumerate(((grads_far, grads_near), (second_far, second_near), (first_far, first_near))):
            source = far.at[:, :, :, columns, :] if j == 0 else far.at[:, :, columns, :]
            copies.append(pltpu.make_async_copy(source, near.at[side], sems.at[side, j]))
            copies[-1].start()
    for copy in copies:
        copy.wait()
    for side, out_ref in ((0, right_ref), (1, left_ref)):
        start = 8 if side == 0 else 0
        grads_ref, second_ref, first_ref = grads_near.at[side], second_near.at[side], first_near.at[side]
        for h in range(heads):
            for b in range(batch):
                block = grads_ref[h, b, :, start : start + 8, :].astype(F32)
                edges[(h * batch + b) * height * 8 : (h * batch + b + 1) * height * 8, :] = block.reshape(height * 8, LANES)
        for j, ref in enumerate((second_ref, first_ref)):
            for s in range(samples):
                block = ref[s, :, start : start + 8, :].astype(F32)
                at = (j * samples + s) * height * 8
                for half in range(2):
                    lanes = slice(half * LANES, (half + 1) * LANES)
                    edges_wide[half, at : at + height * 8, :] = block[:, :, lanes].reshape(height * 8, LANES)
        for b in range(batch):
            for col in range(3):
                inner = 5 + col if side == 0 else col
                for h in range(heads):
                    at = b * rows + (col * 2 + h) * height
                    packed[at : at + height, :] = edges[pl.ds((h * batch + b) * height * 8 + inner, height, stride=8), :]
        for s in range(samples):
            for q in range(3):
                j, col, width = (0, q, 2) if q < 2 else (1, 0, 1)
                inner = 8 - width + col if side == 0 else col
                for half in range(2):
                    at = (batch + s) * rows + (q * 2 + half) * height
                    packed[at : at + height, :] = edges_wide[
                        half, pl.ds((j * samples + s) * height * 8 + inner, height, stride=8), :
                    ]
        out_ref[...] = packed[...].astype(BF).reshape(out_ref.shape)


def pack(head_grads, pre_second, pre_first):
    heads, batch, height, _, _ = head_grads.shape
    samples = pre_second.shape[0]
    shape = jax.ShapeDtypeStruct((batch + samples, 6 * height, LANES), BF)
    return run(
        "pack_columns",
        pack_kernel,
        [shape, shape],
        [head_grads, pre_second, pre_first],
        [
            pltpu.VMEM((2, heads, batch, height, 16, LANES), BF),
            pltpu.VMEM((2, samples, height, 16, 2 * LANES), BF),
            pltpu.VMEM((2, samples, height, 16, 2 * LANES), BF),
            pltpu.VMEM((heads * batch * height * 8, LANES), F32),
            pltpu.VMEM((2, 2 * samples * height * 8, LANES), F32),
            pltpu.VMEM(((batch + samples) * 6 * height, LANES), F32),
            pltpu.SemaphoreType.DMA((2, 3)),
        ],
        far=True,
    )


def stage_kernel(*refs):
    count = len(refs) // 2
    sems = refs[-1]
    copies = [pltpu.make_async_copy(refs[i], refs[count + i], sems.at[i]) for i in range(count)]
    for copy in copies:
        copy.start()
    for copy in copies:
        copy.wait()


def stage(*arrays):
    shapes = [pltpu.VMEM(a.shape, a.dtype) for a in arrays]
    return run("stage", stage_kernel, shapes, list(arrays), [pltpu.SemaphoreType.DMA((len(arrays),))], far=True, flops=1 << 30)


def heads_kernel(other_core, other_chip, sample, samples, grads_ref, low_ref, high_ref, weights_ref, out_ref, wide, shifted, total):
    heads, batch, height, breadth, _ = grads_ref.shape
    slots, _, kept, depth = out_ref.shape
    pitch = kept + 16
    own = 8 + EDGE
    core, chip = core_and_chip()
    core = 1 - core if other_core else core
    for slot in range(slots):
        if sample is None:
            group, s = 1 - chip if other_chip else chip, slot
        else:
            group, s = 1 - chip if slot % 2 else chip, sample + slot // 2
        b = (2 * group + core) * samples + s
        low = low_ref[b].astype(F32)
        high = high_ref[b].astype(F32)
        for r in range(height):
            at = (slot * height + r) * pitch + own
            for h in range(heads):
                wide[h, at : at + breadth, :] = grads_ref[h, b, r].astype(F32)
        for col in range(3):
            for h in range(heads):
                here = (col * 2 + h) * height
                at = slot * height * pitch + own + col
                wide[h, pl.ds(at - 3, height, stride=pitch), :] = low[here : here + height]
                wide[h, pl.ds(at + breadth, height, stride=pitch), :] = high[here : here + height]
        for v in STEPS:
            for h in range(heads):
                starts = [(slot * height + r) * pitch + 8 - v for r in range(height)]
                moved = jnp.concatenate([wide[h, at : at + kept, :] for at in starts], axis=0).astype(BF)
                lane = ((v + 1) * heads + h) * LANES
                shifted[slot * height * kept : (slot + 1) * height * kept, lane : lane + LANES] = moved
    total[:, height:, :, :] = jnp.zeros((slots, 2, kept, depth), F32)
    for u in STEPS:
        weights = jnp.concatenate(
            [weights_ref[h, 3 * (u + 1) + (v + 1)] for v in STEPS for h in range(heads)], axis=1
        )
        part = dot_last(shifted[...], weights).reshape(slots, height, kept, depth)
        if u == -1:
            total[:, :height] = part
        else:
            total[:, 1 + u : 1 + u + height] += part
    if out_ref.shape[1] == height + 2:
        out_ref[...] = total[...].astype(BF)
    else:
        out_ref[...] = total[:, pl.ds(1 - lax.axis_index("lat"), height + 1)].astype(BF)


def head_conv(other_core, other_chip, sample, head_grads, low, high, head_weights, slots, rows):
    samples = head_grads.shape[1] // lax.axis_size("lead")
    heads, batch, height, breadth, _ = head_grads.shape
    depth = head_weights.shape[2]
    kept = breadth + 2 * EDGE
    return run(
        "head_conv",
        functools.partial(heads_kernel, other_core, other_chip, sample, samples),
        [jax.ShapeDtypeStruct((slots, rows, kept, depth), BF)],
        [head_grads, low, high, head_weights],
        [
            pltpu.VMEM((heads, slots * height * (kept + 16), LANES), F32),
            pltpu.VMEM((slots * height * kept, 3 * heads * LANES), BF),
            pltpu.VMEM((slots, height + 2, kept, depth), F32),
        ],
        flops=2 * slots * height * kept * 9 * heads * LANES * depth,
    )[0]


def inside_kernel(samples, grads_ref, weights_ref, total_ref, wide, shifted):
    heads, _, height, breadth, _ = grads_ref.shape
    slots, _, kept, depth = total_ref.shape
    pitch = kept + 16
    own = 8 + EDGE
    core, chip = core_and_chip()
    blank = jnp.zeros((height, LANES), F32)
    for slot in range(slots):
        group, s = 1 - chip if slot % 2 else chip, slot // 2
        b = (2 * group + 1 - core) * samples + s
        for h in range(heads):
            for r in range(height):
                at = (slot * height + r) * pitch + own
                wide[h, at : at + breadth, :] = grads_ref[h, b, r].astype(F32)
            for col in range(3):
                at = slot * height * pitch + own + col
                wide[h, pl.ds(at - 3, height, stride=pitch), :] = blank
                wide[h, pl.ds(at + breadth, height, stride=pitch), :] = blank
            for v in STEPS:
                starts = [(slot * height + r) * pitch + 8 - v for r in range(height)]
                moved = jnp.concatenate([wide[h, at : at + kept, :] for at in starts], axis=0).astype(BF)
                lane = ((v + 1) * heads + h) * LANES
                shifted[slot * height * kept : (slot + 1) * height * kept, lane : lane + LANES] = moved
    total_ref[:, height:, :, :] = jnp.zeros((slots, 2, kept, depth), F32)
    for u in STEPS:
        weights = jnp.concatenate(
            [weights_ref[h, 3 * (u + 1) + (v + 1)] for v in STEPS for h in range(heads)], axis=1
        )
        part = dot_last(shifted[...], weights).reshape(slots, height, kept, depth)
        if u == -1:
            total_ref[:, :height] = part
        else:
            total_ref[:, 1 + u : 1 + u + height] += part


def edges_kernel(samples, inside_ref, low_ref, high_ref, weights_ref, out_ref, wide, shifted, total):
    slots, rows, kept, depth = inside_ref.shape
    height, heads, pitch = rows - 2, weights_ref.shape[0], 24
    core, chip = core_and_chip()
    wide[...] = jnp.zeros(wide.shape, F32)
    for side, packed_ref in ((0, low_ref), (1, high_ref)):
        for slot in range(slots):
            group, s = 1 - chip if slot % 2 else chip, slot // 2
            packed = packed_ref[(2 * group + 1 - core) * samples + s].astype(F32)
            first = (side * slots + slot) * height
            for h in range(heads):
                for col in range(3):
                    here = (col * 2 + h) * height
                    at = first * pitch + 9 + 3 * side + col
                    wide[h, pl.ds(at, height, stride=pitch), :] = packed[here : here + height]
                for v in STEPS:
                    starts = [(first + r) * pitch + 8 - v for r in range(height)]
                    moved = jnp.concatenate([wide[h, at : at + 8, :] for at in starts], axis=0).astype(BF)
                    lane = ((v + 1) * heads + h) * LANES
                    shifted[first * 8 : (first + height) * 8, lane : lane + LANES] = moved
    for u in STEPS:
        weights = jnp.concatenate(
            [weights_ref[h, 3 * (u + 1) + (v + 1)] for v in STEPS for h in range(heads)], axis=1
        )
        part = dot_last(shifted[...], weights).reshape(2, slots, height, 8, depth)
        if u == -1:
            total[:, :, :height] = part
            total[:, :, height:] = jnp.zeros((2, slots, 2, 8, depth), F32)
        else:
            total[:, :, 1 + u : 1 + u + height] += part
    here = pl.ds(1 - lax.axis_index("lat"), height + 1)
    out_ref[:, :, 8 : kept - 8] = inside_ref[:, here, 8 : kept - 8].astype(BF)
    for side, columns in enumerate((slice(0, 8), slice(kept - 8, kept))):
        out_ref[:, :, columns] = (inside_ref[:, here, columns] + total[side, :, here]).astype(BF)


def inside_conv(head_grads, head_weights, slots):
    samples = head_grads.shape[1] // lax.axis_size("lead")
    heads, _, height, breadth, _ = head_grads.shape
    kept = breadth + 2 * EDGE
    return run(
        "head_conv_inside",
        functools.partial(inside_kernel, samples),
        [jax.ShapeDtypeStruct((slots, height + 2, kept, head_weights.shape[2]), F32)],
        [head_grads, head_weights],
        [
            pltpu.VMEM((heads, slots * height * (kept + 16), LANES), F32),
            pltpu.VMEM((slots * height * kept, 3 * heads * LANES), BF),
        ],
    )[0]


def edges_conv(inside, low, high, head_weights):
    slots, rows, kept, depth = inside.shape
    samples, heads, height = slots // 2, head_weights.shape[0], rows - 2
    return run(
        "head_conv_edges",
        functools.partial(edges_kernel, samples),
        [jax.ShapeDtypeStruct((slots, rows - 1, kept, depth), BF)],
        [inside, low, high, head_weights],
        [
            pltpu.VMEM((heads, 2 * slots * height * 24, LANES), F32),
            pltpu.VMEM((2 * slots * height * 8, 3 * heads * LANES), BF),
            pltpu.VMEM((2, slots, rows, 8, depth), F32),
        ],
    )[0]


def saved_kernel(second_ref, first_ref, input_ref, low_ref, high_ref, second_out, first_out, slope_second, slope_first, act_out, input_out, wide):
    samples, height, breadth, depth = second_ref.shape
    kept = breadth + 2 * EDGE
    batch = low_ref.shape[0] - samples
    for ref, width, out_ref, slope_ref in (
        (second_ref, 2, second_out, slope_second),
        (first_ref, 1, first_out, slope_first),
    ):
        wide[...] = jnp.zeros(wide.shape, F32)
        for s in range(samples):
            for r in range(height):
                at = (s * height + r) * kept + EDGE
                for half in range(2):
                    lanes = slice(half * LANES, (half + 1) * LANES)
                    wide[half, at : at + breadth, :] = ref[s, r, :, lanes].astype(F32)
            low = low_ref[batch + s].astype(F32)
            high = high_ref[batch + s].astype(F32)
            for col in range(width):
                for half in range(2):
                    here = ((col if width == 2 else 2) * 2 + half) * height
                    at = s * height * kept + EDGE + col
                    wide[half, pl.ds(at - width, height, stride=kept), :] = low[here : here + height]
                    wide[half, pl.ds(at + breadth, height, stride=kept), :] = high[here : here + height]
        value = jnp.concatenate([wide[0], wide[1]], axis=1)
        out_ref[...] = value.astype(BF).reshape(out_ref.shape)
        slope_ref[...] = gelu_slope(value).reshape(slope_ref.shape)
    active = gelu_value(first_ref[...].astype(F32).reshape(samples * height * breadth, depth)).astype(BF).astype(F32)
    act_out[...] = active.T.astype(BF)
    cells = input_ref[...].astype(F32).reshape(samples * height * breadth, input_ref.shape[3])
    input_out[...] = cells.T.astype(BF)


def saved(pre_second, pre_first, encoder_input, low, high):
    samples, height, breadth, depth = pre_second.shape
    kept = breadth + 2 * EDGE
    cells = samples * height * breadth
    return run(
        "saved_parts",
        saved_kernel,
        [
            jax.ShapeDtypeStruct((samples, height, kept, depth), BF),
            jax.ShapeDtypeStruct((samples, height, kept, depth), BF),
            jax.ShapeDtypeStruct((samples, height, kept, depth), F32),
            jax.ShapeDtypeStruct((samples, height, kept, depth), F32),
            jax.ShapeDtypeStruct((depth, cells), BF),
            jax.ShapeDtypeStruct((encoder_input.shape[3], cells), BF),
        ],
        [pre_second, pre_first, encoder_input, low, high],
        [pltpu.VMEM((2, samples * height * kept, LANES), F32)],
    )


def goes_down(way, ways):
    return 1 - lax.axis_index("lat") if ways == 1 else 1 - way


def cross_kernel(mine_ref, got_ref, cross_ref, *strips):
    height = mine_ref.shape[1] - 2
    cross_ref[...] = (mine_ref[...].astype(F32) + got_ref[...].astype(F32)).astype(BF)
    for way, corner_ref in enumerate(strips):
        corner_ref[...] = cross_ref[:, pl.ds((height - 1) * goes_down(way, len(strips)), 3)]


def own_kernel(mine_ref, got_ref, second_ref, first_ref, own_ref, *strips):
    height = second_ref.shape[1]
    own_ref[...] = (mine_ref[...].astype(F32) + got_ref[...].astype(F32)).astype(BF)
    for way, line_ref in enumerate(strips):
        down = goes_down(way, len(strips))
        line_ref[:, 0:3] = own_ref[:, pl.ds((height - 1) * down, 3)]
        line_ref[:, 3:5] = second_ref[:, pl.ds((height - 2) * down, 2)]
        line_ref[:, 5:6] = first_ref[:, pl.ds((height - 1) * down, 1)]


def spread_cross(mine, got, ways):
    samples, _, kept, depth = mine.shape
    strip = jax.ShapeDtypeStruct((samples, 3, kept, depth), BF)
    return run("core_sum_cross", cross_kernel, [jax.ShapeDtypeStruct(mine.shape, BF)] + [strip] * ways, [mine, got])


def spread_own(mine, got, second, first, ways):
    samples, _, kept, depth = mine.shape
    strip = jax.ShapeDtypeStruct((samples, 6, kept, depth), BF)
    return run("core_sum_own", own_kernel, [jax.ShapeDtypeStruct(mine.shape, BF)] + [strip] * ways, [mine, got, second, first])


def latent_kernel(ways, bands, own_ref, cross_ref, *refs):
    strips, refs = refs[: 2 * ways], refs[2 * ways :]
    slope_second_ref, slope_first_ref, grad_ref, away_ref, slope_out, latent, slope_second = refs
    samples, rows, kept, depth = own_ref.shape
    height = rows - 2
    lat = lax.axis_index("lat")
    _, chip = core_and_chip()
    blank = jnp.zeros((samples, kept, depth), F32)
    latent[:, 0] = blank
    latent[:, height + 3] = blank
    latent[:, 1 : height + 3] = own_ref[...].astype(F32) + cross_ref[...].astype(F32)
    slope_second[:, 2 : 2 + height] = slope_second_ref[...]
    slope_out[:, 1 : 1 + height] = slope_first_ref[...]
    for way in range(ways):
        line_ref, corner_ref = strips[2 * way], strips[2 * way + 1]
        below = 1 - lat if ways == 1 else way
        at = (height + 1) * below
        latent[:, pl.ds(at, 3)] += line_ref[:, 0:3].astype(F32) + corner_ref[...].astype(F32)
        slope_second[:, pl.ds((height + 2) * below, 2)] = gelu_slope(line_ref[:, 3:5].astype(F32))
        slope_out[:, pl.ds((height + 1) * below, 1)] = gelu_slope(line_ref[:, 5:6].astype(F32))
    for i in range(height + 4):
        row = lat * height + i - 2
        valid = jnp.logical_and(row >= 0, row < bands * height)
        value = latent[:, i] * slope_second[:, i]
        if i < 2 or i >= height + 2:
            value = jnp.where(valid, value, 0.0)
        grad_ref[:, i] = value.astype(BF)
        if 0 < i < height + 3:
            away_ref[:, i - 1] = jnp.where(chip == 0, value[:, :, LANES:], value[:, :, :LANES]).astype(BF)


def latent_grads(ways, bands, own, cross, strips, slope_second, slope_first):
    samples, rows, kept, depth = own.shape
    return run(
        "latent_grads",
        functools.partial(latent_kernel, ways, bands),
        [
            jax.ShapeDtypeStruct((samples, rows + 2, kept, depth), BF),
            jax.ShapeDtypeStruct((samples, rows, kept, LANES), BF),
            jax.ShapeDtypeStruct((samples, rows, kept, depth), F32),
        ],
        [own, cross, *strips, slope_second, slope_first],
        [
            pltpu.VMEM((samples, rows + 2, kept, depth), F32),
            pltpu.VMEM((samples, rows + 2, kept, depth), F32),
        ],
    )


def encoder_kernel(norm_factor, bands, grad_ref, slope_ref, input_ref, weights_ref, moved_out, mine_ref, other_ref, wide, cat, wide_first):
    samples, tall, kept, depth = grad_ref.shape
    rows = tall - 2
    height = rows - 2
    breadth = kept - 2 * EDGE
    lat = lax.axis_index("lat")
    core, _ = core_and_chip()
    own = 8 + EDGE
    wide[:, :, 8 : 8 + kept, :] = grad_ref[...].astype(F32)
    for v in STEPS:
        lanes = slice((v + 1) * depth, (v + 2) * depth)
        cat[:, :, :, lanes] = wide[:, :, 8 - v : 8 - v + kept + 8, :].astype(BF)
    linear = None
    for u in STEPS:
        weights = jnp.concatenate([weights_ref[3 * (u + 1) + (v + 1)] for v in STEPS], axis=1)
        left = cat[:, 1 - u : 1 - u + rows].reshape(samples * rows * (kept + 8), 3 * depth)
        part = dot_last(left, weights)
        linear = part if linear is None else linear + part
    linear = linear.reshape(samples, rows, kept + 8, depth)
    for i in range(rows):
        row = lat * height + i - 1
        valid = jnp.logical_and(row >= 0, row < bands * height)
        value = linear[:, i, :kept] * slope_ref[:, i]
        if i < 1 or i >= height + 1:
            value = jnp.where(valid, value, 0.0)
        wide_first[:, i, 8 : 8 + kept, :] = value.astype(BF).astype(F32)
    for v in STEPS:
        lanes = slice((v + 1) * depth, (v + 2) * depth)
        moved_out[:, :, :, lanes] = wide_first[:, :, own - v : own - v + breadth, :].astype(BF)
    for u in STEPS:
        right = moved_out[:, 1 - u : 1 - u + height].reshape(samples * height * breadth, 3 * depth)
        part = dot_plain(input_ref[...], right) * norm_factor
        for v in STEPS:
            k = 3 * (u + 1) + (v + 1)
            lower = part[:, (v + 1) * depth : (v + 1) * depth + LANES]
            upper = part[:, (v + 1) * depth + LANES : (v + 2) * depth]
            mine_ref[k] = jnp.where(core == 0, lower, upper).astype(BF)
            other_ref[k] = jnp.where(core == 0, upper, lower).astype(BF)


def encoder(norm_factor, bands, grad, slope, cells_in, w_second):
    samples, tall, kept, depth = grad.shape
    rows, height, breadth = tall - 2, tall - 4, kept - 2 * EDGE
    channels = cells_in.shape[0]
    half = jax.ShapeDtypeStruct((9, channels, LANES), BF)
    return run(
        "encoder_grads",
        functools.partial(encoder_kernel, norm_factor, bands),
        [jax.ShapeDtypeStruct((samples, rows, breadth, 3 * depth), BF), half, half],
        [grad, slope, cells_in, w_second],
        [
            pltpu.VMEM((samples, tall, kept + 24, depth), F32),
            pltpu.VMEM((samples, tall, kept + 8, 3 * depth), BF),
            pltpu.VMEM((samples, rows, kept + 16, depth), F32),
        ],
        flops=2 * 9 * depth * (samples * rows * (kept + 8) * depth + samples * height * breadth * channels),
    )


def second_kernel(norm_factor, shares, grad_ref, got_ref, act_ref, act_got_ref, *refs):
    full_ref, wide, cat = refs[-3:]
    samples, tall, kept, depth = grad_ref.shape
    rows, height, breadth = tall - 2, tall - 4, kept - 2 * EDGE
    core, chip = core_and_chip()
    own = 8 + EDGE
    lower = grad_ref[:, 1 : 1 + rows, :, :LANES].astype(F32)
    upper = grad_ref[:, 1 : 1 + rows, :, LANES:].astype(F32)
    wide[:samples, :, 8 : 8 + kept, :] = jnp.where(chip == 0, lower, upper)
    wide[samples:, :, 8 : 8 + kept, :] = got_ref[...].astype(F32)
    for v in STEPS:
        lanes = slice((v + 1) * LANES, (v + 2) * LANES)
        cat[:, :, :, lanes] = wide[:, :, own - v : own - v + breadth, :].astype(BF)
    cells = samples * height * breadth
    for u in STEPS:
        right = cat[:, 1 - u : 1 - u + height].reshape(2 * cells, 3 * LANES)
        part = dot_plain(act_ref[...], right[:cells]) + dot_plain(act_got_ref[...], right[cells:])
        part = part * norm_factor
        for v in STEPS:
            k = 3 * (u + 1) + (v + 1)
            full_ref[k * depth : (k + 1) * depth, :] = part[:, (v + 1) * LANES : (v + 2) * LANES].astype(BF)
    if len(refs) == 5:
        size = 9 * depth // shares // 2
        for i in range(shares):
            for out_ref, half in ((refs[0], core), (refs[1], 1 - core)):
                out_ref[i] = full_ref[pl.ds(pl.multiple_of((2 * i + half) * size, 16), size), :]


def second_grads(norm_factor, shares, grad, got, act, act_got):
    samples, tall, kept, depth = grad.shape
    rows, height, breadth = tall - 2, tall - 4, kept - 2 * EDGE
    size = 9 * depth // shares // 2
    inside = size % 16 == 0
    half = jax.ShapeDtypeStruct((shares, size, LANES), BF)
    scratch = [
        pltpu.VMEM((2 * samples, rows, kept + 16, LANES), F32),
        pltpu.VMEM((2 * samples, rows, breadth, 3 * LANES), BF),
    ]
    results = run(
        "second_weight_grads",
        functools.partial(second_kernel, norm_factor, shares),
        [half, half] if inside else [jax.ShapeDtypeStruct((9 * depth, LANES), BF)],
        [grad, got, act, act_got],
        [pltpu.VMEM((9 * depth, LANES), BF)] + scratch if inside else scratch,
        flops=2 * 9 * depth * LANES * 2 * samples * height * breadth,
    )
    if inside:
        return results
    halves = results[0].reshape(shares, 2, size, LANES)
    core, _ = core_and_chip()
    return [lax.dynamic_index_in_dim(halves, part, 1, keepdims=False) for part in (core, 1 - core)]


def act_kernel(source_ref, out_ref):
    samples, height, breadth, depth = source_ref.shape
    active = gelu_value(source_ref[...].astype(F32).reshape(samples * height * breadth, depth)).astype(BF).astype(F32)
    out_ref[...] = active.T.astype(BF)


def activated(source):
    samples, height, breadth, depth = source.shape
    return run("activated", act_kernel, [jax.ShapeDtypeStruct((depth, samples * height * breadth), BF)], [source])[0]


def other_band_kernel(*refs):
    band = 1 - lax.rem(lax.axis_index("lat"), 2)
    parts = [t[band].astype(F32) for t in refs[:-1]]
    refs[-1][...] = sum(parts[1:], parts[0]).astype(BF)


def partner(index, step, count):
    return index ^ step if count & (count - 1) == 0 else (index + step) % count


def own_band_kernel(*refs):
    columns = refs[0].shape[1]
    terms, came, outs = refs[: -columns - 2], refs[-columns - 2 : -columns], refs[-columns:]
    band, lon = lax.rem(lax.axis_index("lat"), 2), lax.axis_index("lon")
    for step in range(columns):
        block = partner(lon, step, columns)
        for layer in range(2):
            parts = [t[band, block].astype(F32) for t in terms[layer * len(terms) // 2 : (layer + 1) * len(terms) // 2]]
            outs[step][layer] = sum(parts, came[layer][block].astype(F32)).astype(BF)


def sum_kernel(*refs):
    total = refs[0][...].astype(F32)
    for ref in refs[1:-1]:
        total = total + ref[...].astype(F32)
    refs[-1][...] = total.astype(BF)


def input_kernel(moved_ref, w_first_ref, out_ref):
    samples, rows, breadth, triple = moved_ref.shape
    height = rows - 2
    total = None
    for u in STEPS:
        weights = jnp.concatenate([w_first_ref[3 * (u + 1) + (v + 1)] for v in STEPS], axis=1)
        part = dot_last(moved_ref[:, 1 - u : 1 - u + height].reshape(samples * height * breadth, triple), weights)
        total = part if total is None else total + part
    out_ref[...] = total.astype(BF).reshape(out_ref.shape)


def input_conv(moved, w_first):
    samples, rows, breadth, triple = moved.shape
    shape = (samples, rows - 2, breadth, w_first.shape[1])
    return run(
        "input_conv",
        input_kernel,
        [jax.ShapeDtypeStruct(shape, BF)],
        [moved, w_first],
        flops=2 * 3 * math.prod(shape) * triple,
    )[0]


def chips_kernel(mine_ref, cross_ref, out_ref):
    _, chip = core_and_chip()
    out_ref[0] = (mine_ref[0].astype(F32) + cross_ref[0].astype(F32)).astype(BF)
    out_ref[1] = jnp.where(chip == 0, mine_ref[1], cross_ref[1])
    out_ref[2] = jnp.where(chip == 0, cross_ref[1], mine_ref[1])


def cores_kernel(mine_ref, other_ref, first_ref, second_ref):
    core, _ = core_and_chip()
    rows = mine_ref.shape[1]
    mine, other = (ref[...].astype(F32) for ref in (mine_ref, other_ref))
    for part in range(2):
        value = jnp.where(core == part, mine, other)
        first_ref[pl.ds(part, rows, stride=2), :] = value[0]
        second_ref[pl.ds(2 * rows * part, rows, stride=2), :] = value[1]
        second_ref[pl.ds(2 * rows * part + 1, rows, stride=2), :] = value[2]


def swap(array, axis, flip):
    count = lax.axis_size(axis)
    return lax.ppermute(array, axis, [(i, i ^ flip) for i in range(count)])


def around(array, axis, step, periodic=True):
    count = lax.axis_size(axis)
    pairs = [(i, (i + step) % count) for i in range(count) if periodic or 0 <= i + step < count]
    return lax.ppermute(array, axis, pairs)


def corner(array, step):
    lead, lat = lax.axis_size("lead"), lax.axis_size("lat")
    pairs = []
    for a in range(lead):
        for b in range(lat):
            target = (b ^ 1) if step is None else b + step
            if 0 <= target < lat:
                pairs.append((a * lat + b, (a ^ 2) * lat + target))
    return lax.ppermute(array, ("lead", "lat"), pairs)


def other_band(terms, columns):
    shape = (columns, terms[0].size // LANES // columns // 2, LANES)
    return run("other_band", other_band_kernel, [jax.ShapeDtypeStruct(shape, BF)], [t.reshape(2, *shape) for t in terms])[0]


def pairwise(terms, bands):
    lat = lax.axis_index("lat")
    total = sum(t.reshape(-1, LANES).astype(F32) for t in terms).astype(BF)
    left = bands
    while left > 2:
        left //= 2
        bit = (lat // left) % 2
        halves = total.reshape(2, -1, LANES)
        send = lax.dynamic_index_in_dim(halves, 1 - bit, 0, keepdims=False)
        keep = lax.dynamic_index_in_dim(halves, bit, 0, keepdims=False)
        total = (keep.astype(F32) + swap(send, "lat", left).astype(F32)).astype(BF)
    return total


def near_kernel(second_ref, first_ref, input_ref, low_ref, high_ref, slope_second, slope_first, halo_ref, wide, cells):
    samples, height, breadth, depth = second_ref.shape
    kept = breadth + 2 * EDGE
    batch = low_ref.shape[0] - samples
    for ref, width, first_cell, slope_ref in ((second_ref, 2, 0, slope_second), (first_ref, 1, 4 * height, slope_first)):
        wide[...] = jnp.zeros(wide.shape, F32)
        for s in range(samples):
            for r in range(height):
                at = (s * height + r) * kept + EDGE
                for half in range(2):
                    wide[half, at : at + breadth, :] = ref[s, r, :, half * LANES : (half + 1) * LANES].astype(F32)
            for side, packed_ref in ((0, low_ref), (1, high_ref)):
                packed = packed_ref[batch + s].astype(F32)
                for col in range(width):
                    for half in range(2):
                        here = ((col if width == 2 else 2) * 2 + half) * height
                        value = packed[here : here + height]
                        at = s * height * kept + EDGE + col + (breadth if side else -width)
                        wide[half, pl.ds(at, height, stride=kept), :] = value
                        at = first_cell + (side * width + col) * height
                        cells[s, at : at + height, half * LANES : (half + 1) * LANES] = value
        value = jnp.concatenate([wide[0], wide[1]], axis=1)
        slope_ref[...] = gelu_slope(value).reshape(slope_ref.shape)
    halo_ref[:, : cells.shape[1]] = cells[...].astype(BF)
    half = height // 2
    for part in range(2):
        values = input_ref[:, part * half : (part + 1) * half].reshape(samples, half * breadth, LANES)
        halo_ref[:, cells.shape[1] :, part * LANES : (part + 1) * LANES] = values


def near_parts(pre_second, pre_first, encoder_input, low, high):
    samples, height, breadth, depth = pre_second.shape
    kept = breadth + 2 * EDGE
    slope = jax.ShapeDtypeStruct((samples, height, kept, depth), F32)
    return run(
        "near_parts",
        near_kernel,
        [slope, slope, jax.ShapeDtypeStruct((samples, 6 * height + height * breadth // 2, depth), BF)],
        [pre_second, pre_first, encoder_input, low, high],
        [pltpu.VMEM((2, samples * height * kept, LANES), F32), pltpu.VMEM((samples, 6 * height, depth), F32)],
    )


def far_kernel(first_ref, tile_second, tile_first, slope_second, slope_first, act_out, wide, act):
    samples, height, breadth, depth = first_ref.shape
    kept = breadth + 2 * EDGE
    lat = lax.axis_index("lat")
    for source_ref, slope_ref in ((tile_second, slope_second), (tile_first, slope_first)):
        wide[...] = jnp.zeros(wide.shape, F32)
        for s in range(samples):
            for half in range(2):
                for r in range(height):
                    at = (s * height + r) * kept + EDGE
                    wide[half, at : at + breadth, :] = source_ref[s, r, :, half * LANES : (half + 1) * LANES].astype(F32)
        value = jnp.concatenate([wide[0], wide[1]], axis=1)
        slope_ref[...] = gelu_slope(value).reshape(slope_ref.shape)
    own, other = pl.ds(height * lat, height), pl.ds(height * (1 - lat), height)
    act[:, own] = gelu_value(first_ref[...].astype(F32))
    act[:, other] = gelu_value(tile_first[...].astype(F32))
    act_out[...] = act[...].reshape(act_out.shape[1], depth).T.astype(BF)


def far_parts(pre_first, tile_second, tile_first):
    samples, height, breadth, depth = pre_first.shape
    kept = breadth + 2 * EDGE
    slope = jax.ShapeDtypeStruct((samples, height, kept, depth), F32)
    return run(
        "far_parts",
        far_kernel,
        [slope, slope, jax.ShapeDtypeStruct((depth, 2 * samples * height * breadth), BF)],
        [pre_first, tile_second, tile_first],
        [
            pltpu.VMEM((2, samples * height * kept, LANES), F32),
            pltpu.VMEM((samples, 2 * height, breadth, depth), F32),
        ],
    )


def put_slopes(sample, slope, near_ref, far_ref, halo_ref, width, first_cell):
    _, height, kept, _ = near_ref.shape
    lat = lax.axis_index("lat")
    other = pl.ds(height * (1 - lat), height)
    slope[pl.ds(height * lat, height)] = near_ref[sample]
    slope[other] = far_ref[sample]
    beside = gelu_slope(halo_ref[sample, : 6 * height].astype(F32))
    for side in range(2):
        for col in range(width):
            here = first_cell + (side * width + col) * height
            at = kept - EDGE + col if side else EDGE - width + col
            slope[other, at, :] = beside[here : here + height]


def globe_kernel(sample, near_ref, far_ref, halo_ref, total_ref, line_ref, cat_ref, moved_ref, latent, slope, wide):
    rows, kept, depth = total_ref.shape
    height = rows - 1
    tall = 2 * height
    breadth = kept - 2 * EDGE
    lat = lax.axis_index("lat")
    own = 8 + EDGE
    latent[...] = jnp.zeros(latent.shape, F32)
    latent[pl.ds((height - 1) * lat, rows)] = total_ref[...].astype(F32)
    latent[pl.ds((height - 1) * (1 - lat), rows)] += line_ref[...].astype(F32)
    put_slopes(sample, slope, near_ref, far_ref, halo_ref, 2, 0)
    wide[:, 8 : 8 + kept, :] = (latent[...] * slope[...]).astype(BF).astype(F32)
    for v in STEPS:
        lanes = slice((v + 1) * depth, (v + 2) * depth)
        cat_ref[1 : 1 + tall, :, lanes] = wide[:, 8 - v : 8 - v + kept, :].astype(BF)
        moved_ref[v + 1, 1 : 1 + tall] = wide[:, own - v : own - v + breadth, :].astype(BF)
    for row in (0, tall + 1):
        cat_ref[row] = jnp.zeros(cat_ref.shape[1:], BF)
        moved_ref[:, row] = jnp.zeros(moved_ref.shape[:1] + moved_ref.shape[2:], BF)


def globe(sample, total, line, near, far, halo):
    rows, kept, depth = total.shape
    tall, breadth = 2 * (rows - 1), kept - 2 * EDGE
    return run(
        "latent_grads",
        functools.partial(globe_kernel, sample),
        [
            jax.ShapeDtypeStruct((tall + 2, kept, 3 * depth), BF),
            jax.ShapeDtypeStruct((3, tall + 2, breadth, depth), BF),
        ],
        [near, far, halo, total, line],
        [
            pltpu.VMEM((tall, kept, depth), F32),
            pltpu.VMEM((tall, kept, depth), F32),
            pltpu.VMEM((tall, kept + 24, depth), F32),
        ],
    )


def band_rows(norm_factor, lefts, moved, mine_ref, other_ref):
    channels, cells = lefts[0].shape
    _, padded, breadth, depth = moved[0].shape
    tall = padded - 2
    lat = lax.axis_index("lat")
    core, _ = core_and_chip()
    half = channels // 2

    def put(parts, u, v, start, size):
        total = None
        for left, ref in zip(parts, moved):
            part = dot_plain(left, ref[v + 1, pl.ds(1 - u, tall)].reshape(cells, depth))
            total = part if total is None else total + part
        total = total * norm_factor
        lower, upper = total[:, :LANES], total[:, LANES:]
        here = pl.ds(pl.multiple_of(start, half), size)
        mine_ref[here, :] = jnp.where(core == 0, lower, upper).astype(BF)
        other_ref[here, :] = jnp.where(core == 0, upper, lower).astype(BF)

    for j in range(4):
        (u0, v0), (u1, v1) = (divmod(k, 3) for k in (j, 5 + j))
        put(lefts, u0 - 1 + lat * (u1 - u0), v0 - 1 + lat * (v1 - v0), lat * half + j * channels, channels)
    put([jnp.where(lat == 0, left[:half], left[half:]) for left in lefts], 0, 0, (1 - lat) * 4 * channels, half)


def second_band_kernel(norm_factor, act_ref, *refs):
    moved, (mine_ref, other_ref) = refs[:-2], refs[-2:]
    cells = act_ref.shape[1] // len(moved)
    lefts = [act_ref[:, s * cells : (s + 1) * cells] for s in range(len(moved))]
    band_rows(norm_factor, lefts, moved, mine_ref, other_ref)


def second_band(norm_factor, act, moved):
    half = jax.ShapeDtypeStruct((9 * act.shape[0] // 2, LANES), BF)
    return run("second_weight_grads", functools.partial(second_band_kernel, norm_factor), [half, half], [act, *moved])


def first_kernel(sample, cat_ref, near_ref, far_ref, halo_ref, weights_ref, moved_ref, slope, wide):
    padded, kept, triple = cat_ref.shape
    tall, depth = padded - 2, triple // 3
    breadth = kept - 2 * EDGE
    own = 8 + EDGE
    put_slopes(sample, slope, near_ref, far_ref, halo_ref, 1, 2 * tall)
    linear = None
    for u in STEPS:
        weights = jnp.concatenate([weights_ref[3 * (u + 1) + (v + 1)] for v in STEPS], axis=1)
        part = dot_last(cat_ref[1 - u : 1 - u + tall].reshape(tall * kept, triple), weights)
        linear = part if linear is None else linear + part
    wide[:, 8 : 8 + kept, :] = (linear.reshape(tall, kept, depth) * slope[...]).astype(BF).astype(F32)
    for v in STEPS:
        moved_ref[v + 1, 1 : 1 + tall] = wide[:, own - v : own - v + breadth, :].astype(BF)
    for row in (0, tall + 1):
        moved_ref[:, row] = jnp.zeros(moved_ref.shape[:1] + moved_ref.shape[2:], BF)


def first_grad(sample, cat, near, far, halo, w_second):
    padded, kept, triple = cat.shape
    tall, depth = padded - 2, triple // 3
    return run(
        "second_conv",
        functools.partial(first_kernel, sample),
        [jax.ShapeDtypeStruct((3, padded, kept - 2 * EDGE, depth), BF)],
        [cat, near, far, halo, w_second],
        [pltpu.VMEM((tall, kept, depth), F32), pltpu.VMEM((tall, kept + 16, depth), F32)],
    )[0]


def first_band_kernel(norm_factor, halo_ref, input_ref, *refs):
    moved, (mine_ref, other_ref, cells) = refs[:-3], refs[-3:]
    samples, height, breadth, channels = input_ref.shape
    lat = lax.axis_index("lat")
    cells[:, pl.ds(height * lat, height)] = input_ref[...].astype(F32)
    half = height // 2
    for part in range(2):
        values = halo_ref[:, 6 * height :, part * LANES : (part + 1) * LANES].astype(F32)
        cells[:, pl.ds(height * (1 - lat) + part * half, half)] = values.reshape(samples, half, breadth, LANES)
    lefts = [cells[s].reshape(2 * height * breadth, channels).T.astype(BF) for s in range(samples)]
    band_rows(norm_factor, lefts, moved, mine_ref, other_ref)


def first_band(norm_factor, halo, encoder_input, moved):
    samples, height, breadth, channels = encoder_input.shape
    half = jax.ShapeDtypeStruct((9 * channels // 2, LANES), BF)
    return run(
        "first_weight_grads",
        functools.partial(first_band_kernel, norm_factor),
        [half, half],
        [halo, encoder_input, *moved],
        [pltpu.VMEM((samples, 2 * height, breadth, channels), F32)],
    )


def input_band_kernel(w_first_ref, *refs):
    moved, out_ref = refs[:-1], refs[-1]
    _, height, breadth, channels = out_ref.shape
    depth = moved[0].shape[3]
    lat = lax.axis_index("lat")
    total = None
    for u in STEPS:
        weights = jnp.concatenate([w_first_ref[3 * (u + 1) + (v + 1)] for v in STEPS], axis=1)
        here = pl.ds(height * lat + 1 - u, height)
        left = [jnp.concatenate([ref[v + 1, here].reshape(-1, depth) for v in STEPS], axis=1) for ref in moved]
        part = dot_last(jnp.concatenate(left, axis=0), weights)
        total = part if total is None else total + part
    out_ref[...] = total.astype(BF).reshape(out_ref.shape)


def blocks_kernel(first_mine, first_got, second_mine, second_got, *outs):
    lon = lax.axis_index("lon")
    rows = first_mine.shape[1]
    for step, out_ref in enumerate(outs):
        block = partner(lon, step, len(outs))
        out_ref[:rows] = (first_mine[block].astype(F32) + first_got[block].astype(F32)).astype(BF)
        out_ref[rows:] = (second_mine[block].astype(F32) + second_got[block].astype(F32)).astype(BF)


def halves_kernel(mine_ref, other_ref, first_ref, second_ref):
    core, _ = core_and_chip()
    mine, other = mine_ref[...].astype(F32), other_ref[...].astype(F32)
    rows = mine.shape[0] // 3
    for part in range(2):
        value = jnp.where(core == part, mine, other)
        first_ref[pl.ds(part, rows, stride=2), :] = value[:rows]
        second_ref[pl.ds(part, 2 * rows, stride=2), :] = value[rows:]


def to_partner(array, step):
    count = lax.axis_size("lon")
    return lax.ppermute(array, "lon", [(partner(i, step, count), i) for i in range(count)])


def two_bands(head_grads, head_weights, encoder_input, pre_first, pre_second, w_first, w_second, norm_factor):
    samples, height, breadth, _ = encoder_input.shape
    columns = lax.axis_size("lon")
    tiles = [swap(array, "lat", 1) for array in (pre_second, pre_first)]
    to_right, to_left = pack(head_grads, pre_second, pre_first)
    low = around(to_right, "lon", 1)
    high = around(to_left, "lon", -1)
    head_grads, head_weights, w_second, pre_second, pre_first, encoder_input = stage(
        head_grads, head_weights, w_second, pre_second, pre_first, encoder_input
    )
    inside = inside_conv(head_grads, head_weights, 2 * samples)
    low, high, inside, *tiles = lax.optimization_barrier((low, high, inside, *tiles))
    heads_of = functools.partial(
        head_conv,
        head_grads=head_grads,
        low=low,
        high=high,
        head_weights=head_weights,
        slots=2 * samples,
        rows=height + 1,
    )
    everyone = range(samples)
    got = swap(edges_conv(inside, low, high, head_weights), "lead", 1)
    part_shape = jax.ShapeDtypeStruct(got.shape[1:], BF)
    parts = run("core_sum", core_sum_kernel, [part_shape] * (2 * samples), [heads_of(False, False, 0), got])
    own, cross = parts[0::2], list(parts[1::2])
    near_second, near_first, halo = near_parts(pre_second, pre_first, encoder_input, low, high)
    cross[-1], halo = lax.optimization_barrier((cross[-1], halo))
    cross = [swap(part, "lead", 2) for part in cross]
    halo = swap(halo, "lat", 1)
    cross[-1], halo = lax.optimization_barrier((cross[-1], halo))
    totals = [run("chip_sum", sum_kernel, [part_shape], [own[s], cross[s]])[0] for s in everyone]
    lines = [swap(total, "lat", 1) for total in totals]
    far_second, far_first, act = far_parts(pre_first, *tiles)

    moved_second, moved_first = [], []
    for s in everyone:
        cat, moved = globe(s, totals[s], lines[s], near_second, far_second, halo)
        moved_second.append(moved)
        if s < samples - 1:
            moved_first.append(first_grad(s, cat, near_first, far_first, halo, w_second))
            near_second, moved_first[s] = lax.optimization_barrier((near_second, moved_first[s]))
    second_mine, second_other = second_band(norm_factor, act, moved_second)
    second_got = swap(second_other, "lead", 1)
    moved_first.append(first_grad(samples - 1, cat, near_first, far_first, halo, w_second))
    first_mine, first_other = first_band(norm_factor, halo, encoder_input, moved_first)
    first_got = swap(first_other, "lead", 1)
    input_grad = run(
        "input_conv", input_band_kernel, [jax.ShapeDtypeStruct(encoder_input.shape, BF)], [w_first, *moved_first]
    )[0]

    blocks = [t.reshape(columns, -1, LANES) for t in (first_mine, first_got, second_mine, second_got)]
    rows = blocks[0].shape[1]
    share_shape = jax.ShapeDtypeStruct((3 * rows, LANES), BF)
    shares = run("blocks", blocks_kernel, [share_shape] * columns, blocks)
    parts = [to_partner(shares[step], step) for step in ((2, 1, 3) if columns == 4 else range(1, columns))]
    share = run("share", sum_kernel, [share_shape], [shares[0], *parts])[0]
    both = run("chips", sum_kernel, [share_shape], [share, swap(share, "lead", 2)])[0]
    result_first, result_second = run(
        "cores",
        halves_kernel,
        [jax.ShapeDtypeStruct((2 * rows, LANES), F32), jax.ShapeDtypeStruct((4 * rows, LANES), F32)],
        [both, swap(both, "lead", 1)],
    )
    return input_grad, result_first.reshape(-1), result_second.reshape(-1)


def core_sum_kernel(mine_ref, got_ref, *outs):
    for slot, out_ref in enumerate(outs):
        out_ref[...] = (mine_ref[slot].astype(F32) + got_ref[slot].astype(F32)).astype(BF)


def general(head_grads, head_weights, encoder_input, pre_first, pre_second, w_first, w_second, norm_factor):
    samples, height, breadth, _ = encoder_input.shape
    bands, columns = lax.axis_size("lat"), lax.axis_size("lon")
    to_right, to_left = pack(head_grads, pre_second, pre_first)
    to_right, to_left, to_cross = lax.optimization_barrier((to_right, to_left, pre_first))
    low = around(to_right, "lon", 1)
    high = around(to_left, "lon", -1)
    act_got = activated(swap(to_cross, "lead", 2))
    head_grads, head_weights, w_second, pre_second, pre_first, encoder_input = stage(
        head_grads, head_weights, w_second, pre_second, pre_first, encoder_input
    )
    low, high, act_got = lax.optimization_barrier((low, high, act_got))

    steps = [1, -1]
    heads_of = functools.partial(head_conv, head_grads=head_grads, high=high, head_weights=head_weights, slots=samples, rows=height + 2)
    got_cross = swap(heads_of(True, True, None, low=low), "lead", 1)
    got_own = swap(heads_of(True, False, None, low=low), "lead", 1)
    cross, *angles = spread_cross(heads_of(False, True, None, low=low), got_cross, len(steps))
    low_later, cross, *angles = lax.optimization_barrier((low, cross, *angles))
    cross = swap(cross, "lead", 2)
    angles = [corner(angle, step) for angle, step in zip(angles, steps)]
    second, first, slope_second, slope_first, act, cells_in = saved(pre_second, pre_first, encoder_input, low, high)
    own, *lines = spread_own(heads_of(False, False, None, low=low_later), got_own, second, first, len(steps))
    lines = [swap(line, "lat", 1) if step is None else around(line, "lat", step, False) for line, step in zip(lines, steps)]
    strips = [strip for pair in zip(lines, angles) for strip in pair]

    grad, away, slope = latent_grads(len(steps), bands, own, cross, strips, slope_second, slope_first)
    grad_got = swap(away, "lead", 2)
    moved, first_mine, first_other = encoder(norm_factor, bands, grad, slope, cells_in, w_second)
    input_grad = input_conv(moved, w_first)
    first_got = swap(first_other, "lead", 1)
    second_mine, second_other = second_grads(norm_factor, bands * columns, grad, grad_got, act, act_got)
    second_got = swap(second_other, "lead", 1)

    first_terms = [pairwise([first_mine, first_got], bands)]
    second_terms = [pairwise([second_mine, second_got], bands)]
    first_came = swap(other_band(first_terms, columns), "lat", 1)
    second_came = swap(other_band(second_terms, columns), "lat", 1)
    blocks = [t.reshape(2, columns, -1, LANES) for t in first_terms + second_terms]
    rows = blocks[0].shape[2]
    share_shape = jax.ShapeDtypeStruct((2, rows, LANES), BF)
    shares = run("own_band", own_band_kernel, [share_shape] * columns, blocks + [first_came, second_came])
    parts = [to_partner(shares[step], step) for step in ((2, 1, 3) if columns == 4 else range(1, columns))]
    share = run("share", sum_kernel, [share_shape], [shares[0], *parts])[0]
    both = run("chips", chips_kernel, [jax.ShapeDtypeStruct((3, rows, LANES), BF)], [share, swap(share, "lead", 2)])[0]
    result_first, result_second = run(
        "cores",
        cores_kernel,
        [jax.ShapeDtypeStruct((2 * rows, LANES), F32), jax.ShapeDtypeStruct((4 * rows, LANES), F32)],
        [both, swap(both, "lead", 1)],
    )
    return input_grad, result_first.reshape(-1), result_second.reshape(-1)


def per_device(head_grads, head_weights, encoder_input, pre_first, pre_second, w_first, w_second):
    samples, height, breadth, channels = encoder_input.shape
    bands, columns = lax.axis_size("lat"), lax.axis_size("lon")
    cells_total = samples * lax.axis_size("lead") * height * bands * breadth * columns
    norm_factor = 1.0 / math.sqrt(cells_total)
    plan = two_bands if bands == 2 and 9 * channels // (bands * columns) % 16 == 0 else general
    return plan(head_grads, head_weights, encoder_input, pre_first, pre_second, w_first, w_second, norm_factor)


def solution(mesh):
    in_specs = (
        P("lead", None, "lat", "lon", None),
        P("lead", None, None, None),
        P("lead", "lat", "lon", None),
        P("lead", "lat", "lon", None),
        P("lead", "lat", "lon", None),
        P(),
        P(),
    )
    out_specs = (P("lead", "lat", "lon", None), P(("lat", "lon")), P(("lat", "lon")))
    return jax.shard_map(
        per_device, mesh=mesh, in_specs=in_specs, out_specs=out_specs, check_vma=False
    )
```

```python
import functools
import math

import jax
import jax.numpy as jnp
from jax import lax
from jax.experimental import pallas as pl
from jax.experimental.pallas import tpu as pltpu
from jax.sharding import PartitionSpec as P

BF = jnp.bfloat16
F32 = jnp.float32
STEPS = (-1, 0, 1)
EDGE = 4
LANES = 128
VMEM_BYTES = 24 * 1024 * 1024


def erf_part(values):
    return 0.5 * (1.0 + lax.erf(values * 0.7071067811865476))


def gelu_slope(values):
    return erf_part(values) + values * jnp.exp(-0.5 * values * values) * 0.3989422804014327


def gelu_value(values):
    return values * erf_part(values)


def dot_last(left, right):
    return lax.dot_general(left, right, (((1,), (1,)), ((), ())), preferred_element_type=F32)


def dot_plain(left, right):
    return lax.dot_general(left, right, (((1,), (0,)), ((), ())), preferred_element_type=F32)


def core_and_chip():
    lead = lax.axis_index("lead")
    return lax.rem(lead, 2), lax.div(lead, 2)


def run(name, kernel, out_shape, arrays, scratch=(), flops=0, far=False):
    specs = [pl.BlockSpec(memory_space=pltpu.HBM if far else pltpu.VMEM)] * len(arrays)
    if far:
        arrays = [pltpu.with_memory_space_constraint(a, pltpu.HBM) for a in arrays]
    touched = sum(a.size * a.dtype.itemsize for a in arrays)
    touched += sum(math.prod(s.shape) * s.dtype.itemsize for s in out_shape)
    return pl.pallas_call(
        kernel,
        name=name,
        out_shape=out_shape,
        in_specs=specs,
        out_specs=[pl.BlockSpec(memory_space=pltpu.VMEM)] * len(out_shape),
        scratch_shapes=list(scratch),
        compiler_params=pltpu.CompilerParams(vmem_limit_bytes=VMEM_BYTES),
        cost_estimate=pl.CostEstimate(flops=1, bytes_accessed=1, transcendentals=0),
    )(*arrays)


def pack_kernel(with_tile, grads_far, second_far, first_far, right_ref, left_ref, *refs):
    grads_near, second_near, first_near, edges, edges_wide, packed, sems, tile_sems = refs[-8:]
    heads, batch, height, breadth, _ = grads_far.shape
    samples = second_far.shape[0]
    rows = 6 * height
    copies = []
    for side in range(2):
        columns = pl.ds(breadth - 16 if side == 0 else 0, 16)
        for j, (far, near) in enumerate(((grads_far, grads_near), (second_far, second_near), (first_far, first_near))):
            source = far.at[:, :, :, columns, :] if j == 0 else far.at[:, :, columns, :]
            copies.append(pltpu.make_async_copy(source, near.at[side], sems.at[side, j]))
            copies[-1].start()
    tile_copies = []
    if with_tile:
        for j, far in enumerate((second_far, first_far)):
            tile_copies.append(pltpu.make_async_copy(far, refs[0].at[j], tile_sems.at[j]))
            tile_copies[-1].start()
    for copy in copies:
        copy.wait()
    for side, out_ref in ((0, right_ref), (1, left_ref)):
        start = 8 if side == 0 else 0
        grads_ref, second_ref, first_ref = grads_near.at[side], second_near.at[side], first_near.at[side]
        for h in range(heads):
            for b in range(batch):
                block = grads_ref[h, b].astype(F32)[:, start : start + 8, :]
                edges[(h * batch + b) * height * 8 : (h * batch + b + 1) * height * 8, :] = block.reshape(height * 8, LANES)
        for j, ref in enumerate((second_ref, first_ref)):
            for s in range(samples):
                block = ref[s].astype(F32)[:, start : start + 8, :]
                at = (j * samples + s) * height * 8
                for half in range(2):
                    lanes = slice(half * LANES, (half + 1) * LANES)
                    edges_wide[half, at : at + height * 8, :] = block[:, :, lanes].reshape(height * 8, LANES)
        for b in range(batch):
            for col in range(3):
                inner = 5 + col if side == 0 else col
                for h in range(heads):
                    at = b * rows + (col * 2 + h) * height
                    packed[at : at + height, :] = edges[pl.ds((h * batch + b) * height * 8 + inner, height, stride=8), :]
        for s in range(samples):
            for q in range(3):
                j, col, width = (0, q, 2) if q < 2 else (1, 0, 1)
                inner = 8 - width + col if side == 0 else col
                for half in range(2):
                    at = (batch + s) * rows + (q * 2 + half) * height
                    packed[at : at + height, :] = edges_wide[
                        half, pl.ds((j * samples + s) * height * 8 + inner, height, stride=8), :
                    ]
        out_ref[...] = packed[: (batch + samples) * rows].astype(BF).reshape(out_ref.shape)
    for copy in tile_copies:
        copy.wait()


def pack(head_grads, pre_second, pre_first, with_tile):
    heads, batch, height, _, _ = head_grads.shape
    samples = pre_second.shape[0]
    shape = jax.ShapeDtypeStruct((batch + samples, 6 * height, LANES), BF)
    return run(
        "pack_columns",
        functools.partial(pack_kernel, with_tile),
        [shape, shape] + [jax.ShapeDtypeStruct((2,) + pre_second.shape, BF)] * with_tile,
        [head_grads, pre_second, pre_first],
        [
            pltpu.VMEM((2, heads, batch, height, 16, LANES), BF),
            pltpu.VMEM((2, samples, height, 16, 2 * LANES), BF),
            pltpu.VMEM((2, samples, height, 16, 2 * LANES), BF),
            pltpu.VMEM((heads * batch * height * 8 + 64, LANES), F32),
            pltpu.VMEM((2, 2 * samples * height * 8 + 64, LANES), F32),
            pltpu.VMEM(((batch + samples) * 6 * height + 16, LANES), F32),
            pltpu.SemaphoreType.DMA((2, 3)),
            pltpu.SemaphoreType.DMA((2,)),
        ],
        far=True,
    )


def stage_kernel(*refs):
    count = len(refs) // 2
    sems = refs[-1]
    copies = [pltpu.make_async_copy(refs[i], refs[count + i], sems.at[i]) for i in range(count)]
    for copy in copies:
        copy.start()
    for copy in copies:
        copy.wait()


def stage(*arrays):
    shapes = [pltpu.VMEM(a.shape, a.dtype) for a in arrays]
    return run("stage", stage_kernel, shapes, list(arrays), [pltpu.SemaphoreType.DMA((len(arrays),))], far=True, flops=1 << 30)


def heads_kernel(other_core, other_chip, sample, samples, grads_ref, low_ref, high_ref, weights_ref, out_ref, wide, shifted, total):
    heads, batch, height, breadth, _ = grads_ref.shape
    slots, _, kept, depth = out_ref.shape
    pitch = kept + 16
    own = 8 + EDGE
    core, chip = core_and_chip()
    core = 1 - core if other_core else core
    for slot in range(slots):
        if sample is None:
            group, s = 1 - chip if other_chip else chip, slot
        else:
            group, s = 1 - chip if slot % 2 else chip, sample + slot // 2
        b = (2 * group + core) * samples + s
        low = low_ref[b].astype(F32)
        high = high_ref[b].astype(F32)
        for r in range(height):
            at = (slot * height + r) * pitch + own
            for h in range(heads):
                wide[h, at : at + breadth, :] = grads_ref[h, b, r].astype(F32)
        for col in range(3):
            for h in range(heads):
                here = (col * 2 + h) * height
                at = slot * height * pitch + own + col
                wide[h, pl.ds(at - 3, height, stride=pitch), :] = low[here : here + height]
                wide[h, pl.ds(at + breadth, height, stride=pitch), :] = high[here : here + height]
        for v in STEPS:
            for h in range(heads):
                starts = [(slot * height + r) * pitch + 8 - v for r in range(height)]
                moved = jnp.concatenate([wide[h, at : at + kept, :] for at in starts], axis=0).astype(BF)
                lane = ((v + 1) * heads + h) * LANES
                shifted[slot * height * kept : (slot + 1) * height * kept, lane : lane + LANES] = moved
    total[:, height:, :, :] = jnp.zeros((slots, 2, kept, depth), F32)
    for u in STEPS:
        weights = jnp.concatenate(
            [weights_ref[h, 3 * (u + 1) + (v + 1)] for v in STEPS for h in range(heads)], axis=1
        )
        part = dot_last(shifted[...], weights).reshape(slots, height, kept, depth)
        if u == -1:
            total[:, :height] = part
        else:
            total[:, 1 + u : 1 + u + height] += part
    if out_ref.shape[1] == height + 2:
        out_ref[...] = total[...].astype(BF)
    else:
        out_ref[...] = total[:, pl.ds(1 - lax.axis_index("lat"), height + 1)].astype(BF)


def head_conv(other_core, other_chip, sample, head_grads, low, high, head_weights, slots, rows):
    samples = head_grads.shape[1] // lax.axis_size("lead")
    heads, batch, height, breadth, _ = head_grads.shape
    depth = head_weights.shape[2]
    kept = breadth + 2 * EDGE
    return run(
        "head_conv",
        functools.partial(heads_kernel, other_core, other_chip, sample, samples),
        [jax.ShapeDtypeStruct((slots, rows, kept, depth), BF)],
        [head_grads, low, high, head_weights],
        [
            pltpu.VMEM((heads, (slots * height + 8) * (kept + 16), LANES), F32),
            pltpu.VMEM((slots * height * kept, 3 * heads * LANES), BF),
            pltpu.VMEM((slots, height + 2, kept, depth), F32),
        ],
        flops=2 * slots * height * kept * 9 * heads * LANES * depth,
    )[0]


def inside_kernel(samples, grads_ref, weights_ref, total_ref, wide, shifted):
    heads, _, height, breadth, _ = grads_ref.shape
    slots, _, kept, depth = total_ref.shape
    pitch = kept + 16
    own = 8 + EDGE
    core, chip = core_and_chip()
    blank = jnp.zeros((height, LANES), F32)
    for slot in range(slots):
        group, s = 1 - chip if slot % 2 else chip, slot // 2
        b = (2 * group + 1 - core) * samples + s
        for h in range(heads):
            for r in range(height):
                at = (slot * height + r) * pitch + own
                wide[h, at : at + breadth, :] = grads_ref[h, b, r].astype(F32)
            for col in range(3):
                at = slot * height * pitch + own + col
                wide[h, pl.ds(at - 3, height, stride=pitch), :] = blank
                wide[h, pl.ds(at + breadth, height, stride=pitch), :] = blank
            for v in STEPS:
                starts = [(slot * height + r) * pitch + 8 - v for r in range(height)]
                moved = jnp.concatenate([wide[h, at : at + kept, :] for at in starts], axis=0).astype(BF)
                lane = ((v + 1) * heads + h) * LANES
                shifted[slot * height * kept : (slot + 1) * height * kept, lane : lane + LANES] = moved
    total_ref[:, height:, :, :] = jnp.zeros((slots, 2, kept, depth), F32)
    for u in STEPS:
        weights = jnp.concatenate(
            [weights_ref[h, 3 * (u + 1) + (v + 1)] for v in STEPS for h in range(heads)], axis=1
        )
        part = dot_last(shifted[...], weights).reshape(slots, height, kept, depth)
        if u == -1:
            total_ref[:, :height] = part
        else:
            total_ref[:, 1 + u : 1 + u + height] += part


def edges_kernel(samples, inside_ref, low_ref, high_ref, weights_ref, out_ref, wide, shifted, total):
    slots, rows, kept, depth = inside_ref.shape
    height, heads, pitch = rows - 2, weights_ref.shape[0], 24
    core, chip = core_and_chip()
    wide[...] = jnp.zeros(wide.shape, F32)
    total[...] = inside_ref[...]
    for side, packed_ref in ((0, low_ref), (1, high_ref)):
        for slot in range(slots):
            group, s = 1 - chip if slot % 2 else chip, slot // 2
            packed = packed_ref[(2 * group + 1 - core) * samples + s].astype(F32)
            first = (side * slots + slot) * height
            for h in range(heads):
                for col in range(3):
                    here = (col * 2 + h) * height
                    at = first * pitch + 9 + 3 * side + col
                    wide[h, pl.ds(at, height, stride=pitch), :] = packed[here : here + height]
                for v in STEPS:
                    starts = [(first + r) * pitch + 8 - v for r in range(height)]
                    moved = jnp.concatenate([wide[h, at : at + 8, :] for at in starts], axis=0).astype(BF)
                    lane = ((v + 1) * heads + h) * LANES
                    shifted[first * 8 : (first + height) * 8, lane : lane + LANES] = moved
    for u in STEPS:
        weights = jnp.concatenate(
            [weights_ref[h, 3 * (u + 1) + (v + 1)] for v in STEPS for h in range(heads)], axis=1
        )
        part = dot_last(shifted[...], weights).reshape(2, slots, height, 8, depth)
        total[:, 1 + u : 1 + u + height, :8] += part[0]
        total[:, 1 + u : 1 + u + height, kept - 8 :] += part[1]
    out_ref[...] = total[:, pl.ds(1 - lax.axis_index("lat"), height + 1)].astype(BF)


def inside_conv(head_grads, head_weights, slots):
    samples = head_grads.shape[1] // lax.axis_size("lead")
    heads, _, height, breadth, _ = head_grads.shape
    kept = breadth + 2 * EDGE
    return run(
        "head_conv_inside",
        functools.partial(inside_kernel, samples),
        [jax.ShapeDtypeStruct((slots, height + 2, kept, head_weights.shape[2]), F32)],
        [head_grads, head_weights],
        [
            pltpu.VMEM((heads, (slots * height + 8) * (kept + 16), LANES), F32),
            pltpu.VMEM((slots * height * kept, 3 * heads * LANES), BF),
        ],
    )[0]


def edges_conv(inside, low, high, head_weights):
    slots, rows, kept, depth = inside.shape
    samples, heads, height = slots // 2, head_weights.shape[0], rows - 2
    return run(
        "head_conv_edges",
        functools.partial(edges_kernel, samples),
        [jax.ShapeDtypeStruct((slots, rows - 1, kept, depth), BF)],
        [inside, low, high, head_weights],
        [
            pltpu.VMEM((heads, (2 * slots * height + 8) * 24, LANES), F32),
            pltpu.VMEM((2 * slots * height * 8, 3 * heads * LANES), BF),
            pltpu.VMEM((slots, rows, kept, depth), F32),
        ],
    )[0]


def saved_kernel(second_ref, first_ref, input_ref, low_ref, high_ref, second_out, first_out, slope_second, slope_first, act_out, input_out, wide):
    samples, height, breadth, depth = second_ref.shape
    kept = breadth + 2 * EDGE
    batch = low_ref.shape[0] - samples
    for ref, width, out_ref, slope_ref in (
        (second_ref, 2, second_out, slope_second),
        (first_ref, 1, first_out, slope_first),
    ):
        wide[...] = jnp.zeros(wide.shape, F32)
        for s in range(samples):
            for r in range(height):
                at = (s * height + r) * kept + EDGE
                for half in range(2):
                    lanes = slice(half * LANES, (half + 1) * LANES)
                    wide[half, at : at + breadth, :] = ref[s, r, :, lanes].astype(F32)
            low = low_ref[batch + s].astype(F32)
            high = high_ref[batch + s].astype(F32)
            for col in range(width):
                for half in range(2):
                    here = ((col if width == 2 else 2) * 2 + half) * height
                    at = s * height * kept + EDGE + col
                    wide[half, pl.ds(at - width, height, stride=kept), :] = low[here : here + height]
                    wide[half, pl.ds(at + breadth, height, stride=kept), :] = high[here : here + height]
        value = jnp.concatenate([wide[half, : samples * height * kept] for half in range(2)], axis=1)
        out_ref[...] = value.astype(BF).reshape(out_ref.shape)
        slope_ref[...] = gelu_slope(value).reshape(slope_ref.shape)
    active = gelu_value(first_ref[...].astype(F32).reshape(samples * height * breadth, depth)).astype(BF).astype(F32)
    act_out[...] = active.T.astype(BF)
    cells = input_ref[...].astype(F32).reshape(samples * height * breadth, input_ref.shape[3])
    input_out[...] = cells.T.astype(BF)


def saved(pre_second, pre_first, encoder_input, low, high):
    samples, height, breadth, depth = pre_second.shape
    kept = breadth + 2 * EDGE
    cells = samples * height * breadth
    return run(
        "saved_parts",
        saved_kernel,
        [
            jax.ShapeDtypeStruct((samples, height, kept, depth), BF),
            jax.ShapeDtypeStruct((samples, height, kept, depth), BF),
            jax.ShapeDtypeStruct((samples, height, kept, depth), F32),
            jax.ShapeDtypeStruct((samples, height, kept, depth), F32),
            jax.ShapeDtypeStruct((depth, cells), BF),
            jax.ShapeDtypeStruct((encoder_input.shape[3], cells), BF),
        ],
        [pre_second, pre_first, encoder_input, low, high],
        [pltpu.VMEM((2, (samples * height + 8) * kept, LANES), F32)],
    )


def goes_down(way, ways):
    return 1 - lax.axis_index("lat") if ways == 1 else 1 - way


def cross_kernel(mine_ref, got_ref, cross_ref, *strips):
    height = mine_ref.shape[1] - 2
    cross_ref[...] = (mine_ref[...].astype(F32) + got_ref[...].astype(F32)).astype(BF)
    for way, corner_ref in enumerate(strips):
        corner_ref[...] = cross_ref[:, pl.ds((height - 1) * goes_down(way, len(strips)), 3)]


def own_kernel(mine_ref, got_ref, second_ref, first_ref, own_ref, *strips):
    height = second_ref.shape[1]
    own_ref[...] = (mine_ref[...].astype(F32) + got_ref[...].astype(F32)).astype(BF)
    for way, line_ref in enumerate(strips):
        down = goes_down(way, len(strips))
        line_ref[:, 0:3] = own_ref[:, pl.ds((height - 1) * down, 3)]
        line_ref[:, 3:5] = second_ref[:, pl.ds((height - 2) * down, 2)]
        line_ref[:, 5:6] = first_ref[:, pl.ds((height - 1) * down, 1)]


def spread_cross(mine, got, ways):
    samples, _, kept, depth = mine.shape
    strip = jax.ShapeDtypeStruct((samples, 3, kept, depth), BF)
    return run("core_sum_cross", cross_kernel, [jax.ShapeDtypeStruct(mine.shape, BF)] + [strip] * ways, [mine, got])


def spread_own(mine, got, second, first, ways):
    samples, _, kept, depth = mine.shape
    strip = jax.ShapeDtypeStruct((samples, 6, kept, depth), BF)
    return run("core_sum_own", own_kernel, [jax.ShapeDtypeStruct(mine.shape, BF)] + [strip] * ways, [mine, got, second, first])


def latent_kernel(ways, bands, own_ref, cross_ref, *refs):
    strips, refs = refs[: 2 * ways], refs[2 * ways :]
    slope_second_ref, slope_first_ref, grad_ref, away_ref, slope_out, latent, slope_second = refs
    samples, rows, kept, depth = own_ref.shape
    height = rows - 2
    lat = lax.axis_index("lat")
    _, chip = core_and_chip()
    blank = jnp.zeros((samples, kept, depth), F32)
    latent[:, 0] = blank
    latent[:, height + 3] = blank
    latent[:, 1 : height + 3] = own_ref[...].astype(F32) + cross_ref[...].astype(F32)
    slope_second[:, 2 : 2 + height] = slope_second_ref[...]
    slope_out[:, 1 : 1 + height] = slope_first_ref[...]
    for way in range(ways):
        line_ref, corner_ref = strips[2 * way], strips[2 * way + 1]
        below = 1 - lat if ways == 1 else way
        at = (height + 1) * below
        latent[:, pl.ds(at, 3)] += line_ref[:, 0:3].astype(F32) + corner_ref[...].astype(F32)
        slope_second[:, pl.ds((height + 2) * below, 2)] = gelu_slope(line_ref[:, 3:5].astype(F32))
        slope_out[:, pl.ds((height + 1) * below, 1)] = gelu_slope(line_ref[:, 5:6].astype(F32))
    for i in range(height + 4):
        row = lat * height + i - 2
        valid = jnp.logical_and(row >= 0, row < bands * height)
        value = latent[:, i] * slope_second[:, i]
        if i < 2 or i >= height + 2:
            value = jnp.where(valid, value, 0.0)
        grad_ref[:, i] = value.astype(BF)
        if 0 < i < height + 3:
            away_ref[:, i - 1] = jnp.where(chip == 0, value[:, :, LANES:], value[:, :, :LANES]).astype(BF)


def latent_grads(ways, bands, own, cross, strips, slope_second, slope_first):
    samples, rows, kept, depth = own.shape
    return run(
        "latent_grads",
        functools.partial(latent_kernel, ways, bands),
        [
            jax.ShapeDtypeStruct((samples, rows + 2, kept, depth), BF),
            jax.ShapeDtypeStruct((samples, rows, kept, LANES), BF),
            jax.ShapeDtypeStruct((samples, rows, kept, depth), F32),
        ],
        [own, cross, *strips, slope_second, slope_first],
        [
            pltpu.VMEM((samples, rows + 2, kept, depth), F32),
            pltpu.VMEM((samples, rows + 2, kept, depth), F32),
        ],
    )


def encoder_kernel(norm_factor, bands, grad_ref, slope_ref, input_ref, weights_ref, moved_out, mine_ref, other_ref, wide, cat, wide_first):
    samples, tall, kept, depth = grad_ref.shape
    rows = tall - 2
    height = rows - 2
    breadth = kept - 2 * EDGE
    lat = lax.axis_index("lat")
    core, _ = core_and_chip()
    own = 8 + EDGE
    wide[:, :, 8 : 8 + kept, :] = grad_ref[...].astype(F32)
    for v in STEPS:
        lanes = slice((v + 1) * depth, (v + 2) * depth)
        cat[:, :, :, lanes] = wide[:, :, 8 - v : 8 - v + kept + 8, :].astype(BF)
    linear = None
    for u in STEPS:
        weights = jnp.concatenate([weights_ref[3 * (u + 1) + (v + 1)] for v in STEPS], axis=1)
        left = cat[:, 1 - u : 1 - u + rows].reshape(samples * rows * (kept + 8), 3 * depth)
        part = dot_last(left, weights)
        linear = part if linear is None else linear + part
    linear = linear.reshape(samples, rows, kept + 8, depth)
    for i in range(rows):
        row = lat * height + i - 1
        valid = jnp.logical_and(row >= 0, row < bands * height)
        value = linear[:, i, :kept] * slope_ref[:, i]
        if i < 1 or i >= height + 1:
            value = jnp.where(valid, value, 0.0)
        wide_first[:, i, 8 : 8 + kept, :] = value.astype(BF).astype(F32)
    for v in STEPS:
        lanes = slice((v + 1) * depth, (v + 2) * depth)
        moved_out[:, :, :, lanes] = wide_first[:, :, own - v : own - v + breadth, :].astype(BF)
    for u in STEPS:
        right = moved_out[:, 1 - u : 1 - u + height].reshape(samples * height * breadth, 3 * depth)
        part = dot_plain(input_ref[...], right) * norm_factor
        for v in STEPS:
            k = 3 * (u + 1) + (v + 1)
            lower = part[:, (v + 1) * depth : (v + 1) * depth + LANES]
            upper = part[:, (v + 1) * depth + LANES : (v + 2) * depth]
            mine_ref[k] = jnp.where(core == 0, lower, upper).astype(BF)
            other_ref[k] = jnp.where(core == 0, upper, lower).astype(BF)


def encoder(norm_factor, bands, grad, slope, cells_in, w_second):
    samples, tall, kept, depth = grad.shape
    rows, height, breadth = tall - 2, tall - 4, kept - 2 * EDGE
    channels = cells_in.shape[0]
    half = jax.ShapeDtypeStruct((9, channels, LANES), BF)
    return run(
        "encoder_grads",
        functools.partial(encoder_kernel, norm_factor, bands),
        [jax.ShapeDtypeStruct((samples, rows, breadth, 3 * depth), BF), half, half],
        [grad, slope, cells_in, w_second],
        [
            pltpu.VMEM((samples, tall, kept + 24, depth), F32),
            pltpu.VMEM((samples, tall, kept + 8, 3 * depth), BF),
            pltpu.VMEM((samples, rows, kept + 16, depth), F32),
        ],
        flops=2 * 9 * depth * (samples * rows * (kept + 8) * depth + samples * height * breadth * channels),
    )


def second_kernel(norm_factor, shares, grad_ref, got_ref, act_ref, act_got_ref, *refs):
    full_ref, wide, cat = refs[-3:]
    samples, tall, kept, depth = grad_ref.shape
    rows, height, breadth = tall - 2, tall - 4, kept - 2 * EDGE
    core, chip = core_and_chip()
    own = 8 + EDGE
    lower = grad_ref[:, 1 : 1 + rows, :, :LANES].astype(F32)
    upper = grad_ref[:, 1 : 1 + rows, :, LANES:].astype(F32)
    wide[:samples, :, 8 : 8 + kept, :] = jnp.where(chip == 0, lower, upper)
    wide[samples:, :, 8 : 8 + kept, :] = got_ref[...].astype(F32)
    for v in STEPS:
        lanes = slice((v + 1) * LANES, (v + 2) * LANES)
        cat[:, :, :, lanes] = wide[:, :, own - v : own - v + breadth, :].astype(BF)
    cells = samples * height * breadth
    for u in STEPS:
        right = cat[:, 1 - u : 1 - u + height].reshape(2 * cells, 3 * LANES)
        part = dot_plain(act_ref[...], right[:cells]) + dot_plain(act_got_ref[...], right[cells:])
        part = part * norm_factor
        for v in STEPS:
            k = 3 * (u + 1) + (v + 1)
            full_ref[k * depth : (k + 1) * depth, :] = part[:, (v + 1) * LANES : (v + 2) * LANES].astype(BF)
    if len(refs) == 5:
        size = 9 * depth // shares // 2
        for i in range(shares):
            for out_ref, half in ((refs[0], core), (refs[1], 1 - core)):
                out_ref[i] = full_ref[pl.ds(pl.multiple_of((2 * i + half) * size, 16), size), :]


def second_grads(norm_factor, shares, grad, got, act, act_got):
    samples, tall, kept, depth = grad.shape
    rows, height, breadth = tall - 2, tall - 4, kept - 2 * EDGE
    size = 9 * depth // shares // 2
    inside = size % 16 == 0
    half = jax.ShapeDtypeStruct((shares, size, LANES), BF)
    scratch = [
        pltpu.VMEM((2 * samples, rows, kept + 16, LANES), F32),
        pltpu.VMEM((2 * samples, rows, breadth, 3 * LANES), BF),
    ]
    results = run(
        "second_weight_grads",
        functools.partial(second_kernel, norm_factor, shares),
        [half, half] if inside else [jax.ShapeDtypeStruct((9 * depth, LANES), BF)],
        [grad, got, act, act_got],
        [pltpu.VMEM((9 * depth, LANES), BF)] + scratch if inside else scratch,
        flops=2 * 9 * depth * LANES * 2 * samples * height * breadth,
    )
    if inside:
        return results
    halves = results[0].reshape(shares, 2, size, LANES)
    core, _ = core_and_chip()
    return [lax.dynamic_index_in_dim(halves, part, 1, keepdims=False) for part in (core, 1 - core)]


def act_kernel(source_ref, out_ref):
    samples, height, breadth, depth = source_ref.shape
    active = gelu_value(source_ref[...].astype(F32).reshape(samples * height * breadth, depth)).astype(BF).astype(F32)
    out_ref[...] = active.T.astype(BF)


def activated(source):
    samples, height, breadth, depth = source.shape
    return run("activated", act_kernel, [jax.ShapeDtypeStruct((depth, samples * height * breadth), BF)], [source])[0]


def other_band_kernel(*refs):
    band = 1 - lax.rem(lax.axis_index("lat"), 2)
    parts = [t[band].astype(F32) for t in refs[:-1]]
    refs[-1][...] = sum(parts[1:], parts[0]).astype(BF)


def partner(index, step, count):
    return index ^ step if count & (count - 1) == 0 else (index + step) % count


def own_band_kernel(*refs):
    columns = refs[0].shape[1]
    terms, came, outs = refs[: -columns - 2], refs[-columns - 2 : -columns], refs[-columns:]
    band, lon = lax.rem(lax.axis_index("lat"), 2), lax.axis_index("lon")
    for step in range(columns):
        block = partner(lon, step, columns)
        for layer in range(2):
            parts = [t[band, block].astype(F32) for t in terms[layer * len(terms) // 2 : (layer + 1) * len(terms) // 2]]
            outs[step][layer] = sum(parts, came[layer][block].astype(F32)).astype(BF)


def sum_kernel(*refs):
    total = refs[0][...].astype(F32)
    for ref in refs[1:-1]:
        total = total + ref[...].astype(F32)
    refs[-1][...] = total.astype(BF)


def input_kernel(moved_ref, w_first_ref, out_ref):
    samples, rows, breadth, triple = moved_ref.shape
    height = rows - 2
    total = None
    for u in STEPS:
        weights = jnp.concatenate([w_first_ref[3 * (u + 1) + (v + 1)] for v in STEPS], axis=1)
        part = dot_last(moved_ref[:, 1 - u : 1 - u + height].reshape(samples * height * breadth, triple), weights)
        total = part if total is None else total + part
    out_ref[...] = total.astype(BF).reshape(out_ref.shape)


def input_conv(moved, w_first):
    samples, rows, breadth, triple = moved.shape
    shape = (samples, rows - 2, breadth, w_first.shape[1])
    return run(
        "input_conv",
        input_kernel,
        [jax.ShapeDtypeStruct(shape, BF)],
        [moved, w_first],
        flops=2 * 3 * math.prod(shape) * triple,
    )[0]


def chips_kernel(mine_ref, cross_ref, out_ref):
    _, chip = core_and_chip()
    out_ref[0] = (mine_ref[0].astype(F32) + cross_ref[0].astype(F32)).astype(BF)
    out_ref[1] = jnp.where(chip == 0, mine_ref[1], cross_ref[1])
    out_ref[2] = jnp.where(chip == 0, cross_ref[1], mine_ref[1])


def cores_kernel(mine_ref, other_ref, first_ref, second_ref):
    core, _ = core_and_chip()
    rows = mine_ref.shape[1]
    mine, other = (ref[...].astype(F32) for ref in (mine_ref, other_ref))
    for part in range(2):
        value = jnp.where(core == part, mine, other)
        first_ref[pl.ds(part, rows, stride=2), :] = value[0]
        second_ref[pl.ds(2 * rows * part, rows, stride=2), :] = value[1]
        second_ref[pl.ds(2 * rows * part + 1, rows, stride=2), :] = value[2]


def swap(array, axis, flip):
    count = lax.axis_size(axis)
    return lax.ppermute(array, axis, [(i, i ^ flip) for i in range(count)])


def around(array, axis, step, periodic=True):
    count = lax.axis_size(axis)
    pairs = [(i, (i + step) % count) for i in range(count) if periodic or 0 <= i + step < count]
    return lax.ppermute(array, axis, pairs)


def corner(array, step):
    lead, lat = lax.axis_size("lead"), lax.axis_size("lat")
    pairs = []
    for a in range(lead):
        for b in range(lat):
            target = (b ^ 1) if step is None else b + step
            if 0 <= target < lat:
                pairs.append((a * lat + b, (a ^ 2) * lat + target))
    return lax.ppermute(array, ("lead", "lat"), pairs)


def other_band(terms, columns):
    shape = (columns, terms[0].size // LANES // columns // 2, LANES)
    return run("other_band", other_band_kernel, [jax.ShapeDtypeStruct(shape, BF)], [t.reshape(2, *shape) for t in terms])[0]


def pairwise(terms, bands):
    lat = lax.axis_index("lat")
    total = sum(t.reshape(-1, LANES).astype(F32) for t in terms).astype(BF)
    left = bands
    while left > 2:
        left //= 2
        bit = (lat // left) % 2
        halves = total.reshape(2, -1, LANES)
        send = lax.dynamic_index_in_dim(halves, 1 - bit, 0, keepdims=False)
        keep = lax.dynamic_index_in_dim(halves, bit, 0, keepdims=False)
        total = (keep.astype(F32) + swap(send, "lat", left).astype(F32)).astype(BF)
    return total


def near_kernel(second_ref, first_ref, input_ref, low_ref, high_ref, slope_second, slope_first, halo_ref, wide, cells):
    samples, height, breadth, depth = second_ref.shape
    kept = breadth + 2 * EDGE
    batch = low_ref.shape[0] - samples
    for ref, width, first_cell, slope_ref in ((second_ref, 2, 0, slope_second), (first_ref, 1, 4 * height, slope_first)):
        wide[...] = jnp.zeros(wide.shape, F32)
        for s in range(samples):
            for r in range(height):
                at = (s * height + r) * kept + EDGE
                for half in range(2):
                    wide[half, at : at + breadth, :] = ref[s, r, :, half * LANES : (half + 1) * LANES].astype(F32)
            for side, packed_ref in ((0, low_ref), (1, high_ref)):
                packed = packed_ref[batch + s].astype(F32)
                for col in range(width):
                    for half in range(2):
                        here = ((col if width == 2 else 2) * 2 + half) * height
                        value = packed[here : here + height]
                        at = s * height * kept + EDGE + col + (breadth if side else -width)
                        wide[half, pl.ds(at, height, stride=kept), :] = value
                        at = first_cell + (side * width + col) * height
                        cells[s, at : at + height, half * LANES : (half + 1) * LANES] = value
        value = jnp.concatenate([wide[half, : samples * height * kept] for half in range(2)], axis=1)
        slope_ref[...] = gelu_slope(value).reshape(slope_ref.shape)
    half = height // 2
    for part in range(2):
        values = input_ref[:, part * half : (part + 1) * half].reshape(samples, half * breadth, LANES)
        halo_ref[:, : half * breadth, part * LANES : (part + 1) * LANES] = values
    halo_ref[:, half * breadth :] = cells[:, : 6 * height].astype(BF)


def near_parts(pre_second, pre_first, encoder_input, low, high):
    samples, height, breadth, depth = pre_second.shape
    kept = breadth + 2 * EDGE
    slope = jax.ShapeDtypeStruct((samples, height, kept, depth), F32)
    return run(
        "near_parts",
        near_kernel,
        [slope, slope, jax.ShapeDtypeStruct((samples, 6 * height + height * breadth // 2, depth), BF)],
        [pre_second, pre_first, encoder_input, low, high],
        [
            pltpu.VMEM((2, (samples * height + 8) * kept, LANES), F32),
            pltpu.VMEM((samples, 6 * height + 8, depth), F32),
        ],
    )


def far_kernel(first_ref, tile_ref, slope_second, slope_first, act_out, wide, act):
    samples, height, breadth, depth = first_ref.shape
    kept = breadth + 2 * EDGE
    lat = lax.axis_index("lat")
    for source_ref, slope_ref in ((tile_ref.at[0], slope_second), (tile_ref.at[1], slope_first)):
        wide[...] = jnp.zeros(wide.shape, F32)
        for s in range(samples):
            for half in range(2):
                for r in range(height):
                    at = (s * height + r) * kept + EDGE
                    wide[half, at : at + breadth, :] = source_ref[s, r, :, half * LANES : (half + 1) * LANES].astype(F32)
        value = jnp.concatenate([wide[0], wide[1]], axis=1)
        slope_ref[...] = gelu_slope(value).reshape(slope_ref.shape)
    own, other = pl.ds(height * lat, height), pl.ds(height * (1 - lat), height)
    act[:, own] = gelu_value(first_ref[...].astype(F32))
    act[:, other] = gelu_value(tile_ref[1].astype(F32))
    act_out[...] = act[...].reshape(act_out.shape[1], depth).T.astype(BF)


def far_parts(pre_first, tile):
    samples, height, breadth, depth = pre_first.shape
    kept = breadth + 2 * EDGE
    slope = jax.ShapeDtypeStruct((samples, height, kept, depth), F32)
    return run(
        "far_parts",
        far_kernel,
        [slope, slope, jax.ShapeDtypeStruct((depth, 2 * samples * height * breadth), BF)],
        [pre_first, tile],
        [
            pltpu.VMEM((2, samples * height * kept, LANES), F32),
            pltpu.VMEM((samples, 2 * height, breadth, depth), F32),
        ],
    )


def put_slopes(sample, slope, near_ref, far_ref, halo_ref, width, first_cell):
    _, height, kept, _ = near_ref.shape
    lat = lax.axis_index("lat")
    other = pl.ds(height * (1 - lat), height)
    slope[pl.ds(height * lat, height)] = near_ref[sample]
    slope[other] = far_ref[sample]
    beside = gelu_slope(halo_ref[sample, halo_ref.shape[1] - 6 * height :].astype(F32))
    for side in range(2):
        for col in range(width):
            here = first_cell + (side * width + col) * height
            at = kept - EDGE + col if side else EDGE - width + col
            slope[other, at, :] = beside[here : here + height]


def globe_kernel(sample, near_ref, far_ref, halo_ref, total_ref, line_ref, cat_ref, moved_ref, latent, slope, wide):
    rows, kept, depth = total_ref.shape
    height = rows - 1
    tall = 2 * height
    breadth = kept - 2 * EDGE
    lat = lax.axis_index("lat")
    own = 8 + EDGE
    latent[...] = jnp.zeros(latent.shape, F32)
    latent[pl.ds((height - 1) * lat, rows)] = total_ref[...].astype(F32)
    latent[pl.ds((height - 1) * (1 - lat), rows)] += line_ref[...].astype(F32)
    put_slopes(sample, slope, near_ref, far_ref, halo_ref, 2, 0)
    wide[:, 8 : 8 + kept, :] = (latent[...] * slope[...]).astype(BF).astype(F32)
    for v in STEPS:
        lanes = slice((v + 1) * depth, (v + 2) * depth)
        cat_ref[1 : 1 + tall, :, lanes] = wide[:, 8 - v : 8 - v + kept, :].astype(BF)
        moved_ref[v + 1, 1 : 1 + tall] = wide[:, own - v : own - v + breadth, :].astype(BF)
    for row in (0, tall + 1):
        cat_ref[row] = jnp.zeros(cat_ref.shape[1:], BF)
        moved_ref[:, row] = jnp.zeros(moved_ref.shape[:1] + moved_ref.shape[2:], BF)


def globe(sample, total, line, near, far, halo):
    rows, kept, depth = total.shape
    tall, breadth = 2 * (rows - 1), kept - 2 * EDGE
    return run(
        "latent_grads",
        functools.partial(globe_kernel, sample),
        [
            jax.ShapeDtypeStruct((tall + 2, kept, 3 * depth), BF),
            jax.ShapeDtypeStruct((3, tall + 2, breadth, depth), BF),
        ],
        [near, far, halo, total, line],
        [
            pltpu.VMEM((tall, kept, depth), F32),
            pltpu.VMEM((tall, kept, depth), F32),
            pltpu.VMEM((tall, kept + 24, depth), F32),
        ],
    )


def band_rows(norm_factor, lefts, moved, mine_ref, other_ref):
    channels, cells = lefts[0].shape
    _, padded, breadth, depth = moved[0].shape
    tall = padded - 2
    lat = lax.axis_index("lat")
    core, _ = core_and_chip()
    half = channels // 2

    def put(parts, u, v, start, size):
        total = None
        for left, ref in zip(parts, moved):
            part = dot_plain(left, ref[v + 1, pl.ds(1 - u, tall)].reshape(cells, depth))
            total = part if total is None else total + part
        total = total * norm_factor
        lower, upper = total[:, :LANES], total[:, LANES:]
        here = pl.ds(pl.multiple_of(start, half), size)
        mine_ref[here, :] = jnp.where(core == 0, lower, upper).astype(BF)
        other_ref[here, :] = jnp.where(core == 0, upper, lower).astype(BF)

    for j in range(4):
        (u0, v0), (u1, v1) = (divmod(k, 3) for k in (j, 5 + j))
        put(lefts, u0 - 1 + lat * (u1 - u0), v0 - 1 + lat * (v1 - v0), lat * half + j * channels, channels)
    put([jnp.where(lat == 0, left[:half], left[half:]) for left in lefts], 0, 0, (1 - lat) * 4 * channels, half)


def second_band_kernel(norm_factor, act_ref, *refs):
    moved, (mine_ref, other_ref) = refs[:-2], refs[-2:]
    cells = act_ref.shape[1] // len(moved)
    lefts = [act_ref[:, s * cells : (s + 1) * cells] for s in range(len(moved))]
    band_rows(norm_factor, lefts, moved, mine_ref, other_ref)


def second_band(norm_factor, act, moved):
    half = jax.ShapeDtypeStruct((9 * act.shape[0] // 2, LANES), BF)
    return run("second_weight_grads", functools.partial(second_band_kernel, norm_factor), [half, half], [act, *moved])


def first_kernel(sample, cat_ref, near_ref, far_ref, halo_ref, weights_ref, moved_ref, slope, wide):
    padded, kept, triple = cat_ref.shape
    tall, depth = padded - 2, triple // 3
    breadth = kept - 2 * EDGE
    own = 8 + EDGE
    put_slopes(sample, slope, near_ref, far_ref, halo_ref, 1, 2 * tall)
    linear = None
    for u in STEPS:
        weights = jnp.concatenate([weights_ref[3 * (u + 1) + (v + 1)] for v in STEPS], axis=1)
        part = dot_last(cat_ref[1 - u : 1 - u + tall].reshape(tall * kept, triple), weights)
        linear = part if linear is None else linear + part
    wide[:, 8 : 8 + kept, :] = (linear.reshape(tall, kept, depth) * slope[...]).astype(BF).astype(F32)
    for v in STEPS:
        moved_ref[v + 1, 1 : 1 + tall] = wide[:, own - v : own - v + breadth, :].astype(BF)
    for row in (0, tall + 1):
        moved_ref[:, row] = jnp.zeros(moved_ref.shape[:1] + moved_ref.shape[2:], BF)


def first_grad(sample, cat, near, far, halo, w_second):
    padded, kept, triple = cat.shape
    tall, depth = padded - 2, triple // 3
    return run(
        "second_conv",
        functools.partial(first_kernel, sample),
        [jax.ShapeDtypeStruct((3, padded, kept - 2 * EDGE, depth), BF)],
        [cat, near, far, halo, w_second],
        [pltpu.VMEM((tall, kept, depth), F32), pltpu.VMEM((tall, kept + 16, depth), F32)],
    )[0]


def first_band_kernel(norm_factor, halo_ref, input_ref, *refs):
    moved, (mine_ref, other_ref, cells) = refs[:-3], refs[-3:]
    samples, height, breadth, channels = input_ref.shape
    lat = lax.axis_index("lat")
    cells[:, pl.ds(height * lat, height)] = input_ref[...].astype(F32)
    half = height // 2
    for part in range(2):
        values = halo_ref[:, : half * breadth, part * LANES : (part + 1) * LANES].astype(F32)
        cells[:, pl.ds(height * (1 - lat) + part * half, half)] = values.reshape(samples, half, breadth, LANES)
    lefts = [cells[s].reshape(2 * height * breadth, channels).T.astype(BF) for s in range(samples)]
    band_rows(norm_factor, lefts, moved, mine_ref, other_ref)


def first_band(norm_factor, halo, encoder_input, moved):
    samples, height, breadth, channels = encoder_input.shape
    half = jax.ShapeDtypeStruct((9 * channels // 2, LANES), BF)
    return run(
        "first_weight_grads",
        functools.partial(first_band_kernel, norm_factor),
        [half, half],
        [halo, encoder_input, *moved],
        [pltpu.VMEM((samples, 2 * height, breadth, channels), F32)],
    )


def input_band_kernel(w_first_ref, *refs):
    moved, out_ref = refs[:-1], refs[-1]
    _, height, breadth, channels = out_ref.shape
    depth = moved[0].shape[3]
    lat = lax.axis_index("lat")
    total = None
    for u in STEPS:
        weights = jnp.concatenate([w_first_ref[3 * (u + 1) + (v + 1)] for v in STEPS], axis=1)
        here = pl.ds(height * lat + 1 - u, height)
        left = [jnp.concatenate([ref[v + 1, here].reshape(-1, depth) for v in STEPS], axis=1) for ref in moved]
        part = dot_last(jnp.concatenate(left, axis=0), weights)
        total = part if total is None else total + part
    out_ref[...] = total.astype(BF).reshape(out_ref.shape)


def blocks_kernel(first_mine, first_got, second_mine, second_got, *outs):
    lon = lax.axis_index("lon")
    rows = first_mine.shape[1]
    for step, out_ref in enumerate(outs):
        block = partner(lon, step, len(outs))
        out_ref[:rows] = (first_mine[block].astype(F32) + first_got[block].astype(F32)).astype(BF)
        out_ref[rows:] = (second_mine[block].astype(F32) + second_got[block].astype(F32)).astype(BF)


def halves_kernel(mine_ref, other_ref, first_ref, second_ref):
    core, _ = core_and_chip()
    mine, other = mine_ref[...].astype(F32), other_ref[...].astype(F32)
    rows = mine.shape[0] // 3
    for part in range(2):
        value = jnp.where(core == part, mine, other)
        first_ref[pl.ds(part, rows, stride=2), :] = value[:rows]
        second_ref[pl.ds(part, 2 * rows, stride=2), :] = value[rows:]


def to_partner(array, step):
    count = lax.axis_size("lon")
    return lax.ppermute(array, "lon", [(partner(i, step, count), i) for i in range(count)])


def two_bands(head_grads, head_weights, encoder_input, pre_first, pre_second, w_first, w_second, norm_factor):
    samples, height, breadth, _ = encoder_input.shape
    columns = lax.axis_size("lon")
    to_right, to_left, tile = pack(head_grads, pre_second, pre_first, True)
    tile = swap(tile, "lat", 1)
    low = around(to_right, "lon", 1)
    high = around(to_left, "lon", -1)
    head_grads, head_weights, w_second, pre_second, pre_first, encoder_input = stage(
        head_grads, head_weights, w_second, pre_second, pre_first, encoder_input
    )
    inside = inside_conv(head_grads, head_weights, 2 * samples)
    low, high, inside, tile = lax.optimization_barrier((low, high, inside, tile))
    heads_of = functools.partial(
        head_conv,
        head_grads=head_grads,
        low=low,
        high=high,
        head_weights=head_weights,
        slots=2 * samples,
        rows=height + 1,
    )
    everyone = range(samples)
    got = swap(edges_conv(inside, low, high, head_weights), "lead", 1)
    part_shape = jax.ShapeDtypeStruct(got.shape[1:], BF)
    parts = run("core_sum", core_sum_kernel, [part_shape] * (2 * samples), [heads_of(False, False, 0), got])
    own, cross = parts[0::2], list(parts[1::2])
    near_second, near_first, halo = near_parts(pre_second, pre_first, encoder_input, low, high)
    cross[-1], halo = lax.optimization_barrier((cross[-1], halo))
    cross = [swap(part, "lead", 2) for part in cross]
    halo = swap(halo, "lat", 1)
    cross[-1], halo = lax.optimization_barrier((cross[-1], halo))
    totals = [run("chip_sum", sum_kernel, [part_shape], [own[s], cross[s]])[0] for s in everyone]
    lines = [swap(total, "lat", 1) for total in totals]
    far_second, far_first, act = far_parts(pre_first, tile)

    moved_second, moved_first = [], []
    for s in everyone:
        cat, moved = globe(s, totals[s], lines[s], near_second, far_second, halo)
        moved_second.append(moved)
        if s < samples - 1:
            moved_first.append(first_grad(s, cat, near_first, far_first, halo, w_second))
            near_second, moved_first[s] = lax.optimization_barrier((near_second, moved_first[s]))
    second_mine, second_other = second_band(norm_factor, act, moved_second)
    second_got = swap(second_other, "lead", 1)
    moved_first.append(first_grad(samples - 1, cat, near_first, far_first, halo, w_second))
    first_mine, first_other = first_band(norm_factor, halo, encoder_input, moved_first)
    first_got = swap(first_other, "lead", 1)
    input_grad = run(
        "input_conv", input_band_kernel, [jax.ShapeDtypeStruct(encoder_input.shape, BF)], [w_first, *moved_first]
    )[0]

    blocks = [t.reshape(columns, -1, LANES) for t in (first_mine, first_got, second_mine, second_got)]
    rows = blocks[0].shape[1]
    share_shape = jax.ShapeDtypeStruct((3 * rows, LANES), BF)
    shares = run("blocks", blocks_kernel, [share_shape] * columns, blocks)
    parts = [to_partner(shares[step], step) for step in ((2, 1, 3) if columns == 4 else range(1, columns))]
    share = run("share", sum_kernel, [share_shape], [shares[0], *parts])[0]
    both = run("chips", sum_kernel, [share_shape], [share, swap(share, "lead", 2)])[0]
    result_first, result_second = run(
        "cores",
        halves_kernel,
        [jax.ShapeDtypeStruct((2 * rows, LANES), F32), jax.ShapeDtypeStruct((4 * rows, LANES), F32)],
        [both, swap(both, "lead", 1)],
    )
    return input_grad, result_first.reshape(-1), result_second.reshape(-1)


def core_sum_kernel(mine_ref, got_ref, *outs):
    for slot, out_ref in enumerate(outs):
        out_ref[...] = (mine_ref[slot].astype(F32) + got_ref[slot].astype(F32)).astype(BF)


def general(head_grads, head_weights, encoder_input, pre_first, pre_second, w_first, w_second, norm_factor):
    samples, height, breadth, _ = encoder_input.shape
    bands, columns = lax.axis_size("lat"), lax.axis_size("lon")
    to_right, to_left = pack(head_grads, pre_second, pre_first, False)
    to_right, to_left, to_cross = lax.optimization_barrier((to_right, to_left, pre_first))
    low = around(to_right, "lon", 1)
    high = around(to_left, "lon", -1)
    act_got = activated(swap(to_cross, "lead", 2))
    head_grads, head_weights, w_second, pre_second, pre_first, encoder_input = stage(
        head_grads, head_weights, w_second, pre_second, pre_first, encoder_input
    )
    low, high, act_got = lax.optimization_barrier((low, high, act_got))

    steps = [1, -1]
    heads_of = functools.partial(head_conv, head_grads=head_grads, high=high, head_weights=head_weights, slots=samples, rows=height + 2)
    got_cross = swap(heads_of(True, True, None, low=low), "lead", 1)
    got_own = swap(heads_of(True, False, None, low=low), "lead", 1)
    cross, *angles = spread_cross(heads_of(False, True, None, low=low), got_cross, len(steps))
    low_later, cross, *angles = lax.optimization_barrier((low, cross, *angles))
    cross = swap(cross, "lead", 2)
    angles = [corner(angle, step) for angle, step in zip(angles, steps)]
    second, first, slope_second, slope_first, act, cells_in = saved(pre_second, pre_first, encoder_input, low, high)
    own, *lines = spread_own(heads_of(False, False, None, low=low_later), got_own, second, first, len(steps))
    lines = [swap(line, "lat", 1) if step is None else around(line, "lat", step, False) for line, step in zip(lines, steps)]
    strips = [strip for pair in zip(lines, angles) for strip in pair]

    grad, away, slope = latent_grads(len(steps), bands, own, cross, strips, slope_second, slope_first)
    grad_got = swap(away, "lead", 2)
    moved, first_mine, first_other = encoder(norm_factor, bands, grad, slope, cells_in, w_second)
    input_grad = input_conv(moved, w_first)
    first_got = swap(first_other, "lead", 1)
    second_mine, second_other = second_grads(norm_factor, bands * columns, grad, grad_got, act, act_got)
    second_got = swap(second_other, "lead", 1)

    first_terms = [pairwise([first_mine, first_got], bands)]
    second_terms = [pairwise([second_mine, second_got], bands)]
    first_came = swap(other_band(first_terms, columns), "lat", 1)
    second_came = swap(other_band(second_terms, columns), "lat", 1)
    blocks = [t.reshape(2, columns, -1, LANES) for t in first_terms + second_terms]
    rows = blocks[0].shape[2]
    share_shape = jax.ShapeDtypeStruct((2, rows, LANES), BF)
    shares = run("own_band", own_band_kernel, [share_shape] * columns, blocks + [first_came, second_came])
    parts = [to_partner(shares[step], step) for step in ((2, 1, 3) if columns == 4 else range(1, columns))]
    share = run("share", sum_kernel, [share_shape], [shares[0], *parts])[0]
    both = run("chips", chips_kernel, [jax.ShapeDtypeStruct((3, rows, LANES), BF)], [share, swap(share, "lead", 2)])[0]
    result_first, result_second = run(
        "cores",
        cores_kernel,
        [jax.ShapeDtypeStruct((2 * rows, LANES), F32), jax.ShapeDtypeStruct((4 * rows, LANES), F32)],
        [both, swap(both, "lead", 1)],
    )
    return input_grad, result_first.reshape(-1), result_second.reshape(-1)


def per_device(head_grads, head_weights, encoder_input, pre_first, pre_second, w_first, w_second):
    samples, height, breadth, channels = encoder_input.shape
    bands, columns = lax.axis_size("lat"), lax.axis_size("lon")
    cells_total = samples * lax.axis_size("lead") * height * bands * breadth * columns
    norm_factor = 1.0 / math.sqrt(cells_total)
    plan = two_bands if bands == 2 and 9 * channels // (bands * columns) % 16 == 0 else general
    return plan(head_grads, head_weights, encoder_input, pre_first, pre_second, w_first, w_second, norm_factor)


def solution(mesh):
    in_specs = (
        P("lead", None, "lat", "lon", None),
        P("lead", None, None, None),
        P("lead", "lat", "lon", None),
        P("lead", "lat", "lon", None),
        P("lead", "lat", "lon", None),
        P(),
        P(),
    )
    out_specs = (P("lead", "lat", "lon", None), P(("lat", "lon")), P(("lat", "lon")))
    return jax.shard_map(
        per_device, mesh=mesh, in_specs=in_specs, out_specs=out_specs, check_vma=False
    )
```

```python
import functools
import math

import jax
import jax.numpy as jnp
from jax import lax
from jax.experimental import pallas as pl
from jax.experimental.pallas import tpu as pltpu
from jax.sharding import PartitionSpec as P

BF = jnp.bfloat16
F32 = jnp.float32
STEPS = (-1, 0, 1)
EDGE = 4
LANES = 128
VMEM_BYTES = 24 * 1024 * 1024


def erf_part(values):
    return 0.5 * (1.0 + lax.erf(values * 0.7071067811865476))


def gelu_slope(values):
    return erf_part(values) + values * jnp.exp(-0.5 * values * values) * 0.3989422804014327


def gelu_value(values):
    return values * erf_part(values)


def dot_last(left, right):
    return lax.dot_general(left, right, (((1,), (1,)), ((), ())), preferred_element_type=F32)


def dot_plain(left, right):
    return lax.dot_general(left, right, (((1,), (0,)), ((), ())), preferred_element_type=F32)


def core_and_chip():
    lead = lax.axis_index("lead")
    return lax.rem(lead, 2), lax.div(lead, 2)


def run(name, kernel, out_shape, arrays, scratch=(), flops=0, far=False):
    specs = [pl.BlockSpec(memory_space=pltpu.HBM if far else pltpu.VMEM)] * len(arrays)
    if far:
        arrays = [pltpu.with_memory_space_constraint(a, pltpu.HBM) for a in arrays]
    touched = sum(a.size * a.dtype.itemsize for a in arrays)
    touched += sum(math.prod(s.shape) * s.dtype.itemsize for s in out_shape)
    return pl.pallas_call(
        kernel,
        name=name,
        out_shape=out_shape,
        in_specs=specs,
        out_specs=[pl.BlockSpec(memory_space=pltpu.VMEM)] * len(out_shape),
        scratch_shapes=list(scratch),
        compiler_params=pltpu.CompilerParams(vmem_limit_bytes=VMEM_BYTES),
        cost_estimate=pl.CostEstimate(flops=1, bytes_accessed=1, transcendentals=0),
    )(*arrays)


def pack_kernel(grads_far, second_far, first_far, right_ref, left_ref, grads_near, second_near, first_near, edges, edges_wide, packed, sems):
    heads, batch, height, breadth, _ = grads_far.shape
    samples = second_far.shape[0]
    rows = 6 * height
    copies = []
    for side in range(2):
        columns = pl.ds(breadth - 16 if side == 0 else 0, 16)
        for j, (far, near) in enumerate(((grads_far, grads_near), (second_far, second_near), (first_far, first_near))):
            source = far.at[:, :, :, columns, :] if j == 0 else far.at[:, :, columns, :]
            copies.append(pltpu.make_async_copy(source, near.at[side], sems.at[side, j]))
            copies[-1].start()
    for copy in copies:
        copy.wait()
    for side, out_ref in ((0, right_ref), (1, left_ref)):
        start = 8 if side == 0 else 0
        grads_ref, second_ref, first_ref = grads_near.at[side], second_near.at[side], first_near.at[side]
        for h in range(heads):
            for b in range(batch):
                block = grads_ref[h, b].astype(F32)[:, start : start + 8, :]
                edges[(h * batch + b) * height * 8 : (h * batch + b + 1) * height * 8, :] = block.reshape(height * 8, LANES)
        for j, ref in enumerate((second_ref, first_ref)):
            for s in range(samples):
                block = ref[s].astype(F32)[:, start : start + 8, :]
                at = (j * samples + s) * height * 8
                for half in range(2):
                    lanes = slice(half * LANES, (half + 1) * LANES)
                    edges_wide[half, at : at + height * 8, :] = block[:, :, lanes].reshape(height * 8, LANES)
        for b in range(batch):
            for col in range(3):
                inner = 5 + col if side == 0 else col
                for h in range(heads):
                    at = b * rows + (col * 2 + h) * height
                    packed[at : at + height, :] = edges[pl.ds((h * batch + b) * height * 8 + inner, height, stride=8), :]
        for s in range(samples):
            for q in range(3):
                j, col, width = (0, q, 2) if q < 2 else (1, 0, 1)
                inner = 8 - width + col if side == 0 else col
                for half in range(2):
                    at = (batch + s) * rows + (q * 2 + half) * height
                    packed[at : at + height, :] = edges_wide[
                        half, pl.ds((j * samples + s) * height * 8 + inner, height, stride=8), :
                    ]
        out_ref[...] = packed[: (batch + samples) * rows].astype(BF).reshape(out_ref.shape)


def pack(head_grads, pre_second, pre_first):
    heads, batch, height, _, _ = head_grads.shape
    samples = pre_second.shape[0]
    shape = jax.ShapeDtypeStruct((batch + samples, 6 * height, LANES), BF)
    return run(
        "pack_columns",
        pack_kernel,
        [shape, shape],
        [head_grads, pre_second, pre_first],
        [
            pltpu.VMEM((2, heads, batch, height, 16, LANES), BF),
            pltpu.VMEM((2, samples, height, 16, 2 * LANES), BF),
            pltpu.VMEM((2, samples, height, 16, 2 * LANES), BF),
            pltpu.VMEM((heads * batch * height * 8 + 64, LANES), F32),
            pltpu.VMEM((2, 2 * samples * height * 8 + 64, LANES), F32),
            pltpu.VMEM(((batch + samples) * 6 * height + 16, LANES), F32),
            pltpu.SemaphoreType.DMA((2, 3)),
        ],
        far=True,
    )


def stage_kernel(*refs):
    count = len(refs) // 2
    sems = refs[-1]
    copies = [pltpu.make_async_copy(refs[i], refs[count + i], sems.at[i]) for i in range(count)]
    for copy in copies:
        copy.start()
    for copy in copies:
        copy.wait()


def stage(*arrays):
    shapes = [pltpu.VMEM(a.shape, a.dtype) for a in arrays]
    return run("stage", stage_kernel, shapes, list(arrays), [pltpu.SemaphoreType.DMA((len(arrays),))], far=True, flops=1 << 30)


def heads_kernel(other_core, other_chip, sample, samples, grads_ref, low_ref, high_ref, weights_ref, out_ref, wide, shifted, total):
    heads, batch, height, breadth, _ = grads_ref.shape
    slots, _, kept, depth = out_ref.shape
    pitch = kept + 16
    own = 8 + EDGE
    core, chip = core_and_chip()
    core = 1 - core if other_core else core
    for slot in range(slots):
        if sample is None:
            group, s = 1 - chip if other_chip else chip, slot
        else:
            group, s = 1 - chip if slot % 2 else chip, sample + slot // 2
        b = (2 * group + core) * samples + s
        low = low_ref[b].astype(F32)
        high = high_ref[b].astype(F32)
        for r in range(height):
            at = (slot * height + r) * pitch + own
            for h in range(heads):
                wide[h, at : at + breadth, :] = grads_ref[h, b, r].astype(F32)
        for col in range(3):
            for h in range(heads):
                here = (col * 2 + h) * height
                at = slot * height * pitch + own + col
                wide[h, pl.ds(at - 3, height, stride=pitch), :] = low[here : here + height]
                wide[h, pl.ds(at + breadth, height, stride=pitch), :] = high[here : here + height]
        for v in STEPS:
            for h in range(heads):
                starts = [(slot * height + r) * pitch + 8 - v for r in range(height)]
                moved = jnp.concatenate([wide[h, at : at + kept, :] for at in starts], axis=0).astype(BF)
                lane = ((v + 1) * heads + h) * LANES
                shifted[slot * height * kept : (slot + 1) * height * kept, lane : lane + LANES] = moved
    total[:, height:, :, :] = jnp.zeros((slots, 2, kept, depth), F32)
    for u in STEPS:
        weights = jnp.concatenate(
            [weights_ref[h, 3 * (u + 1) + (v + 1)] for v in STEPS for h in range(heads)], axis=1
        )
        part = dot_last(shifted[...], weights).reshape(slots, height, kept, depth)
        if u == -1:
            total[:, :height] = part
        else:
            total[:, 1 + u : 1 + u + height] += part
    if out_ref.shape[1] == height + 2:
        out_ref[...] = total[...].astype(BF)
    else:
        out_ref[...] = total[:, pl.ds(1 - lax.axis_index("lat"), height + 1)].astype(BF)


def head_conv(other_core, other_chip, sample, head_grads, low, high, head_weights, slots, rows):
    samples = head_grads.shape[1] // lax.axis_size("lead")
    heads, batch, height, breadth, _ = head_grads.shape
    depth = head_weights.shape[2]
    kept = breadth + 2 * EDGE
    return run(
        "head_conv",
        functools.partial(heads_kernel, other_core, other_chip, sample, samples),
        [jax.ShapeDtypeStruct((slots, rows, kept, depth), BF)],
        [head_grads, low, high, head_weights],
        [
            pltpu.VMEM((heads, (slots * height + 8) * (kept + 16), LANES), F32),
            pltpu.VMEM((slots * height * kept, 3 * heads * LANES), BF),
            pltpu.VMEM((slots, height + 2, kept, depth), F32),
        ],
        flops=2 * slots * height * kept * 9 * heads * LANES * depth,
    )[0]


def inside_kernel(samples, grads_ref, weights_ref, total_ref, wide, shifted):
    heads, _, height, breadth, _ = grads_ref.shape
    slots, _, kept, depth = total_ref.shape
    pitch = kept + 16
    own = 8 + EDGE
    core, chip = core_and_chip()
    blank = jnp.zeros((height, LANES), F32)
    for slot in range(slots):
        group, s = 1 - chip if slot % 2 else chip, slot // 2
        b = (2 * group + 1 - core) * samples + s
        for h in range(heads):
            for r in range(height):
                at = (slot * height + r) * pitch + own
                wide[h, at : at + breadth, :] = grads_ref[h, b, r].astype(F32)
            for col in range(3):
                at = slot * height * pitch + own + col
                wide[h, pl.ds(at - 3, height, stride=pitch), :] = blank
                wide[h, pl.ds(at + breadth, height, stride=pitch), :] = blank
            for v in STEPS:
                starts = [(slot * height + r) * pitch + 8 - v for r in range(height)]
                moved = jnp.concatenate([wide[h, at : at + kept, :] for at in starts], axis=0).astype(BF)
                lane = ((v + 1) * heads + h) * LANES
                shifted[slot * height * kept : (slot + 1) * height * kept, lane : lane + LANES] = moved
    total_ref[:, height:, :, :] = jnp.zeros((slots, 2, kept, depth), F32)
    for u in STEPS:
        weights = jnp.concatenate(
            [weights_ref[h, 3 * (u + 1) + (v + 1)] for v in STEPS for h in range(heads)], axis=1
        )
        part = dot_last(shifted[...], weights).reshape(slots, height, kept, depth)
        if u == -1:
            total_ref[:, :height] = part
        else:
            total_ref[:, 1 + u : 1 + u + height] += part


def edges_kernel(samples, inside_ref, low_ref, high_ref, weights_ref, out_ref, wide, shifted, total):
    slots, rows, kept, depth = inside_ref.shape
    height, heads, pitch = rows - 2, weights_ref.shape[0], 24
    core, chip = core_and_chip()
    wide[...] = jnp.zeros(wide.shape, F32)
    total[...] = inside_ref[...]
    for side, packed_ref in ((0, low_ref), (1, high_ref)):
        for slot in range(slots):
            group, s = 1 - chip if slot % 2 else chip, slot // 2
            packed = packed_ref[(2 * group + 1 - core) * samples + s].astype(F32)
            first = (side * slots + slot) * height
            for h in range(heads):
                for col in range(3):
                    here = (col * 2 + h) * height
                    at = first * pitch + 9 + 3 * side + col
                    wide[h, pl.ds(at, height, stride=pitch), :] = packed[here : here + height]
                for v in STEPS:
                    starts = [(first + r) * pitch + 8 - v for r in range(height)]
                    moved = jnp.concatenate([wide[h, at : at + 8, :] for at in starts], axis=0).astype(BF)
                    lane = ((v + 1) * heads + h) * LANES
                    shifted[first * 8 : (first + height) * 8, lane : lane + LANES] = moved
    for u in STEPS:
        weights = jnp.concatenate(
            [weights_ref[h, 3 * (u + 1) + (v + 1)] for v in STEPS for h in range(heads)], axis=1
        )
        part = dot_last(shifted[...], weights).reshape(2, slots, height, 8, depth)
        total[:, 1 + u : 1 + u + height, :8] += part[0]
        total[:, 1 + u : 1 + u + height, kept - 8 :] += part[1]
    out_ref[...] = total[:, pl.ds(1 - lax.axis_index("lat"), height + 1)].astype(BF)


def inside_conv(head_grads, head_weights, slots):
    samples = head_grads.shape[1] // lax.axis_size("lead")
    heads, _, height, breadth, _ = head_grads.shape
    kept = breadth + 2 * EDGE
    return run(
        "head_conv_inside",
        functools.partial(inside_kernel, samples),
        [jax.ShapeDtypeStruct((slots, height + 2, kept, head_weights.shape[2]), F32)],
        [head_grads, head_weights],
        [
            pltpu.VMEM((heads, (slots * height + 8) * (kept + 16), LANES), F32),
            pltpu.VMEM((slots * height * kept, 3 * heads * LANES), BF),
        ],
    )[0]


def edges_conv(inside, low, high, head_weights):
    slots, rows, kept, depth = inside.shape
    samples, heads, height = slots // 2, head_weights.shape[0], rows - 2
    return run(
        "head_conv_edges",
        functools.partial(edges_kernel, samples),
        [jax.ShapeDtypeStruct((slots, rows - 1, kept, depth), BF)],
        [inside, low, high, head_weights],
        [
            pltpu.VMEM((heads, (2 * slots * height + 8) * 24, LANES), F32),
            pltpu.VMEM((2 * slots * height * 8, 3 * heads * LANES), BF),
            pltpu.VMEM((slots, rows, kept, depth), F32),
        ],
    )[0]


def saved_kernel(second_ref, first_ref, input_ref, low_ref, high_ref, second_out, first_out, slope_second, slope_first, act_out, input_out, wide):
    samples, height, breadth, depth = second_ref.shape
    kept = breadth + 2 * EDGE
    batch = low_ref.shape[0] - samples
    for ref, width, out_ref, slope_ref in (
        (second_ref, 2, second_out, slope_second),
        (first_ref, 1, first_out, slope_first),
    ):
        wide[...] = jnp.zeros(wide.shape, F32)
        for s in range(samples):
            for r in range(height):
                at = (s * height + r) * kept + EDGE
                for half in range(2):
                    lanes = slice(half * LANES, (half + 1) * LANES)
                    wide[half, at : at + breadth, :] = ref[s, r, :, lanes].astype(F32)
            low = low_ref[batch + s].astype(F32)
            high = high_ref[batch + s].astype(F32)
            for col in range(width):
                for half in range(2):
                    here = ((col if width == 2 else 2) * 2 + half) * height
                    at = s * height * kept + EDGE + col
                    wide[half, pl.ds(at - width, height, stride=kept), :] = low[here : here + height]
                    wide[half, pl.ds(at + breadth, height, stride=kept), :] = high[here : here + height]
        value = jnp.concatenate([wide[half, : samples * height * kept] for half in range(2)], axis=1)
        out_ref[...] = value.astype(BF).reshape(out_ref.shape)
        slope_ref[...] = gelu_slope(value).reshape(slope_ref.shape)
    active = gelu_value(first_ref[...].astype(F32).reshape(samples * height * breadth, depth)).astype(BF).astype(F32)
    act_out[...] = active.T.astype(BF)
    cells = input_ref[...].astype(F32).reshape(samples * height * breadth, input_ref.shape[3])
    input_out[...] = cells.T.astype(BF)


def saved(pre_second, pre_first, encoder_input, low, high):
    samples, height, breadth, depth = pre_second.shape
    kept = breadth + 2 * EDGE
    cells = samples * height * breadth
    return run(
        "saved_parts",
        saved_kernel,
        [
            jax.ShapeDtypeStruct((samples, height, kept, depth), BF),
            jax.ShapeDtypeStruct((samples, height, kept, depth), BF),
            jax.ShapeDtypeStruct((samples, height, kept, depth), F32),
            jax.ShapeDtypeStruct((samples, height, kept, depth), F32),
            jax.ShapeDtypeStruct((depth, cells), BF),
            jax.ShapeDtypeStruct((encoder_input.shape[3], cells), BF),
        ],
        [pre_second, pre_first, encoder_input, low, high],
        [pltpu.VMEM((2, (samples * height + 8) * kept, LANES), F32)],
    )


def goes_down(way, ways):
    return 1 - lax.axis_index("lat") if ways == 1 else 1 - way


def cross_kernel(mine_ref, got_ref, cross_ref, *strips):
    height = mine_ref.shape[1] - 2
    cross_ref[...] = (mine_ref[...].astype(F32) + got_ref[...].astype(F32)).astype(BF)
    for way, corner_ref in enumerate(strips):
        corner_ref[...] = cross_ref[:, pl.ds((height - 1) * goes_down(way, len(strips)), 3)]


def own_kernel(mine_ref, got_ref, second_ref, first_ref, own_ref, *strips):
    height = second_ref.shape[1]
    own_ref[...] = (mine_ref[...].astype(F32) + got_ref[...].astype(F32)).astype(BF)
    for way, line_ref in enumerate(strips):
        down = goes_down(way, len(strips))
        line_ref[:, 0:3] = own_ref[:, pl.ds((height - 1) * down, 3)]
        line_ref[:, 3:5] = second_ref[:, pl.ds((height - 2) * down, 2)]
        line_ref[:, 5:6] = first_ref[:, pl.ds((height - 1) * down, 1)]


def spread_cross(mine, got, ways):
    samples, _, kept, depth = mine.shape
    strip = jax.ShapeDtypeStruct((samples, 3, kept, depth), BF)
    return run("core_sum_cross", cross_kernel, [jax.ShapeDtypeStruct(mine.shape, BF)] + [strip] * ways, [mine, got])


def spread_own(mine, got, second, first, ways):
    samples, _, kept, depth = mine.shape
    strip = jax.ShapeDtypeStruct((samples, 6, kept, depth), BF)
    return run("core_sum_own", own_kernel, [jax.ShapeDtypeStruct(mine.shape, BF)] + [strip] * ways, [mine, got, second, first])


def latent_kernel(ways, bands, own_ref, cross_ref, *refs):
    strips, refs = refs[: 2 * ways], refs[2 * ways :]
    slope_second_ref, slope_first_ref, grad_ref, away_ref, slope_out, latent, slope_second = refs
    samples, rows, kept, depth = own_ref.shape
    height = rows - 2
    lat = lax.axis_index("lat")
    _, chip = core_and_chip()
    blank = jnp.zeros((samples, kept, depth), F32)
    latent[:, 0] = blank
    latent[:, height + 3] = blank
    latent[:, 1 : height + 3] = own_ref[...].astype(F32) + cross_ref[...].astype(F32)
    slope_second[:, 2 : 2 + height] = slope_second_ref[...]
    slope_out[:, 1 : 1 + height] = slope_first_ref[...]
    for way in range(ways):
        line_ref, corner_ref = strips[2 * way], strips[2 * way + 1]
        below = 1 - lat if ways == 1 else way
        at = (height + 1) * below
        latent[:, pl.ds(at, 3)] += line_ref[:, 0:3].astype(F32) + corner_ref[...].astype(F32)
        slope_second[:, pl.ds((height + 2) * below, 2)] = gelu_slope(line_ref[:, 3:5].astype(F32))
        slope_out[:, pl.ds((height + 1) * below, 1)] = gelu_slope(line_ref[:, 5:6].astype(F32))
    for i in range(height + 4):
        row = lat * height + i - 2
        valid = jnp.logical_and(row >= 0, row < bands * height)
        value = latent[:, i] * slope_second[:, i]
        if i < 2 or i >= height + 2:
            value = jnp.where(valid, value, 0.0)
        grad_ref[:, i] = value.astype(BF)
        if 0 < i < height + 3:
            away_ref[:, i - 1] = jnp.where(chip == 0, value[:, :, LANES:], value[:, :, :LANES]).astype(BF)


def latent_grads(ways, bands, own, cross, strips, slope_second, slope_first):
    samples, rows, kept, depth = own.shape
    return run(
        "latent_grads",
        functools.partial(latent_kernel, ways, bands),
        [
            jax.ShapeDtypeStruct((samples, rows + 2, kept, depth), BF),
            jax.ShapeDtypeStruct((samples, rows, kept, LANES), BF),
            jax.ShapeDtypeStruct((samples, rows, kept, depth), F32),
        ],
        [own, cross, *strips, slope_second, slope_first],
        [
            pltpu.VMEM((samples, rows + 2, kept, depth), F32),
            pltpu.VMEM((samples, rows + 2, kept, depth), F32),
        ],
    )


def encoder_kernel(norm_factor, bands, grad_ref, slope_ref, input_ref, weights_ref, moved_out, mine_ref, other_ref, wide, cat, wide_first):
    samples, tall, kept, depth = grad_ref.shape
    rows = tall - 2
    height = rows - 2
    breadth = kept - 2 * EDGE
    lat = lax.axis_index("lat")
    core, _ = core_and_chip()
    own = 8 + EDGE
    wide[:, :, 8 : 8 + kept, :] = grad_ref[...].astype(F32)
    for v in STEPS:
        lanes = slice((v + 1) * depth, (v + 2) * depth)
        cat[:, :, :, lanes] = wide[:, :, 8 - v : 8 - v + kept + 8, :].astype(BF)
    linear = None
    for u in STEPS:
        weights = jnp.concatenate([weights_ref[3 * (u + 1) + (v + 1)] for v in STEPS], axis=1)
        left = cat[:, 1 - u : 1 - u + rows].reshape(samples * rows * (kept + 8), 3 * depth)
        part = dot_last(left, weights)
        linear = part if linear is None else linear + part
    linear = linear.reshape(samples, rows, kept + 8, depth)
    for i in range(rows):
        row = lat * height + i - 1
        valid = jnp.logical_and(row >= 0, row < bands * height)
        value = linear[:, i, :kept] * slope_ref[:, i]
        if i < 1 or i >= height + 1:
            value = jnp.where(valid, value, 0.0)
        wide_first[:, i, 8 : 8 + kept, :] = value.astype(BF).astype(F32)
    for v in STEPS:
        lanes = slice((v + 1) * depth, (v + 2) * depth)
        moved_out[:, :, :, lanes] = wide_first[:, :, own - v : own - v + breadth, :].astype(BF)
    for u in STEPS:
        right = moved_out[:, 1 - u : 1 - u + height].reshape(samples * height * breadth, 3 * depth)
        part = dot_plain(input_ref[...], right) * norm_factor
        for v in STEPS:
            k = 3 * (u + 1) + (v + 1)
            lower = part[:, (v + 1) * depth : (v + 1) * depth + LANES]
            upper = part[:, (v + 1) * depth + LANES : (v + 2) * depth]
            mine_ref[k] = jnp.where(core == 0, lower, upper).astype(BF)
            other_ref[k] = jnp.where(core == 0, upper, lower).astype(BF)


def encoder(norm_factor, bands, grad, slope, cells_in, w_second):
    samples, tall, kept, depth = grad.shape
    rows, height, breadth = tall - 2, tall - 4, kept - 2 * EDGE
    channels = cells_in.shape[0]
    half = jax.ShapeDtypeStruct((9, channels, LANES), BF)
    return run(
        "encoder_grads",
        functools.partial(encoder_kernel, norm_factor, bands),
        [jax.ShapeDtypeStruct((samples, rows, breadth, 3 * depth), BF), half, half],
        [grad, slope, cells_in, w_second],
        [
            pltpu.VMEM((samples, tall, kept + 24, depth), F32),
            pltpu.VMEM((samples, tall, kept + 8, 3 * depth), BF),
            pltpu.VMEM((samples, rows, kept + 16, depth), F32),
        ],
        flops=2 * 9 * depth * (samples * rows * (kept + 8) * depth + samples * height * breadth * channels),
    )


def second_kernel(norm_factor, shares, grad_ref, got_ref, act_ref, act_got_ref, *refs):
    full_ref, wide, cat = refs[-3:]
    samples, tall, kept, depth = grad_ref.shape
    rows, height, breadth = tall - 2, tall - 4, kept - 2 * EDGE
    core, chip = core_and_chip()
    own = 8 + EDGE
    lower = grad_ref[:, 1 : 1 + rows, :, :LANES].astype(F32)
    upper = grad_ref[:, 1 : 1 + rows, :, LANES:].astype(F32)
    wide[:samples, :, 8 : 8 + kept, :] = jnp.where(chip == 0, lower, upper)
    wide[samples:, :, 8 : 8 + kept, :] = got_ref[...].astype(F32)
    for v in STEPS:
        lanes = slice((v + 1) * LANES, (v + 2) * LANES)
        cat[:, :, :, lanes] = wide[:, :, own - v : own - v + breadth, :].astype(BF)
    cells = samples * height * breadth
    for u in STEPS:
        right = cat[:, 1 - u : 1 - u + height].reshape(2 * cells, 3 * LANES)
        part = dot_plain(act_ref[...], right[:cells]) + dot_plain(act_got_ref[...], right[cells:])
        part = part * norm_factor
        for v in STEPS:
            k = 3 * (u + 1) + (v + 1)
            full_ref[k * depth : (k + 1) * depth, :] = part[:, (v + 1) * LANES : (v + 2) * LANES].astype(BF)
    if len(refs) == 5:
        size = 9 * depth // shares // 2
        for i in range(shares):
            for out_ref, half in ((refs[0], core), (refs[1], 1 - core)):
                out_ref[i] = full_ref[pl.ds(pl.multiple_of((2 * i + half) * size, 16), size), :]


def second_grads(norm_factor, shares, grad, got, act, act_got):
    samples, tall, kept, depth = grad.shape
    rows, height, breadth = tall - 2, tall - 4, kept - 2 * EDGE
    size = 9 * depth // shares // 2
    inside = size % 16 == 0
    half = jax.ShapeDtypeStruct((shares, size, LANES), BF)
    scratch = [
        pltpu.VMEM((2 * samples, rows, kept + 16, LANES), F32),
        pltpu.VMEM((2 * samples, rows, breadth, 3 * LANES), BF),
    ]
    results = run(
        "second_weight_grads",
        functools.partial(second_kernel, norm_factor, shares),
        [half, half] if inside else [jax.ShapeDtypeStruct((9 * depth, LANES), BF)],
        [grad, got, act, act_got],
        [pltpu.VMEM((9 * depth, LANES), BF)] + scratch if inside else scratch,
        flops=2 * 9 * depth * LANES * 2 * samples * height * breadth,
    )
    if inside:
        return results
    halves = results[0].reshape(shares, 2, size, LANES)
    core, _ = core_and_chip()
    return [lax.dynamic_index_in_dim(halves, part, 1, keepdims=False) for part in (core, 1 - core)]


def act_kernel(source_ref, out_ref):
    samples, height, breadth, depth = source_ref.shape
    active = gelu_value(source_ref[...].astype(F32).reshape(samples * height * breadth, depth)).astype(BF).astype(F32)
    out_ref[...] = active.T.astype(BF)


def activated(source):
    samples, height, breadth, depth = source.shape
    return run("activated", act_kernel, [jax.ShapeDtypeStruct((depth, samples * height * breadth), BF)], [source])[0]


def other_band_kernel(*refs):
    band = 1 - lax.rem(lax.axis_index("lat"), 2)
    parts = [t[band].astype(F32) for t in refs[:-1]]
    refs[-1][...] = sum(parts[1:], parts[0]).astype(BF)


def partner(index, step, count):
    return index ^ step if count & (count - 1) == 0 else (index + step) % count


def own_band_kernel(*refs):
    columns = refs[0].shape[1]
    terms, came, outs = refs[: -columns - 2], refs[-columns - 2 : -columns], refs[-columns:]
    band, lon = lax.rem(lax.axis_index("lat"), 2), lax.axis_index("lon")
    for step in range(columns):
        block = partner(lon, step, columns)
        for layer in range(2):
            parts = [t[band, block].astype(F32) for t in terms[layer * len(terms) // 2 : (layer + 1) * len(terms) // 2]]
            outs[step][layer] = sum(parts, came[layer][block].astype(F32)).astype(BF)


def sum_kernel(*refs):
    total = refs[0][...].astype(F32)
    for ref in refs[1:-1]:
        total = total + ref[...].astype(F32)
    refs[-1][...] = total.astype(BF)


def input_kernel(moved_ref, w_first_ref, out_ref):
    samples, rows, breadth, triple = moved_ref.shape
    height = rows - 2
    total = None
    for u in STEPS:
        weights = jnp.concatenate([w_first_ref[3 * (u + 1) + (v + 1)] for v in STEPS], axis=1)
        part = dot_last(moved_ref[:, 1 - u : 1 - u + height].reshape(samples * height * breadth, triple), weights)
        total = part if total is None else total + part
    out_ref[...] = total.astype(BF).reshape(out_ref.shape)


def input_conv(moved, w_first):
    samples, rows, breadth, triple = moved.shape
    shape = (samples, rows - 2, breadth, w_first.shape[1])
    return run(
        "input_conv",
        input_kernel,
        [jax.ShapeDtypeStruct(shape, BF)],
        [moved, w_first],
        flops=2 * 3 * math.prod(shape) * triple,
    )[0]


def chips_kernel(mine_ref, cross_ref, out_ref):
    _, chip = core_and_chip()
    out_ref[0] = (mine_ref[0].astype(F32) + cross_ref[0].astype(F32)).astype(BF)
    out_ref[1] = jnp.where(chip == 0, mine_ref[1], cross_ref[1])
    out_ref[2] = jnp.where(chip == 0, cross_ref[1], mine_ref[1])


def cores_kernel(mine_ref, other_ref, first_ref, second_ref):
    core, _ = core_and_chip()
    rows = mine_ref.shape[1]
    mine, other = (ref[...].astype(F32) for ref in (mine_ref, other_ref))
    for part in range(2):
        value = jnp.where(core == part, mine, other)
        first_ref[pl.ds(part, rows, stride=2), :] = value[0]
        second_ref[pl.ds(2 * rows * part, rows, stride=2), :] = value[1]
        second_ref[pl.ds(2 * rows * part + 1, rows, stride=2), :] = value[2]


def swap(array, axis, flip):
    count = lax.axis_size(axis)
    return lax.ppermute(array, axis, [(i, i ^ flip) for i in range(count)])


def around(array, axis, step, periodic=True):
    count = lax.axis_size(axis)
    pairs = [(i, (i + step) % count) for i in range(count) if periodic or 0 <= i + step < count]
    return lax.ppermute(array, axis, pairs)


def corner(array, step):
    lead, lat = lax.axis_size("lead"), lax.axis_size("lat")
    pairs = []
    for a in range(lead):
        for b in range(lat):
            target = (b ^ 1) if step is None else b + step
            if 0 <= target < lat:
                pairs.append((a * lat + b, (a ^ 2) * lat + target))
    return lax.ppermute(array, ("lead", "lat"), pairs)


def other_band(terms, columns):
    shape = (columns, terms[0].size // LANES // columns // 2, LANES)
    return run("other_band", other_band_kernel, [jax.ShapeDtypeStruct(shape, BF)], [t.reshape(2, *shape) for t in terms])[0]


def pairwise(terms, bands):
    lat = lax.axis_index("lat")
    total = sum(t.reshape(-1, LANES).astype(F32) for t in terms).astype(BF)
    left = bands
    while left > 2:
        left //= 2
        bit = (lat // left) % 2
        halves = total.reshape(2, -1, LANES)
        send = lax.dynamic_index_in_dim(halves, 1 - bit, 0, keepdims=False)
        keep = lax.dynamic_index_in_dim(halves, bit, 0, keepdims=False)
        total = (keep.astype(F32) + swap(send, "lat", left).astype(F32)).astype(BF)
    return total


def near_kernel(second_ref, first_ref, input_ref, low_ref, high_ref, slope_second, slope_first, halo_ref, wide, cells):
    samples, height, breadth, depth = second_ref.shape
    kept = breadth + 2 * EDGE
    batch = low_ref.shape[0] - samples
    for ref, width, first_cell, slope_ref in ((second_ref, 2, 0, slope_second), (first_ref, 1, 4 * height, slope_first)):
        wide[...] = jnp.zeros(wide.shape, F32)
        for s in range(samples):
            for r in range(height):
                at = (s * height + r) * kept + EDGE
                for half in range(2):
                    wide[half, at : at + breadth, :] = ref[s, r, :, half * LANES : (half + 1) * LANES].astype(F32)
            for side, packed_ref in ((0, low_ref), (1, high_ref)):
                packed = packed_ref[batch + s].astype(F32)
                for col in range(width):
                    for half in range(2):
                        here = ((col if width == 2 else 2) * 2 + half) * height
                        value = packed[here : here + height]
                        at = s * height * kept + EDGE + col + (breadth if side else -width)
                        wide[half, pl.ds(at, height, stride=kept), :] = value
                        at = first_cell + (side * width + col) * height
                        cells[s, at : at + height, half * LANES : (half + 1) * LANES] = value
        value = jnp.concatenate([wide[half, : samples * height * kept] for half in range(2)], axis=1)
        slope_ref[...] = gelu_slope(value).reshape(slope_ref.shape)
    half = height // 2
    for part in range(2):
        values = input_ref[:, part * half : (part + 1) * half].reshape(samples, half * breadth, LANES)
        halo_ref[:, : half * breadth, part * LANES : (part + 1) * LANES] = values
    halo_ref[:, half * breadth :] = cells[:, : 6 * height].astype(BF)


def near_parts(pre_second, pre_first, encoder_input, low, high):
    samples, height, breadth, depth = pre_second.shape
    kept = breadth + 2 * EDGE
    slope = jax.ShapeDtypeStruct((samples, height, kept, depth), F32)
    return run(
        "near_parts",
        near_kernel,
        [slope, slope, jax.ShapeDtypeStruct((samples, 6 * height + height * breadth // 2, depth), BF)],
        [pre_second, pre_first, encoder_input, low, high],
        [
            pltpu.VMEM((2, (samples * height + 8) * kept, LANES), F32),
            pltpu.VMEM((samples, 6 * height + 8, depth), F32),
        ],
    )


def far_kernel(first_ref, tile_second, tile_first, slope_second, slope_first, act_out, wide, act):
    samples, height, breadth, depth = first_ref.shape
    kept = breadth + 2 * EDGE
    lat = lax.axis_index("lat")
    for source_ref, slope_ref in ((tile_second, slope_second), (tile_first, slope_first)):
        wide[...] = jnp.zeros(wide.shape, F32)
        for s in range(samples):
            for half in range(2):
                for r in range(height):
                    at = (s * height + r) * kept + EDGE
                    wide[half, at : at + breadth, :] = source_ref[s, r, :, half * LANES : (half + 1) * LANES].astype(F32)
        value = jnp.concatenate([wide[0], wide[1]], axis=1)
        slope_ref[...] = gelu_slope(value).reshape(slope_ref.shape)
    own, other = pl.ds(height * lat, height), pl.ds(height * (1 - lat), height)
    act[:, own] = gelu_value(first_ref[...].astype(F32))
    act[:, other] = gelu_value(tile_first[...].astype(F32))
    act_out[...] = act[...].reshape(act_out.shape[1], depth).T.astype(BF)


def far_parts(pre_first, tile_second, tile_first):
    samples, height, breadth, depth = pre_first.shape
    kept = breadth + 2 * EDGE
    slope = jax.ShapeDtypeStruct((samples, height, kept, depth), F32)
    return run(
        "far_parts",
        far_kernel,
        [slope, slope, jax.ShapeDtypeStruct((depth, 2 * samples * height * breadth), BF)],
        [pre_first, tile_second, tile_first],
        [
            pltpu.VMEM((2, samples * height * kept, LANES), F32),
            pltpu.VMEM((samples, 2 * height, breadth, depth), F32),
        ],
    )


def put_slopes(sample, slope, near_ref, far_ref, halo_ref, width, first_cell):
    _, height, kept, _ = near_ref.shape
    lat = lax.axis_index("lat")
    other = pl.ds(height * (1 - lat), height)
    slope[pl.ds(height * lat, height)] = near_ref[sample]
    slope[other] = far_ref[sample]
    beside = gelu_slope(halo_ref[sample, halo_ref.shape[1] - 6 * height :].astype(F32))
    for side in range(2):
        for col in range(width):
            here = first_cell + (side * width + col) * height
            at = kept - EDGE + col if side else EDGE - width + col
            slope[other, at, :] = beside[here : here + height]


def globe_kernel(sample, near_ref, far_ref, halo_ref, total_ref, line_ref, cat_ref, moved_ref, latent, slope, wide):
    rows, kept, depth = total_ref.shape
    height = rows - 1
    tall = 2 * height
    breadth = kept - 2 * EDGE
    lat = lax.axis_index("lat")
    own = 8 + EDGE
    latent[...] = jnp.zeros(latent.shape, F32)
    latent[pl.ds((height - 1) * lat, rows)] = total_ref[...].astype(F32)
    latent[pl.ds((height - 1) * (1 - lat), rows)] += line_ref[...].astype(F32)
    put_slopes(sample, slope, near_ref, far_ref, halo_ref, 2, 0)
    wide[:, 8 : 8 + kept, :] = (latent[...] * slope[...]).astype(BF).astype(F32)
    for v in STEPS:
        lanes = slice((v + 1) * depth, (v + 2) * depth)
        cat_ref[1 : 1 + tall, :, lanes] = wide[:, 8 - v : 8 - v + kept, :].astype(BF)
        moved_ref[v + 1, 1 : 1 + tall] = wide[:, own - v : own - v + breadth, :].astype(BF)
    for row in (0, tall + 1):
        cat_ref[row] = jnp.zeros(cat_ref.shape[1:], BF)
        moved_ref[:, row] = jnp.zeros(moved_ref.shape[:1] + moved_ref.shape[2:], BF)


def globe(sample, total, line, near, far, halo):
    rows, kept, depth = total.shape
    tall, breadth = 2 * (rows - 1), kept - 2 * EDGE
    return run(
        "latent_grads",
        functools.partial(globe_kernel, sample),
        [
            jax.ShapeDtypeStruct((tall + 2, kept, 3 * depth), BF),
            jax.ShapeDtypeStruct((3, tall + 2, breadth, depth), BF),
        ],
        [near, far, halo, total, line],
        [
            pltpu.VMEM((tall, kept, depth), F32),
            pltpu.VMEM((tall, kept, depth), F32),
            pltpu.VMEM((tall, kept + 24, depth), F32),
        ],
    )


def band_rows(norm_factor, lefts, moved, mine_ref, other_ref):
    channels, cells = lefts[0].shape
    _, padded, breadth, depth = moved[0].shape
    tall = padded - 2
    lat = lax.axis_index("lat")
    core, _ = core_and_chip()
    half = channels // 2

    def put(parts, u, v, start, size):
        total = None
        for left, ref in zip(parts, moved):
            part = dot_plain(left, ref[v + 1, pl.ds(1 - u, tall)].reshape(cells, depth))
            total = part if total is None else total + part
        total = total * norm_factor
        lower, upper = total[:, :LANES], total[:, LANES:]
        here = pl.ds(pl.multiple_of(start, half), size)
        mine_ref[here, :] = jnp.where(core == 0, lower, upper).astype(BF)
        other_ref[here, :] = jnp.where(core == 0, upper, lower).astype(BF)

    for j in range(4):
        (u0, v0), (u1, v1) = (divmod(k, 3) for k in (j, 5 + j))
        put(lefts, u0 - 1 + lat * (u1 - u0), v0 - 1 + lat * (v1 - v0), lat * half + j * channels, channels)
    put([jnp.where(lat == 0, left[:half], left[half:]) for left in lefts], 0, 0, (1 - lat) * 4 * channels, half)


def second_band_kernel(norm_factor, act_ref, *refs):
    moved, (mine_ref, other_ref) = refs[:-2], refs[-2:]
    cells = act_ref.shape[1] // len(moved)
    lefts = [act_ref[:, s * cells : (s + 1) * cells] for s in range(len(moved))]
    band_rows(norm_factor, lefts, moved, mine_ref, other_ref)


def second_band(norm_factor, act, moved):
    half = jax.ShapeDtypeStruct((9 * act.shape[0] // 2, LANES), BF)
    return run("second_weight_grads", functools.partial(second_band_kernel, norm_factor), [half, half], [act, *moved])


def first_kernel(sample, cat_ref, near_ref, far_ref, halo_ref, weights_ref, moved_ref, slope, wide):
    padded, kept, triple = cat_ref.shape
    tall, depth = padded - 2, triple // 3
    breadth = kept - 2 * EDGE
    own = 8 + EDGE
    put_slopes(sample, slope, near_ref, far_ref, halo_ref, 1, 2 * tall)
    linear = None
    for u in STEPS:
        weights = jnp.concatenate([weights_ref[3 * (u + 1) + (v + 1)] for v in STEPS], axis=1)
        part = dot_last(cat_ref[1 - u : 1 - u + tall].reshape(tall * kept, triple), weights)
        linear = part if linear is None else linear + part
    wide[:, 8 : 8 + kept, :] = (linear.reshape(tall, kept, depth) * slope[...]).astype(BF).astype(F32)
    for v in STEPS:
        moved_ref[v + 1, 1 : 1 + tall] = wide[:, own - v : own - v + breadth, :].astype(BF)
    for row in (0, tall + 1):
        moved_ref[:, row] = jnp.zeros(moved_ref.shape[:1] + moved_ref.shape[2:], BF)


def first_grad(sample, cat, near, far, halo, w_second):
    padded, kept, triple = cat.shape
    tall, depth = padded - 2, triple // 3
    return run(
        "second_conv",
        functools.partial(first_kernel, sample),
        [jax.ShapeDtypeStruct((3, padded, kept - 2 * EDGE, depth), BF)],
        [cat, near, far, halo, w_second],
        [pltpu.VMEM((tall, kept, depth), F32), pltpu.VMEM((tall, kept + 16, depth), F32)],
    )[0]


def first_band_kernel(norm_factor, halo_ref, input_ref, *refs):
    moved, (mine_ref, other_ref, cells) = refs[:-3], refs[-3:]
    samples, height, breadth, channels = input_ref.shape
    lat = lax.axis_index("lat")
    cells[:, pl.ds(height * lat, height)] = input_ref[...].astype(F32)
    half = height // 2
    for part in range(2):
        values = halo_ref[:, : half * breadth, part * LANES : (part + 1) * LANES].astype(F32)
        cells[:, pl.ds(height * (1 - lat) + part * half, half)] = values.reshape(samples, half, breadth, LANES)
    lefts = [cells[s].reshape(2 * height * breadth, channels).T.astype(BF) for s in range(samples)]
    band_rows(norm_factor, lefts, moved, mine_ref, other_ref)


def first_band(norm_factor, halo, encoder_input, moved):
    samples, height, breadth, channels = encoder_input.shape
    half = jax.ShapeDtypeStruct((9 * channels // 2, LANES), BF)
    return run(
        "first_weight_grads",
        functools.partial(first_band_kernel, norm_factor),
        [half, half],
        [halo, encoder_input, *moved],
        [pltpu.VMEM((samples, 2 * height, breadth, channels), F32)],
    )


def input_band_kernel(w_first_ref, *refs):
    moved, out_ref = refs[:-1], refs[-1]
    _, height, breadth, channels = out_ref.shape
    depth = moved[0].shape[3]
    lat = lax.axis_index("lat")
    total = None
    for u in STEPS:
        weights = jnp.concatenate([w_first_ref[3 * (u + 1) + (v + 1)] for v in STEPS], axis=1)
        here = pl.ds(height * lat + 1 - u, height)
        left = [jnp.concatenate([ref[v + 1, here].reshape(-1, depth) for v in STEPS], axis=1) for ref in moved]
        part = dot_last(jnp.concatenate(left, axis=0), weights)
        total = part if total is None else total + part
    out_ref[...] = total.astype(BF).reshape(out_ref.shape)


def blocks_kernel(first_mine, first_got, second_mine, second_got, *outs):
    lon = lax.axis_index("lon")
    rows = first_mine.shape[1]
    for step, out_ref in enumerate(outs):
        block = partner(lon, step, len(outs))
        out_ref[:rows] = (first_mine[block].astype(F32) + first_got[block].astype(F32)).astype(BF)
        out_ref[rows:] = (second_mine[block].astype(F32) + second_got[block].astype(F32)).astype(BF)


def halves_kernel(mine_ref, other_ref, first_ref, second_ref):
    core, _ = core_and_chip()
    mine, other = mine_ref[...].astype(F32), other_ref[...].astype(F32)
    rows = mine.shape[0] // 3
    for part in range(2):
        value = jnp.where(core == part, mine, other)
        first_ref[pl.ds(part, rows, stride=2), :] = value[:rows]
        second_ref[pl.ds(part, 2 * rows, stride=2), :] = value[rows:]


def to_partner(array, step):
    count = lax.axis_size("lon")
    return lax.ppermute(array, "lon", [(partner(i, step, count), i) for i in range(count)])


def two_bands(head_grads, head_weights, encoder_input, pre_first, pre_second, w_first, w_second, norm_factor):
    samples, height, breadth, _ = encoder_input.shape
    columns = lax.axis_size("lon")
    tiles = [swap(array, "lat", 1) for array in (pre_second, pre_first)]
    to_right, to_left = pack(head_grads, pre_second, pre_first)
    low = around(to_right, "lon", 1)
    high = around(to_left, "lon", -1)
    head_grads, head_weights, w_second, pre_second, pre_first, encoder_input = stage(
        head_grads, head_weights, w_second, pre_second, pre_first, encoder_input
    )
    inside = inside_conv(head_grads, head_weights, 2 * samples)
    low, high, inside, *tiles = lax.optimization_barrier((low, high, inside, *tiles))
    heads_of = functools.partial(
        head_conv,
        head_grads=head_grads,
        low=low,
        high=high,
        head_weights=head_weights,
        slots=2 * samples,
        rows=height + 1,
    )
    everyone = range(samples)
    got = swap(edges_conv(inside, low, high, head_weights), "lead", 1)
    part_shape = jax.ShapeDtypeStruct(got.shape[1:], BF)
    parts = run("core_sum", core_sum_kernel, [part_shape] * (2 * samples), [heads_of(False, False, 0), got])
    own, cross = parts[0::2], list(parts[1::2])
    near_second, near_first, halo = near_parts(pre_second, pre_first, encoder_input, low, high)
    cross[-1], halo = lax.optimization_barrier((cross[-1], halo))
    cross = [swap(part, "lead", 2) for part in cross]
    halo = swap(halo, "lat", 1)
    cross[-1], halo = lax.optimization_barrier((cross[-1], halo))
    totals = [run("chip_sum", sum_kernel, [part_shape], [own[s], cross[s]])[0] for s in everyone]
    lines = [swap(total, "lat", 1) for total in totals]
    far_second, far_first, act = far_parts(pre_first, *tiles)

    moved_second, moved_first = [], []
    for s in everyone:
        cat, moved = globe(s, totals[s], lines[s], near_second, far_second, halo)
        moved_second.append(moved)
        if s < samples - 1:
            moved_first.append(first_grad(s, cat, near_first, far_first, halo, w_second))
            near_second, moved_first[s] = lax.optimization_barrier((near_second, moved_first[s]))
    second_mine, second_other = second_band(norm_factor, act, moved_second)
    second_got = swap(second_other, "lead", 1)
    moved_first.append(first_grad(samples - 1, cat, near_first, far_first, halo, w_second))
    first_mine, first_other = first_band(norm_factor, halo, encoder_input, moved_first)
    first_got = swap(first_other, "lead", 1)
    input_grad = run(
        "input_conv", input_band_kernel, [jax.ShapeDtypeStruct(encoder_input.shape, BF)], [w_first, *moved_first]
    )[0]

    blocks = [t.reshape(columns, -1, LANES) for t in (first_mine, first_got, second_mine, second_got)]
    rows = blocks[0].shape[1]
    share_shape = jax.ShapeDtypeStruct((3 * rows, LANES), BF)
    shares = run("blocks", blocks_kernel, [share_shape] * columns, blocks)
    parts = [to_partner(shares[step], step) for step in ((2, 1, 3) if columns == 4 else range(1, columns))]
    share = run("share", sum_kernel, [share_shape], [shares[0], *parts])[0]
    both = run("chips", sum_kernel, [share_shape], [share, swap(share, "lead", 2)])[0]
    result_first, result_second = run(
        "cores",
        halves_kernel,
        [jax.ShapeDtypeStruct((2 * rows, LANES), F32), jax.ShapeDtypeStruct((4 * rows, LANES), F32)],
        [both, swap(both, "lead", 1)],
    )
    return input_grad, result_first.reshape(-1), result_second.reshape(-1)


def core_sum_kernel(mine_ref, got_ref, *outs):
    for slot, out_ref in enumerate(outs):
        out_ref[...] = (mine_ref[slot].astype(F32) + got_ref[slot].astype(F32)).astype(BF)


def general(head_grads, head_weights, encoder_input, pre_first, pre_second, w_first, w_second, norm_factor):
    samples, height, breadth, _ = encoder_input.shape
    bands, columns = lax.axis_size("lat"), lax.axis_size("lon")
    to_right, to_left = pack(head_grads, pre_second, pre_first)
    to_right, to_left, to_cross = lax.optimization_barrier((to_right, to_left, pre_first))
    low = around(to_right, "lon", 1)
    high = around(to_left, "lon", -1)
    act_got = activated(swap(to_cross, "lead", 2))
    head_grads, head_weights, w_second, pre_second, pre_first, encoder_input = stage(
        head_grads, head_weights, w_second, pre_second, pre_first, encoder_input
    )
    low, high, act_got = lax.optimization_barrier((low, high, act_got))

    steps = [1, -1]
    heads_of = functools.partial(head_conv, head_grads=head_grads, high=high, head_weights=head_weights, slots=samples, rows=height + 2)
    got_cross = swap(heads_of(True, True, None, low=low), "lead", 1)
    got_own = swap(heads_of(True, False, None, low=low), "lead", 1)
    cross, *angles = spread_cross(heads_of(False, True, None, low=low), got_cross, len(steps))
    low_later, cross, *angles = lax.optimization_barrier((low, cross, *angles))
    cross = swap(cross, "lead", 2)
    angles = [corner(angle, step) for angle, step in zip(angles, steps)]
    second, first, slope_second, slope_first, act, cells_in = saved(pre_second, pre_first, encoder_input, low, high)
    own, *lines = spread_own(heads_of(False, False, None, low=low_later), got_own, second, first, len(steps))
    lines = [swap(line, "lat", 1) if step is None else around(line, "lat", step, False) for line, step in zip(lines, steps)]
    strips = [strip for pair in zip(lines, angles) for strip in pair]

    grad, away, slope = latent_grads(len(steps), bands, own, cross, strips, slope_second, slope_first)
    grad_got = swap(away, "lead", 2)
    moved, first_mine, first_other = encoder(norm_factor, bands, grad, slope, cells_in, w_second)
    input_grad = input_conv(moved, w_first)
    first_got = swap(first_other, "lead", 1)
    second_mine, second_other = second_grads(norm_factor, bands * columns, grad, grad_got, act, act_got)
    second_got = swap(second_other, "lead", 1)

    first_terms = [pairwise([first_mine, first_got], bands)]
    second_terms = [pairwise([second_mine, second_got], bands)]
    first_came = swap(other_band(first_terms, columns), "lat", 1)
    second_came = swap(other_band(second_terms, columns), "lat", 1)
    blocks = [t.reshape(2, columns, -1, LANES) for t in first_terms + second_terms]
    rows = blocks[0].shape[2]
    share_shape = jax.ShapeDtypeStruct((2, rows, LANES), BF)
    shares = run("own_band", own_band_kernel, [share_shape] * columns, blocks + [first_came, second_came])
    parts = [to_partner(shares[step], step) for step in ((2, 1, 3) if columns == 4 else range(1, columns))]
    share = run("share", sum_kernel, [share_shape], [shares[0], *parts])[0]
    both = run("chips", chips_kernel, [jax.ShapeDtypeStruct((3, rows, LANES), BF)], [share, swap(share, "lead", 2)])[0]
    result_first, result_second = run(
        "cores",
        cores_kernel,
        [jax.ShapeDtypeStruct((2 * rows, LANES), F32), jax.ShapeDtypeStruct((4 * rows, LANES), F32)],
        [both, swap(both, "lead", 1)],
    )
    return input_grad, result_first.reshape(-1), result_second.reshape(-1)


def per_device(head_grads, head_weights, encoder_input, pre_first, pre_second, w_first, w_second):
    samples, height, breadth, channels = encoder_input.shape
    bands, columns = lax.axis_size("lat"), lax.axis_size("lon")
    cells_total = samples * lax.axis_size("lead") * height * bands * breadth * columns
    norm_factor = 1.0 / math.sqrt(cells_total)
    plan = two_bands if bands == 2 and 9 * channels // (bands * columns) % 16 == 0 else general
    return plan(head_grads, head_weights, encoder_input, pre_first, pre_second, w_first, w_second, norm_factor)


def solution(mesh):
    in_specs = (
        P("lead", None, "lat", "lon", None),
        P("lead", None, None, None),
        P("lead", "lat", "lon", None),
        P("lead", "lat", "lon", None),
        P("lead", "lat", "lon", None),
        P(),
        P(),
    )
    out_specs = (P("lead", "lat", "lon", None), P(("lat", "lon")), P(("lat", "lon")))
    return jax.shard_map(
        per_device, mesh=mesh, in_specs=in_specs, out_specs=out_specs, check_vma=False
    )
```

```python
import functools
import math

import jax
import jax.numpy as jnp
from jax import lax
from jax.experimental import pallas as pl
from jax.experimental.pallas import tpu as pltpu
from jax.sharding import PartitionSpec as P

BF = jnp.bfloat16
F32 = jnp.float32
STEPS = (-1, 0, 1)
EDGE = 4
LANES = 128
VMEM_BYTES = 24 * 1024 * 1024


def erf_part(values):
    return 0.5 * (1.0 + lax.erf(values * 0.7071067811865476))


def gelu_slope(values):
    return erf_part(values) + values * jnp.exp(-0.5 * values * values) * 0.3989422804014327


def gelu_value(values):
    return values * erf_part(values)


def dot_last(left, right):
    return lax.dot_general(left, right, (((1,), (1,)), ((), ())), preferred_element_type=F32)


def dot_plain(left, right):
    return lax.dot_general(left, right, (((1,), (0,)), ((), ())), preferred_element_type=F32)


def core_and_chip():
    lead = lax.axis_index("lead")
    return lax.rem(lead, 2), lax.div(lead, 2)


def run(name, kernel, out_shape, arrays, scratch=(), flops=0, far=False):
    specs = [pl.BlockSpec(memory_space=pltpu.HBM if far else pltpu.VMEM)] * len(arrays)
    if far:
        arrays = [pltpu.with_memory_space_constraint(a, pltpu.HBM) for a in arrays]
    touched = sum(a.size * a.dtype.itemsize for a in arrays)
    touched += sum(math.prod(s.shape) * s.dtype.itemsize for s in out_shape)
    return pl.pallas_call(
        kernel,
        name=name,
        out_shape=out_shape,
        in_specs=specs,
        out_specs=[pl.BlockSpec(memory_space=pltpu.VMEM)] * len(out_shape),
        scratch_shapes=list(scratch),
        compiler_params=pltpu.CompilerParams(vmem_limit_bytes=VMEM_BYTES),
        cost_estimate=pl.CostEstimate(flops=1, bytes_accessed=1, transcendentals=0),
    )(*arrays)


def pack_kernel(grads_far, second_far, first_far, right_ref, left_ref, grads_near, second_near, first_near, edges, edges_wide, packed, sems):
    heads, batch, height, breadth, _ = grads_far.shape
    samples = second_far.shape[0]
    rows = 6 * height
    copies = []
    for side in range(2):
        columns = pl.ds(breadth - 16 if side == 0 else 0, 16)
        for j, (far, near) in enumerate(((grads_far, grads_near), (second_far, second_near), (first_far, first_near))):
            source = far.at[:, :, :, columns, :] if j == 0 else far.at[:, :, columns, :]
            copies.append(pltpu.make_async_copy(source, near.at[side], sems.at[side, j]))
            copies[-1].start()
    for copy in copies:
        copy.wait()
    for side, out_ref in ((0, right_ref), (1, left_ref)):
        start = 8 if side == 0 else 0
        grads_ref, second_ref, first_ref = grads_near.at[side], second_near.at[side], first_near.at[side]
        for h in range(heads):
            for b in range(batch):
                block = grads_ref[h, b].astype(F32)[:, start : start + 8, :]
                edges[(h * batch + b) * height * 8 : (h * batch + b + 1) * height * 8, :] = block.reshape(height * 8, LANES)
        for j, ref in enumerate((second_ref, first_ref)):
            for s in range(samples):
                block = ref[s].astype(F32)[:, start : start + 8, :]
                at = (j * samples + s) * height * 8
                for half in range(2):
                    lanes = slice(half * LANES, (half + 1) * LANES)
                    edges_wide[half, at : at + height * 8, :] = block[:, :, lanes].reshape(height * 8, LANES)
        for b in range(batch):
            for col in range(3):
                inner = 5 + col if side == 0 else col
                for h in range(heads):
                    at = b * rows + (col * 2 + h) * height
                    packed[at : at + height, :] = edges[pl.ds((h * batch + b) * height * 8 + inner, height, stride=8), :]
        for s in range(samples):
            for q in range(3):
                j, col, width = (0, q, 2) if q < 2 else (1, 0, 1)
                inner = 8 - width + col if side == 0 else col
                for half in range(2):
                    at = (batch + s) * rows + (q * 2 + half) * height
                    packed[at : at + height, :] = edges_wide[
                        half, pl.ds((j * samples + s) * height * 8 + inner, height, stride=8), :
                    ]
        out_ref[...] = packed[: (batch + samples) * rows].astype(BF).reshape(out_ref.shape)


def pack(head_grads, pre_second, pre_first):
    heads, batch, height, _, _ = head_grads.shape
    samples = pre_second.shape[0]
    shape = jax.ShapeDtypeStruct((batch + samples, 6 * height, LANES), BF)
    return run(
        "pack_columns",
        pack_kernel,
        [shape, shape],
        [head_grads, pre_second, pre_first],
        [
            pltpu.VMEM((2, heads, batch, height, 16, LANES), BF),
            pltpu.VMEM((2, samples, height, 16, 2 * LANES), BF),
            pltpu.VMEM((2, samples, height, 16, 2 * LANES), BF),
            pltpu.VMEM((heads * batch * height * 8 + 64, LANES), F32),
            pltpu.VMEM((2, 2 * samples * height * 8 + 64, LANES), F32),
            pltpu.VMEM(((batch + samples) * 6 * height + 16, LANES), F32),
            pltpu.SemaphoreType.DMA((2, 3)),
        ],
        far=True,
    )


def stage_kernel(*refs):
    count = len(refs) // 2
    sems = refs[-1]
    copies = [pltpu.make_async_copy(refs[i], refs[count + i], sems.at[i]) for i in range(count)]
    for copy in copies:
        copy.start()
    for copy in copies:
        copy.wait()


def stage(*arrays):
    shapes = [pltpu.VMEM(a.shape, a.dtype) for a in arrays]
    return run("stage", stage_kernel, shapes, list(arrays), [pltpu.SemaphoreType.DMA((len(arrays),))], far=True, flops=1 << 30)


def heads_kernel(other_core, other_chip, sample, samples, grads_ref, low_ref, high_ref, weights_ref, out_ref, wide, shifted, total):
    heads, batch, height, breadth, _ = grads_ref.shape
    slots, _, kept, depth = out_ref.shape
    pitch = kept + 16
    own = 8 + EDGE
    core, chip = core_and_chip()
    core = 1 - core if other_core else core
    for slot in range(slots):
        if sample is None:
            group, s = 1 - chip if other_chip else chip, slot
        else:
            group, s = 1 - chip if slot % 2 else chip, sample + slot // 2
        b = (2 * group + core) * samples + s
        low = low_ref[b].astype(F32)
        high = high_ref[b].astype(F32)
        for r in range(height):
            at = (slot * height + r) * pitch + own
            for h in range(heads):
                wide[h, at : at + breadth, :] = grads_ref[h, b, r].astype(F32)
        for col in range(3):
            for h in range(heads):
                here = (col * 2 + h) * height
                at = slot * height * pitch + own + col
                wide[h, pl.ds(at - 3, height, stride=pitch), :] = low[here : here + height]
                wide[h, pl.ds(at + breadth, height, stride=pitch), :] = high[here : here + height]
        for v in STEPS:
            for h in range(heads):
                starts = [(slot * height + r) * pitch + 8 - v for r in range(height)]
                moved = jnp.concatenate([wide[h, at : at + kept, :] for at in starts], axis=0).astype(BF)
                lane = ((v + 1) * heads + h) * LANES
                shifted[slot * height * kept : (slot + 1) * height * kept, lane : lane + LANES] = moved
    total[:, height:, :, :] = jnp.zeros((slots, 2, kept, depth), F32)
    for u in STEPS:
        weights = jnp.concatenate(
            [weights_ref[h, 3 * (u + 1) + (v + 1)] for v in STEPS for h in range(heads)], axis=1
        )
        part = dot_last(shifted[...], weights).reshape(slots, height, kept, depth)
        if u == -1:
            total[:, :height] = part
        else:
            total[:, 1 + u : 1 + u + height] += part
    if out_ref.shape[1] == height + 2:
        out_ref[...] = total[...].astype(BF)
    else:
        out_ref[...] = total[:, pl.ds(1 - lax.axis_index("lat"), height + 1)].astype(BF)


def head_conv(other_core, other_chip, sample, head_grads, low, high, head_weights, slots, rows):
    samples = head_grads.shape[1] // lax.axis_size("lead")
    heads, batch, height, breadth, _ = head_grads.shape
    depth = head_weights.shape[2]
    kept = breadth + 2 * EDGE
    return run(
        "head_conv",
        functools.partial(heads_kernel, other_core, other_chip, sample, samples),
        [jax.ShapeDtypeStruct((slots, rows, kept, depth), BF)],
        [head_grads, low, high, head_weights],
        [
            pltpu.VMEM((heads, (slots * height + 8) * (kept + 16), LANES), F32),
            pltpu.VMEM((slots * height * kept, 3 * heads * LANES), BF),
            pltpu.VMEM((slots, height + 2, kept, depth), F32),
        ],
        flops=2 * slots * height * kept * 9 * heads * LANES * depth,
    )[0]


def inside_kernel(samples, grads_ref, weights_ref, total_ref, wide, shifted):
    heads, _, height, breadth, _ = grads_ref.shape
    slots, _, kept, depth = total_ref.shape
    pitch = kept + 16
    own = 8 + EDGE
    core, chip = core_and_chip()
    blank = jnp.zeros((height, LANES), F32)
    for slot in range(slots):
        group, s = 1 - chip if slot % 2 else chip, slot // 2
        b = (2 * group + 1 - core) * samples + s
        for h in range(heads):
            for r in range(height):
                at = (slot * height + r) * pitch + own
                wide[h, at : at + breadth, :] = grads_ref[h, b, r].astype(F32)
            for col in range(3):
                at = slot * height * pitch + own + col
                wide[h, pl.ds(at - 3, height, stride=pitch), :] = blank
                wide[h, pl.ds(at + breadth, height, stride=pitch), :] = blank
            for v in STEPS:
                starts = [(slot * height + r) * pitch + 8 - v for r in range(height)]
                moved = jnp.concatenate([wide[h, at : at + kept, :] for at in starts], axis=0).astype(BF)
                lane = ((v + 1) * heads + h) * LANES
                shifted[slot * height * kept : (slot + 1) * height * kept, lane : lane + LANES] = moved
    total_ref[:, height:, :, :] = jnp.zeros((slots, 2, kept, depth), F32)
    for u in STEPS:
        weights = jnp.concatenate(
            [weights_ref[h, 3 * (u + 1) + (v + 1)] for v in STEPS for h in range(heads)], axis=1
        )
        part = dot_last(shifted[...], weights).reshape(slots, height, kept, depth)
        if u == -1:
            total_ref[:, :height] = part
        else:
            total_ref[:, 1 + u : 1 + u + height] += part


def edges_kernel(samples, inside_ref, low_ref, high_ref, weights_ref, own_out, cross_out, wide, shifted, total):
    slots, rows, kept, depth = inside_ref.shape
    height, heads, pitch = rows - 2, weights_ref.shape[0], 24
    core, chip = core_and_chip()
    wide[...] = jnp.zeros(wide.shape, F32)
    total[...] = inside_ref[...]
    for side, packed_ref in ((0, low_ref), (1, high_ref)):
        for slot in range(slots):
            group, s = 1 - chip if slot % 2 else chip, slot // 2
            packed = packed_ref[(2 * group + 1 - core) * samples + s].astype(F32)
            first = (side * slots + slot) * height
            for h in range(heads):
                for col in range(3):
                    here = (col * 2 + h) * height
                    at = first * pitch + 9 + 3 * side + col
                    wide[h, pl.ds(at, height, stride=pitch), :] = packed[here : here + height]
                for v in STEPS:
                    starts = [(first + r) * pitch + 8 - v for r in range(height)]
                    moved = jnp.concatenate([wide[h, at : at + 8, :] for at in starts], axis=0).astype(BF)
                    lane = ((v + 1) * heads + h) * LANES
                    shifted[first * 8 : (first + height) * 8, lane : lane + LANES] = moved
    for u in STEPS:
        weights = jnp.concatenate(
            [weights_ref[h, 3 * (u + 1) + (v + 1)] for v in STEPS for h in range(heads)], axis=1
        )
        part = dot_last(shifted[...], weights).reshape(2, slots, height, 8, depth)
        total[:, 1 + u : 1 + u + height, :8] += part[0]
        total[:, 1 + u : 1 + u + height, kept - 8 :] += part[1]
    here = pl.ds(1 - lax.axis_index("lat"), height + 1)
    for s in range(samples):
        own_out[s] = total[2 * s, here].astype(BF)
        cross_out[s] = total[2 * s + 1, here].astype(BF)


def inside_conv(head_grads, head_weights, slots):
    samples = head_grads.shape[1] // lax.axis_size("lead")
    heads, _, height, breadth, _ = head_grads.shape
    kept = breadth + 2 * EDGE
    return run(
        "head_conv_inside",
        functools.partial(inside_kernel, samples),
        [jax.ShapeDtypeStruct((slots, height + 2, kept, head_weights.shape[2]), F32)],
        [head_grads, head_weights],
        [
            pltpu.VMEM((heads, (slots * height + 8) * (kept + 16), LANES), F32),
            pltpu.VMEM((slots * height * kept, 3 * heads * LANES), BF),
        ],
    )[0]


def edges_conv(inside, low, high, head_weights):
    slots, rows, kept, depth = inside.shape
    samples, heads, height = slots // 2, head_weights.shape[0], rows - 2
    return run(
        "head_conv_edges",
        functools.partial(edges_kernel, samples),
        [jax.ShapeDtypeStruct((samples, rows - 1, kept, depth), BF)] * 2,
        [inside, low, high, head_weights],
        [
            pltpu.VMEM((heads, (2 * slots * height + 8) * 24, LANES), F32),
            pltpu.VMEM((2 * slots * height * 8, 3 * heads * LANES), BF),
            pltpu.VMEM((slots, rows, kept, depth), F32),
        ],
    )


def saved_kernel(second_ref, first_ref, input_ref, low_ref, high_ref, second_out, first_out, slope_second, slope_first, act_out, input_out, wide):
    samples, height, breadth, depth = second_ref.shape
    kept = breadth + 2 * EDGE
    batch = low_ref.shape[0] - samples
    for ref, width, out_ref, slope_ref in (
        (second_ref, 2, second_out, slope_second),
        (first_ref, 1, first_out, slope_first),
    ):
        wide[...] = jnp.zeros(wide.shape, F32)
        for s in range(samples):
            for r in range(height):
                at = (s * height + r) * kept + EDGE
                for half in range(2):
                    lanes = slice(half * LANES, (half + 1) * LANES)
                    wide[half, at : at + breadth, :] = ref[s, r, :, lanes].astype(F32)
            low = low_ref[batch + s].astype(F32)
            high = high_ref[batch + s].astype(F32)
            for col in range(width):
                for half in range(2):
                    here = ((col if width == 2 else 2) * 2 + half) * height
                    at = s * height * kept + EDGE + col
                    wide[half, pl.ds(at - width, height, stride=kept), :] = low[here : here + height]
                    wide[half, pl.ds(at + breadth, height, stride=kept), :] = high[here : here + height]
        value = jnp.concatenate([wide[half, : samples * height * kept] for half in range(2)], axis=1)
        out_ref[...] = value.astype(BF).reshape(out_ref.shape)
        slope_ref[...] = gelu_slope(value).reshape(slope_ref.shape)
    active = gelu_value(first_ref[...].astype(F32).reshape(samples * height * breadth, depth)).astype(BF).astype(F32)
    act_out[...] = active.T.astype(BF)
    cells = input_ref[...].astype(F32).reshape(samples * height * breadth, input_ref.shape[3])
    input_out[...] = cells.T.astype(BF)


def saved(pre_second, pre_first, encoder_input, low, high):
    samples, height, breadth, depth = pre_second.shape
    kept = breadth + 2 * EDGE
    cells = samples * height * breadth
    return run(
        "saved_parts",
        saved_kernel,
        [
            jax.ShapeDtypeStruct((samples, height, kept, depth), BF),
            jax.ShapeDtypeStruct((samples, height, kept, depth), BF),
            jax.ShapeDtypeStruct((samples, height, kept, depth), F32),
            jax.ShapeDtypeStruct((samples, height, kept, depth), F32),
            jax.ShapeDtypeStruct((depth, cells), BF),
            jax.ShapeDtypeStruct((encoder_input.shape[3], cells), BF),
        ],
        [pre_second, pre_first, encoder_input, low, high],
        [pltpu.VMEM((2, (samples * height + 8) * kept, LANES), F32)],
    )


def goes_down(way, ways):
    return 1 - lax.axis_index("lat") if ways == 1 else 1 - way


def cross_kernel(mine_ref, got_ref, cross_ref, *strips):
    height = mine_ref.shape[1] - 2
    cross_ref[...] = (mine_ref[...].astype(F32) + got_ref[...].astype(F32)).astype(BF)
    for way, corner_ref in enumerate(strips):
        corner_ref[...] = cross_ref[:, pl.ds((height - 1) * goes_down(way, len(strips)), 3)]


def own_kernel(mine_ref, got_ref, second_ref, first_ref, own_ref, *strips):
    height = second_ref.shape[1]
    own_ref[...] = (mine_ref[...].astype(F32) + got_ref[...].astype(F32)).astype(BF)
    for way, line_ref in enumerate(strips):
        down = goes_down(way, len(strips))
        line_ref[:, 0:3] = own_ref[:, pl.ds((height - 1) * down, 3)]
        line_ref[:, 3:5] = second_ref[:, pl.ds((height - 2) * down, 2)]
        line_ref[:, 5:6] = first_ref[:, pl.ds((height - 1) * down, 1)]


def spread_cross(mine, got, ways):
    samples, _, kept, depth = mine.shape
    strip = jax.ShapeDtypeStruct((samples, 3, kept, depth), BF)
    return run("core_sum_cross", cross_kernel, [jax.ShapeDtypeStruct(mine.shape, BF)] + [strip] * ways, [mine, got])


def spread_own(mine, got, second, first, ways):
    samples, _, kept, depth = mine.shape
    strip = jax.ShapeDtypeStruct((samples, 6, kept, depth), BF)
    return run("core_sum_own", own_kernel, [jax.ShapeDtypeStruct(mine.shape, BF)] + [strip] * ways, [mine, got, second, first])


def latent_kernel(ways, bands, own_ref, cross_ref, *refs):
    strips, refs = refs[: 2 * ways], refs[2 * ways :]
    slope_second_ref, slope_first_ref, grad_ref, away_ref, slope_out, latent, slope_second = refs
    samples, rows, kept, depth = own_ref.shape
    height = rows - 2
    lat = lax.axis_index("lat")
    _, chip = core_and_chip()
    blank = jnp.zeros((samples, kept, depth), F32)
    latent[:, 0] = blank
    latent[:, height + 3] = blank
    latent[:, 1 : height + 3] = own_ref[...].astype(F32) + cross_ref[...].astype(F32)
    slope_second[:, 2 : 2 + height] = slope_second_ref[...]
    slope_out[:, 1 : 1 + height] = slope_first_ref[...]
    for way in range(ways):
        line_ref, corner_ref = strips[2 * way], strips[2 * way + 1]
        below = 1 - lat if ways == 1 else way
        at = (height + 1) * below
        latent[:, pl.ds(at, 3)] += line_ref[:, 0:3].astype(F32) + corner_ref[...].astype(F32)
        slope_second[:, pl.ds((height + 2) * below, 2)] = gelu_slope(line_ref[:, 3:5].astype(F32))
        slope_out[:, pl.ds((height + 1) * below, 1)] = gelu_slope(line_ref[:, 5:6].astype(F32))
    for i in range(height + 4):
        row = lat * height + i - 2
        valid = jnp.logical_and(row >= 0, row < bands * height)
        value = latent[:, i] * slope_second[:, i]
        if i < 2 or i >= height + 2:
            value = jnp.where(valid, value, 0.0)
        grad_ref[:, i] = value.astype(BF)
        if 0 < i < height + 3:
            away_ref[:, i - 1] = jnp.where(chip == 0, value[:, :, LANES:], value[:, :, :LANES]).astype(BF)


def latent_grads(ways, bands, own, cross, strips, slope_second, slope_first):
    samples, rows, kept, depth = own.shape
    return run(
        "latent_grads",
        functools.partial(latent_kernel, ways, bands),
        [
            jax.ShapeDtypeStruct((samples, rows + 2, kept, depth), BF),
            jax.ShapeDtypeStruct((samples, rows, kept, LANES), BF),
            jax.ShapeDtypeStruct((samples, rows, kept, depth), F32),
        ],
        [own, cross, *strips, slope_second, slope_first],
        [
            pltpu.VMEM((samples, rows + 2, kept, depth), F32),
            pltpu.VMEM((samples, rows + 2, kept, depth), F32),
        ],
    )


def encoder_kernel(norm_factor, bands, grad_ref, slope_ref, input_ref, weights_ref, moved_out, mine_ref, other_ref, wide, cat, wide_first):
    samples, tall, kept, depth = grad_ref.shape
    rows = tall - 2
    height = rows - 2
    breadth = kept - 2 * EDGE
    lat = lax.axis_index("lat")
    core, _ = core_and_chip()
    own = 8 + EDGE
    wide[:, :, 8 : 8 + kept, :] = grad_ref[...].astype(F32)
    for v in STEPS:
        lanes = slice((v + 1) * depth, (v + 2) * depth)
        cat[:, :, :, lanes] = wide[:, :, 8 - v : 8 - v + kept + 8, :].astype(BF)
    linear = None
    for u in STEPS:
        weights = jnp.concatenate([weights_ref[3 * (u + 1) + (v + 1)] for v in STEPS], axis=1)
        left = cat[:, 1 - u : 1 - u + rows].reshape(samples * rows * (kept + 8), 3 * depth)
        part = dot_last(left, weights)
        linear = part if linear is None else linear + part
    linear = linear.reshape(samples, rows, kept + 8, depth)
    for i in range(rows):
        row = lat * height + i - 1
        valid = jnp.logical_and(row >= 0, row < bands * height)
        value = linear[:, i, :kept] * slope_ref[:, i]
        if i < 1 or i >= height + 1:
            value = jnp.where(valid, value, 0.0)
        wide_first[:, i, 8 : 8 + kept, :] = value.astype(BF).astype(F32)
    for v in STEPS:
        lanes = slice((v + 1) * depth, (v + 2) * depth)
        moved_out[:, :, :, lanes] = wide_first[:, :, own - v : own - v + breadth, :].astype(BF)
    for u in STEPS:
        right = moved_out[:, 1 - u : 1 - u + height].reshape(samples * height * breadth, 3 * depth)
        part = dot_plain(input_ref[...], right) * norm_factor
        for v in STEPS:
            k = 3 * (u + 1) + (v + 1)
            lower = part[:, (v + 1) * depth : (v + 1) * depth + LANES]
            upper = part[:, (v + 1) * depth + LANES : (v + 2) * depth]
            mine_ref[k] = jnp.where(core == 0, lower, upper).astype(BF)
            other_ref[k] = jnp.where(core == 0, upper, lower).astype(BF)


def encoder(norm_factor, bands, grad, slope, cells_in, w_second):
    samples, tall, kept, depth = grad.shape
    rows, height, breadth = tall - 2, tall - 4, kept - 2 * EDGE
    channels = cells_in.shape[0]
    half = jax.ShapeDtypeStruct((9, channels, LANES), BF)
    return run(
        "encoder_grads",
        functools.partial(encoder_kernel, norm_factor, bands),
        [jax.ShapeDtypeStruct((samples, rows, breadth, 3 * depth), BF), half, half],
        [grad, slope, cells_in, w_second],
        [
            pltpu.VMEM((samples, tall, kept + 24, depth), F32),
            pltpu.VMEM((samples, tall, kept + 8, 3 * depth), BF),
            pltpu.VMEM((samples, rows, kept + 16, depth), F32),
        ],
        flops=2 * 9 * depth * (samples * rows * (kept + 8) * depth + samples * height * breadth * channels),
    )


def second_kernel(norm_factor, shares, grad_ref, got_ref, act_ref, act_got_ref, *refs):
    full_ref, wide, cat = refs[-3:]
    samples, tall, kept, depth = grad_ref.shape
    rows, height, breadth = tall - 2, tall - 4, kept - 2 * EDGE
    core, chip = core_and_chip()
    own = 8 + EDGE
    lower = grad_ref[:, 1 : 1 + rows, :, :LANES].astype(F32)
    upper = grad_ref[:, 1 : 1 + rows, :, LANES:].astype(F32)
    wide[:samples, :, 8 : 8 + kept, :] = jnp.where(chip == 0, lower, upper)
    wide[samples:, :, 8 : 8 + kept, :] = got_ref[...].astype(F32)
    for v in STEPS:
        lanes = slice((v + 1) * LANES, (v + 2) * LANES)
        cat[:, :, :, lanes] = wide[:, :, own - v : own - v + breadth, :].astype(BF)
    cells = samples * height * breadth
    for u in STEPS:
        right = cat[:, 1 - u : 1 - u + height].reshape(2 * cells, 3 * LANES)
        part = dot_plain(act_ref[...], right[:cells]) + dot_plain(act_got_ref[...], right[cells:])
        part = part * norm_factor
        for v in STEPS:
            k = 3 * (u + 1) + (v + 1)
            full_ref[k * depth : (k + 1) * depth, :] = part[:, (v + 1) * LANES : (v + 2) * LANES].astype(BF)
    if len(refs) == 5:
        size = 9 * depth // shares // 2
        for i in range(shares):
            for out_ref, half in ((refs[0], core), (refs[1], 1 - core)):
                out_ref[i] = full_ref[pl.ds(pl.multiple_of((2 * i + half) * size, 16), size), :]


def second_grads(norm_factor, shares, grad, got, act, act_got):
    samples, tall, kept, depth = grad.shape
    rows, height, breadth = tall - 2, tall - 4, kept - 2 * EDGE
    size = 9 * depth // shares // 2
    inside = size % 16 == 0
    half = jax.ShapeDtypeStruct((shares, size, LANES), BF)
    scratch = [
        pltpu.VMEM((2 * samples, rows, kept + 16, LANES), F32),
        pltpu.VMEM((2 * samples, rows, breadth, 3 * LANES), BF),
    ]
    results = run(
        "second_weight_grads",
        functools.partial(second_kernel, norm_factor, shares),
        [half, half] if inside else [jax.ShapeDtypeStruct((9 * depth, LANES), BF)],
        [grad, got, act, act_got],
        [pltpu.VMEM((9 * depth, LANES), BF)] + scratch if inside else scratch,
        flops=2 * 9 * depth * LANES * 2 * samples * height * breadth,
    )
    if inside:
        return results
    halves = results[0].reshape(shares, 2, size, LANES)
    core, _ = core_and_chip()
    return [lax.dynamic_index_in_dim(halves, part, 1, keepdims=False) for part in (core, 1 - core)]


def act_kernel(source_ref, out_ref):
    samples, height, breadth, depth = source_ref.shape
    active = gelu_value(source_ref[...].astype(F32).reshape(samples * height * breadth, depth)).astype(BF).astype(F32)
    out_ref[...] = active.T.astype(BF)


def activated(source):
    samples, height, breadth, depth = source.shape
    return run("activated", act_kernel, [jax.ShapeDtypeStruct((depth, samples * height * breadth), BF)], [source])[0]


def other_band_kernel(*refs):
    band = 1 - lax.rem(lax.axis_index("lat"), 2)
    parts = [t[band].astype(F32) for t in refs[:-1]]
    refs[-1][...] = sum(parts[1:], parts[0]).astype(BF)


def partner(index, step, count):
    return index ^ step if count & (count - 1) == 0 else (index + step) % count


def own_band_kernel(*refs):
    columns = refs[0].shape[1]
    terms, came, outs = refs[: -columns - 2], refs[-columns - 2 : -columns], refs[-columns:]
    band, lon = lax.rem(lax.axis_index("lat"), 2), lax.axis_index("lon")
    for step in range(columns):
        block = partner(lon, step, columns)
        for layer in range(2):
            parts = [t[band, block].astype(F32) for t in terms[layer * len(terms) // 2 : (layer + 1) * len(terms) // 2]]
            outs[step][layer] = sum(parts, came[layer][block].astype(F32)).astype(BF)


def sum_kernel(*refs):
    total = refs[0][...].astype(F32)
    for ref in refs[1:-1]:
        total = total + ref[...].astype(F32)
    refs[-1][...] = total.astype(BF)


def input_kernel(moved_ref, w_first_ref, out_ref):
    samples, rows, breadth, triple = moved_ref.shape
    height = rows - 2
    total = None
    for u in STEPS:
        weights = jnp.concatenate([w_first_ref[3 * (u + 1) + (v + 1)] for v in STEPS], axis=1)
        part = dot_last(moved_ref[:, 1 - u : 1 - u + height].reshape(samples * height * breadth, triple), weights)
        total = part if total is None else total + part
    out_ref[...] = total.astype(BF).reshape(out_ref.shape)


def input_conv(moved, w_first):
    samples, rows, breadth, triple = moved.shape
    shape = (samples, rows - 2, breadth, w_first.shape[1])
    return run(
        "input_conv",
        input_kernel,
        [jax.ShapeDtypeStruct(shape, BF)],
        [moved, w_first],
        flops=2 * 3 * math.prod(shape) * triple,
    )[0]


def chips_kernel(mine_ref, cross_ref, out_ref):
    _, chip = core_and_chip()
    out_ref[0] = (mine_ref[0].astype(F32) + cross_ref[0].astype(F32)).astype(BF)
    out_ref[1] = jnp.where(chip == 0, mine_ref[1], cross_ref[1])
    out_ref[2] = jnp.where(chip == 0, cross_ref[1], mine_ref[1])


def cores_kernel(mine_ref, other_ref, first_ref, second_ref):
    core, _ = core_and_chip()
    rows = mine_ref.shape[1]
    mine, other = (ref[...].astype(F32) for ref in (mine_ref, other_ref))
    for part in range(2):
        value = jnp.where(core == part, mine, other)
        first_ref[pl.ds(part, rows, stride=2), :] = value[0]
        second_ref[pl.ds(2 * rows * part, rows, stride=2), :] = value[1]
        second_ref[pl.ds(2 * rows * part + 1, rows, stride=2), :] = value[2]


def swap(array, axis, flip):
    count = lax.axis_size(axis)
    return lax.ppermute(array, axis, [(i, i ^ flip) for i in range(count)])


def around(array, axis, step, periodic=True):
    count = lax.axis_size(axis)
    pairs = [(i, (i + step) % count) for i in range(count) if periodic or 0 <= i + step < count]
    return lax.ppermute(array, axis, pairs)


def corner(array, step):
    lead, lat = lax.axis_size("lead"), lax.axis_size("lat")
    pairs = []
    for a in range(lead):
        for b in range(lat):
            target = (b ^ 1) if step is None else b + step
            if 0 <= target < lat:
                pairs.append((a * lat + b, (a ^ 2) * lat + target))
    return lax.ppermute(array, ("lead", "lat"), pairs)


def other_band(terms, columns):
    shape = (columns, terms[0].size // LANES // columns // 2, LANES)
    return run("other_band", other_band_kernel, [jax.ShapeDtypeStruct(shape, BF)], [t.reshape(2, *shape) for t in terms])[0]


def pairwise(terms, bands):
    lat = lax.axis_index("lat")
    total = sum(t.reshape(-1, LANES).astype(F32) for t in terms).astype(BF)
    left = bands
    while left > 2:
        left //= 2
        bit = (lat // left) % 2
        halves = total.reshape(2, -1, LANES)
        send = lax.dynamic_index_in_dim(halves, 1 - bit, 0, keepdims=False)
        keep = lax.dynamic_index_in_dim(halves, bit, 0, keepdims=False)
        total = (keep.astype(F32) + swap(send, "lat", left).astype(F32)).astype(BF)
    return total


def near_kernel(second_ref, first_ref, input_ref, low_ref, high_ref, slope_second, slope_first, halo_ref, wide, cells):
    samples, height, breadth, depth = second_ref.shape
    kept = breadth + 2 * EDGE
    batch = low_ref.shape[0] - samples
    for ref, width, first_cell, slope_ref in ((second_ref, 2, 0, slope_second), (first_ref, 1, 4 * height, slope_first)):
        wide[...] = jnp.zeros(wide.shape, F32)
        for s in range(samples):
            for r in range(height):
                at = (s * height + r) * kept + EDGE
                for half in range(2):
                    wide[half, at : at + breadth, :] = ref[s, r, :, half * LANES : (half + 1) * LANES].astype(F32)
            for side, packed_ref in ((0, low_ref), (1, high_ref)):
                packed = packed_ref[batch + s].astype(F32)
                for col in range(width):
                    for half in range(2):
                        here = ((col if width == 2 else 2) * 2 + half) * height
                        value = packed[here : here + height]
                        at = s * height * kept + EDGE + col + (breadth if side else -width)
                        wide[half, pl.ds(at, height, stride=kept), :] = value
                        at = first_cell + (side * width + col) * height
                        cells[s, at : at + height, half * LANES : (half + 1) * LANES] = value
        value = jnp.concatenate([wide[half, : samples * height * kept] for half in range(2)], axis=1)
        slope_ref[...] = gelu_slope(value).reshape(slope_ref.shape)
    half = height // 2
    for part in range(2):
        values = input_ref[:, part * half : (part + 1) * half].reshape(samples, half * breadth, LANES)
        halo_ref[:, : half * breadth, part * LANES : (part + 1) * LANES] = values
    halo_ref[:, half * breadth :] = cells[:, : 6 * height].astype(BF)


def near_parts(pre_second, pre_first, encoder_input, low, high):
    samples, height, breadth, depth = pre_second.shape
    kept = breadth + 2 * EDGE
    slope = jax.ShapeDtypeStruct((samples, height, kept, depth), F32)
    return run(
        "near_parts",
        near_kernel,
        [slope, slope, jax.ShapeDtypeStruct((samples, 6 * height + height * breadth // 2, depth), BF)],
        [pre_second, pre_first, encoder_input, low, high],
        [
            pltpu.VMEM((2, (samples * height + 8) * kept, LANES), F32),
            pltpu.VMEM((samples, 6 * height + 8, depth), F32),
        ],
    )


def far_kernel(first_ref, tile_second, tile_first, slope_second, slope_first, act_out, wide, act):
    samples, height, breadth, depth = first_ref.shape
    kept = breadth + 2 * EDGE
    lat = lax.axis_index("lat")
    for source_ref, slope_ref in ((tile_second, slope_second), (tile_first, slope_first)):
        wide[...] = jnp.zeros(wide.shape, F32)
        for s in range(samples):
            for half in range(2):
                for r in range(height):
                    at = (s * height + r) * kept + EDGE
                    wide[half, at : at + breadth, :] = source_ref[s, r, :, half * LANES : (half + 1) * LANES].astype(F32)
        value = jnp.concatenate([wide[0], wide[1]], axis=1)
        slope_ref[...] = gelu_slope(value).reshape(slope_ref.shape)
    own, other = pl.ds(height * lat, height), pl.ds(height * (1 - lat), height)
    act[:, own] = gelu_value(first_ref[...].astype(F32))
    act[:, other] = gelu_value(tile_first[...].astype(F32))
    act_out[...] = act[...].reshape(act_out.shape[1], depth).T.astype(BF)


def far_parts(pre_first, tile_second, tile_first):
    samples, height, breadth, depth = pre_first.shape
    kept = breadth + 2 * EDGE
    slope = jax.ShapeDtypeStruct((samples, height, kept, depth), F32)
    return run(
        "far_parts",
        far_kernel,
        [slope, slope, jax.ShapeDtypeStruct((depth, 2 * samples * height * breadth), BF)],
        [pre_first, tile_second, tile_first],
        [
            pltpu.VMEM((2, samples * height * kept, LANES), F32),
            pltpu.VMEM((samples, 2 * height, breadth, depth), F32),
        ],
    )


def put_slopes(sample, slope, near_ref, far_ref, halo_ref, width, first_cell):
    _, height, kept, _ = near_ref.shape
    lat = lax.axis_index("lat")
    other = pl.ds(height * (1 - lat), height)
    slope[pl.ds(height * lat, height)] = near_ref[sample]
    slope[other] = far_ref[sample]
    beside = gelu_slope(halo_ref[sample, halo_ref.shape[1] - 6 * height :].astype(F32))
    for side in range(2):
        for col in range(width):
            here = first_cell + (side * width + col) * height
            at = kept - EDGE + col if side else EDGE - width + col
            slope[other, at, :] = beside[here : here + height]


def globe_kernel(sample, near_ref, far_ref, halo_ref, total_ref, line_ref, cat_ref, moved_ref, latent, slope, wide):
    rows, kept, depth = total_ref.shape
    height = rows - 1
    tall = 2 * height
    breadth = kept - 2 * EDGE
    lat = lax.axis_index("lat")
    own = 8 + EDGE
    latent[...] = jnp.zeros(latent.shape, F32)
    latent[pl.ds((height - 1) * lat, rows)] = total_ref[...].astype(F32)
    latent[pl.ds((height - 1) * (1 - lat), rows)] += line_ref[...].astype(F32)
    put_slopes(sample, slope, near_ref, far_ref, halo_ref, 2, 0)
    wide[:, 8 : 8 + kept, :] = (latent[...] * slope[...]).astype(BF).astype(F32)
    for v in STEPS:
        lanes = slice((v + 1) * depth, (v + 2) * depth)
        cat_ref[1 : 1 + tall, :, lanes] = wide[:, 8 - v : 8 - v + kept, :].astype(BF)
        moved_ref[v + 1, 1 : 1 + tall] = wide[:, own - v : own - v + breadth, :].astype(BF)
    for row in (0, tall + 1):
        cat_ref[row] = jnp.zeros(cat_ref.shape[1:], BF)
        moved_ref[:, row] = jnp.zeros(moved_ref.shape[:1] + moved_ref.shape[2:], BF)


def globe(sample, total, line, near, far, halo):
    rows, kept, depth = total.shape
    tall, breadth = 2 * (rows - 1), kept - 2 * EDGE
    return run(
        "latent_grads",
        functools.partial(globe_kernel, sample),
        [
            jax.ShapeDtypeStruct((tall + 2, kept, 3 * depth), BF),
            jax.ShapeDtypeStruct((3, tall + 2, breadth, depth), BF),
        ],
        [near, far, halo, total, line],
        [
            pltpu.VMEM((tall, kept, depth), F32),
            pltpu.VMEM((tall, kept, depth), F32),
            pltpu.VMEM((tall, kept + 24, depth), F32),
        ],
    )


def band_rows(norm_factor, lefts, moved, mine_ref, other_ref):
    channels, cells = lefts[0].shape
    _, padded, breadth, depth = moved[0].shape
    tall = padded - 2
    lat = lax.axis_index("lat")
    core, _ = core_and_chip()
    half = channels // 2

    def put(parts, u, v, start, size):
        total = None
        for left, ref in zip(parts, moved):
            part = dot_plain(left, ref[v + 1, pl.ds(1 - u, tall)].reshape(cells, depth))
            total = part if total is None else total + part
        total = total * norm_factor
        lower, upper = total[:, :LANES], total[:, LANES:]
        here = pl.ds(pl.multiple_of(start, half), size)
        mine_ref[here, :] = jnp.where(core == 0, lower, upper).astype(BF)
        other_ref[here, :] = jnp.where(core == 0, upper, lower).astype(BF)

    for j in range(4):
        (u0, v0), (u1, v1) = (divmod(k, 3) for k in (j, 5 + j))
        put(lefts, u0 - 1 + lat * (u1 - u0), v0 - 1 + lat * (v1 - v0), lat * half + j * channels, channels)
    put([jnp.where(lat == 0, left[:half], left[half:]) for left in lefts], 0, 0, (1 - lat) * 4 * channels, half)


def second_band_kernel(norm_factor, act_ref, *refs):
    moved, (mine_ref, other_ref) = refs[:-2], refs[-2:]
    cells = act_ref.shape[1] // len(moved)
    lefts = [act_ref[:, s * cells : (s + 1) * cells] for s in range(len(moved))]
    band_rows(norm_factor, lefts, moved, mine_ref, other_ref)


def second_band(norm_factor, act, moved):
    half = jax.ShapeDtypeStruct((9 * act.shape[0] // 2, LANES), BF)
    return run("second_weight_grads", functools.partial(second_band_kernel, norm_factor), [half, half], [act, *moved])


def first_kernel(sample, cat_ref, near_ref, far_ref, halo_ref, weights_ref, moved_ref, slope, wide):
    padded, kept, triple = cat_ref.shape
    tall, depth = padded - 2, triple // 3
    breadth = kept - 2 * EDGE
    own = 8 + EDGE
    put_slopes(sample, slope, near_ref, far_ref, halo_ref, 1, 2 * tall)
    linear = None
    for u in STEPS:
        weights = jnp.concatenate([weights_ref[3 * (u + 1) + (v + 1)] for v in STEPS], axis=1)
        part = dot_last(cat_ref[1 - u : 1 - u + tall].reshape(tall * kept, triple), weights)
        linear = part if linear is None else linear + part
    wide[:, 8 : 8 + kept, :] = (linear.reshape(tall, kept, depth) * slope[...]).astype(BF).astype(F32)
    for v in STEPS:
        moved_ref[v + 1, 1 : 1 + tall] = wide[:, own - v : own - v + breadth, :].astype(BF)
    for row in (0, tall + 1):
        moved_ref[:, row] = jnp.zeros(moved_ref.shape[:1] + moved_ref.shape[2:], BF)


def first_grad(sample, cat, near, far, halo, w_second):
    padded, kept, triple = cat.shape
    tall, depth = padded - 2, triple // 3
    return run(
        "second_conv",
        functools.partial(first_kernel, sample),
        [jax.ShapeDtypeStruct((3, padded, kept - 2 * EDGE, depth), BF)],
        [cat, near, far, halo, w_second],
        [pltpu.VMEM((tall, kept, depth), F32), pltpu.VMEM((tall, kept + 16, depth), F32)],
    )[0]


def first_band_kernel(norm_factor, halo_ref, input_ref, *refs):
    moved, (mine_ref, other_ref, cells) = refs[:-3], refs[-3:]
    samples, height, breadth, channels = input_ref.shape
    lat = lax.axis_index("lat")
    cells[:, pl.ds(height * lat, height)] = input_ref[...].astype(F32)
    half = height // 2
    for part in range(2):
        values = halo_ref[:, : half * breadth, part * LANES : (part + 1) * LANES].astype(F32)
        cells[:, pl.ds(height * (1 - lat) + part * half, half)] = values.reshape(samples, half, breadth, LANES)
    lefts = [cells[s].reshape(2 * height * breadth, channels).T.astype(BF) for s in range(samples)]
    band_rows(norm_factor, lefts, moved, mine_ref, other_ref)


def first_band(norm_factor, halo, encoder_input, moved):
    samples, height, breadth, channels = encoder_input.shape
    half = jax.ShapeDtypeStruct((9 * channels // 2, LANES), BF)
    return run(
        "first_weight_grads",
        functools.partial(first_band_kernel, norm_factor),
        [half, half],
        [halo, encoder_input, *moved],
        [pltpu.VMEM((samples, 2 * height, breadth, channels), F32)],
    )


def input_band_kernel(w_first_ref, *refs):
    moved, out_ref = refs[:-1], refs[-1]
    _, height, breadth, channels = out_ref.shape
    depth = moved[0].shape[3]
    lat = lax.axis_index("lat")
    total = None
    for u in STEPS:
        weights = jnp.concatenate([w_first_ref[3 * (u + 1) + (v + 1)] for v in STEPS], axis=1)
        here = pl.ds(height * lat + 1 - u, height)
        left = [jnp.concatenate([ref[v + 1, here].reshape(-1, depth) for v in STEPS], axis=1) for ref in moved]
        part = dot_last(jnp.concatenate(left, axis=0), weights)
        total = part if total is None else total + part
    out_ref[...] = total.astype(BF).reshape(out_ref.shape)


def blocks_kernel(first_mine, first_got, second_mine, second_got, *outs):
    lon = lax.axis_index("lon")
    rows = first_mine.shape[1]
    for step, out_ref in enumerate(outs):
        block = partner(lon, step, len(outs))
        out_ref[:rows] = (first_mine[block].astype(F32) + first_got[block].astype(F32)).astype(BF)
        out_ref[rows:] = (second_mine[block].astype(F32) + second_got[block].astype(F32)).astype(BF)


def halves_kernel(mine_ref, other_ref, first_ref, second_ref):
    core, _ = core_and_chip()
    mine, other = mine_ref[...].astype(F32), other_ref[...].astype(F32)
    rows = mine.shape[0] // 3
    for part in range(2):
        value = jnp.where(core == part, mine, other)
        first_ref[pl.ds(part, rows, stride=2), :] = value[:rows]
        second_ref[pl.ds(part, 2 * rows, stride=2), :] = value[rows:]


def to_partner(array, step):
    count = lax.axis_size("lon")
    return lax.ppermute(array, "lon", [(partner(i, step, count), i) for i in range(count)])


def two_bands(head_grads, head_weights, encoder_input, pre_first, pre_second, w_first, w_second, norm_factor):
    samples, height, breadth, _ = encoder_input.shape
    columns = lax.axis_size("lon")
    tiles = [swap(array, "lat", 1) for array in (pre_second, pre_first)]
    to_right, to_left = pack(head_grads, pre_second, pre_first)
    low = around(to_right, "lon", 1)
    high = around(to_left, "lon", -1)
    head_grads, head_weights, w_second, pre_second, pre_first, encoder_input = stage(
        head_grads, head_weights, w_second, pre_second, pre_first, encoder_input
    )
    inside = inside_conv(head_grads, head_weights, 2 * samples)
    low, high, inside, *tiles = lax.optimization_barrier((low, high, inside, *tiles))
    heads_of = functools.partial(
        head_conv,
        head_grads=head_grads,
        high=high,
        head_weights=head_weights,
        slots=samples,
        rows=height + 1,
    )
    everyone = range(samples)
    own_other, cross_other = edges_conv(inside, low, high, head_weights)
    cross_got, own_got = swap(cross_other, "lead", 1), swap(own_other, "lead", 1)
    part_shape = jax.ShapeDtypeStruct(cross_got.shape[1:], BF)
    cross = run("core_sum", core_sum_kernel, [part_shape] * samples, [heads_of(False, True, None, low=low), cross_got])
    low_later, *cross = lax.optimization_barrier((low, *cross))
    own = run("core_sum", core_sum_kernel, [part_shape] * samples, [heads_of(False, False, None, low=low_later), own_got])
    near_second, near_first, halo = near_parts(pre_second, pre_first, encoder_input, low, high)
    cross[-1], halo = lax.optimization_barrier((cross[-1], halo))
    cross = [swap(part, "lead", 2) for part in cross]
    halo = swap(halo, "lat", 1)
    cross[-1], halo = lax.optimization_barrier((cross[-1], halo))
    totals = [run("chip_sum", sum_kernel, [part_shape], [own[s], cross[s]])[0] for s in everyone]
    lines = [swap(total, "lat", 1) for total in totals]
    far_second, far_first, act = far_parts(pre_first, *tiles)

    moved_second, moved_first = [], []
    for s in everyone:
        cat, moved = globe(s, totals[s], lines[s], near_second, far_second, halo)
        moved_second.append(moved)
        if s < samples - 1:
            moved_first.append(first_grad(s, cat, near_first, far_first, halo, w_second))
            near_second, moved_first[s] = lax.optimization_barrier((near_second, moved_first[s]))
    second_mine, second_other = second_band(norm_factor, act, moved_second)
    second_got = swap(second_other, "lead", 1)
    moved_first.append(first_grad(samples - 1, cat, near_first, far_first, halo, w_second))
    first_mine, first_other = first_band(norm_factor, halo, encoder_input, moved_first)
    first_got = swap(first_other, "lead", 1)
    input_grad = run(
        "input_conv", input_band_kernel, [jax.ShapeDtypeStruct(encoder_input.shape, BF)], [w_first, *moved_first]
    )[0]

    blocks = [t.reshape(columns, -1, LANES) for t in (first_mine, first_got, second_mine, second_got)]
    rows = blocks[0].shape[1]
    share_shape = jax.ShapeDtypeStruct((3 * rows, LANES), BF)
    shares = run("blocks", blocks_kernel, [share_shape] * columns, blocks)
    parts = [to_partner(shares[step], step) for step in ((2, 1, 3) if columns == 4 else range(1, columns))]
    share = run("share", sum_kernel, [share_shape], [shares[0], *parts])[0]
    both = run("chips", sum_kernel, [share_shape], [share, swap(share, "lead", 2)])[0]
    result_first, result_second = run(
        "cores",
        halves_kernel,
        [jax.ShapeDtypeStruct((2 * rows, LANES), F32), jax.ShapeDtypeStruct((4 * rows, LANES), F32)],
        [both, swap(both, "lead", 1)],
    )
    return input_grad, result_first.reshape(-1), result_second.reshape(-1)


def core_sum_kernel(mine_ref, got_ref, *outs):
    for slot, out_ref in enumerate(outs):
        out_ref[...] = (mine_ref[slot].astype(F32) + got_ref[slot].astype(F32)).astype(BF)


def general(head_grads, head_weights, encoder_input, pre_first, pre_second, w_first, w_second, norm_factor):
    samples, height, breadth, _ = encoder_input.shape
    bands, columns = lax.axis_size("lat"), lax.axis_size("lon")
    to_right, to_left = pack(head_grads, pre_second, pre_first)
    to_right, to_left, to_cross = lax.optimization_barrier((to_right, to_left, pre_first))
    low = around(to_right, "lon", 1)
    high = around(to_left, "lon", -1)
    act_got = activated(swap(to_cross, "lead", 2))
    head_grads, head_weights, w_second, pre_second, pre_first, encoder_input = stage(
        head_grads, head_weights, w_second, pre_second, pre_first, encoder_input
    )
    low, high, act_got = lax.optimization_barrier((low, high, act_got))

    steps = [1, -1]
    heads_of = functools.partial(head_conv, head_grads=head_grads, high=high, head_weights=head_weights, slots=samples, rows=height + 2)
    got_cross = swap(heads_of(True, True, None, low=low), "lead", 1)
    got_own = swap(heads_of(True, False, None, low=low), "lead", 1)
    cross, *angles = spread_cross(heads_of(False, True, None, low=low), got_cross, len(steps))
    low_later, cross, *angles = lax.optimization_barrier((low, cross, *angles))
    cross = swap(cross, "lead", 2)
    angles = [corner(angle, step) for angle, step in zip(angles, steps)]
    second, first, slope_second, slope_first, act, cells_in = saved(pre_second, pre_first, encoder_input, low, high)
    own, *lines = spread_own(heads_of(False, False, None, low=low_later), got_own, second, first, len(steps))
    lines = [swap(line, "lat", 1) if step is None else around(line, "lat", step, False) for line, step in zip(lines, steps)]
    strips = [strip for pair in zip(lines, angles) for strip in pair]

    grad, away, slope = latent_grads(len(steps), bands, own, cross, strips, slope_second, slope_first)
    grad_got = swap(away, "lead", 2)
    moved, first_mine, first_other = encoder(norm_factor, bands, grad, slope, cells_in, w_second)
    input_grad = input_conv(moved, w_first)
    first_got = swap(first_other, "lead", 1)
    second_mine, second_other = second_grads(norm_factor, bands * columns, grad, grad_got, act, act_got)
    second_got = swap(second_other, "lead", 1)

    first_terms = [pairwise([first_mine, first_got], bands)]
    second_terms = [pairwise([second_mine, second_got], bands)]
    first_came = swap(other_band(first_terms, columns), "lat", 1)
    second_came = swap(other_band(second_terms, columns), "lat", 1)
    blocks = [t.reshape(2, columns, -1, LANES) for t in first_terms + second_terms]
    rows = blocks[0].shape[2]
    share_shape = jax.ShapeDtypeStruct((2, rows, LANES), BF)
    shares = run("own_band", own_band_kernel, [share_shape] * columns, blocks + [first_came, second_came])
    parts = [to_partner(shares[step], step) for step in ((2, 1, 3) if columns == 4 else range(1, columns))]
    share = run("share", sum_kernel, [share_shape], [shares[0], *parts])[0]
    both = run("chips", chips_kernel, [jax.ShapeDtypeStruct((3, rows, LANES), BF)], [share, swap(share, "lead", 2)])[0]
    result_first, result_second = run(
        "cores",
        cores_kernel,
        [jax.ShapeDtypeStruct((2 * rows, LANES), F32), jax.ShapeDtypeStruct((4 * rows, LANES), F32)],
        [both, swap(both, "lead", 1)],
    )
    return input_grad, result_first.reshape(-1), result_second.reshape(-1)


def per_device(head_grads, head_weights, encoder_input, pre_first, pre_second, w_first, w_second):
    samples, height, breadth, channels = encoder_input.shape
    bands, columns = lax.axis_size("lat"), lax.axis_size("lon")
    cells_total = samples * lax.axis_size("lead") * height * bands * breadth * columns
    norm_factor = 1.0 / math.sqrt(cells_total)
    plan = two_bands if bands == 2 and 9 * channels // (bands * columns) % 16 == 0 else general
    return plan(head_grads, head_weights, encoder_input, pre_first, pre_second, w_first, w_second, norm_factor)


def solution(mesh):
    in_specs = (
        P("lead", None, "lat", "lon", None),
        P("lead", None, None, None),
        P("lead", "lat", "lon", None),
        P("lead", "lat", "lon", None),
        P("lead", "lat", "lon", None),
        P(),
        P(),
    )
    out_specs = (P("lead", "lat", "lon", None), P(("lat", "lon")), P(("lat", "lon")))
    return jax.shard_map(
        per_device, mesh=mesh, in_specs=in_specs, out_specs=out_specs, check_vma=False
    )
```

```python
import functools
import math

import jax
import jax.numpy as jnp
from jax import lax
from jax.experimental import pallas as pl
from jax.experimental.pallas import tpu as pltpu
from jax.sharding import PartitionSpec as P

BF = jnp.bfloat16
F32 = jnp.float32
STEPS = (-1, 0, 1)
EDGE = 4
LANES = 128
VMEM_BYTES = 24 * 1024 * 1024


def erf_part(values):
    return 0.5 * (1.0 + lax.erf(values * 0.7071067811865476))


def gelu_slope(values):
    return erf_part(values) + values * jnp.exp(-0.5 * values * values) * 0.3989422804014327


def gelu_value(values):
    return values * erf_part(values)


def dot_last(left, right):
    return lax.dot_general(left, right, (((1,), (1,)), ((), ())), preferred_element_type=F32)


def dot_plain(left, right):
    return lax.dot_general(left, right, (((1,), (0,)), ((), ())), preferred_element_type=F32)


def core_and_chip():
    lead = lax.axis_index("lead")
    return lax.rem(lead, 2), lax.div(lead, 2)


def run(name, kernel, out_shape, arrays, scratch=(), flops=0, far=False):
    specs = [pl.BlockSpec(memory_space=pltpu.HBM if far else pltpu.VMEM)] * len(arrays)
    if far:
        arrays = [pltpu.with_memory_space_constraint(a, pltpu.HBM) for a in arrays]
    touched = sum(a.size * a.dtype.itemsize for a in arrays)
    touched += sum(math.prod(s.shape) * s.dtype.itemsize for s in out_shape)
    return pl.pallas_call(
        kernel,
        name=name,
        out_shape=out_shape,
        in_specs=specs,
        out_specs=[pl.BlockSpec(memory_space=pltpu.VMEM)] * len(out_shape),
        scratch_shapes=list(scratch),
        compiler_params=pltpu.CompilerParams(vmem_limit_bytes=VMEM_BYTES),
        cost_estimate=pl.CostEstimate(flops=1, bytes_accessed=1, transcendentals=0),
    )(*arrays)


def pack_kernel(grads_far, second_far, first_far, right_ref, left_ref, grads_near, second_near, first_near, edges, edges_wide, packed, sems):
    heads, batch, height, breadth, _ = grads_far.shape
    samples = second_far.shape[0]
    rows = 6 * height
    copies = []
    for side in range(2):
        columns = pl.ds(breadth - 16 if side == 0 else 0, 16)
        for j, (far, near) in enumerate(((grads_far, grads_near), (second_far, second_near), (first_far, first_near))):
            source = far.at[:, :, :, columns, :] if j == 0 else far.at[:, :, columns, :]
            copies.append(pltpu.make_async_copy(source, near.at[side], sems.at[side, j]))
            copies[-1].start()
    for copy in copies:
        copy.wait()
    for side, out_ref in ((0, right_ref), (1, left_ref)):
        start = 8 if side == 0 else 0
        grads_ref, second_ref, first_ref = grads_near.at[side], second_near.at[side], first_near.at[side]
        for h in range(heads):
            for b in range(batch):
                block = grads_ref[h, b].astype(F32)[:, start : start + 8, :]
                edges[(h * batch + b) * height * 8 : (h * batch + b + 1) * height * 8, :] = block.reshape(height * 8, LANES)
        for j, ref in enumerate((second_ref, first_ref)):
            for s in range(samples):
                block = ref[s].astype(F32)[:, start : start + 8, :]
                at = (j * samples + s) * height * 8
                for half in range(2):
                    lanes = slice(half * LANES, (half + 1) * LANES)
                    edges_wide[half, at : at + height * 8, :] = block[:, :, lanes].reshape(height * 8, LANES)
        for b in range(batch):
            for col in range(3):
                inner = 5 + col if side == 0 else col
                for h in range(heads):
                    at = b * rows + (col * 2 + h) * height
                    packed[at : at + height, :] = edges[pl.ds((h * batch + b) * height * 8 + inner, height, stride=8), :]
        for s in range(samples):
            for q in range(3):
                j, col, width = (0, q, 2) if q < 2 else (1, 0, 1)
                inner = 8 - width + col if side == 0 else col
                for half in range(2):
                    at = (batch + s) * rows + (q * 2 + half) * height
                    packed[at : at + height, :] = edges_wide[
                        half, pl.ds((j * samples + s) * height * 8 + inner, height, stride=8), :
                    ]
        out_ref[...] = packed[: (batch + samples) * rows].astype(BF).reshape(out_ref.shape)


def pack(head_grads, pre_second, pre_first):
    heads, batch, height, _, _ = head_grads.shape
    samples = pre_second.shape[0]
    shape = jax.ShapeDtypeStruct((batch + samples, 6 * height, LANES), BF)
    return run(
        "pack_columns",
        pack_kernel,
        [shape, shape],
        [head_grads, pre_second, pre_first],
        [
            pltpu.VMEM((2, heads, batch, height, 16, LANES), BF),
            pltpu.VMEM((2, samples, height, 16, 2 * LANES), BF),
            pltpu.VMEM((2, samples, height, 16, 2 * LANES), BF),
            pltpu.VMEM((heads * batch * height * 8 + 64, LANES), F32),
            pltpu.VMEM((2, 2 * samples * height * 8 + 64, LANES), F32),
            pltpu.VMEM(((batch + samples) * 6 * height + 16, LANES), F32),
            pltpu.SemaphoreType.DMA((2, 3)),
        ],
        far=True,
    )


def stage_kernel(*refs):
    count = len(refs) // 2
    sems = refs[-1]
    copies = [pltpu.make_async_copy(refs[i], refs[count + i], sems.at[i]) for i in range(count)]
    for copy in copies:
        copy.start()
    for copy in copies:
        copy.wait()


def stage(*arrays):
    shapes = [pltpu.VMEM(a.shape, a.dtype) for a in arrays]
    return run("stage", stage_kernel, shapes, list(arrays), [pltpu.SemaphoreType.DMA((len(arrays),))], far=True, flops=1 << 30)


def heads_kernel(other_core, other_chip, sample, samples, grads_ref, low_ref, high_ref, weights_ref, out_ref, wide, shifted, total):
    heads, batch, height, breadth, _ = grads_ref.shape
    slots, _, kept, depth = out_ref.shape
    pitch = kept + 16
    own = 8 + EDGE
    core, chip = core_and_chip()
    core = 1 - core if other_core else core
    for slot in range(slots):
        if sample is None:
            group, s = 1 - chip if other_chip else chip, slot
        else:
            group, s = 1 - chip if slot % 2 else chip, sample + slot // 2
        b = (2 * group + core) * samples + s
        low = low_ref[b].astype(F32)
        high = high_ref[b].astype(F32)
        for r in range(height):
            at = (slot * height + r) * pitch + own
            for h in range(heads):
                wide[h, at : at + breadth, :] = grads_ref[h, b, r].astype(F32)
        for col in range(3):
            for h in range(heads):
                here = (col * 2 + h) * height
                at = slot * height * pitch + own + col
                wide[h, pl.ds(at - 3, height, stride=pitch), :] = low[here : here + height]
                wide[h, pl.ds(at + breadth, height, stride=pitch), :] = high[here : here + height]
        for v in STEPS:
            for h in range(heads):
                starts = [(slot * height + r) * pitch + 8 - v for r in range(height)]
                moved = jnp.concatenate([wide[h, at : at + kept, :] for at in starts], axis=0).astype(BF)
                lane = ((v + 1) * heads + h) * LANES
                shifted[slot * height * kept : (slot + 1) * height * kept, lane : lane + LANES] = moved
    total[:, height:, :, :] = jnp.zeros((slots, 2, kept, depth), F32)
    for u in STEPS:
        weights = jnp.concatenate(
            [weights_ref[h, 3 * (u + 1) + (v + 1)] for v in STEPS for h in range(heads)], axis=1
        )
        part = dot_last(shifted[...], weights).reshape(slots, height, kept, depth)
        if u == -1:
            total[:, :height] = part
        else:
            total[:, 1 + u : 1 + u + height] += part
    if out_ref.shape[1] == height + 2:
        out_ref[...] = total[...].astype(BF)
    else:
        out_ref[...] = total[:, pl.ds(1 - lax.axis_index("lat"), height + 1)].astype(BF)


def head_conv(other_core, other_chip, sample, head_grads, low, high, head_weights, slots, rows):
    samples = head_grads.shape[1] // lax.axis_size("lead")
    heads, batch, height, breadth, _ = head_grads.shape
    depth = head_weights.shape[2]
    kept = breadth + 2 * EDGE
    return run(
        "head_conv",
        functools.partial(heads_kernel, other_core, other_chip, sample, samples),
        [jax.ShapeDtypeStruct((slots, rows, kept, depth), BF)],
        [head_grads, low, high, head_weights],
        [
            pltpu.VMEM((heads, (slots * height + 8) * (kept + 16), LANES), F32),
            pltpu.VMEM((slots * height * kept, 3 * heads * LANES), BF),
            pltpu.VMEM((slots, height + 2, kept, depth), F32),
        ],
        flops=2 * slots * height * kept * 9 * heads * LANES * depth,
    )[0]


def inside_kernel(samples, grads_ref, weights_ref, total_ref, wide, shifted):
    heads, _, height, breadth, _ = grads_ref.shape
    slots, _, kept, depth = total_ref.shape
    pitch = kept + 16
    own = 8 + EDGE
    core, chip = core_and_chip()
    blank = jnp.zeros((height, LANES), F32)
    for slot in range(slots):
        group, s = 1 - chip if slot % 2 else chip, slot // 2
        b = (2 * group + 1 - core) * samples + s
        for h in range(heads):
            for r in range(height):
                at = (slot * height + r) * pitch + own
                wide[h, at : at + breadth, :] = grads_ref[h, b, r].astype(F32)
            for col in range(3):
                at = slot * height * pitch + own + col
                wide[h, pl.ds(at - 3, height, stride=pitch), :] = blank
                wide[h, pl.ds(at + breadth, height, stride=pitch), :] = blank
            for v in STEPS:
                starts = [(slot * height + r) * pitch + 8 - v for r in range(height)]
                moved = jnp.concatenate([wide[h, at : at + kept, :] for at in starts], axis=0).astype(BF)
                lane = ((v + 1) * heads + h) * LANES
                shifted[slot * height * kept : (slot + 1) * height * kept, lane : lane + LANES] = moved
    total_ref[:, height:, :, :] = jnp.zeros((slots, 2, kept, depth), F32)
    for u in STEPS:
        weights = jnp.concatenate(
            [weights_ref[h, 3 * (u + 1) + (v + 1)] for v in STEPS for h in range(heads)], axis=1
        )
        part = dot_last(shifted[...], weights).reshape(slots, height, kept, depth)
        if u == -1:
            total_ref[:, :height] = part
        else:
            total_ref[:, 1 + u : 1 + u + height] += part


def edges_kernel(samples, inside_ref, low_ref, high_ref, weights_ref, own_out, cross_out, wide, shifted, total):
    slots, rows, kept, depth = inside_ref.shape
    height, heads, pitch = rows - 2, weights_ref.shape[0], 24
    core, chip = core_and_chip()
    wide[...] = jnp.zeros(wide.shape, F32)
    total[...] = inside_ref[...]
    for side, packed_ref in ((0, low_ref), (1, high_ref)):
        for slot in range(slots):
            group, s = 1 - chip if slot % 2 else chip, slot // 2
            packed = packed_ref[(2 * group + 1 - core) * samples + s].astype(F32)
            first = (side * slots + slot) * height
            for h in range(heads):
                for col in range(3):
                    here = (col * 2 + h) * height
                    at = first * pitch + 9 + 3 * side + col
                    wide[h, pl.ds(at, height, stride=pitch), :] = packed[here : here + height]
                for v in STEPS:
                    starts = [(first + r) * pitch + 8 - v for r in range(height)]
                    moved = jnp.concatenate([wide[h, at : at + 8, :] for at in starts], axis=0).astype(BF)
                    lane = ((v + 1) * heads + h) * LANES
                    shifted[first * 8 : (first + height) * 8, lane : lane + LANES] = moved
    for u in STEPS:
        weights = jnp.concatenate(
            [weights_ref[h, 3 * (u + 1) + (v + 1)] for v in STEPS for h in range(heads)], axis=1
        )
        part = dot_last(shifted[...], weights).reshape(2, slots, height, 8, depth)
        total[:, 1 + u : 1 + u + height, :8] += part[0]
        total[:, 1 + u : 1 + u + height, kept - 8 :] += part[1]
    here = pl.ds(1 - lax.axis_index("lat"), height + 1)
    for s in range(samples):
        own_out[s] = total[2 * s, here].astype(BF)
        cross_out[s] = total[2 * s + 1, here].astype(BF)


def inside_conv(head_grads, head_weights, slots):
    samples = head_grads.shape[1] // lax.axis_size("lead")
    heads, _, height, breadth, _ = head_grads.shape
    kept = breadth + 2 * EDGE
    return run(
        "head_conv_inside",
        functools.partial(inside_kernel, samples),
        [jax.ShapeDtypeStruct((slots, height + 2, kept, head_weights.shape[2]), F32)],
        [head_grads, head_weights],
        [
            pltpu.VMEM((heads, (slots * height + 8) * (kept + 16), LANES), F32),
            pltpu.VMEM((slots * height * kept, 3 * heads * LANES), BF),
        ],
    )[0]


def edges_conv(inside, low, high, head_weights):
    slots, rows, kept, depth = inside.shape
    samples, heads, height = slots // 2, head_weights.shape[0], rows - 2
    return run(
        "head_conv_edges",
        functools.partial(edges_kernel, samples),
        [jax.ShapeDtypeStruct((samples, rows - 1, kept, depth), BF)] * 2,
        [inside, low, high, head_weights],
        [
            pltpu.VMEM((heads, (2 * slots * height + 8) * 24, LANES), F32),
            pltpu.VMEM((2 * slots * height * 8, 3 * heads * LANES), BF),
            pltpu.VMEM((slots, rows, kept, depth), F32),
        ],
    )


def saved_kernel(second_ref, first_ref, input_ref, low_ref, high_ref, second_out, first_out, slope_second, slope_first, act_out, input_out, wide):
    samples, height, breadth, depth = second_ref.shape
    kept = breadth + 2 * EDGE
    batch = low_ref.shape[0] - samples
    for ref, width, out_ref, slope_ref in (
        (second_ref, 2, second_out, slope_second),
        (first_ref, 1, first_out, slope_first),
    ):
        wide[...] = jnp.zeros(wide.shape, F32)
        for s in range(samples):
            for r in range(height):
                at = (s * height + r) * kept + EDGE
                for half in range(2):
                    lanes = slice(half * LANES, (half + 1) * LANES)
                    wide[half, at : at + breadth, :] = ref[s, r, :, lanes].astype(F32)
            low = low_ref[batch + s].astype(F32)
            high = high_ref[batch + s].astype(F32)
            for col in range(width):
                for half in range(2):
                    here = ((col if width == 2 else 2) * 2 + half) * height
                    at = s * height * kept + EDGE + col
                    wide[half, pl.ds(at - width, height, stride=kept), :] = low[here : here + height]
                    wide[half, pl.ds(at + breadth, height, stride=kept), :] = high[here : here + height]
        value = jnp.concatenate([wide[half, : samples * height * kept] for half in range(2)], axis=1)
        out_ref[...] = value.astype(BF).reshape(out_ref.shape)
        slope_ref[...] = gelu_slope(value).reshape(slope_ref.shape)
    active = gelu_value(first_ref[...].astype(F32).reshape(samples * height * breadth, depth)).astype(BF).astype(F32)
    act_out[...] = active.T.astype(BF)
    cells = input_ref[...].astype(F32).reshape(samples * height * breadth, input_ref.shape[3])
    input_out[...] = cells.T.astype(BF)


def saved(pre_second, pre_first, encoder_input, low, high):
    samples, height, breadth, depth = pre_second.shape
    kept = breadth + 2 * EDGE
    cells = samples * height * breadth
    return run(
        "saved_parts",
        saved_kernel,
        [
            jax.ShapeDtypeStruct((samples, height, kept, depth), BF),
            jax.ShapeDtypeStruct((samples, height, kept, depth), BF),
            jax.ShapeDtypeStruct((samples, height, kept, depth), F32),
            jax.ShapeDtypeStruct((samples, height, kept, depth), F32),
            jax.ShapeDtypeStruct((depth, cells), BF),
            jax.ShapeDtypeStruct((encoder_input.shape[3], cells), BF),
        ],
        [pre_second, pre_first, encoder_input, low, high],
        [pltpu.VMEM((2, (samples * height + 8) * kept, LANES), F32)],
    )


def goes_down(way, ways):
    return 1 - lax.axis_index("lat") if ways == 1 else 1 - way


def cross_kernel(mine_ref, got_ref, cross_ref, *strips):
    height = mine_ref.shape[1] - 2
    cross_ref[...] = (mine_ref[...].astype(F32) + got_ref[...].astype(F32)).astype(BF)
    for way, corner_ref in enumerate(strips):
        corner_ref[...] = cross_ref[:, pl.ds((height - 1) * goes_down(way, len(strips)), 3)]


def own_kernel(mine_ref, got_ref, second_ref, first_ref, own_ref, *strips):
    height = second_ref.shape[1]
    own_ref[...] = (mine_ref[...].astype(F32) + got_ref[...].astype(F32)).astype(BF)
    for way, line_ref in enumerate(strips):
        down = goes_down(way, len(strips))
        line_ref[:, 0:3] = own_ref[:, pl.ds((height - 1) * down, 3)]
        line_ref[:, 3:5] = second_ref[:, pl.ds((height - 2) * down, 2)]
        line_ref[:, 5:6] = first_ref[:, pl.ds((height - 1) * down, 1)]


def spread_cross(mine, got, ways):
    samples, _, kept, depth = mine.shape
    strip = jax.ShapeDtypeStruct((samples, 3, kept, depth), BF)
    return run("core_sum_cross", cross_kernel, [jax.ShapeDtypeStruct(mine.shape, BF)] + [strip] * ways, [mine, got])


def spread_own(mine, got, second, first, ways):
    samples, _, kept, depth = mine.shape
    strip = jax.ShapeDtypeStruct((samples, 6, kept, depth), BF)
    return run("core_sum_own", own_kernel, [jax.ShapeDtypeStruct(mine.shape, BF)] + [strip] * ways, [mine, got, second, first])


def latent_kernel(ways, bands, own_ref, cross_ref, *refs):
    strips, refs = refs[: 2 * ways], refs[2 * ways :]
    slope_second_ref, slope_first_ref, grad_ref, away_ref, slope_out, latent, slope_second = refs
    samples, rows, kept, depth = own_ref.shape
    height = rows - 2
    lat = lax.axis_index("lat")
    _, chip = core_and_chip()
    blank = jnp.zeros((samples, kept, depth), F32)
    latent[:, 0] = blank
    latent[:, height + 3] = blank
    latent[:, 1 : height + 3] = own_ref[...].astype(F32) + cross_ref[...].astype(F32)
    slope_second[:, 2 : 2 + height] = slope_second_ref[...]
    slope_out[:, 1 : 1 + height] = slope_first_ref[...]
    for way in range(ways):
        line_ref, corner_ref = strips[2 * way], strips[2 * way + 1]
        below = 1 - lat if ways == 1 else way
        at = (height + 1) * below
        latent[:, pl.ds(at, 3)] += line_ref[:, 0:3].astype(F32) + corner_ref[...].astype(F32)
        slope_second[:, pl.ds((height + 2) * below, 2)] = gelu_slope(line_ref[:, 3:5].astype(F32))
        slope_out[:, pl.ds((height + 1) * below, 1)] = gelu_slope(line_ref[:, 5:6].astype(F32))
    for i in range(height + 4):
        row = lat * height + i - 2
        valid = jnp.logical_and(row >= 0, row < bands * height)
        value = latent[:, i] * slope_second[:, i]
        if i < 2 or i >= height + 2:
            value = jnp.where(valid, value, 0.0)
        grad_ref[:, i] = value.astype(BF)
        if 0 < i < height + 3:
            away_ref[:, i - 1] = jnp.where(chip == 0, value[:, :, LANES:], value[:, :, :LANES]).astype(BF)


def latent_grads(ways, bands, own, cross, strips, slope_second, slope_first):
    samples, rows, kept, depth = own.shape
    return run(
        "latent_grads",
        functools.partial(latent_kernel, ways, bands),
        [
            jax.ShapeDtypeStruct((samples, rows + 2, kept, depth), BF),
            jax.ShapeDtypeStruct((samples, rows, kept, LANES), BF),
            jax.ShapeDtypeStruct((samples, rows, kept, depth), F32),
        ],
        [own, cross, *strips, slope_second, slope_first],
        [
            pltpu.VMEM((samples, rows + 2, kept, depth), F32),
            pltpu.VMEM((samples, rows + 2, kept, depth), F32),
        ],
    )


def encoder_kernel(norm_factor, bands, grad_ref, slope_ref, input_ref, weights_ref, moved_out, mine_ref, other_ref, wide, cat, wide_first):
    samples, tall, kept, depth = grad_ref.shape
    rows = tall - 2
    height = rows - 2
    breadth = kept - 2 * EDGE
    lat = lax.axis_index("lat")
    core, _ = core_and_chip()
    own = 8 + EDGE
    wide[:, :, 8 : 8 + kept, :] = grad_ref[...].astype(F32)
    for v in STEPS:
        lanes = slice((v + 1) * depth, (v + 2) * depth)
        cat[:, :, :, lanes] = wide[:, :, 8 - v : 8 - v + kept + 8, :].astype(BF)
    linear = None
    for u in STEPS:
        weights = jnp.concatenate([weights_ref[3 * (u + 1) + (v + 1)] for v in STEPS], axis=1)
        left = cat[:, 1 - u : 1 - u + rows].reshape(samples * rows * (kept + 8), 3 * depth)
        part = dot_last(left, weights)
        linear = part if linear is None else linear + part
    linear = linear.reshape(samples, rows, kept + 8, depth)
    for i in range(rows):
        row = lat * height + i - 1
        valid = jnp.logical_and(row >= 0, row < bands * height)
        value = linear[:, i, :kept] * slope_ref[:, i]
        if i < 1 or i >= height + 1:
            value = jnp.where(valid, value, 0.0)
        wide_first[:, i, 8 : 8 + kept, :] = value.astype(BF).astype(F32)
    for v in STEPS:
        lanes = slice((v + 1) * depth, (v + 2) * depth)
        moved_out[:, :, :, lanes] = wide_first[:, :, own - v : own - v + breadth, :].astype(BF)
    for u in STEPS:
        right = moved_out[:, 1 - u : 1 - u + height].reshape(samples * height * breadth, 3 * depth)
        part = dot_plain(input_ref[...], right) * norm_factor
        for v in STEPS:
            k = 3 * (u + 1) + (v + 1)
            lower = part[:, (v + 1) * depth : (v + 1) * depth + LANES]
            upper = part[:, (v + 1) * depth + LANES : (v + 2) * depth]
            mine_ref[k] = jnp.where(core == 0, lower, upper).astype(BF)
            other_ref[k] = jnp.where(core == 0, upper, lower).astype(BF)


def encoder(norm_factor, bands, grad, slope, cells_in, w_second):
    samples, tall, kept, depth = grad.shape
    rows, height, breadth = tall - 2, tall - 4, kept - 2 * EDGE
    channels = cells_in.shape[0]
    half = jax.ShapeDtypeStruct((9, channels, LANES), BF)
    return run(
        "encoder_grads",
        functools.partial(encoder_kernel, norm_factor, bands),
        [jax.ShapeDtypeStruct((samples, rows, breadth, 3 * depth), BF), half, half],
        [grad, slope, cells_in, w_second],
        [
            pltpu.VMEM((samples, tall, kept + 24, depth), F32),
            pltpu.VMEM((samples, tall, kept + 8, 3 * depth), BF),
            pltpu.VMEM((samples, rows, kept + 16, depth), F32),
        ],
        flops=2 * 9 * depth * (samples * rows * (kept + 8) * depth + samples * height * breadth * channels),
    )


def second_kernel(norm_factor, shares, grad_ref, got_ref, act_ref, act_got_ref, *refs):
    full_ref, wide, cat = refs[-3:]
    samples, tall, kept, depth = grad_ref.shape
    rows, height, breadth = tall - 2, tall - 4, kept - 2 * EDGE
    core, chip = core_and_chip()
    own = 8 + EDGE
    lower = grad_ref[:, 1 : 1 + rows, :, :LANES].astype(F32)
    upper = grad_ref[:, 1 : 1 + rows, :, LANES:].astype(F32)
    wide[:samples, :, 8 : 8 + kept, :] = jnp.where(chip == 0, lower, upper)
    wide[samples:, :, 8 : 8 + kept, :] = got_ref[...].astype(F32)
    for v in STEPS:
        lanes = slice((v + 1) * LANES, (v + 2) * LANES)
        cat[:, :, :, lanes] = wide[:, :, own - v : own - v + breadth, :].astype(BF)
    cells = samples * height * breadth
    for u in STEPS:
        right = cat[:, 1 - u : 1 - u + height].reshape(2 * cells, 3 * LANES)
        part = dot_plain(act_ref[...], right[:cells]) + dot_plain(act_got_ref[...], right[cells:])
        part = part * norm_factor
        for v in STEPS:
            k = 3 * (u + 1) + (v + 1)
            full_ref[k * depth : (k + 1) * depth, :] = part[:, (v + 1) * LANES : (v + 2) * LANES].astype(BF)
    if len(refs) == 5:
        size = 9 * depth // shares // 2
        for i in range(shares):
            for out_ref, half in ((refs[0], core), (refs[1], 1 - core)):
                out_ref[i] = full_ref[pl.ds(pl.multiple_of((2 * i + half) * size, 16), size), :]


def second_grads(norm_factor, shares, grad, got, act, act_got):
    samples, tall, kept, depth = grad.shape
    rows, height, breadth = tall - 2, tall - 4, kept - 2 * EDGE
    size = 9 * depth // shares // 2
    inside = size % 16 == 0
    half = jax.ShapeDtypeStruct((shares, size, LANES), BF)
    scratch = [
        pltpu.VMEM((2 * samples, rows, kept + 16, LANES), F32),
        pltpu.VMEM((2 * samples, rows, breadth, 3 * LANES), BF),
    ]
    results = run(
        "second_weight_grads",
        functools.partial(second_kernel, norm_factor, shares),
        [half, half] if inside else [jax.ShapeDtypeStruct((9 * depth, LANES), BF)],
        [grad, got, act, act_got],
        [pltpu.VMEM((9 * depth, LANES), BF)] + scratch if inside else scratch,
        flops=2 * 9 * depth * LANES * 2 * samples * height * breadth,
    )
    if inside:
        return results
    halves = results[0].reshape(shares, 2, size, LANES)
    core, _ = core_and_chip()
    return [lax.dynamic_index_in_dim(halves, part, 1, keepdims=False) for part in (core, 1 - core)]


def act_kernel(source_ref, out_ref):
    samples, height, breadth, depth = source_ref.shape
    active = gelu_value(source_ref[...].astype(F32).reshape(samples * height * breadth, depth)).astype(BF).astype(F32)
    out_ref[...] = active.T.astype(BF)


def activated(source):
    samples, height, breadth, depth = source.shape
    return run("activated", act_kernel, [jax.ShapeDtypeStruct((depth, samples * height * breadth), BF)], [source])[0]


def other_band_kernel(*refs):
    band = 1 - lax.rem(lax.axis_index("lat"), 2)
    parts = [t[band].astype(F32) for t in refs[:-1]]
    refs[-1][...] = sum(parts[1:], parts[0]).astype(BF)


def partner(index, step, count):
    return index ^ step if count & (count - 1) == 0 else (index + step) % count


def own_band_kernel(*refs):
    columns = refs[0].shape[1]
    terms, came, outs = refs[: -columns - 2], refs[-columns - 2 : -columns], refs[-columns:]
    band, lon = lax.rem(lax.axis_index("lat"), 2), lax.axis_index("lon")
    for step in range(columns):
        block = partner(lon, step, columns)
        for layer in range(2):
            parts = [t[band, block].astype(F32) for t in terms[layer * len(terms) // 2 : (layer + 1) * len(terms) // 2]]
            outs[step][layer] = sum(parts, came[layer][block].astype(F32)).astype(BF)


def sum_kernel(*refs):
    total = refs[0][...].astype(F32)
    for ref in refs[1:-1]:
        total = total + ref[...].astype(F32)
    refs[-1][...] = total.astype(BF)


def input_kernel(moved_ref, w_first_ref, out_ref):
    samples, rows, breadth, triple = moved_ref.shape
    height = rows - 2
    total = None
    for u in STEPS:
        weights = jnp.concatenate([w_first_ref[3 * (u + 1) + (v + 1)] for v in STEPS], axis=1)
        part = dot_last(moved_ref[:, 1 - u : 1 - u + height].reshape(samples * height * breadth, triple), weights)
        total = part if total is None else total + part
    out_ref[...] = total.astype(BF).reshape(out_ref.shape)


def input_conv(moved, w_first):
    samples, rows, breadth, triple = moved.shape
    shape = (samples, rows - 2, breadth, w_first.shape[1])
    return run(
        "input_conv",
        input_kernel,
        [jax.ShapeDtypeStruct(shape, BF)],
        [moved, w_first],
        flops=2 * 3 * math.prod(shape) * triple,
    )[0]


def chips_kernel(mine_ref, cross_ref, out_ref):
    _, chip = core_and_chip()
    out_ref[0] = (mine_ref[0].astype(F32) + cross_ref[0].astype(F32)).astype(BF)
    out_ref[1] = jnp.where(chip == 0, mine_ref[1], cross_ref[1])
    out_ref[2] = jnp.where(chip == 0, cross_ref[1], mine_ref[1])


def cores_kernel(mine_ref, other_ref, first_ref, second_ref):
    core, _ = core_and_chip()
    rows = mine_ref.shape[1]
    mine, other = (ref[...].astype(F32) for ref in (mine_ref, other_ref))
    for part in range(2):
        value = jnp.where(core == part, mine, other)
        first_ref[pl.ds(part, rows, stride=2), :] = value[0]
        second_ref[pl.ds(2 * rows * part, rows, stride=2), :] = value[1]
        second_ref[pl.ds(2 * rows * part + 1, rows, stride=2), :] = value[2]


def swap(array, axis, flip):
    count = lax.axis_size(axis)
    return lax.ppermute(array, axis, [(i, i ^ flip) for i in range(count)])


def around(array, axis, step, periodic=True):
    count = lax.axis_size(axis)
    pairs = [(i, (i + step) % count) for i in range(count) if periodic or 0 <= i + step < count]
    return lax.ppermute(array, axis, pairs)


def corner(array, step):
    lead, lat = lax.axis_size("lead"), lax.axis_size("lat")
    pairs = []
    for a in range(lead):
        for b in range(lat):
            target = (b ^ 1) if step is None else b + step
            if 0 <= target < lat:
                pairs.append((a * lat + b, (a ^ 2) * lat + target))
    return lax.ppermute(array, ("lead", "lat"), pairs)


def other_band(terms, columns):
    shape = (columns, terms[0].size // LANES // columns // 2, LANES)
    return run("other_band", other_band_kernel, [jax.ShapeDtypeStruct(shape, BF)], [t.reshape(2, *shape) for t in terms])[0]


def pairwise(terms, bands):
    lat = lax.axis_index("lat")
    total = sum(t.reshape(-1, LANES).astype(F32) for t in terms).astype(BF)
    left = bands
    while left > 2:
        left //= 2
        bit = (lat // left) % 2
        halves = total.reshape(2, -1, LANES)
        send = lax.dynamic_index_in_dim(halves, 1 - bit, 0, keepdims=False)
        keep = lax.dynamic_index_in_dim(halves, bit, 0, keepdims=False)
        total = (keep.astype(F32) + swap(send, "lat", left).astype(F32)).astype(BF)
    return total


def near_kernel(second_ref, first_ref, input_ref, low_ref, high_ref, slope_second, slope_first, halo_ref, wide, cells):
    samples, height, breadth, depth = second_ref.shape
    kept = breadth + 2 * EDGE
    batch = low_ref.shape[0] - samples
    for ref, width, first_cell, slope_ref in ((second_ref, 2, 0, slope_second), (first_ref, 1, 4 * height, slope_first)):
        wide[...] = jnp.zeros(wide.shape, F32)
        for s in range(samples):
            for r in range(height):
                at = (s * height + r) * kept + EDGE
                for half in range(2):
                    wide[half, at : at + breadth, :] = ref[s, r, :, half * LANES : (half + 1) * LANES].astype(F32)
            for side, packed_ref in ((0, low_ref), (1, high_ref)):
                packed = packed_ref[batch + s].astype(F32)
                for col in range(width):
                    for half in range(2):
                        here = ((col if width == 2 else 2) * 2 + half) * height
                        value = packed[here : here + height]
                        at = s * height * kept + EDGE + col + (breadth if side else -width)
                        wide[half, pl.ds(at, height, stride=kept), :] = value
                        at = first_cell + (side * width + col) * height
                        cells[s, at : at + height, half * LANES : (half + 1) * LANES] = value
        value = jnp.concatenate([wide[half, : samples * height * kept] for half in range(2)], axis=1)
        slope_ref[...] = gelu_slope(value).reshape(slope_ref.shape)
    half = height // 2
    for part in range(2):
        values = input_ref[:, part * half : (part + 1) * half].reshape(samples, half * breadth, LANES)
        halo_ref[:, : half * breadth, part * LANES : (part + 1) * LANES] = values
    halo_ref[:, half * breadth :] = cells[:, : 6 * height].astype(BF)


def near_parts(pre_second, pre_first, encoder_input, low, high):
    samples, height, breadth, depth = pre_second.shape
    kept = breadth + 2 * EDGE
    slope = jax.ShapeDtypeStruct((samples, height, kept, depth), F32)
    return run(
        "near_parts",
        near_kernel,
        [slope, slope, jax.ShapeDtypeStruct((samples, 6 * height + height * breadth // 2, depth), BF)],
        [pre_second, pre_first, encoder_input, low, high],
        [
            pltpu.VMEM((2, (samples * height + 8) * kept, LANES), F32),
            pltpu.VMEM((samples, 6 * height + 8, depth), F32),
        ],
    )


def far_kernel(first_ref, tile_second, tile_first, slope_second, slope_first, act_out, wide, act):
    samples, height, breadth, depth = first_ref.shape
    kept = breadth + 2 * EDGE
    lat = lax.axis_index("lat")
    for source_ref, slope_ref in ((tile_second, slope_second), (tile_first, slope_first)):
        wide[...] = jnp.zeros(wide.shape, F32)
        for s in range(samples):
            for half in range(2):
                for r in range(height):
                    at = (s * height + r) * kept + EDGE
                    wide[half, at : at + breadth, :] = source_ref[s, r, :, half * LANES : (half + 1) * LANES].astype(F32)
        value = jnp.concatenate([wide[0], wide[1]], axis=1)
        slope_ref[...] = gelu_slope(value).reshape(slope_ref.shape)
    own, other = pl.ds(height * lat, height), pl.ds(height * (1 - lat), height)
    act[:, own] = gelu_value(first_ref[...].astype(F32))
    act[:, other] = gelu_value(tile_first[...].astype(F32))
    act_out[...] = act[...].reshape(act_out.shape[1], depth).T.astype(BF)


def far_parts(pre_first, tile_second, tile_first):
    samples, height, breadth, depth = pre_first.shape
    kept = breadth + 2 * EDGE
    slope = jax.ShapeDtypeStruct((samples, height, kept, depth), F32)
    return run(
        "far_parts",
        far_kernel,
        [slope, slope, jax.ShapeDtypeStruct((depth, 2 * samples * height * breadth), BF)],
        [pre_first, tile_second, tile_first],
        [
            pltpu.VMEM((2, samples * height * kept, LANES), F32),
            pltpu.VMEM((samples, 2 * height, breadth, depth), F32),
        ],
    )


def put_slopes(sample, slope, near_ref, far_ref, halo_ref, width, first_cell):
    _, height, kept, _ = near_ref.shape
    lat = lax.axis_index("lat")
    other = pl.ds(height * (1 - lat), height)
    slope[pl.ds(height * lat, height)] = near_ref[sample]
    slope[other] = far_ref[sample]
    beside = gelu_slope(halo_ref[sample, halo_ref.shape[1] - 6 * height :].astype(F32))
    for side in range(2):
        for col in range(width):
            here = first_cell + (side * width + col) * height
            at = kept - EDGE + col if side else EDGE - width + col
            slope[other, at, :] = beside[here : here + height]


def globe_kernel(sample, near_ref, far_ref, halo_ref, total_ref, line_ref, cat_ref, moved_ref, latent, slope, wide):
    rows, kept, depth = total_ref.shape
    height = rows - 1
    tall = 2 * height
    breadth = kept - 2 * EDGE
    lat = lax.axis_index("lat")
    own = 8 + EDGE
    latent[...] = jnp.zeros(latent.shape, F32)
    latent[pl.ds((height - 1) * lat, rows)] = total_ref[...].astype(F32)
    latent[pl.ds((height - 1) * (1 - lat), rows)] += line_ref[...].astype(F32)
    put_slopes(sample, slope, near_ref, far_ref, halo_ref, 2, 0)
    wide[:, 8 : 8 + kept, :] = (latent[...] * slope[...]).astype(BF).astype(F32)
    for v in STEPS:
        lanes = slice((v + 1) * depth, (v + 2) * depth)
        cat_ref[1 : 1 + tall, :, lanes] = wide[:, 8 - v : 8 - v + kept, :].astype(BF)
        moved_ref[v + 1, 1 : 1 + tall] = wide[:, own - v : own - v + breadth, :].astype(BF)
    for row in (0, tall + 1):
        cat_ref[row] = jnp.zeros(cat_ref.shape[1:], BF)
        moved_ref[:, row] = jnp.zeros(moved_ref.shape[:1] + moved_ref.shape[2:], BF)


def globe(sample, total, line, near, far, halo):
    rows, kept, depth = total.shape
    tall, breadth = 2 * (rows - 1), kept - 2 * EDGE
    return run(
        "latent_grads",
        functools.partial(globe_kernel, sample),
        [
            jax.ShapeDtypeStruct((tall + 2, kept, 3 * depth), BF),
            jax.ShapeDtypeStruct((3, tall + 2, breadth, depth), BF),
        ],
        [near, far, halo, total, line],
        [
            pltpu.VMEM((tall, kept, depth), F32),
            pltpu.VMEM((tall, kept, depth), F32),
            pltpu.VMEM((tall, kept + 24, depth), F32),
        ],
    )


def band_rows(norm_factor, lefts, moved, mine_ref, other_ref):
    channels, cells = lefts[0].shape
    _, padded, breadth, depth = moved[0].shape
    tall = padded - 2
    lat = lax.axis_index("lat")
    core, _ = core_and_chip()
    half = channels // 2

    def put(parts, u, v, start, size):
        total = None
        for left, ref in zip(parts, moved):
            part = dot_plain(left, ref[v + 1, pl.ds(1 - u, tall)].reshape(cells, depth))
            total = part if total is None else total + part
        total = total * norm_factor
        lower, upper = total[:, :LANES], total[:, LANES:]
        here = pl.ds(pl.multiple_of(start, half), size)
        mine_ref[here, :] = jnp.where(core == 0, lower, upper).astype(BF)
        other_ref[here, :] = jnp.where(core == 0, upper, lower).astype(BF)

    for j in range(4):
        (u0, v0), (u1, v1) = (divmod(k, 3) for k in (j, 5 + j))
        put(lefts, u0 - 1 + lat * (u1 - u0), v0 - 1 + lat * (v1 - v0), lat * half + j * channels, channels)
    put([jnp.where(lat == 0, left[:half], left[half:]) for left in lefts], 0, 0, (1 - lat) * 4 * channels, half)


def second_band_kernel(norm_factor, act_ref, *refs):
    moved, (mine_ref, other_ref) = refs[:-2], refs[-2:]
    cells = act_ref.shape[1] // len(moved)
    lefts = [act_ref[:, s * cells : (s + 1) * cells] for s in range(len(moved))]
    band_rows(norm_factor, lefts, moved, mine_ref, other_ref)


def second_band(norm_factor, act, moved):
    half = jax.ShapeDtypeStruct((9 * act.shape[0] // 2, LANES), BF)
    return run("second_weight_grads", functools.partial(second_band_kernel, norm_factor), [half, half], [act, *moved])


def first_kernel(sample, cat_ref, near_ref, far_ref, halo_ref, weights_ref, moved_ref, slope, wide):
    padded, kept, triple = cat_ref.shape
    tall, depth = padded - 2, triple // 3
    breadth = kept - 2 * EDGE
    own = 8 + EDGE
    put_slopes(sample, slope, near_ref, far_ref, halo_ref, 1, 2 * tall)
    linear = None
    for u in STEPS:
        weights = jnp.concatenate([weights_ref[3 * (u + 1) + (v + 1)] for v in STEPS], axis=1)
        part = dot_last(cat_ref[1 - u : 1 - u + tall].reshape(tall * kept, triple), weights)
        linear = part if linear is None else linear + part
    wide[:, 8 : 8 + kept, :] = (linear.reshape(tall, kept, depth) * slope[...]).astype(BF).astype(F32)
    for v in STEPS:
        moved_ref[v + 1, 1 : 1 + tall] = wide[:, own - v : own - v + breadth, :].astype(BF)
    for row in (0, tall + 1):
        moved_ref[:, row] = jnp.zeros(moved_ref.shape[:1] + moved_ref.shape[2:], BF)


def first_grad(sample, cat, near, far, halo, w_second):
    padded, kept, triple = cat.shape
    tall, depth = padded - 2, triple // 3
    return run(
        "second_conv",
        functools.partial(first_kernel, sample),
        [jax.ShapeDtypeStruct((3, padded, kept - 2 * EDGE, depth), BF)],
        [cat, near, far, halo, w_second],
        [pltpu.VMEM((tall, kept, depth), F32), pltpu.VMEM((tall, kept + 16, depth), F32)],
    )[0]


def first_band_kernel(norm_factor, halo_ref, input_ref, *refs):
    moved, (mine_ref, other_ref, cells) = refs[:-3], refs[-3:]
    samples, height, breadth, channels = input_ref.shape
    lat = lax.axis_index("lat")
    cells[:, pl.ds(height * lat, height)] = input_ref[...].astype(F32)
    half = height // 2
    for part in range(2):
        values = halo_ref[:, : half * breadth, part * LANES : (part + 1) * LANES].astype(F32)
        cells[:, pl.ds(height * (1 - lat) + part * half, half)] = values.reshape(samples, half, breadth, LANES)
    lefts = [cells[s].reshape(2 * height * breadth, channels).T.astype(BF) for s in range(samples)]
    band_rows(norm_factor, lefts, moved, mine_ref, other_ref)


def first_band(norm_factor, halo, encoder_input, moved):
    samples, height, breadth, channels = encoder_input.shape
    half = jax.ShapeDtypeStruct((9 * channels // 2, LANES), BF)
    return run(
        "first_weight_grads",
        functools.partial(first_band_kernel, norm_factor),
        [half, half],
        [halo, encoder_input, *moved],
        [pltpu.VMEM((samples, 2 * height, breadth, channels), F32)],
    )


def input_band_kernel(w_first_ref, *refs):
    moved, out_ref = refs[:-1], refs[-1]
    _, height, breadth, channels = out_ref.shape
    depth = moved[0].shape[3]
    lat = lax.axis_index("lat")
    total = None
    for u in STEPS:
        weights = jnp.concatenate([w_first_ref[3 * (u + 1) + (v + 1)] for v in STEPS], axis=1)
        here = pl.ds(height * lat + 1 - u, height)
        left = [jnp.concatenate([ref[v + 1, here].reshape(-1, depth) for v in STEPS], axis=1) for ref in moved]
        part = dot_last(jnp.concatenate(left, axis=0), weights)
        total = part if total is None else total + part
    out_ref[...] = total.astype(BF).reshape(out_ref.shape)


def blocks_kernel(first_mine, first_got, second_mine, second_got, *outs):
    lon = lax.axis_index("lon")
    rows = first_mine.shape[1]
    for step, out_ref in enumerate(outs):
        block = partner(lon, step, len(outs))
        out_ref[:rows] = (first_mine[block].astype(F32) + first_got[block].astype(F32)).astype(BF)
        out_ref[rows:] = (second_mine[block].astype(F32) + second_got[block].astype(F32)).astype(BF)


def halves_kernel(mine_ref, other_ref, first_ref, second_ref):
    core, _ = core_and_chip()
    mine, other = mine_ref[...].astype(F32), other_ref[...].astype(F32)
    rows = mine.shape[0] // 3
    for part in range(2):
        value = jnp.where(core == part, mine, other)
        first_ref[pl.ds(part, rows, stride=2), :] = value[:rows]
        second_ref[pl.ds(part, 2 * rows, stride=2), :] = value[rows:]


def to_partner(array, step):
    count = lax.axis_size("lon")
    return lax.ppermute(array, "lon", [(partner(i, step, count), i) for i in range(count)])


def two_bands(head_grads, head_weights, encoder_input, pre_first, pre_second, w_first, w_second, norm_factor):
    samples, height, breadth, _ = encoder_input.shape
    columns = lax.axis_size("lon")
    tiles = [swap(array, "lat", 1) for array in (pre_second, pre_first)]
    to_right, to_left = pack(head_grads, pre_second, pre_first)
    low = around(to_right, "lon", 1)
    high = around(to_left, "lon", -1)
    head_grads, head_weights, w_second, pre_second, pre_first, encoder_input = stage(
        head_grads, head_weights, w_second, pre_second, pre_first, encoder_input
    )
    inside = inside_conv(head_grads, head_weights, 2 * samples)
    low, high, inside, *tiles = lax.optimization_barrier((low, high, inside, *tiles))
    heads_of = functools.partial(
        head_conv,
        head_grads=head_grads,
        high=high,
        head_weights=head_weights,
        slots=samples,
        rows=height + 1,
    )
    everyone = range(samples)
    own_other, cross_other = edges_conv(inside, low, high, head_weights)
    cross_got, own_got = swap(cross_other, "lead", 1), swap(own_other, "lead", 1)
    part_shape = jax.ShapeDtypeStruct(cross_got.shape[1:], BF)
    cross = run("core_sum", core_sum_kernel, [part_shape] * samples, [heads_of(False, True, None, low=low), cross_got])
    low_later, *cross = lax.optimization_barrier((low, *cross))
    own = run("core_sum", core_sum_kernel, [part_shape] * samples, [heads_of(False, False, None, low=low_later), own_got])
    near_second, near_first, halo = near_parts(pre_second, pre_first, encoder_input, low, high)
    cross[-1], halo = lax.optimization_barrier((cross[-1], halo))
    cross = [swap(part, "lead", 2) for part in cross]
    halo = swap(halo, "lat", 1)
    cross[-1], halo = lax.optimization_barrier((cross[-1], halo))
    totals = [run("chip_sum", sum_kernel, [part_shape], [own[s], cross[s]])[0] for s in everyone]
    lines = [swap(total, "lat", 1) for total in totals]
    far_second, far_first, act = far_parts(pre_first, *tiles)

    moved_second, moved_first = [], []
    for s in everyone:
        cat, moved = globe(s, totals[s], lines[s], near_second, far_second, halo)
        moved_second.append(moved)
        if s < samples - 1:
            moved_first.append(first_grad(s, cat, near_first, far_first, halo, w_second))
            near_second, moved_first[s] = lax.optimization_barrier((near_second, moved_first[s]))
    second_mine, second_other = second_band(norm_factor, act, moved_second)
    second_got = swap(second_other, "lead", 1)
    moved_first.append(first_grad(samples - 1, cat, near_first, far_first, halo, w_second))
    first_mine, first_other = first_band(norm_factor, halo, encoder_input, moved_first)
    first_got = swap(first_other, "lead", 1)
    input_grad = run(
        "input_conv", input_band_kernel, [jax.ShapeDtypeStruct(encoder_input.shape, BF)], [w_first, *moved_first]
    )[0]

    blocks = [t.reshape(columns, -1, LANES) for t in (first_mine, first_got, second_mine, second_got)]
    rows = blocks[0].shape[1]
    share_shape = jax.ShapeDtypeStruct((3 * rows, LANES), BF)
    shares = run("blocks", blocks_kernel, [share_shape] * columns, blocks)
    parts = [to_partner(shares[step], step) for step in ((2, 1, 3) if columns == 4 else range(1, columns))]
    early = run("share", sum_kernel, [share_shape], [shares[0], *parts[:-1]])[0]
    early_got, late_got = swap(early, "lead", 2), swap(parts[-1], "lead", 2)
    both = run("chips", sum_kernel, [share_shape], [early, parts[-1], early_got, late_got])[0]
    result_first, result_second = run(
        "cores",
        halves_kernel,
        [jax.ShapeDtypeStruct((2 * rows, LANES), F32), jax.ShapeDtypeStruct((4 * rows, LANES), F32)],
        [both, swap(both, "lead", 1)],
    )
    return input_grad, result_first.reshape(-1), result_second.reshape(-1)


def core_sum_kernel(mine_ref, got_ref, *outs):
    for slot, out_ref in enumerate(outs):
        out_ref[...] = (mine_ref[slot].astype(F32) + got_ref[slot].astype(F32)).astype(BF)


def general(head_grads, head_weights, encoder_input, pre_first, pre_second, w_first, w_second, norm_factor):
    samples, height, breadth, _ = encoder_input.shape
    bands, columns = lax.axis_size("lat"), lax.axis_size("lon")
    to_right, to_left = pack(head_grads, pre_second, pre_first)
    to_right, to_left, to_cross = lax.optimization_barrier((to_right, to_left, pre_first))
    low = around(to_right, "lon", 1)
    high = around(to_left, "lon", -1)
    act_got = activated(swap(to_cross, "lead", 2))
    head_grads, head_weights, w_second, pre_second, pre_first, encoder_input = stage(
        head_grads, head_weights, w_second, pre_second, pre_first, encoder_input
    )
    low, high, act_got = lax.optimization_barrier((low, high, act_got))

    steps = [1, -1]
    heads_of = functools.partial(head_conv, head_grads=head_grads, high=high, head_weights=head_weights, slots=samples, rows=height + 2)
    got_cross = swap(heads_of(True, True, None, low=low), "lead", 1)
    got_own = swap(heads_of(True, False, None, low=low), "lead", 1)
    cross, *angles = spread_cross(heads_of(False, True, None, low=low), got_cross, len(steps))
    low_later, cross, *angles = lax.optimization_barrier((low, cross, *angles))
    cross = swap(cross, "lead", 2)
    angles = [corner(angle, step) for angle, step in zip(angles, steps)]
    second, first, slope_second, slope_first, act, cells_in = saved(pre_second, pre_first, encoder_input, low, high)
    own, *lines = spread_own(heads_of(False, False, None, low=low_later), got_own, second, first, len(steps))
    lines = [swap(line, "lat", 1) if step is None else around(line, "lat", step, False) for line, step in zip(lines, steps)]
    strips = [strip for pair in zip(lines, angles) for strip in pair]

    grad, away, slope = latent_grads(len(steps), bands, own, cross, strips, slope_second, slope_first)
    grad_got = swap(away, "lead", 2)
    moved, first_mine, first_other = encoder(norm_factor, bands, grad, slope, cells_in, w_second)
    input_grad = input_conv(moved, w_first)
    first_got = swap(first_other, "lead", 1)
    second_mine, second_other = second_grads(norm_factor, bands * columns, grad, grad_got, act, act_got)
    second_got = swap(second_other, "lead", 1)

    first_terms = [pairwise([first_mine, first_got], bands)]
    second_terms = [pairwise([second_mine, second_got], bands)]
    first_came = swap(other_band(first_terms, columns), "lat", 1)
    second_came = swap(other_band(second_terms, columns), "lat", 1)
    blocks = [t.reshape(2, columns, -1, LANES) for t in first_terms + second_terms]
    rows = blocks[0].shape[2]
    share_shape = jax.ShapeDtypeStruct((2, rows, LANES), BF)
    shares = run("own_band", own_band_kernel, [share_shape] * columns, blocks + [first_came, second_came])
    parts = [to_partner(shares[step], step) for step in ((2, 1, 3) if columns == 4 else range(1, columns))]
    share = run("share", sum_kernel, [share_shape], [shares[0], *parts])[0]
    both = run("chips", chips_kernel, [jax.ShapeDtypeStruct((3, rows, LANES), BF)], [share, swap(share, "lead", 2)])[0]
    result_first, result_second = run(
        "cores",
        cores_kernel,
        [jax.ShapeDtypeStruct((2 * rows, LANES), F32), jax.ShapeDtypeStruct((4 * rows, LANES), F32)],
        [both, swap(both, "lead", 1)],
    )
    return input_grad, result_first.reshape(-1), result_second.reshape(-1)


def per_device(head_grads, head_weights, encoder_input, pre_first, pre_second, w_first, w_second):
    samples, height, breadth, channels = encoder_input.shape
    bands, columns = lax.axis_size("lat"), lax.axis_size("lon")
    cells_total = samples * lax.axis_size("lead") * height * bands * breadth * columns
    norm_factor = 1.0 / math.sqrt(cells_total)
    plan = two_bands if bands == 2 and 9 * channels // (bands * columns) % 16 == 0 else general
    return plan(head_grads, head_weights, encoder_input, pre_first, pre_second, w_first, w_second, norm_factor)


def solution(mesh):
    in_specs = (
        P("lead", None, "lat", "lon", None),
        P("lead", None, None, None),
        P("lead", "lat", "lon", None),
        P("lead", "lat", "lon", None),
        P("lead", "lat", "lon", None),
        P(),
        P(),
    )
    out_specs = (P("lead", "lat", "lon", None), P(("lat", "lon")), P(("lat", "lon")))
    return jax.shard_map(
        per_device, mesh=mesh, in_specs=in_specs, out_specs=out_specs, check_vma=False
    )
```

```python
import functools
import math

import jax
import jax.numpy as jnp
from jax import lax
from jax.experimental import pallas as pl
from jax.experimental.pallas import tpu as pltpu
from jax.sharding import PartitionSpec as P

BF = jnp.bfloat16
F32 = jnp.float32
STEPS = (-1, 0, 1)
EDGE = 4
LANES = 128
VMEM_BYTES = 24 * 1024 * 1024


def erf_part(values):
    return 0.5 * (1.0 + lax.erf(values * 0.7071067811865476))


def gelu_slope(values):
    return erf_part(values) + values * jnp.exp(-0.5 * values * values) * 0.3989422804014327


def gelu_value(values):
    return values * erf_part(values)


def dot_last(left, right):
    return lax.dot_general(left, right, (((1,), (1,)), ((), ())), preferred_element_type=F32)


def dot_plain(left, right):
    return lax.dot_general(left, right, (((1,), (0,)), ((), ())), preferred_element_type=F32)


def core_and_chip():
    lead = lax.axis_index("lead")
    return lax.rem(lead, 2), lax.div(lead, 2)


def run(name, kernel, out_shape, arrays, scratch=(), flops=0, far=False):
    specs = [pl.BlockSpec(memory_space=pltpu.HBM if far else pltpu.VMEM)] * len(arrays)
    if far:
        arrays = [pltpu.with_memory_space_constraint(a, pltpu.HBM) for a in arrays]
    touched = sum(a.size * a.dtype.itemsize for a in arrays)
    touched += sum(math.prod(s.shape) * s.dtype.itemsize for s in out_shape)
    return pl.pallas_call(
        kernel,
        name=name,
        out_shape=out_shape,
        in_specs=specs,
        out_specs=[pl.BlockSpec(memory_space=pltpu.VMEM)] * len(out_shape),
        scratch_shapes=list(scratch),
        compiler_params=pltpu.CompilerParams(vmem_limit_bytes=VMEM_BYTES),
        cost_estimate=pl.CostEstimate(flops=1, bytes_accessed=1, transcendentals=0),
    )(*arrays)


def pack_kernel(grads_far, second_far, first_far, right_ref, left_ref, grads_near, second_near, first_near, edges, edges_wide, packed, sems):
    heads, batch, height, breadth, _ = grads_far.shape
    samples = second_far.shape[0]
    rows = 6 * height
    copies = []
    for side in range(2):
        columns = pl.ds(breadth - 16 if side == 0 else 0, 16)
        for j, (far, near) in enumerate(((grads_far, grads_near), (second_far, second_near), (first_far, first_near))):
            source = far.at[:, :, :, columns, :] if j == 0 else far.at[:, :, columns, :]
            copies.append(pltpu.make_async_copy(source, near.at[side], sems.at[side, j]))
            copies[-1].start()
    for copy in copies:
        copy.wait()
    for side, out_ref in ((0, right_ref), (1, left_ref)):
        start = 8 if side == 0 else 0
        grads_ref, second_ref, first_ref = grads_near.at[side], second_near.at[side], first_near.at[side]
        for h in range(heads):
            for b in range(batch):
                block = grads_ref[h, b].astype(F32)[:, start : start + 8, :]
                edges[(h * batch + b) * height * 8 : (h * batch + b + 1) * height * 8, :] = block.reshape(height * 8, LANES)
        for j, ref in enumerate((second_ref, first_ref)):
            for s in range(samples):
                block = ref[s].astype(F32)[:, start : start + 8, :]
                at = (j * samples + s) * height * 8
                for half in range(2):
                    lanes = slice(half * LANES, (half + 1) * LANES)
                    edges_wide[half, at : at + height * 8, :] = block[:, :, lanes].reshape(height * 8, LANES)
        for b in range(batch):
            for col in range(3):
                inner = 5 + col if side == 0 else col
                for h in range(heads):
                    at = b * rows + (col * 2 + h) * height
                    packed[at : at + height, :] = edges[pl.ds((h * batch + b) * height * 8 + inner, height, stride=8), :]
        for s in range(samples):
            for q in range(3):
                j, col, width = (0, q, 2) if q < 2 else (1, 0, 1)
                inner = 8 - width + col if side == 0 else col
                for half in range(2):
                    at = (batch + s) * rows + (q * 2 + half) * height
                    packed[at : at + height, :] = edges_wide[
                        half, pl.ds((j * samples + s) * height * 8 + inner, height, stride=8), :
                    ]
        out_ref[...] = packed[: (batch + samples) * rows].astype(BF).reshape(out_ref.shape)


def pack(head_grads, pre_second, pre_first):
    heads, batch, height, _, _ = head_grads.shape
    samples = pre_second.shape[0]
    shape = jax.ShapeDtypeStruct((batch + samples, 6 * height, LANES), BF)
    return run(
        "pack_columns",
        pack_kernel,
        [shape, shape],
        [head_grads, pre_second, pre_first],
        [
            pltpu.VMEM((2, heads, batch, height, 16, LANES), BF),
            pltpu.VMEM((2, samples, height, 16, 2 * LANES), BF),
            pltpu.VMEM((2, samples, height, 16, 2 * LANES), BF),
            pltpu.VMEM((heads * batch * height * 8 + 64, LANES), F32),
            pltpu.VMEM((2, 2 * samples * height * 8 + 64, LANES), F32),
            pltpu.VMEM(((batch + samples) * 6 * height + 16, LANES), F32),
            pltpu.SemaphoreType.DMA((2, 3)),
        ],
        far=True,
    )


def stage_kernel(*refs):
    count = len(refs) // 2
    sems = refs[-1]
    copies = [pltpu.make_async_copy(refs[i], refs[count + i], sems.at[i]) for i in range(count)]
    for copy in copies:
        copy.start()
    for copy in copies:
        copy.wait()


def stage(*arrays):
    shapes = [pltpu.VMEM(a.shape, a.dtype) for a in arrays]
    return run("stage", stage_kernel, shapes, list(arrays), [pltpu.SemaphoreType.DMA((len(arrays),))], far=True, flops=1 << 30)


def heads_kernel(other_core, other_chip, sample, samples, grads_ref, low_ref, high_ref, weights_ref, out_ref, wide, shifted, total):
    heads, batch, height, breadth, _ = grads_ref.shape
    slots, _, kept, depth = out_ref.shape
    pitch = kept + 16
    own = 8 + EDGE
    core, chip = core_and_chip()
    core = 1 - core if other_core else core
    for slot in range(slots):
        if sample is None:
            group, s = 1 - chip if other_chip else chip, slot
        else:
            group, s = 1 - chip if slot % 2 else chip, sample + slot // 2
        b = (2 * group + core) * samples + s
        low = low_ref[b].astype(F32)
        high = high_ref[b].astype(F32)
        for r in range(height):
            at = (slot * height + r) * pitch + own
            for h in range(heads):
                wide[h, at : at + breadth, :] = grads_ref[h, b, r].astype(F32)
        for col in range(3):
            for h in range(heads):
                here = (col * 2 + h) * height
                at = slot * height * pitch + own + col
                wide[h, pl.ds(at - 3, height, stride=pitch), :] = low[here : here + height]
                wide[h, pl.ds(at + breadth, height, stride=pitch), :] = high[here : here + height]
        for v in STEPS:
            for h in range(heads):
                starts = [(slot * height + r) * pitch + 8 - v for r in range(height)]
                moved = jnp.concatenate([wide[h, at : at + kept, :] for at in starts], axis=0).astype(BF)
                lane = ((v + 1) * heads + h) * LANES
                shifted[slot * height * kept : (slot + 1) * height * kept, lane : lane + LANES] = moved
    total[:, height:, :, :] = jnp.zeros((slots, 2, kept, depth), F32)
    for u in STEPS:
        weights = jnp.concatenate(
            [weights_ref[h, 3 * (u + 1) + (v + 1)] for v in STEPS for h in range(heads)], axis=1
        )
        part = dot_last(shifted[...], weights).reshape(slots, height, kept, depth)
        if u == -1:
            total[:, :height] = part
        else:
            total[:, 1 + u : 1 + u + height] += part
    if out_ref.shape[1] == height + 2:
        out_ref[...] = total[...].astype(BF)
    else:
        out_ref[...] = total[:, pl.ds(1 - lax.axis_index("lat"), height + 1)].astype(BF)


def head_conv(other_core, other_chip, sample, head_grads, low, high, head_weights, slots, rows):
    samples = head_grads.shape[1] // lax.axis_size("lead")
    heads, batch, height, breadth, _ = head_grads.shape
    depth = head_weights.shape[2]
    kept = breadth + 2 * EDGE
    return run(
        "head_conv",
        functools.partial(heads_kernel, other_core, other_chip, sample, samples),
        [jax.ShapeDtypeStruct((slots, rows, kept, depth), BF)],
        [head_grads, low, high, head_weights],
        [
            pltpu.VMEM((heads, (slots * height + 8) * (kept + 16), LANES), F32),
            pltpu.VMEM((slots * height * kept, 3 * heads * LANES), BF),
            pltpu.VMEM((slots, height + 2, kept, depth), F32),
        ],
        flops=2 * slots * height * kept * 9 * heads * LANES * depth,
    )[0]


def inside_kernel(samples, grads_ref, weights_ref, total_ref, wide, shifted):
    heads, _, height, breadth, _ = grads_ref.shape
    slots, _, kept, depth = total_ref.shape
    pitch = kept + 16
    own = 8 + EDGE
    core, chip = core_and_chip()
    blank = jnp.zeros((height, LANES), F32)
    for slot in range(slots):
        group, s = 1 - chip if slot % 2 else chip, slot // 2
        b = (2 * group + 1 - core) * samples + s
        for h in range(heads):
            for r in range(height):
                at = (slot * height + r) * pitch + own
                wide[h, at : at + breadth, :] = grads_ref[h, b, r].astype(F32)
            for col in range(3):
                at = slot * height * pitch + own + col
                wide[h, pl.ds(at - 3, height, stride=pitch), :] = blank
                wide[h, pl.ds(at + breadth, height, stride=pitch), :] = blank
            for v in STEPS:
                starts = [(slot * height + r) * pitch + 8 - v for r in range(height)]
                moved = jnp.concatenate([wide[h, at : at + kept, :] for at in starts], axis=0).astype(BF)
                lane = ((v + 1) * heads + h) * LANES
                shifted[slot * height * kept : (slot + 1) * height * kept, lane : lane + LANES] = moved
    total_ref[:, height:, :, :] = jnp.zeros((slots, 2, kept, depth), F32)
    for u in STEPS:
        weights = jnp.concatenate(
            [weights_ref[h, 3 * (u + 1) + (v + 1)] for v in STEPS for h in range(heads)], axis=1
        )
        part = dot_last(shifted[...], weights).reshape(slots, height, kept, depth)
        if u == -1:
            total_ref[:, :height] = part
        else:
            total_ref[:, 1 + u : 1 + u + height] += part


def edges_kernel(samples, inside_ref, low_ref, high_ref, weights_ref, own_out, cross_out, wide, shifted, total):
    slots, rows, kept, depth = inside_ref.shape
    height, heads, pitch = rows - 2, weights_ref.shape[0], 24
    core, chip = core_and_chip()
    wide[...] = jnp.zeros(wide.shape, F32)
    total[...] = inside_ref[...]
    for side, packed_ref in ((0, low_ref), (1, high_ref)):
        for slot in range(slots):
            group, s = 1 - chip if slot % 2 else chip, slot // 2
            packed = packed_ref[(2 * group + 1 - core) * samples + s].astype(F32)
            first = (side * slots + slot) * height
            for h in range(heads):
                for col in range(3):
                    here = (col * 2 + h) * height
                    at = first * pitch + 9 + 3 * side + col
                    wide[h, pl.ds(at, height, stride=pitch), :] = packed[here : here + height]
                for v in STEPS:
                    starts = [(first + r) * pitch + 8 - v for r in range(height)]
                    moved = jnp.concatenate([wide[h, at : at + 8, :] for at in starts], axis=0).astype(BF)
                    lane = ((v + 1) * heads + h) * LANES
                    shifted[first * 8 : (first + height) * 8, lane : lane + LANES] = moved
    for u in STEPS:
        weights = jnp.concatenate(
            [weights_ref[h, 3 * (u + 1) + (v + 1)] for v in STEPS for h in range(heads)], axis=1
        )
        part = dot_last(shifted[...], weights).reshape(2, slots, height, 8, depth)
        total[:, 1 + u : 1 + u + height, :8] += part[0]
        total[:, 1 + u : 1 + u + height, kept - 8 :] += part[1]
    here = pl.ds(1 - lax.axis_index("lat"), height + 1)
    for s in range(samples):
        own_out[s] = total[2 * s, here].astype(BF)
        cross_out[s] = total[2 * s + 1, here].astype(BF)


def inside_conv(head_grads, head_weights, slots):
    samples = head_grads.shape[1] // lax.axis_size("lead")
    heads, _, height, breadth, _ = head_grads.shape
    kept = breadth + 2 * EDGE
    return run(
        "head_conv_inside",
        functools.partial(inside_kernel, samples),
        [jax.ShapeDtypeStruct((slots, height + 2, kept, head_weights.shape[2]), F32)],
        [head_grads, head_weights],
        [
            pltpu.VMEM((heads, (slots * height + 8) * (kept + 16), LANES), F32),
            pltpu.VMEM((slots * height * kept, 3 * heads * LANES), BF),
        ],
    )[0]


def edges_conv(inside, low, high, head_weights):
    slots, rows, kept, depth = inside.shape
    samples, heads, height = slots // 2, head_weights.shape[0], rows - 2
    return run(
        "head_conv_edges",
        functools.partial(edges_kernel, samples),
        [jax.ShapeDtypeStruct((samples, rows - 1, kept, depth), BF)] * 2,
        [inside, low, high, head_weights],
        [
            pltpu.VMEM((heads, (2 * slots * height + 8) * 24, LANES), F32),
            pltpu.VMEM((2 * slots * height * 8, 3 * heads * LANES), BF),
            pltpu.VMEM((slots, rows, kept, depth), F32),
        ],
    )


def saved_kernel(second_ref, first_ref, input_ref, low_ref, high_ref, second_out, first_out, slope_second, slope_first, act_out, input_out, wide):
    samples, height, breadth, depth = second_ref.shape
    kept = breadth + 2 * EDGE
    batch = low_ref.shape[0] - samples
    for ref, width, out_ref, slope_ref in (
        (second_ref, 2, second_out, slope_second),
        (first_ref, 1, first_out, slope_first),
    ):
        wide[...] = jnp.zeros(wide.shape, F32)
        for s in range(samples):
            for r in range(height):
                at = (s * height + r) * kept + EDGE
                for half in range(2):
                    lanes = slice(half * LANES, (half + 1) * LANES)
                    wide[half, at : at + breadth, :] = ref[s, r, :, lanes].astype(F32)
            low = low_ref[batch + s].astype(F32)
            high = high_ref[batch + s].astype(F32)
            for col in range(width):
                for half in range(2):
                    here = ((col if width == 2 else 2) * 2 + half) * height
                    at = s * height * kept + EDGE + col
                    wide[half, pl.ds(at - width, height, stride=kept), :] = low[here : here + height]
                    wide[half, pl.ds(at + breadth, height, stride=kept), :] = high[here : here + height]
        value = jnp.concatenate([wide[half, : samples * height * kept] for half in range(2)], axis=1)
        out_ref[...] = value.astype(BF).reshape(out_ref.shape)
        slope_ref[...] = gelu_slope(value).reshape(slope_ref.shape)
    active = gelu_value(first_ref[...].astype(F32).reshape(samples * height * breadth, depth)).astype(BF).astype(F32)
    act_out[...] = active.T.astype(BF)
    cells = input_ref[...].astype(F32).reshape(samples * height * breadth, input_ref.shape[3])
    input_out[...] = cells.T.astype(BF)


def saved(pre_second, pre_first, encoder_input, low, high):
    samples, height, breadth, depth = pre_second.shape
    kept = breadth + 2 * EDGE
    cells = samples * height * breadth
    return run(
        "saved_parts",
        saved_kernel,
        [
            jax.ShapeDtypeStruct((samples, height, kept, depth), BF),
            jax.ShapeDtypeStruct((samples, height, kept, depth), BF),
            jax.ShapeDtypeStruct((samples, height, kept, depth), F32),
            jax.ShapeDtypeStruct((samples, height, kept, depth), F32),
            jax.ShapeDtypeStruct((depth, cells), BF),
            jax.ShapeDtypeStruct((encoder_input.shape[3], cells), BF),
        ],
        [pre_second, pre_first, encoder_input, low, high],
        [pltpu.VMEM((2, (samples * height + 8) * kept, LANES), F32)],
    )


def goes_down(way, ways):
    return 1 - lax.axis_index("lat") if ways == 1 else 1 - way


def cross_kernel(mine_ref, got_ref, cross_ref, *strips):
    height = mine_ref.shape[1] - 2
    cross_ref[...] = (mine_ref[...].astype(F32) + got_ref[...].astype(F32)).astype(BF)
    for way, corner_ref in enumerate(strips):
        corner_ref[...] = cross_ref[:, pl.ds((height - 1) * goes_down(way, len(strips)), 3)]


def own_kernel(mine_ref, got_ref, second_ref, first_ref, own_ref, *strips):
    height = second_ref.shape[1]
    own_ref[...] = (mine_ref[...].astype(F32) + got_ref[...].astype(F32)).astype(BF)
    for way, line_ref in enumerate(strips):
        down = goes_down(way, len(strips))
        line_ref[:, 0:3] = own_ref[:, pl.ds((height - 1) * down, 3)]
        line_ref[:, 3:5] = second_ref[:, pl.ds((height - 2) * down, 2)]
        line_ref[:, 5:6] = first_ref[:, pl.ds((height - 1) * down, 1)]


def spread_cross(mine, got, ways):
    samples, _, kept, depth = mine.shape
    strip = jax.ShapeDtypeStruct((samples, 3, kept, depth), BF)
    return run("core_sum_cross", cross_kernel, [jax.ShapeDtypeStruct(mine.shape, BF)] + [strip] * ways, [mine, got])


def spread_own(mine, got, second, first, ways):
    samples, _, kept, depth = mine.shape
    strip = jax.ShapeDtypeStruct((samples, 6, kept, depth), BF)
    return run("core_sum_own", own_kernel, [jax.ShapeDtypeStruct(mine.shape, BF)] + [strip] * ways, [mine, got, second, first])


def latent_kernel(ways, bands, own_ref, cross_ref, *refs):
    strips, refs = refs[: 2 * ways], refs[2 * ways :]
    slope_second_ref, slope_first_ref, grad_ref, away_ref, slope_out, latent, slope_second = refs
    samples, rows, kept, depth = own_ref.shape
    height = rows - 2
    lat = lax.axis_index("lat")
    _, chip = core_and_chip()
    blank = jnp.zeros((samples, kept, depth), F32)
    latent[:, 0] = blank
    latent[:, height + 3] = blank
    latent[:, 1 : height + 3] = own_ref[...].astype(F32) + cross_ref[...].astype(F32)
    slope_second[:, 2 : 2 + height] = slope_second_ref[...]
    slope_out[:, 1 : 1 + height] = slope_first_ref[...]
    for way in range(ways):
        line_ref, corner_ref = strips[2 * way], strips[2 * way + 1]
        below = 1 - lat if ways == 1 else way
        at = (height + 1) * below
        latent[:, pl.ds(at, 3)] += line_ref[:, 0:3].astype(F32) + corner_ref[...].astype(F32)
        slope_second[:, pl.ds((height + 2) * below, 2)] = gelu_slope(line_ref[:, 3:5].astype(F32))
        slope_out[:, pl.ds((height + 1) * below, 1)] = gelu_slope(line_ref[:, 5:6].astype(F32))
    for i in range(height + 4):
        row = lat * height + i - 2
        valid = jnp.logical_and(row >= 0, row < bands * height)
        value = latent[:, i] * slope_second[:, i]
        if i < 2 or i >= height + 2:
            value = jnp.where(valid, value, 0.0)
        grad_ref[:, i] = value.astype(BF)
        if 0 < i < height + 3:
            away_ref[:, i - 1] = jnp.where(chip == 0, value[:, :, LANES:], value[:, :, :LANES]).astype(BF)


def latent_grads(ways, bands, own, cross, strips, slope_second, slope_first):
    samples, rows, kept, depth = own.shape
    return run(
        "latent_grads",
        functools.partial(latent_kernel, ways, bands),
        [
            jax.ShapeDtypeStruct((samples, rows + 2, kept, depth), BF),
            jax.ShapeDtypeStruct((samples, rows, kept, LANES), BF),
            jax.ShapeDtypeStruct((samples, rows, kept, depth), F32),
        ],
        [own, cross, *strips, slope_second, slope_first],
        [
            pltpu.VMEM((samples, rows + 2, kept, depth), F32),
            pltpu.VMEM((samples, rows + 2, kept, depth), F32),
        ],
    )


def encoder_kernel(norm_factor, bands, grad_ref, slope_ref, input_ref, weights_ref, moved_out, mine_ref, other_ref, wide, cat, wide_first):
    samples, tall, kept, depth = grad_ref.shape
    rows = tall - 2
    height = rows - 2
    breadth = kept - 2 * EDGE
    lat = lax.axis_index("lat")
    core, _ = core_and_chip()
    own = 8 + EDGE
    wide[:, :, 8 : 8 + kept, :] = grad_ref[...].astype(F32)
    for v in STEPS:
        lanes = slice((v + 1) * depth, (v + 2) * depth)
        cat[:, :, :, lanes] = wide[:, :, 8 - v : 8 - v + kept + 8, :].astype(BF)
    linear = None
    for u in STEPS:
        weights = jnp.concatenate([weights_ref[3 * (u + 1) + (v + 1)] for v in STEPS], axis=1)
        left = cat[:, 1 - u : 1 - u + rows].reshape(samples * rows * (kept + 8), 3 * depth)
        part = dot_last(left, weights)
        linear = part if linear is None else linear + part
    linear = linear.reshape(samples, rows, kept + 8, depth)
    for i in range(rows):
        row = lat * height + i - 1
        valid = jnp.logical_and(row >= 0, row < bands * height)
        value = linear[:, i, :kept] * slope_ref[:, i]
        if i < 1 or i >= height + 1:
            value = jnp.where(valid, value, 0.0)
        wide_first[:, i, 8 : 8 + kept, :] = value.astype(BF).astype(F32)
    for v in STEPS:
        lanes = slice((v + 1) * depth, (v + 2) * depth)
        moved_out[:, :, :, lanes] = wide_first[:, :, own - v : own - v + breadth, :].astype(BF)
    for u in STEPS:
        right = moved_out[:, 1 - u : 1 - u + height].reshape(samples * height * breadth, 3 * depth)
        part = dot_plain(input_ref[...], right) * norm_factor
        for v in STEPS:
            k = 3 * (u + 1) + (v + 1)
            lower = part[:, (v + 1) * depth : (v + 1) * depth + LANES]
            upper = part[:, (v + 1) * depth + LANES : (v + 2) * depth]
            mine_ref[k] = jnp.where(core == 0, lower, upper).astype(BF)
            other_ref[k] = jnp.where(core == 0, upper, lower).astype(BF)


def encoder(norm_factor, bands, grad, slope, cells_in, w_second):
    samples, tall, kept, depth = grad.shape
    rows, height, breadth = tall - 2, tall - 4, kept - 2 * EDGE
    channels = cells_in.shape[0]
    half = jax.ShapeDtypeStruct((9, channels, LANES), BF)
    return run(
        "encoder_grads",
        functools.partial(encoder_kernel, norm_factor, bands),
        [jax.ShapeDtypeStruct((samples, rows, breadth, 3 * depth), BF), half, half],
        [grad, slope, cells_in, w_second],
        [
            pltpu.VMEM((samples, tall, kept + 24, depth), F32),
            pltpu.VMEM((samples, tall, kept + 8, 3 * depth), BF),
            pltpu.VMEM((samples, rows, kept + 16, depth), F32),
        ],
        flops=2 * 9 * depth * (samples * rows * (kept + 8) * depth + samples * height * breadth * channels),
    )


def second_kernel(norm_factor, shares, grad_ref, got_ref, act_ref, act_got_ref, *refs):
    full_ref, wide, cat = refs[-3:]
    samples, tall, kept, depth = grad_ref.shape
    rows, height, breadth = tall - 2, tall - 4, kept - 2 * EDGE
    core, chip = core_and_chip()
    own = 8 + EDGE
    lower = grad_ref[:, 1 : 1 + rows, :, :LANES].astype(F32)
    upper = grad_ref[:, 1 : 1 + rows, :, LANES:].astype(F32)
    wide[:samples, :, 8 : 8 + kept, :] = jnp.where(chip == 0, lower, upper)
    wide[samples:, :, 8 : 8 + kept, :] = got_ref[...].astype(F32)
    for v in STEPS:
        lanes = slice((v + 1) * LANES, (v + 2) * LANES)
        cat[:, :, :, lanes] = wide[:, :, own - v : own - v + breadth, :].astype(BF)
    cells = samples * height * breadth
    for u in STEPS:
        right = cat[:, 1 - u : 1 - u + height].reshape(2 * cells, 3 * LANES)
        part = dot_plain(act_ref[...], right[:cells]) + dot_plain(act_got_ref[...], right[cells:])
        part = part * norm_factor
        for v in STEPS:
            k = 3 * (u + 1) + (v + 1)
            full_ref[k * depth : (k + 1) * depth, :] = part[:, (v + 1) * LANES : (v + 2) * LANES].astype(BF)
    if len(refs) == 5:
        size = 9 * depth // shares // 2
        for i in range(shares):
            for out_ref, half in ((refs[0], core), (refs[1], 1 - core)):
                out_ref[i] = full_ref[pl.ds(pl.multiple_of((2 * i + half) * size, 16), size), :]


def second_grads(norm_factor, shares, grad, got, act, act_got):
    samples, tall, kept, depth = grad.shape
    rows, height, breadth = tall - 2, tall - 4, kept - 2 * EDGE
    size = 9 * depth // shares // 2
    inside = size % 16 == 0
    half = jax.ShapeDtypeStruct((shares, size, LANES), BF)
    scratch = [
        pltpu.VMEM((2 * samples, rows, kept + 16, LANES), F32),
        pltpu.VMEM((2 * samples, rows, breadth, 3 * LANES), BF),
    ]
    results = run(
        "second_weight_grads",
        functools.partial(second_kernel, norm_factor, shares),
        [half, half] if inside else [jax.ShapeDtypeStruct((9 * depth, LANES), BF)],
        [grad, got, act, act_got],
        [pltpu.VMEM((9 * depth, LANES), BF)] + scratch if inside else scratch,
        flops=2 * 9 * depth * LANES * 2 * samples * height * breadth,
    )
    if inside:
        return results
    halves = results[0].reshape(shares, 2, size, LANES)
    core, _ = core_and_chip()
    return [lax.dynamic_index_in_dim(halves, part, 1, keepdims=False) for part in (core, 1 - core)]


def act_kernel(source_ref, out_ref):
    samples, height, breadth, depth = source_ref.shape
    active = gelu_value(source_ref[...].astype(F32).reshape(samples * height * breadth, depth)).astype(BF).astype(F32)
    out_ref[...] = active.T.astype(BF)


def activated(source):
    samples, height, breadth, depth = source.shape
    return run("activated", act_kernel, [jax.ShapeDtypeStruct((depth, samples * height * breadth), BF)], [source])[0]


def other_band_kernel(*refs):
    band = 1 - lax.rem(lax.axis_index("lat"), 2)
    parts = [t[band].astype(F32) for t in refs[:-1]]
    refs[-1][...] = sum(parts[1:], parts[0]).astype(BF)


def partner(index, step, count):
    return index ^ step if count & (count - 1) == 0 else (index + step) % count


def own_band_kernel(*refs):
    columns = refs[0].shape[1]
    terms, came, outs = refs[: -columns - 2], refs[-columns - 2 : -columns], refs[-columns:]
    band, lon = lax.rem(lax.axis_index("lat"), 2), lax.axis_index("lon")
    for step in range(columns):
        block = partner(lon, step, columns)
        for layer in range(2):
            parts = [t[band, block].astype(F32) for t in terms[layer * len(terms) // 2 : (layer + 1) * len(terms) // 2]]
            outs[step][layer] = sum(parts, came[layer][block].astype(F32)).astype(BF)


def sum_kernel(*refs):
    total = refs[0][...].astype(F32)
    for ref in refs[1:-1]:
        total = total + ref[...].astype(F32)
    refs[-1][...] = total.astype(BF)


def input_kernel(moved_ref, w_first_ref, out_ref):
    samples, rows, breadth, triple = moved_ref.shape
    height = rows - 2
    total = None
    for u in STEPS:
        weights = jnp.concatenate([w_first_ref[3 * (u + 1) + (v + 1)] for v in STEPS], axis=1)
        part = dot_last(moved_ref[:, 1 - u : 1 - u + height].reshape(samples * height * breadth, triple), weights)
        total = part if total is None else total + part
    out_ref[...] = total.astype(BF).reshape(out_ref.shape)


def input_conv(moved, w_first):
    samples, rows, breadth, triple = moved.shape
    shape = (samples, rows - 2, breadth, w_first.shape[1])
    return run(
        "input_conv",
        input_kernel,
        [jax.ShapeDtypeStruct(shape, BF)],
        [moved, w_first],
        flops=2 * 3 * math.prod(shape) * triple,
    )[0]


def chips_kernel(mine_ref, cross_ref, out_ref):
    _, chip = core_and_chip()
    out_ref[0] = (mine_ref[0].astype(F32) + cross_ref[0].astype(F32)).astype(BF)
    out_ref[1] = jnp.where(chip == 0, mine_ref[1], cross_ref[1])
    out_ref[2] = jnp.where(chip == 0, cross_ref[1], mine_ref[1])


def cores_kernel(mine_ref, other_ref, first_ref, second_ref):
    core, _ = core_and_chip()
    rows = mine_ref.shape[1]
    mine, other = (ref[...].astype(F32) for ref in (mine_ref, other_ref))
    for part in range(2):
        value = jnp.where(core == part, mine, other)
        first_ref[pl.ds(part, rows, stride=2), :] = value[0]
        second_ref[pl.ds(2 * rows * part, rows, stride=2), :] = value[1]
        second_ref[pl.ds(2 * rows * part + 1, rows, stride=2), :] = value[2]


def swap(array, axis, flip):
    count = lax.axis_size(axis)
    return lax.ppermute(array, axis, [(i, i ^ flip) for i in range(count)])


def around(array, axis, step, periodic=True):
    count = lax.axis_size(axis)
    pairs = [(i, (i + step) % count) for i in range(count) if periodic or 0 <= i + step < count]
    return lax.ppermute(array, axis, pairs)


def corner(array, step):
    lead, lat = lax.axis_size("lead"), lax.axis_size("lat")
    pairs = []
    for a in range(lead):
        for b in range(lat):
            target = (b ^ 1) if step is None else b + step
            if 0 <= target < lat:
                pairs.append((a * lat + b, (a ^ 2) * lat + target))
    return lax.ppermute(array, ("lead", "lat"), pairs)


def other_band(terms, columns):
    shape = (columns, terms[0].size // LANES // columns // 2, LANES)
    return run("other_band", other_band_kernel, [jax.ShapeDtypeStruct(shape, BF)], [t.reshape(2, *shape) for t in terms])[0]


def pairwise(terms, bands):
    lat = lax.axis_index("lat")
    total = sum(t.reshape(-1, LANES).astype(F32) for t in terms).astype(BF)
    left = bands
    while left > 2:
        left //= 2
        bit = (lat // left) % 2
        halves = total.reshape(2, -1, LANES)
        send = lax.dynamic_index_in_dim(halves, 1 - bit, 0, keepdims=False)
        keep = lax.dynamic_index_in_dim(halves, bit, 0, keepdims=False)
        total = (keep.astype(F32) + swap(send, "lat", left).astype(F32)).astype(BF)
    return total


def near_kernel(second_ref, first_ref, input_ref, low_ref, high_ref, slope_second, slope_first, halo_ref, wide, cells):
    samples, height, breadth, depth = second_ref.shape
    kept = breadth + 2 * EDGE
    batch = low_ref.shape[0] - samples
    for ref, width, first_cell, slope_ref in ((second_ref, 2, 0, slope_second), (first_ref, 1, 4 * height, slope_first)):
        wide[...] = jnp.zeros(wide.shape, F32)
        for s in range(samples):
            for r in range(height):
                at = (s * height + r) * kept + EDGE
                for half in range(2):
                    wide[half, at : at + breadth, :] = ref[s, r, :, half * LANES : (half + 1) * LANES].astype(F32)
            for side, packed_ref in ((0, low_ref), (1, high_ref)):
                packed = packed_ref[batch + s].astype(F32)
                for col in range(width):
                    for half in range(2):
                        here = ((col if width == 2 else 2) * 2 + half) * height
                        value = packed[here : here + height]
                        at = s * height * kept + EDGE + col + (breadth if side else -width)
                        wide[half, pl.ds(at, height, stride=kept), :] = value
                        at = first_cell + (side * width + col) * height
                        cells[s, at : at + height, half * LANES : (half + 1) * LANES] = value
        value = jnp.concatenate([wide[half, : samples * height * kept] for half in range(2)], axis=1)
        slope_ref[...] = gelu_slope(value).reshape(slope_ref.shape)
    half = height // 2
    for part in range(2):
        values = input_ref[:, part * half : (part + 1) * half].reshape(samples, half * breadth, LANES)
        halo_ref[:, : half * breadth, part * LANES : (part + 1) * LANES] = values
    halo_ref[:, half * breadth :] = cells[:, : 6 * height].astype(BF)


def near_parts(pre_second, pre_first, encoder_input, low, high):
    samples, height, breadth, depth = pre_second.shape
    kept = breadth + 2 * EDGE
    slope = jax.ShapeDtypeStruct((samples, height, kept, depth), F32)
    return run(
        "near_parts",
        near_kernel,
        [slope, slope, jax.ShapeDtypeStruct((samples, 6 * height + height * breadth // 2, depth), BF)],
        [pre_second, pre_first, encoder_input, low, high],
        [
            pltpu.VMEM((2, (samples * height + 8) * kept, LANES), F32),
            pltpu.VMEM((samples, 6 * height + 8, depth), F32),
        ],
    )


def far_kernel(first_ref, tile_second, tile_first, slope_second, slope_first, act_out, wide, act):
    samples, height, breadth, depth = first_ref.shape
    kept = breadth + 2 * EDGE
    lat = lax.axis_index("lat")
    for source_ref, slope_ref in ((tile_second, slope_second), (tile_first, slope_first)):
        wide[...] = jnp.zeros(wide.shape, F32)
        for s in range(samples):
            for half in range(2):
                for r in range(height):
                    at = (s * height + r) * kept + EDGE
                    wide[half, at : at + breadth, :] = source_ref[s, r, :, half * LANES : (half + 1) * LANES].astype(F32)
        value = jnp.concatenate([wide[0], wide[1]], axis=1)
        slope_ref[...] = gelu_slope(value).reshape(slope_ref.shape)
    own, other = pl.ds(height * lat, height), pl.ds(height * (1 - lat), height)
    act[:, own] = gelu_value(first_ref[...].astype(F32))
    act[:, other] = gelu_value(tile_first[...].astype(F32))
    act_out[...] = act[...].reshape(act_out.shape[1], depth).T.astype(BF)


def far_parts(pre_first, tile_second, tile_first):
    samples, height, breadth, depth = pre_first.shape
    kept = breadth + 2 * EDGE
    slope = jax.ShapeDtypeStruct((samples, height, kept, depth), F32)
    return run(
        "far_parts",
        far_kernel,
        [slope, slope, jax.ShapeDtypeStruct((depth, 2 * samples * height * breadth), BF)],
        [pre_first, tile_second, tile_first],
        [
            pltpu.VMEM((2, samples * height * kept, LANES), F32),
            pltpu.VMEM((samples, 2 * height, breadth, depth), F32),
        ],
    )


def put_slopes(sample, slope, near_ref, far_ref, halo_ref, width, first_cell):
    _, height, kept, _ = near_ref.shape
    lat = lax.axis_index("lat")
    other = pl.ds(height * (1 - lat), height)
    slope[pl.ds(height * lat, height)] = near_ref[sample]
    slope[other] = far_ref[sample]
    beside = gelu_slope(halo_ref[sample, halo_ref.shape[1] - 6 * height :].astype(F32))
    for side in range(2):
        for col in range(width):
            here = first_cell + (side * width + col) * height
            at = kept - EDGE + col if side else EDGE - width + col
            slope[other, at, :] = beside[here : here + height]


def globe_kernel(sample, near_ref, far_ref, halo_ref, total_ref, line_ref, cat_ref, moved_ref, latent, slope, wide):
    rows, kept, depth = total_ref.shape
    height = rows - 1
    tall = 2 * height
    breadth = kept - 2 * EDGE
    lat = lax.axis_index("lat")
    own = 8 + EDGE
    latent[...] = jnp.zeros(latent.shape, F32)
    latent[pl.ds((height - 1) * lat, rows)] = total_ref[...].astype(F32)
    latent[pl.ds((height - 1) * (1 - lat), rows)] += line_ref[...].astype(F32)
    put_slopes(sample, slope, near_ref, far_ref, halo_ref, 2, 0)
    wide[:, 8 : 8 + kept, :] = (latent[...] * slope[...]).astype(BF).astype(F32)
    for v in STEPS:
        lanes = slice((v + 1) * depth, (v + 2) * depth)
        cat_ref[1 : 1 + tall, :, lanes] = wide[:, 8 - v : 8 - v + kept, :].astype(BF)
        moved_ref[v + 1, 1 : 1 + tall] = wide[:, own - v : own - v + breadth, :].astype(BF)
    for row in (0, tall + 1):
        cat_ref[row] = jnp.zeros(cat_ref.shape[1:], BF)
        moved_ref[:, row] = jnp.zeros(moved_ref.shape[:1] + moved_ref.shape[2:], BF)


def globe(sample, total, line, near, far, halo):
    rows, kept, depth = total.shape
    tall, breadth = 2 * (rows - 1), kept - 2 * EDGE
    return run(
        "latent_grads",
        functools.partial(globe_kernel, sample),
        [
            jax.ShapeDtypeStruct((tall + 2, kept, 3 * depth), BF),
            jax.ShapeDtypeStruct((3, tall + 2, breadth, depth), BF),
        ],
        [near, far, halo, total, line],
        [
            pltpu.VMEM((tall, kept, depth), F32),
            pltpu.VMEM((tall, kept, depth), F32),
            pltpu.VMEM((tall, kept + 24, depth), F32),
        ],
    )


def band_rows(norm_factor, lefts, moved, mine_ref, other_ref):
    channels, cells = lefts[0].shape
    _, padded, breadth, depth = moved[0].shape
    tall = padded - 2
    lat = lax.axis_index("lat")
    core, _ = core_and_chip()
    half = channels // 2

    def put(parts, u, v, start, size):
        total = None
        for left, ref in zip(parts, moved):
            part = dot_plain(left, ref[v + 1, pl.ds(1 - u, tall)].reshape(cells, depth))
            total = part if total is None else total + part
        total = total * norm_factor
        lower, upper = total[:, :LANES], total[:, LANES:]
        here = pl.ds(pl.multiple_of(start, half), size)
        mine_ref[here, :] = jnp.where(core == 0, lower, upper).astype(BF)
        other_ref[here, :] = jnp.where(core == 0, upper, lower).astype(BF)

    for j in range(4):
        (u0, v0), (u1, v1) = (divmod(k, 3) for k in (j, 5 + j))
        put(lefts, u0 - 1 + lat * (u1 - u0), v0 - 1 + lat * (v1 - v0), lat * half + j * channels, channels)
    put([jnp.where(lat == 0, left[:half], left[half:]) for left in lefts], 0, 0, (1 - lat) * 4 * channels, half)


def second_band_kernel(norm_factor, act_ref, *refs):
    moved, (mine_ref, other_ref) = refs[:-2], refs[-2:]
    cells = act_ref.shape[1] // len(moved)
    lefts = [act_ref[:, s * cells : (s + 1) * cells] for s in range(len(moved))]
    band_rows(norm_factor, lefts, moved, mine_ref, other_ref)


def second_band(norm_factor, act, moved):
    half = jax.ShapeDtypeStruct((9 * act.shape[0] // 2, LANES), BF)
    return run("second_weight_grads", functools.partial(second_band_kernel, norm_factor), [half, half], [act, *moved])


def first_kernel(sample, cat_ref, near_ref, far_ref, halo_ref, weights_ref, moved_ref, slope, wide):
    padded, kept, triple = cat_ref.shape
    tall, depth = padded - 2, triple // 3
    breadth = kept - 2 * EDGE
    own = 8 + EDGE
    put_slopes(sample, slope, near_ref, far_ref, halo_ref, 1, 2 * tall)
    linear = None
    for u in STEPS:
        weights = jnp.concatenate([weights_ref[3 * (u + 1) + (v + 1)] for v in STEPS], axis=1)
        part = dot_last(cat_ref[1 - u : 1 - u + tall].reshape(tall * kept, triple), weights)
        linear = part if linear is None else linear + part
    wide[:, 8 : 8 + kept, :] = (linear.reshape(tall, kept, depth) * slope[...]).astype(BF).astype(F32)
    for v in STEPS:
        moved_ref[v + 1, 1 : 1 + tall] = wide[:, own - v : own - v + breadth, :].astype(BF)
    for row in (0, tall + 1):
        moved_ref[:, row] = jnp.zeros(moved_ref.shape[:1] + moved_ref.shape[2:], BF)


def first_grad(sample, cat, near, far, halo, w_second):
    padded, kept, triple = cat.shape
    tall, depth = padded - 2, triple // 3
    return run(
        "second_conv",
        functools.partial(first_kernel, sample),
        [jax.ShapeDtypeStruct((3, padded, kept - 2 * EDGE, depth), BF)],
        [cat, near, far, halo, w_second],
        [pltpu.VMEM((tall, kept, depth), F32), pltpu.VMEM((tall, kept + 16, depth), F32)],
    )[0]


def first_band_kernel(norm_factor, halo_ref, input_ref, *refs):
    moved, (mine_ref, other_ref, cells) = refs[:-3], refs[-3:]
    samples, height, breadth, channels = input_ref.shape
    lat = lax.axis_index("lat")
    cells[:, pl.ds(height * lat, height)] = input_ref[...].astype(F32)
    half = height // 2
    for part in range(2):
        values = halo_ref[:, : half * breadth, part * LANES : (part + 1) * LANES].astype(F32)
        cells[:, pl.ds(height * (1 - lat) + part * half, half)] = values.reshape(samples, half, breadth, LANES)
    lefts = [cells[s].reshape(2 * height * breadth, channels).T.astype(BF) for s in range(samples)]
    band_rows(norm_factor, lefts, moved, mine_ref, other_ref)


def first_band(norm_factor, halo, encoder_input, moved):
    samples, height, breadth, channels = encoder_input.shape
    half = jax.ShapeDtypeStruct((9 * channels // 2, LANES), BF)
    return run(
        "first_weight_grads",
        functools.partial(first_band_kernel, norm_factor),
        [half, half],
        [halo, encoder_input, *moved],
        [pltpu.VMEM((samples, 2 * height, breadth, channels), F32)],
    )


def input_band_kernel(w_first_ref, *refs):
    moved, out_ref = refs[:-1], refs[-1]
    _, height, breadth, channels = out_ref.shape
    depth = moved[0].shape[3]
    lat = lax.axis_index("lat")
    total = None
    for u in STEPS:
        weights = jnp.concatenate([w_first_ref[3 * (u + 1) + (v + 1)] for v in STEPS], axis=1)
        here = pl.ds(height * lat + 1 - u, height)
        left = [jnp.concatenate([ref[v + 1, here].reshape(-1, depth) for v in STEPS], axis=1) for ref in moved]
        part = dot_last(jnp.concatenate(left, axis=0), weights)
        total = part if total is None else total + part
    out_ref[...] = total.astype(BF).reshape(out_ref.shape)


def blocks_kernel(first_mine, first_got, second_mine, second_got, *outs):
    lon = lax.axis_index("lon")
    rows = first_mine.shape[1]
    for step, out_ref in enumerate(outs):
        block = partner(lon, step, len(outs))
        out_ref[:rows] = (first_mine[block].astype(F32) + first_got[block].astype(F32)).astype(BF)
        out_ref[rows:] = (second_mine[block].astype(F32) + second_got[block].astype(F32)).astype(BF)


def halves_kernel(mine_ref, other_ref, first_ref, second_ref):
    core, _ = core_and_chip()
    mine, other = mine_ref[...].astype(F32), other_ref[...].astype(F32)
    rows = mine.shape[0] // 3
    for part in range(2):
        value = jnp.where(core == part, mine, other)
        first_ref[pl.ds(part, rows, stride=2), :] = value[:rows]
        second_ref[pl.ds(part, 2 * rows, stride=2), :] = value[rows:]


def to_partner(array, step):
    count = lax.axis_size("lon")
    return lax.ppermute(array, "lon", [(partner(i, step, count), i) for i in range(count)])


def two_bands(head_grads, head_weights, encoder_input, pre_first, pre_second, w_first, w_second, norm_factor):
    samples, height, breadth, _ = encoder_input.shape
    columns = lax.axis_size("lon")
    tiles = [swap(array, "lat", 1) for array in (pre_second, pre_first)]
    to_right, to_left = pack(head_grads, pre_second, pre_first)
    low = around(to_right, "lon", 1)
    high = around(to_left, "lon", -1)
    head_grads, head_weights, w_second, pre_second, pre_first, encoder_input = stage(
        head_grads, head_weights, w_second, pre_second, pre_first, encoder_input
    )
    inside = inside_conv(head_grads, head_weights, 2 * samples)
    low, high, inside, *tiles = lax.optimization_barrier((low, high, inside, *tiles))
    heads_of = functools.partial(
        head_conv,
        head_grads=head_grads,
        high=high,
        head_weights=head_weights,
        slots=samples,
        rows=height + 1,
    )
    everyone = range(samples)
    own_other, cross_other = edges_conv(inside, low, high, head_weights)
    cross_got, own_got = swap(cross_other, "lead", 1), swap(own_other, "lead", 1)
    part_shape = jax.ShapeDtypeStruct(cross_got.shape[1:], BF)
    cross = run("core_sum", core_sum_kernel, [part_shape] * samples, [heads_of(False, True, None, low=low), cross_got])
    low_later, *cross = lax.optimization_barrier((low, *cross))
    own = run("core_sum", core_sum_kernel, [part_shape] * samples, [heads_of(False, False, None, low=low_later), own_got])
    near_second, near_first, halo = near_parts(pre_second, pre_first, encoder_input, low, high)
    cross[-1], halo = lax.optimization_barrier((cross[-1], halo))
    cross = [swap(part, "lead", 2) for part in cross]
    halo = swap(halo, "lat", 1)
    cross[-1], halo = lax.optimization_barrier((cross[-1], halo))
    totals = [run("chip_sum", sum_kernel, [part_shape], [own[s], cross[s]])[0] for s in everyone]
    lines = [swap(total, "lat", 1) for total in totals]
    far_second, far_first, act = far_parts(pre_first, *tiles)

    moved_second, moved_first = [], []
    for s in everyone:
        cat, moved = globe(s, totals[s], lines[s], near_second, far_second, halo)
        moved_second.append(moved)
        if s < samples - 1:
            moved_first.append(first_grad(s, cat, near_first, far_first, halo, w_second))
            near_second, moved_first[s] = lax.optimization_barrier((near_second, moved_first[s]))
    second_mine, second_other = second_band(norm_factor, act, moved_second)
    second_got = swap(second_other, "lead", 1)
    moved_first.append(first_grad(samples - 1, cat, near_first, far_first, halo, w_second))
    first_mine, first_other = first_band(norm_factor, halo, encoder_input, moved_first)
    first_got = swap(first_other, "lead", 1)
    input_grad = run(
        "input_conv", input_band_kernel, [jax.ShapeDtypeStruct(encoder_input.shape, BF)], [w_first, *moved_first]
    )[0]

    blocks = [t.reshape(columns, -1, LANES) for t in (first_mine, first_got, second_mine, second_got)]
    rows = blocks[0].shape[1]
    share_shape = jax.ShapeDtypeStruct((3 * rows, LANES), BF)
    shares = run("blocks", blocks_kernel, [share_shape] * columns, blocks)
    parts = [to_partner(shares[step], step) for step in ((3, 1, 2) if columns == 4 else range(1, columns))]
    early = run("share", sum_kernel, [share_shape], [shares[0], *parts[:-1]])[0]
    early_got, late_got = swap(early, "lead", 2), swap(parts[-1], "lead", 2)
    both = run("chips", sum_kernel, [share_shape], [early, parts[-1], early_got, late_got])[0]
    result_first, result_second = run(
        "cores",
        halves_kernel,
        [jax.ShapeDtypeStruct((2 * rows, LANES), F32), jax.ShapeDtypeStruct((4 * rows, LANES), F32)],
        [both, swap(both, "lead", 1)],
    )
    return input_grad, result_first.reshape(-1), result_second.reshape(-1)


def core_sum_kernel(mine_ref, got_ref, *outs):
    for slot, out_ref in enumerate(outs):
        out_ref[...] = (mine_ref[slot].astype(F32) + got_ref[slot].astype(F32)).astype(BF)


def general(head_grads, head_weights, encoder_input, pre_first, pre_second, w_first, w_second, norm_factor):
    samples, height, breadth, _ = encoder_input.shape
    bands, columns = lax.axis_size("lat"), lax.axis_size("lon")
    to_right, to_left = pack(head_grads, pre_second, pre_first)
    to_right, to_left, to_cross = lax.optimization_barrier((to_right, to_left, pre_first))
    low = around(to_right, "lon", 1)
    high = around(to_left, "lon", -1)
    act_got = activated(swap(to_cross, "lead", 2))
    head_grads, head_weights, w_second, pre_second, pre_first, encoder_input = stage(
        head_grads, head_weights, w_second, pre_second, pre_first, encoder_input
    )
    low, high, act_got = lax.optimization_barrier((low, high, act_got))

    steps = [1, -1]
    heads_of = functools.partial(head_conv, head_grads=head_grads, high=high, head_weights=head_weights, slots=samples, rows=height + 2)
    got_cross = swap(heads_of(True, True, None, low=low), "lead", 1)
    got_own = swap(heads_of(True, False, None, low=low), "lead", 1)
    cross, *angles = spread_cross(heads_of(False, True, None, low=low), got_cross, len(steps))
    low_later, cross, *angles = lax.optimization_barrier((low, cross, *angles))
    cross = swap(cross, "lead", 2)
    angles = [corner(angle, step) for angle, step in zip(angles, steps)]
    second, first, slope_second, slope_first, act, cells_in = saved(pre_second, pre_first, encoder_input, low, high)
    own, *lines = spread_own(heads_of(False, False, None, low=low_later), got_own, second, first, len(steps))
    lines = [swap(line, "lat", 1) if step is None else around(line, "lat", step, False) for line, step in zip(lines, steps)]
    strips = [strip for pair in zip(lines, angles) for strip in pair]

    grad, away, slope = latent_grads(len(steps), bands, own, cross, strips, slope_second, slope_first)
    grad_got = swap(away, "lead", 2)
    moved, first_mine, first_other = encoder(norm_factor, bands, grad, slope, cells_in, w_second)
    input_grad = input_conv(moved, w_first)
    first_got = swap(first_other, "lead", 1)
    second_mine, second_other = second_grads(norm_factor, bands * columns, grad, grad_got, act, act_got)
    second_got = swap(second_other, "lead", 1)

    first_terms = [pairwise([first_mine, first_got], bands)]
    second_terms = [pairwise([second_mine, second_got], bands)]
    first_came = swap(other_band(first_terms, columns), "lat", 1)
    second_came = swap(other_band(second_terms, columns), "lat", 1)
    blocks = [t.reshape(2, columns, -1, LANES) for t in first_terms + second_terms]
    rows = blocks[0].shape[2]
    share_shape = jax.ShapeDtypeStruct((2, rows, LANES), BF)
    shares = run("own_band", own_band_kernel, [share_shape] * columns, blocks + [first_came, second_came])
    parts = [to_partner(shares[step], step) for step in ((2, 1, 3) if columns == 4 else range(1, columns))]
    share = run("share", sum_kernel, [share_shape], [shares[0], *parts])[0]
    both = run("chips", chips_kernel, [jax.ShapeDtypeStruct((3, rows, LANES), BF)], [share, swap(share, "lead", 2)])[0]
    result_first, result_second = run(
        "cores",
        cores_kernel,
        [jax.ShapeDtypeStruct((2 * rows, LANES), F32), jax.ShapeDtypeStruct((4 * rows, LANES), F32)],
        [both, swap(both, "lead", 1)],
    )
    return input_grad, result_first.reshape(-1), result_second.reshape(-1)


def per_device(head_grads, head_weights, encoder_input, pre_first, pre_second, w_first, w_second):
    samples, height, breadth, channels = encoder_input.shape
    bands, columns = lax.axis_size("lat"), lax.axis_size("lon")
    cells_total = samples * lax.axis_size("lead") * height * bands * breadth * columns
    norm_factor = 1.0 / math.sqrt(cells_total)
    plan = two_bands if bands == 2 and 9 * channels // (bands * columns) % 16 == 0 else general
    return plan(head_grads, head_weights, encoder_input, pre_first, pre_second, w_first, w_second, norm_factor)


def solution(mesh):
    in_specs = (
        P("lead", None, "lat", "lon", None),
        P("lead", None, None, None),
        P("lead", "lat", "lon", None),
        P("lead", "lat", "lon", None),
        P("lead", "lat", "lon", None),
        P(),
        P(),
    )
    out_specs = (P("lead", "lat", "lon", None), P(("lat", "lon")), P(("lat", "lon")))
    return jax.shard_map(
        per_device, mesh=mesh, in_specs=in_specs, out_specs=out_specs, check_vma=False
    )
```
